128 devices in a mesh: rows: 8 (over y, core), seq: 16 (over z, x).
Axes of the slice: x: 4, y: 4, z: 4, core: 2. Of those that a mesh axis runs over, the one named last changes fastest.
Arguments:
- tokens: bfloat16 [8, 2048, 2048], P('rows', 'seq'), may hold values from -6 to 6
- grad_out: bfloat16 [8, 2048, 2048], P('rows', 'seq'), may hold values from -6 to 6
- lengths: int32 [8, 4], P('rows'), may hold values from 1 to 1984, 2048 in all within a row
- ln1_gain: bfloat16 [2048], P(('rows', 'seq')), may hold values from 0.5 to 1.5
- ln1_bias: bfloat16 [2048], P(('rows', 'seq')), may hold values from -3 to 3
- w_qkv: bfloat16 [2048, 6144], P(('rows', 'seq')), may hold values from -0.125 to 0.125
- b_qv: bfloat16 [4096], P(('rows', 'seq')), may hold values from -4 to 4
- w_out: bfloat16 [2048, 2048], P(('rows', 'seq')), may hold values from -2 to 2
- b_out: bfloat16 [2048], P(('rows', 'seq')), may hold values from -4 to 4
- ln2_gain: bfloat16 [2048], P(('rows', 'seq')), may hold values from 0.5 to 1.5
- ln2_bias: bfloat16 [2048], P(('rows', 'seq')), may hold values from -3 to 3
- w_up: bfloat16 [2048, 8192], P(('rows', 'seq')), may hold values from -0.125 to 0.125
- b_up: bfloat16 [8192], P(('rows', 'seq')), may hold values from -6 to 6
- w_down: bfloat16 [8192, 2048], P(('rows', 'seq')), may hold values from -0.0625 to 0.0625
- b_down: bfloat16 [2048], P(('rows', 'seq')), may hold values from -4 to 4
Outputs:
- out: bfloat16 [8, 2048, 2048], P('rows', 'seq')
- grad_tokens: float32 [8, 2048, 2048], P('rows', 'seq')
- g_ln1_gain: float32 [2048], P(('rows', 'seq'))
- g_ln1_bias: float32 [2048], P(('rows', 'seq'))
- g_w_qkv: float32 [2048, 6144], P(('rows', 'seq'))
- g_b_qv: float32 [4096], P(('rows', 'seq'))
- g_w_out: float32 [2048, 2048], P(('rows', 'seq'))
- g_b_out: float32 [2048], P(('rows', 'seq'))
- g_ln2_gain: float32 [2048], P(('rows', 'seq'))
- g_ln2_bias: float32 [2048], P(('rows', 'seq'))
- g_w_up: float32 [2048, 8192], P(('rows', 'seq'))
- g_b_up: float32 [8192], P(('rows', 'seq'))
- g_w_down: float32 [8192, 2048], P(('rows', 'seq'))
- g_b_down: float32 [2048], P(('rows', 'seq'))
The draws below stay inside these ranges and needn't reach their ends.
Inputs may be any that keep to these rules, and one draw needn't show every extreme that they name: Each row's 4 lengths sum to 2048, and the longest is exactly 1984.
All inputs are finite; a program needn't handle non-finite values.
Results may differ from the reference program's by a relative error of at most 0.015.
Values may be sent and summed in bfloat16 or wider, within the bound.
A program may use at most 448 MiB of HBM per device.

```python
import math
import jax
import jax.numpy as jnp
import numpy as np
from jax import lax

D = 2048
HEADS = 16
HEAD = 128
FF = 8192
W = 256
BLK = 128
NDOC = 4
ROWS = 8
LEN = 2048


def shard_levels(rng, shape, split, low, top_value):
    def one(dim, parts):
        heights = jax.random.uniform(jax.random.fold_in(jax.random.fold_in(rng, 6), dim), (parts,), jnp.float32, low / len(split), top_value / len(split))
        return jnp.repeat(jnp.exp(heights), shape[dim] // parts).reshape((-1,) + (1,) * (len(shape) - dim - 1))

    loudness = one(*split[0])
    for cut in split[1:]:
        loudness = loudness * one(*cut)
    return loudness


def profile(amount, total, most, skew):
    weights = [(1 << 20) // math.isqrt(rank ** skew) + 1 for rank in range(2, amount + 1)]
    rest, given = total - most - (amount - 1), [1] * (amount - 1)
    while rest > 0:
        candidates = [i for i in range(amount - 1) if given[i] < most]
        mass, remaining = sum([weights[i] for i in candidates]), rest
        for i in candidates:
            extra = min(most - given[i], max(1, remaining * weights[i] // mass), rest)
            given[i] = given[i] + extra
            rest = rest - extra
    return np.array([most] + given)


def ragged(rng, count, total, reach, lean):
    if count == 2:
        one = jax.random.randint(rng, (), max(1, total - reach), min(reach, total - 1) + 1)
        return jnp.stack([one, total - one])
    sizes = jnp.asarray(profile(count, total, reach, lean), jnp.int32)
    twos = (count - 1) // 2
    source_of, taker = sizes[1:1 + 2 * twos:2], sizes[2:2 + 2 * twos:2]
    slack = jnp.minimum(source_of - 1, reach - taker)
    moved = jax.random.randint(jax.random.fold_in(rng, 1), (twos,), 0, 1 << 20) % (slack + 1)
    sizes = sizes.at[1:1 + 2 * twos:2].set(source_of - moved).at[2:2 + 2 * twos:2].set(taker + moved)
    return sizes[jax.random.permutation(jax.random.fold_in(rng, 2), count)]


def noise(key, extent, deviation, reach, pieces=(), kind=jnp.bfloat16):
    loudness = shard_levels(key, extent, pieces, -0.22, 0.18) if pieces else 1.0
    array = jax.random.normal(key, extent, jnp.float32) * deviation * loudness
    return jnp.minimum(jnp.maximum(array, -reach), reach).astype(kind)


def setup_inputs(seed: int = 0) -> dict:
    splits = jax.random.split(jax.random.key(seed), 16)
    tokens = noise(splits[0], (ROWS, LEN, D), 1.0, 6.0, ((0, 8), (1, 16)))
    grad_out = noise(splits[1], (ROWS, LEN, D), 1.0, 6.0, ((0, 8), (1, 16)))
    lengths = jax.vmap(lambda own: ragged(own, NDOC, LEN, LEN - BLK // 2, 0))(jax.random.split(splits[2], ROWS)).reshape((ROWS, NDOC)).astype(jnp.int32)
    ln1_gain = jnp.clip(1.0 + 0.1 * jax.random.normal(splits[3], (D,), jnp.float32), 0.5, 1.5).astype(jnp.bfloat16)
    ln1_bias = noise(splits[4], (D,), 0.2, 3.0, ((0, 128),))
    w_qkv = noise(splits[5], (D, 3 * D), D ** -0.5, 0.125, ((0, 128),))
    b_qv = noise(splits[6], (2 * D,), 0.3, 4.0, ((0, 128),))
    w_out = noise(splits[7], (D, D), (D // W) ** -0.5, 2.0, ((0, 128),))
    b_out = noise(splits[8], (D,), 0.3, 4.0, ((0, 128),))
    ln2_gain = jnp.clip(1.0 + 0.1 * jax.random.normal(splits[9], (D,), jnp.float32), 0.5, 1.5).astype(jnp.bfloat16)
    ln2_bias = noise(splits[10], (D,), 0.2, 3.0, ((0, 128),))
    w_up = noise(splits[11], (D, FF), D ** -0.5, 0.125, ((0, 128),))
    b_up = noise(splits[12], (FF,), 0.5, 6.0, ((0, 128),))
    w_down = noise(splits[13], (FF, D), FF ** -0.5, 0.0625, ((0, 128),))
    b_down = noise(splits[14], (D,), 0.3, 4.0, ((0, 128),))
    return dict(tokens=tokens, grad_out=grad_out, lengths=lengths, ln1_gain=ln1_gain, ln1_bias=ln1_bias, w_qkv=w_qkv, b_qv=b_qv, w_out=w_out, b_out=b_out, ln2_gain=ln2_gain, ln2_bias=ln2_bias, w_up=w_up, b_up=b_up, w_down=w_down, b_down=b_down)


HIGHEST = lax.Precision.HIGHEST
EPSILON = 1e-05
NEG_FILL = -1e+30

@jax.custom_vjp
def low(v):
    return lax.optimization_barrier(v.astype(jnp.bfloat16)).astype(jnp.float32)

@jax.custom_vjp
def low_back(v):
    return v

def low_keep(v):
    return (low(v), None)

def low_pass(kept, grad):
    return (grad,)

def back_keep(v):
    return (v, None)

def back_low(kept, grad):
    return (low(grad),)
low.defvjp(low_keep, low_pass)
low_back.defvjp(back_keep, back_low)

def layer_norm(values, gain, shift):
    center = lax.optimization_barrier(jnp.mean(values, axis=-1, keepdims=True))
    centred = values - center
    spread = lax.optimization_barrier(jnp.mean(centred * centred, axis=-1, keepdims=True))
    return centred * lax.rsqrt(spread + EPSILON) * gain + shift

def doc_number(positions, doc_ends):
    hits = (doc_ends[None, :] <= positions[:, None]).astype(jnp.int32)
    return lax.optimization_barrier(jnp.sum(hits, axis=1)).astype(jnp.int32)

def block_row(row_input, doc_ends, params):
    gain_one, bias_one, weight_qkv, bias_qv, weight_out, bias_out, gain_two, bias_two, weight_up, bias_up, weight_down, bias_down = params
    hidden_width = HEADS * HEAD
    reach_blocks = W // BLK
    key_span = (reach_blocks + 1) * BLK
    scale_factor = 1.0 / math.sqrt(HEAD)
    normed_one = low(layer_norm(row_input, gain_one, bias_one))
    zero_bias = jnp.zeros((hidden_width,), jnp.float32)
    full_bias = jnp.concatenate([bias_qv[:hidden_width], zero_bias, bias_qv[hidden_width:]])
    projected = low_back(low(jnp.dot(normed_one, weight_qkv, precision=HIGHEST) + full_bias))
    query = projected[:, :hidden_width].reshape(LEN, HEADS, HEAD)
    front_pad = jnp.zeros((reach_blocks * BLK, HEADS, HEAD), jnp.float32)
    key_pad = jnp.concatenate([front_pad, projected[:, hidden_width:2 * hidden_width].reshape(LEN, HEADS, HEAD)])
    value_pad = jnp.concatenate([front_pad, projected[:, 2 * hidden_width:].reshape(LEN, HEADS, HEAD)])

    def attend(block_id):
        q_block = lax.dynamic_slice_in_dim(query, block_id * BLK, BLK, 0)
        k_block = lax.dynamic_slice_in_dim(key_pad, block_id * BLK, key_span, 0)
        v_block = lax.dynamic_slice_in_dim(value_pad, block_id * BLK, key_span, 0)
        q_pos = block_id * BLK + jnp.arange(BLK, dtype=jnp.int32)
        k_pos = (block_id - reach_blocks) * BLK + jnp.arange(key_span, dtype=jnp.int32)
        q_doc = doc_number(q_pos, doc_ends)
        k_doc = doc_number(k_pos, doc_ends)
        visible = (q_doc[:, None] == k_doc[None, :]) & (k_pos[None, :] <= q_pos[:, None])
        visible = visible & (q_pos[:, None] - k_pos[None, :] < W) & (k_pos[None, :] >= 0)
        scores = low_back(jnp.einsum('qhd,khd->hqk', q_block, k_block, precision=HIGHEST) * scale_factor)
        masked = jnp.where(visible[None], scores, NEG_FILL)
        peak = lax.optimization_barrier(jnp.max(masked, axis=-1, keepdims=True))
        expo = jnp.exp(masked - peak)
        probs = low(expo / lax.optimization_barrier(jnp.sum(expo, axis=-1, keepdims=True)))
        return jnp.einsum('hqk,khd->qhd', probs, v_block, precision=HIGHEST)
    mixed = lax.map(jax.checkpoint(attend), jnp.arange(LEN // BLK, dtype=jnp.int32))
    mixed = low_back(low(mixed.reshape(LEN, hidden_width)))
    attn_branch = low_back(jnp.dot(mixed, weight_out, precision=HIGHEST) + bias_out)
    residual = row_input + attn_branch
    normed_two = low(layer_norm(residual, gain_two, bias_two))
    upper = low_back(jnp.dot(normed_two, weight_up, precision=HIGHEST) + bias_up)
    activated = low(jax.nn.gelu(upper, approximate=False))
    return residual + jnp.dot(activated, weight_down, precision=HIGHEST) + bias_down

def reference(tokens, grad_out, lengths, ln1_gain, ln1_bias, w_qkv, b_qv, w_out, b_out, ln2_gain, ln2_bias, w_up, b_up, w_down, b_down):
    params = tuple((item.astype(jnp.float32) for item in (ln1_gain, ln1_bias, w_qkv, b_qv, w_out, b_out, ln2_gain, ln2_bias, w_up, b_up, w_down, b_down)))
    inputs = tokens.astype(jnp.float32)
    doc_ends = jnp.cumsum(lengths, axis=1).astype(jnp.int32)

    def forward(row_inputs, weights):

        def one_row(paired):
            return block_row(paired[0], paired[1], weights)
        return lax.map(jax.checkpoint(one_row), (row_inputs, doc_ends))
    outputs, pullback = jax.vjp(forward, inputs, params)
    grad_inputs, grads = pullback(grad_out.astype(jnp.float32))
    return (outputs.astype(jnp.bfloat16), grad_inputs, grads[0], grads[1], grads[2], grads[3], grads[4], grads[5], grads[6], grads[7], grads[8], grads[9], grads[10], grads[11])
```

```python
import functools
import math

import jax
import jax.numpy as jnp
from jax import lax
from jax.experimental import pallas as pl
from jax.experimental.pallas import tpu as pltpu
from jax.sharding import Mesh, PartitionSpec as P

HEADS = 16
HEAD = 128
W = 256
EPSILON = 1e-05
NEG_FILL = -1e30

AXES = ("y", "core", "z", "x")
SIZE = {"y": 4, "core": 2, "z": 4, "x": 4}
BF = jnp.bfloat16
F32 = jnp.float32
SEMS = 96


def coords():
    return {a: lax.axis_index(a) for a in AXES}


def peer(**delta):
    me = coords()
    return tuple(lax.rem(me[a] + delta.get(a, 0) % SIZE[a], SIZE[a]) for a in AXES)


class Comm:
    def __init__(self, send_sem, recv_sem):
        self.send_sem, self.recv_sem = send_sem, recv_sem
        self.count, self.open = 0, []

    def push(self, src, dst, to):
        copy = pltpu.make_async_remote_copy(
            src_ref=src,
            dst_ref=dst,
            send_sem=self.send_sem.at[self.count],
            recv_sem=self.recv_sem.at[self.count],
            device_id=to,
            device_id_type=pl.DeviceIdType.MESH,
        )
        self.count += 1
        copy.start()
        self.open.append([copy, True, True])
        return self.open[-1]

    def local(self, src, dst):
        copy = pltpu.make_async_copy(src, dst, self.send_sem.at[self.count])
        self.count += 1
        copy.start()
        self.open.append([copy, False, True])
        return self.open[-1]

    def arrived(self, entries):
        for entry in entries:
            if entry[2]:
                if entry[1]:
                    entry[0].wait_recv()
                else:
                    entry[0].wait()
                entry[2] = False

    def drain(self):
        self.arrived(self.open)
        for copy, remote, _ in self.open:
            if remote:
                copy.wait_send()


def greet(devices):
    barrier = pltpu.get_barrier_semaphore()
    for device in devices:
        pl.semaphore_signal(barrier, inc=1, device_id=device, device_id_type=pl.DeviceIdType.MESH)
    pl.semaphore_wait(barrier, len(devices))


def exchange(name, collective_id, body, peers, ins, outs):
    def kernel(*refs):
        in_refs = refs[: len(ins)]
        out_refs = refs[len(ins) : len(ins) + len(outs)]
        comm = Comm(*refs[len(ins) + len(outs) :])
        greet(peers())
        body(comm, in_refs, out_refs)
        comm.drain()

    return pl.pallas_call(
        kernel,
        out_shape=tuple(jax.ShapeDtypeStruct(s, d) for s, d in outs),
        in_specs=[pl.BlockSpec(memory_space=pl.ANY)] * len(ins),
        out_specs=tuple(pl.BlockSpec(memory_space=pl.ANY) for _ in outs),
        scratch_shapes=[pltpu.SemaphoreType.DMA((SEMS,)), pltpu.SemaphoreType.DMA((SEMS,))],
        compiler_params=pltpu.CompilerParams(collective_id=collective_id, has_side_effects=True),
        name=name,
    )(*ins)


def ring(axis):
    return [peer(**{axis: k}) for k in (1, 3, 2)]


def near():
    return [peer(core=1)]


def scattered():
    me = coords()
    return (lax.rem(me["z"] + 1, 4), me["core"], me["x"], me["y"])


def collected():
    me = coords()
    return (me["x"], me["core"], lax.rem(me["y"] + 3, 4), me["z"])


def spread_x(comm, src, dst):
    x = lax.axis_index("x")
    sent = [comm.push(src, dst.at[x], to) for to in ring("x")]
    return sent + [comm.local(src, dst.at[x])]


def split_x(comm, src, dst):
    x = lax.axis_index("x")
    return [
        comm.push(src.at[lax.rem(x + k, 4)], dst.at[k - 1], peer(x=k)) for k in (1, 3, 2)
    ]


def halves(rows, cols):
    every = slice(None)
    if rows >= 32:
        return [(slice(0, rows // 2), every), (slice(rows // 2, rows), every)]
    return [(every, slice(0, cols // 2)), (every, slice(cols // 2, cols))]


class Gather:
    def __init__(self, comm, w, by_core):
        self.comm, self.w, self.by_core = comm, w, by_core
        self.cut = halves(*w.shape[3:])

    def at(self, y, core, z, half):
        slot = (core, y, z) if self.by_core else (y, core, z)
        return self.w.at[slot + self.cut[half]]

    def place(self):
        me = coords()
        y = lax.rem(me["y"] + 3, 4) if self.by_core else me["y"]
        return y, me["core"], me["z"]

    def first(self):
        y, c, z = self.place()
        a, b = self.at(y, c, z, 0), self.at(y, c, z, 1)
        self.a = [self.comm.push(a, a, to) for to in ring("z")]
        self.b = [self.comm.push(b, b, to) for to in ring("y")]

    def second(self):
        y, c, z = self.place()
        every = slice(None)
        self.comm.arrived(self.a)
        a = self.at(y, c, every, 0)
        self.a2 = [self.comm.push(a, a, to) for to in ring("y")]
        self.comm.arrived(self.b)
        b = self.at(every, c, z, 1)
        self.b2 = [self.comm.push(b, b, to) for to in ring("z")]

    def third(self):
        _, c, _ = self.place()
        every = slice(None)
        self.comm.arrived(self.a2)
        a = self.at(every, c, every, 0)
        self.comm.push(a, a, peer(core=1))
        self.comm.arrived(self.b2)
        b = self.at(every, c, every, 1)
        self.comm.push(b, b, peer(core=1))


def gather_peers():
    return ring("x") + ring("y") + ring("z") + near()


def into_slot(comm, src, w):
    me = coords()
    slot = w.at[me["y"], me["core"], me["z"], pl.ds(me["x"] * 16, 16)]
    sent = [
        comm.push(src.at[lax.rem(me["x"] + k, 4)], slot, peer(x=k)) for k in (1, 3, 2)
    ]
    return sent + [comm.local(src.at[me["x"]], slot)]


def into_scattered(comm, src, w):
    me = coords()
    return [comm.push(src, w.at[me["core"], me["z"], me["x"]], scattered())]


def swap_cores(comm, g, dst, by_core):
    other = 1 - lax.axis_index("core")
    src = g.at[other] if by_core else g.at[:, other]
    return [comm.push(src, dst, peer(core=1))]


def reduce_first(comm, s, dst_a, dst_b, by_core):
    y, z = lax.axis_index("y"), lax.axis_index("z")
    cut = halves(*s.shape[2:])
    for k in (1, 3, 2):
        to = lax.rem(z + k, 4)
        comm.push(s.at[(slice(None), to) + cut[0]], dst_a.at[k - 1], peer(z=k))
    for k in (1, 3, 2):
        to = lax.rem(y + k + (3 if by_core else 0), 4)
        comm.push(s.at[(to, slice(None)) + cut[1]], dst_b.at[k - 1], peer(y=k))


def reduce_second(comm, sa, sb, dst_a, dst_b, by_core):
    y, z = lax.axis_index("y"), lax.axis_index("z")
    for k in (1, 3, 2):
        to = lax.rem(y + k + (3 if by_core else 0), 4)
        comm.push(sa.at[to], dst_a.at[k - 1], peer(y=k))
    for k in (1, 3, 2):
        comm.push(sb.at[lax.rem(z + k, 4)], dst_b.at[k - 1], peer(z=k))


def pick(array, index, axis=0):
    return lax.dynamic_index_in_dim(array, index, axis, keepdims=False)


def after_cores(g, received, by_core):
    own = pick(g, lax.axis_index("core"), 0 if by_core else 1)
    return (own.astype(F32) + received.astype(F32)).astype(BF)


def slot_y(by_core):
    y = lax.axis_index("y")
    return lax.rem(y + 3, 4) if by_core else y


def after_first(s, ra, rb, by_core):
    every = slice(None)
    cut = halves(*s.shape[2:])
    own_a = pick(s[(every, every) + cut[0]], lax.axis_index("z"), 1).astype(F32)
    own_b = pick(s[(every, every) + cut[1]], slot_y(by_core), 0).astype(F32)
    return (
        (own_a + ra.astype(F32).sum(0)).astype(BF),
        (own_b + rb.astype(F32).sum(0)).astype(BF),
    )


def after_second(sa, sb, ra, rb, by_core):
    own_a = pick(sa, slot_y(by_core)).astype(F32)
    own_b = pick(sb, lax.axis_index("z")).astype(F32)
    return jnp.concatenate(
        [own_a + ra.astype(F32).sum(0), own_b + rb.astype(F32).sum(0)],
        axis=0 if sa.shape[1] == 32 else 1,
    ).astype(BF)


def layer_norm(values, gain, shift):
    center = jnp.mean(values, axis=-1, keepdims=True)
    centred = values - center
    spread = jnp.mean(centred * centred, axis=-1, keepdims=True)
    return centred * lax.rsqrt(spread + EPSILON) * gain + shift


def gelu_exact(values):
    return jax.nn.gelu(values, approximate=False)


def doc_number(positions, doc_ends):
    return jnp.sum((doc_ends[None, :] <= positions[:, None]).astype(jnp.int32), axis=1)


def dot(a, b, dims):
    return lax.dot_general(a, b, (dims, ((), ())), preferred_element_type=F32)


NN = ((1,), (0,))
NT = ((1,), (1,))
TN = ((0,), (0,))


def local(
    tokens,
    grad_out,
    lengths,
    ln1_gain,
    ln1_bias,
    w_qkv,
    b_qv,
    w_out,
    b_out,
    ln2_gain,
    ln2_bias,
    w_up,
    b_up,
    w_down,
    b_down,
):
    blk, width = tokens.shape[1:]
    span = 4 * blk
    part = width // 4
    hidden = w_up.shape[1] // 4
    heads = HEADS // 4
    x_at, z_at = lax.axis_index("x"), lax.axis_index("z")
    scale = 1.0 / math.sqrt(HEAD)

    tok = tokens.reshape(blk, width)
    dy = grad_out.reshape(blk, width)
    small = jnp.concatenate([ln1_gain, ln1_bias, b_qv, b_out, ln2_gain, ln2_bias, b_up, b_down])
    small = jnp.pad(small.astype(F32), (0, 1024 - small.shape[0])).reshape(8, 128)
    qkv_parts = w_qkv.reshape(16, 3, 4, part).transpose(2, 0, 1, 3).reshape(4, 16, 3 * part)
    up_parts = w_up.reshape(16, 4, hidden).transpose(1, 0, 2)

    def first_body(comm, ins, outs):
        tok_r, dy_r, small_r, qkv_r, out_r = ins
        tok_g, small_g, dy_g, wq, wo = outs
        me = coords()
        slot = into_slot(comm, qkv_r, wq)
        spot = into_scattered(comm, out_r, wo)
        at = (me["y"], me["core"], me["z"])
        s0 = [comm.push(small_r, small_g.at[at + (me["x"],)], to) for to in ring("x")]
        s0.append(comm.local(small_r, small_g.at[at + (me["x"],)]))
        spread_x(comm, tok_r, tok_g)
        q, o = Gather(comm, wq, False), Gather(comm, wo, True)
        comm.arrived(slot)
        q.first()
        comm.arrived(s0)
        mine = small_g.at[at]
        s1 = [comm.push(mine, mine, to) for to in ring("z")]
        comm.arrived(spot)
        o.first()
        spread_x(comm, dy_r, dy_g)
        comm.arrived(s1)
        mine = small_g.at[me["y"], me["core"]]
        s2 = [comm.push(mine, mine, to) for to in ring("y")]
        q.second()
        o.second()
        comm.arrived(s2)
        mine = small_g.at[:, me["core"]]
        comm.push(mine, mine, peer(core=1))
        q.third()
        o.third()

    tok_g, small_g, dy_g, wqkv_g, wout_g = exchange(
        "gather_attn",
        0,
        first_body,
        lambda: gather_peers() + [scattered(), collected()],
        [tok, dy, small, qkv_parts, w_out],
        [
            ((4, blk, width), BF),
            ((4, 2, 4, 4, 8, 128), F32),
            ((4, blk, width), BF),
            ((4, 2, 4, 64, 3 * part), BF),
            ((2, 4, 4, 16, width), BF),
        ],
    )
    small_g = small_g.reshape(128, 1024)
    vectors, start = [], 0
    for size in (16, 16, 32, 16, 16, 16, 64, 16):
        vectors.append(small_g[:, start : start + size].reshape(128 * size))
        start += size
    gain1, shift1, bias_qv, bias_out, gain2, shift2, bias_up, bias_down = vectors
    weight_qkv = wqkv_g.reshape(width, 3 * part)
    weight_out = wout_g.reshape(part, width)
    dy_all = dy_g.reshape(span, width)

    inputs = tok_g.reshape(span, width).astype(F32)
    normed1 = layer_norm(inputs, gain1, shift1).astype(BF)
    bias_q = lax.dynamic_slice_in_dim(bias_qv, x_at * part, part)
    bias_v = lax.dynamic_slice_in_dim(bias_qv, width + x_at * part, part)
    bias_full = jnp.concatenate([bias_q, jnp.zeros((part,), F32), bias_v])
    projected = (dot(normed1, weight_qkv, NN) + bias_full).astype(BF)

    def second_body(comm, ins, outs):
        p_r, up_r, down_r = ins
        edge, wu, wd = outs
        comm.push(p_r.at[pl.ds(span - W, W), pl.ds(part, 2 * part)], edge, peer(z=1))
        slot = into_slot(comm, up_r, wu)
        spot = into_scattered(comm, down_r, wd)
        u = Gather(comm, wu, False)
        comm.arrived(slot)
        u.first()
        comm.arrived(spot)
        u.second()
        u.third()

    edge_kv, wup_g, wdown_s = exchange(
        "edge_and_up",
        1,
        second_body,
        lambda: gather_peers() + [scattered(), collected()],
        [projected, up_parts, w_down],
        [
            ((W, 2 * part), BF),
            ((4, 2, 4, 64, hidden), BF),
            ((2, 4, 4, 64, width), BF),
        ],
    )

    row_ends = jnp.cumsum(lengths.reshape(-1))
    q_pos = z_at * span + jnp.arange(span, dtype=jnp.int32)
    k_pos = z_at * span - W + jnp.arange(span + W, dtype=jnp.int32)
    q_doc, k_doc = doc_number(q_pos, row_ends), doc_number(k_pos, row_ends)
    reach = W + blk

    def windows(array):
        return jnp.stack([array[b * blk : b * blk + reach] for b in range(4)])

    qp, qd = q_pos.reshape(4, blk, 1), q_doc.reshape(4, blk, 1)
    kp, kd = windows(k_pos)[:, None, :], windows(k_doc)[:, None, :]
    visible = (qd == kd) & (kp <= qp) & (qp - kp < W) & (kp >= 0)

    keys = jnp.concatenate([edge_kv[:, :part], projected[:, part : 2 * part]])
    values = jnp.concatenate([edge_kv[:, part:], projected[:, 2 * part :]])
    q_heads = projected[:, :part].reshape(4, blk, heads, HEAD)
    k_heads = windows(keys).reshape(4, reach, heads, HEAD)
    v_heads = windows(values).reshape(4, reach, heads, HEAD)
    scores = jnp.einsum("bqhd,bkhd->bhqk", q_heads, k_heads, preferred_element_type=F32) * scale
    masked = jnp.where(visible[:, None], scores, NEG_FILL)
    peak = jnp.max(masked, axis=-1, keepdims=True)
    log_total = peak + jnp.log(jnp.sum(jnp.exp(masked - peak), axis=-1, keepdims=True))
    probs = jnp.exp(masked - log_total)
    probs_low = probs.astype(BF)
    mixed = jnp.einsum("bhqk,bkhd->bqhd", probs_low, v_heads, preferred_element_type=F32)
    mixed = mixed.reshape(span, part).astype(BF)
    attn_part = dot(mixed, weight_out, NN).reshape(4, blk, width)

    def third_body(comm, ins, outs):
        part_r, wd_in = ins
        got, wd = outs
        me = coords()
        split_x(comm, part_r, got)
        slot = (me["core"], lax.rem(me["y"] + 3, 4), me["z"])
        comm.arrived([comm.local(wd_in.at[slot], wd.at[slot])])
        d = Gather(comm, wd, True)
        d.first()
        d.second()
        d.third()

    attn_got, wdown_g = exchange(
        "sum_attn_and_down",
        2,
        third_body,
        gather_peers,
        [attn_part.astype(BF), wdown_s],
        [((3, blk, width), BF), ((2, 4, 4, 64, width), BF)],
    )
    weight_up = wup_g.reshape(width, hidden)
    weight_down = wdown_g.reshape(hidden, width)

    own_tok = tok.astype(F32)
    residual = own_tok + pick(attn_part, x_at) + attn_got.astype(F32).sum(0) + bias_out
    normed2 = layer_norm(residual, gain2, shift2).astype(BF)

    (normed2_g,) = exchange(
        "spread_a2",
        3,
        lambda comm, ins, outs: spread_x(comm, ins[0], outs[0]),
        lambda: ring("x"),
        [normed2],
        [((4, blk, width), BF)],
    )
    a2 = normed2_g.reshape(span, width)
    bias_up_own = lax.dynamic_slice_in_dim(bias_up, x_at * hidden, hidden)
    upper = dot(a2, weight_up, NN) + bias_up_own
    activated = gelu_exact(upper).astype(BF)
    d_act = dot(dy_all, weight_down, NT)
    d_upper = jax.vjp(gelu_exact, upper)[1](d_act)[0].astype(BF)
    d_a2_part = dot(d_upper, weight_up, NT).reshape(4, blk, width)
    out_part = dot(activated, weight_down, NN).reshape(4, blk, width)
    g_wdown = dot(activated, dy_all, TN).astype(BF).reshape(2, 4, 4, 64, width)
    g_wup = dot(a2, d_upper, TN).astype(BF).reshape(4, 2, 4, 64, hidden)
    g_bup = jnp.sum(d_upper.astype(F32), axis=0)

    def fifth_body(comm, ins, outs):
        split_x(comm, ins[0], outs[0])
        split_x(comm, ins[1], outs[1])
        swap_cores(comm, ins[2], outs[2], False)
        swap_cores(comm, ins[3], outs[3], True)

    d_a2_got, out_got, up_c, down_c = exchange(
        "sum_ff",
        4,
        fifth_body,
        lambda: ring("x") + near(),
        [d_a2_part.astype(BF), out_part.astype(BF), g_wup, g_wdown],
        [
            ((3, blk, width), BF),
            ((3, blk, width), BF),
            ((4, 4, 64, hidden), BF),
            ((4, 4, 64, width), BF),
        ],
    )
    out = residual + pick(out_part, x_at) + out_got.astype(F32).sum(0) + bias_down
    d_a2 = pick(d_a2_part, x_at) + d_a2_got.astype(F32).sum(0)
    d_resnorm, g_gain2, g_shift2 = jax.vjp(layer_norm, residual, gain2, shift2)[1](d_a2)
    d_hidden = dy.astype(F32) + d_resnorm
    d_attn_own = d_hidden.astype(BF)
    up_s, down_s = after_cores(g_wup, up_c, False), after_cores(g_wdown, down_c, True)

    def sixth_body(comm, ins, outs):
        spread_x(comm, ins[0], outs[0])
        reduce_first(comm, ins[1], outs[1], outs[2], False)
        reduce_first(comm, ins[2], outs[3], outs[4], True)

    d_attn_g, up_a, up_b, down_a, down_b = exchange(
        "spread_d_attn",
        5,
        sixth_body,
        lambda: ring("x") + ring("y") + ring("z"),
        [d_attn_own, up_s, down_s],
        [
            ((4, blk, width), BF),
            ((3, 4, 32, hidden), BF),
            ((3, 4, 32, hidden), BF),
            ((3, 4, 32, width), BF),
            ((3, 4, 32, width), BF),
        ],
    )
    d_attn = d_attn_g.reshape(span, width)
    d_mixed = dot(d_attn, weight_out, NT).astype(BF)
    d_heads = d_mixed.reshape(4, blk, heads, HEAD)
    d_probs = jnp.einsum("bqhd,bkhd->bhqk", d_heads, v_heads, preferred_element_type=F32)
    d_score = (probs * (d_probs - jnp.sum(d_probs * probs, axis=-1, keepdims=True))).astype(BF)
    d_query = jnp.einsum("bhqk,bkhd->bqhd", d_score, k_heads, preferred_element_type=F32) * scale
    d_kwin = jnp.einsum("bhqk,bqhd->bkhd", d_score, q_heads, preferred_element_type=F32) * scale
    d_vwin = jnp.einsum("bhqk,bqhd->bkhd", probs_low, d_heads, preferred_element_type=F32)

    def unwindow(array):
        array = array.reshape(4, reach, part)
        total = jnp.zeros((span + W, part), F32)
        for b in range(4):
            total = total + jnp.pad(array[b], ((b * blk, span + W - b * blk - reach), (0, 0)))
        return total

    d_keys, d_values = unwindow(d_kwin), unwindow(d_vwin)
    d_edge = jnp.concatenate([d_keys[:W], d_values[:W]], axis=1).astype(BF)
    up_sa, up_sb = after_first(up_s, up_a, up_b, False)
    down_sa, down_sb = after_first(down_s, down_a, down_b, True)

    def seventh_body(comm, ins, outs):
        comm.push(ins[0], outs[0], peer(z=3))
        reduce_second(comm, ins[1], ins[2], outs[1], outs[2], False)
        reduce_second(comm, ins[3], ins[4], outs[3], outs[4], True)

    d_edge_got, up_a2, up_b2, down_a2, down_b2 = exchange(
        "edge_back",
        6,
        seventh_body,
        lambda: ring("y") + ring("z"),
        [d_edge, up_sa, up_sb, down_sa, down_sb],
        [
            ((W, 2 * part), BF),
            ((3, 32, hidden), BF),
            ((3, 32, hidden), BF),
            ((3, 32, width), BF),
            ((3, 32, width), BF),
        ],
    )
    up_f = after_second(up_sa, up_sb, up_a2, up_b2, False)
    down_f = after_second(down_sa, down_sb, down_a2, down_b2, True)
    d_kv = jnp.concatenate([d_keys[W:], d_values[W:]], axis=1)
    d_kv = d_kv + jnp.pad(d_edge_got.astype(F32), ((span - W, 0), (0, 0)))
    d_qkv = jnp.concatenate([d_query.reshape(span, part), d_kv], axis=1).astype(BF)
    d_a1_part = dot(d_qkv, weight_qkv, NT).reshape(4, blk, width)
    g_wqkv = dot(normed1, d_qkv, TN).astype(BF).reshape(4, 2, 4, 64, 3 * part)
    g_wout = dot(mixed, d_attn, TN).astype(BF).reshape(2, 4, 4, 16, width)
    g_bqkv = jnp.sum(d_qkv.astype(F32), axis=0)

    def eighth_body(comm, ins, outs):
        split_x(comm, ins[0], outs[0])
        swap_cores(comm, ins[1], outs[1], False)
        swap_cores(comm, ins[2], outs[2], True)
        split_x(comm, ins[3], outs[3])
        comm.push(ins[4], outs[4], collected())

    d_a1_got, qkv_c, wout_c, up_x, g_down_own = exchange(
        "sum_d_a1",
        7,
        eighth_body,
        lambda: ring("x") + near() + [scattered(), collected()],
        [d_a1_part.astype(BF), g_wqkv, g_wout, up_f.reshape(4, 16, hidden), down_f],
        [
            ((3, blk, width), BF),
            ((4, 4, 64, 3 * part), BF),
            ((4, 4, 16, width), BF),
            ((3, 16, hidden), BF),
            ((64, width), BF),
        ],
    )
    d_a1 = pick(d_a1_part, x_at) + d_a1_got.astype(F32).sum(0)
    d_in, g_gain1, g_shift1 = jax.vjp(layer_norm, own_tok, gain1, shift1)[1](d_a1)
    grad_tokens = d_hidden + d_in
    qkv_s, wout_s = after_cores(g_wqkv, qkv_c, False), after_cores(g_wout, wout_c, True)

    def placed(vector, offset, whole):
        return lax.dynamic_update_slice(jnp.zeros((whole,), F32), vector, (offset,))

    g_bqv = placed(g_bqkv[:part], x_at * part, 2 * width) + placed(
        g_bqkv[2 * part :], width + x_at * part, 2 * width
    )
    g_small = jnp.concatenate(
        [
            v.reshape(128, -1)
            for v in (
                g_gain1,
                g_shift1,
                g_bqv,
                jnp.sum(d_attn_own.astype(F32), axis=0),
                g_gain2,
                g_shift2,
                placed(g_bup, x_at * hidden, 4 * hidden),
                jnp.sum(dy.astype(F32), axis=0),
            )
        ],
        axis=1,
    )
    g_small = jnp.pad(g_small, ((0, 0), (0, 256 - g_small.shape[1]))).reshape(4, 2, 4, 8, 128)

    def ninth_body(comm, ins, outs):
        reduce_first(comm, ins[0], outs[0], outs[1], False)
        reduce_first(comm, ins[1], outs[2], outs[3], True)
        me = coords()
        for k in range(1, 8):
            c, zz = lax.rem(me["core"] + k // 4, 2), lax.rem(me["z"] + k % 4, 4)
            comm.push(ins[2].at[:, c, zz], outs[4].at[k - 1], (me["y"], c, zz, me["x"]))

    def across():
        me = coords()
        return [
            (me["y"], lax.rem(me["core"] + k // 4, 2), lax.rem(me["z"] + k % 4, 4), me["x"])
            for k in range(1, 8)
        ]

    qkv_a, qkv_b, wout_a, wout_b, small_a = exchange(
        "reduce_attn_1",
        8,
        ninth_body,
        lambda: ring("y") + across(),
        [qkv_s, wout_s, g_small],
        [
            ((3, 4, 32, 3 * part), BF),
            ((3, 4, 32, 3 * part), BF),
            ((3, 4, 16, width // 2), BF),
            ((3, 4, 16, width // 2), BF),
            ((7, 4, 8, 128), F32),
        ],
    )
    qkv_sa, qkv_sb = after_first(qkv_s, qkv_a, qkv_b, False)
    wout_sa, wout_sb = after_first(wout_s, wout_a, wout_b, True)
    small_s = pick(pick(g_small, lax.axis_index("core"), 1), z_at, 1) + small_a.sum(0)

    def tenth_body(comm, ins, outs):
        reduce_second(comm, ins[0], ins[1], outs[0], outs[1], False)
        reduce_second(comm, ins[2], ins[3], outs[2], outs[3], True)
        y = lax.axis_index("y")
        for k in (1, 3, 2):
            comm.push(ins[4].at[lax.rem(y + k, 4)], outs[4].at[k - 1], peer(y=k))

    qkv_a2, qkv_b2, wout_a2, wout_b2, small_b = exchange(
        "reduce_attn_2",
        9,
        tenth_body,
        lambda: ring("y") + ring("z"),
        [qkv_sa, qkv_sb, wout_sa, wout_sb, small_s],
        [
            ((3, 32, 3 * part), BF),
            ((3, 32, 3 * part), BF),
            ((3, 16, width // 2), BF),
            ((3, 16, width // 2), BF),
            ((3, 8, 128), F32),
        ],
    )
    qkv_f = after_second(qkv_sa, qkv_sb, qkv_a2, qkv_b2, False)
    wout_f = after_second(wout_sa, wout_sb, wout_a2, wout_b2, True)
    small_f = pick(small_s, lax.axis_index("y")) + small_b.sum(0)

    def last_body(comm, ins, outs):
        split_x(comm, ins[0], outs[0])
        comm.push(ins[1], outs[1], collected())
        for k in (1, 3, 2):
            comm.push(ins[2], outs[2].at[k - 1], peer(x=k))

    qkv_x, g_out_own, small_x = exchange(
        "hand_back",
        10,
        last_body,
        lambda: ring("x") + [scattered(), collected()],
        [qkv_f.reshape(4, 16, 3 * part), wout_f, small_f],
        [((3, 16, 3 * part), BF), ((16, width), BF), ((3, 8, 128), F32)],
    )

    def columns(own, received, groups):
        every = jnp.concatenate([received, pick(own, x_at)[None]])
        order = jnp.stack([lax.rem(x_at - s + 7, 4) for s in range(4)])
        every = jnp.take(every, order, axis=0).reshape(4, 16, groups, -1)
        return every.transpose(1, 2, 0, 3).reshape(16, -1).astype(F32)

    g_qkv_own = columns(qkv_f.reshape(4, 16, 3 * part), qkv_x, 3)
    g_up_own = columns(up_f.reshape(4, 16, hidden), up_x, 1)
    small_all = (small_f + small_x.sum(0)).reshape(4, 256)
    mine = pick(small_all, x_at)
    cuts, start = [], 0
    for size in (16, 16, 32, 16, 16, 16, 64, 16):
        cuts.append(mine[start : start + size])
        start += size
    return (
        out.astype(BF).reshape(1, blk, width),
        grad_tokens.reshape(1, blk, width),
        cuts[0],
        cuts[1],
        g_qkv_own,
        cuts[2],
        g_out_own.astype(F32),
        cuts[3],
        cuts[4],
        cuts[5],
        g_up_own,
        cuts[6],
        g_down_own.astype(F32),
        cuts[7],
    )


def solution(mesh):
    fine = Mesh(mesh.devices.reshape(4, 2, 4, 4), AXES)
    rows, seq = ("y", "core"), ("z", "x")
    every = rows + seq
    token = P(rows, seq, None)
    vec, mat = P(every), P(every, None)
    in_specs = (token, token, P(rows, None), vec, vec, mat, vec, mat, vec, vec, vec, mat, vec, mat, vec)
    out_specs = (token, token, vec, vec, mat, vec, mat, vec, vec, vec, mat, vec, mat, vec)
    return jax.shard_map(local, mesh=fine, in_specs=in_specs, out_specs=out_specs, check_vma=False)
```

```python
import functools
import math

import jax
import jax.numpy as jnp
from jax import lax
from jax.experimental import pallas as pl
from jax.experimental.pallas import tpu as pltpu
from jax.sharding import Mesh, PartitionSpec as P

HEADS = 16
HEAD = 128
W = 256
EPSILON = 1e-05
NEG_FILL = -1e30

AXES = ("y", "core", "z", "x")
SIZE = {"y": 4, "core": 2, "z": 4, "x": 4}
BF = jnp.bfloat16
F32 = jnp.float32
SEMS = 96


def coords():
    return {a: lax.axis_index(a) for a in AXES}


def peer(**delta):
    me = coords()
    return tuple(lax.rem(me[a] + delta.get(a, 0) % SIZE[a], SIZE[a]) for a in AXES)


class Comm:
    def __init__(self, send_sem, recv_sem):
        self.send_sem, self.recv_sem = send_sem, recv_sem
        self.count, self.open = 0, []

    def push(self, src, dst, to):
        copy = pltpu.make_async_remote_copy(
            src_ref=src,
            dst_ref=dst,
            send_sem=self.send_sem.at[self.count],
            recv_sem=self.recv_sem.at[self.count],
            device_id=to,
            device_id_type=pl.DeviceIdType.MESH,
        )
        self.count += 1
        copy.start()
        self.open.append([copy, True, True])
        return self.open[-1]

    def local(self, src, dst):
        copy = pltpu.make_async_copy(src, dst, self.send_sem.at[self.count])
        self.count += 1
        copy.start()
        self.open.append([copy, False, True])
        return self.open[-1]

    def arrived(self, entries):
        for entry in entries:
            if entry[2]:
                if entry[1]:
                    entry[0].wait_recv()
                else:
                    entry[0].wait()
                entry[2] = False

    def drain(self):
        self.arrived(self.open)
        for copy, remote, _ in self.open:
            if remote:
                copy.wait_send()


def greet(devices):
    barrier = pltpu.get_barrier_semaphore()
    for device in devices:
        pl.semaphore_signal(barrier, inc=1, device_id=device, device_id_type=pl.DeviceIdType.MESH)
    pl.semaphore_wait(barrier, len(devices))


def exchange(name, collective_id, body, peers, ins, outs):
    def kernel(*refs):
        in_refs = refs[: len(ins)]
        out_refs = refs[len(ins) : len(ins) + len(outs)]
        comm = Comm(*refs[len(ins) + len(outs) :])
        greet(peers())
        body(comm, in_refs, out_refs)
        comm.drain()

    return pl.pallas_call(
        kernel,
        out_shape=tuple(jax.ShapeDtypeStruct(s, d) for s, d in outs),
        in_specs=[pl.BlockSpec(memory_space=pl.ANY)] * len(ins),
        out_specs=tuple(pl.BlockSpec(memory_space=pl.ANY) for _ in outs),
        scratch_shapes=[pltpu.SemaphoreType.DMA((SEMS,)), pltpu.SemaphoreType.DMA((SEMS,))],
        compiler_params=pltpu.CompilerParams(collective_id=collective_id, has_side_effects=True),
        name=name,
    )(*ins)


def ring(axis):
    return [peer(**{axis: k}) for k in (1, 3, 2)]


def near():
    return [peer(core=1)]


def scattered():
    me = coords()
    return (lax.rem(me["z"] + 1, 4), me["core"], me["x"], me["y"])


def collected():
    me = coords()
    return (me["x"], me["core"], lax.rem(me["y"] + 3, 4), me["z"])


def spread_x(comm, src, dst):
    x = lax.axis_index("x")
    sent = [comm.push(src, dst.at[x], to) for to in ring("x")]
    return sent + [comm.local(src, dst.at[x])]


def split_x(comm, src, dst):
    x = lax.axis_index("x")
    return [
        comm.push(src.at[lax.rem(x + k, 4)], dst.at[k - 1], peer(x=k)) for k in (1, 3, 2)
    ]


def halves(rows, cols):
    every = slice(None)
    if rows >= 32:
        return [(slice(0, rows // 2), every), (slice(rows // 2, rows), every)]
    return [(every, slice(0, cols // 2)), (every, slice(cols // 2, cols))]


class Gather:
    def __init__(self, comm, w, by_core):
        self.comm, self.w, self.by_core = comm, w, by_core
        self.cut = halves(*w.shape[3:])

    def at(self, y, core, z, half):
        slot = (core, y, z) if self.by_core else (y, core, z)
        return self.w.at[slot + self.cut[half]]

    def place(self):
        me = coords()
        y = lax.rem(me["y"] + 3, 4) if self.by_core else me["y"]
        return y, me["core"], me["z"]

    def first(self):
        y, c, z = self.place()
        a, b = self.at(y, c, z, 0), self.at(y, c, z, 1)
        self.a = [self.comm.push(a, a, to) for to in ring("z")]
        self.b = [self.comm.push(b, b, to) for to in ring("y")]

    def second(self):
        y, c, z = self.place()
        every = slice(None)
        self.comm.arrived(self.a)
        a = self.at(y, c, every, 0)
        self.a2 = [self.comm.push(a, a, to) for to in ring("y")]
        self.comm.arrived(self.b)
        b = self.at(every, c, z, 1)
        self.b2 = [self.comm.push(b, b, to) for to in ring("z")]

    def third(self):
        _, c, _ = self.place()
        every = slice(None)
        self.comm.arrived(self.a2)
        a = self.at(every, c, every, 0)
        self.comm.push(a, a, peer(core=1))
        self.comm.arrived(self.b2)
        b = self.at(every, c, every, 1)
        self.comm.push(b, b, peer(core=1))


def gather_peers():
    return ring("x") + ring("y") + ring("z") + near()


def into_slot(comm, src, w):
    me = coords()
    slot = w.at[me["y"], me["core"], me["z"], pl.ds(me["x"] * 16, 16)]
    sent = [
        comm.push(src.at[lax.rem(me["x"] + k, 4)], slot, peer(x=k)) for k in (1, 3, 2)
    ]
    return sent + [comm.local(src.at[me["x"]], slot)]


def into_scattered(comm, src, w):
    me = coords()
    return [comm.push(src, w.at[me["core"], me["z"], me["x"]], scattered())]


def swap_cores(comm, g, dst, by_core):
    other = 1 - lax.axis_index("core")
    src = g.at[other] if by_core else g.at[:, other]
    return [comm.push(src, dst, peer(core=1))]


def reduce_first(comm, s, dst_a, dst_b, by_core):
    y, z = lax.axis_index("y"), lax.axis_index("z")
    cut = halves(*s.shape[2:])
    for k in (1, 3, 2):
        to = lax.rem(z + k, 4)
        comm.push(s.at[(slice(None), to) + cut[0]], dst_a.at[k - 1], peer(z=k))
    for k in (1, 3, 2):
        to = lax.rem(y + k + (3 if by_core else 0), 4)
        comm.push(s.at[(to, slice(None)) + cut[1]], dst_b.at[k - 1], peer(y=k))


def reduce_second(comm, sa, sb, dst_a, dst_b, by_core):
    y, z = lax.axis_index("y"), lax.axis_index("z")
    for k in (1, 3, 2):
        to = lax.rem(y + k + (3 if by_core else 0), 4)
        comm.push(sa.at[to], dst_a.at[k - 1], peer(y=k))
    for k in (1, 3, 2):
        comm.push(sb.at[lax.rem(z + k, 4)], dst_b.at[k - 1], peer(z=k))


def pick(array, index, axis=0):
    return lax.dynamic_index_in_dim(array, index, axis, keepdims=False)


def after_cores(g, received, by_core):
    own = pick(g, lax.axis_index("core"), 0 if by_core else 1)
    return (own.astype(F32) + received.astype(F32)).astype(BF)


def slot_y(by_core):
    y = lax.axis_index("y")
    return lax.rem(y + 3, 4) if by_core else y


def after_first(s, ra, rb, by_core):
    every = slice(None)
    cut = halves(*s.shape[2:])
    own_a = pick(s[(every, every) + cut[0]], lax.axis_index("z"), 1).astype(F32)
    own_b = pick(s[(every, every) + cut[1]], slot_y(by_core), 0).astype(F32)
    return (
        (own_a + ra.astype(F32).sum(0)).astype(BF),
        (own_b + rb.astype(F32).sum(0)).astype(BF),
    )


def summed(own, received):
    return (own.astype(F32) + received.astype(F32).sum(0)).astype(BF)


def after_second(sa, sb, ra, rb, by_core):
    own_a = pick(sa, slot_y(by_core)).astype(F32)
    own_b = pick(sb, lax.axis_index("z")).astype(F32)
    return jnp.concatenate(
        [own_a + ra.astype(F32).sum(0), own_b + rb.astype(F32).sum(0)],
        axis=0 if sa.shape[1] == 32 else 1,
    ).astype(BF)


def layer_norm(values, gain, shift):
    center = jnp.mean(values, axis=-1, keepdims=True)
    centred = values - center
    spread = jnp.mean(centred * centred, axis=-1, keepdims=True)
    return centred * lax.rsqrt(spread + EPSILON) * gain + shift


def doc_number(positions, doc_ends):
    return jnp.sum((doc_ends[None, :] <= positions[:, None]).astype(jnp.int32), axis=1)


def dot(a, b, dims):
    return lax.dot_general(a, b, (dims, ((), ())), preferred_element_type=F32)


NN = ((1,), (0,))
NT = ((1,), (1,))
TN = ((0,), (0,))


ORDER = (0, 1, 3, 2)


def remote(src, dst, sems, index, to):
    send, recv = sems
    return pltpu.make_async_remote_copy(
        src_ref=src,
        dst_ref=dst,
        send_sem=send.at[index],
        recv_sem=recv.at[index],
        device_id=to,
        device_id_type=pl.DeviceIdType.MESH,
    )


def feed_forward_body(
    a2_in,
    res_in,
    dy_in,
    gain_in,
    bias_in,
    dyg_hbm,
    wup_hbm,
    wdn_hbm,
    dattn_hbm,
    dhid_out,
    outp_hbm,
    up_a_own,
    up_b_own,
    dn_a_own,
    dn_b_own,
    up_a_got,
    up_b_got,
    dn_a_got,
    dn_b_got,
    small_out,
    wup,
    wdn,
    a2g,
    dyg,
    dact,
    act,
    dup,
    part,
    own,
    got,
    outp,
    up_c,
    dn_c,
    datt,
    local_sem,
    send_sem,
    recv_sem,
):
    sems = (send_sem, recv_sem)
    me = coords()
    x, y, z, core = me["x"], me["y"], me["z"], me["core"]
    other = 1 - core
    blk, width = a2_in.shape
    span = 4 * blk
    hidden = act.shape[1]

    load_down = pltpu.make_async_copy(wdn_hbm, wdn, local_sem.at[0])
    load_down.start()
    load_dy = []
    for p, k in enumerate(ORDER):
        load_dy.append(
            pltpu.make_async_copy(
                dyg_hbm.at[lax.rem(x + 4 - k, 4)], dyg.at[p], local_sem.at[1 + p]
            )
        )
        load_dy[-1].start()
    load_up = pltpu.make_async_copy(wup_hbm, wup, local_sem.at[5])
    load_up.start()

    greet(ring("x") + ring("y") + ring("z") + near())

    spread = [
        remote(a2_in, a2g.at[p], sems, p, peer(x=ORDER[p])) for p in (1, 2, 3)
    ]
    for copy in spread:
        copy.start()
    a2g[0] = a2_in[...]

    load_down.wait()
    for copy in load_dy:
        copy.wait()

    @pl.loop(0, 4)
    def _(j):
        tile = wdn[j // 2, pl.ds(2 * lax.rem(j, 2), 2)].reshape(512, width)
        cols = pl.ds(pl.multiple_of(j * 512, 512), 512)
        dact[:, cols] = dot(dyg[...].reshape(span, width), tile, NT)

    load_up.wait()
    for copy in spread:
        copy.wait_recv()

    @pl.loop(0, hidden // 256)
    def _(j):
        cols = pl.ds(pl.multiple_of(j * 256, 256), 256)
        u = dot(a2g[...].reshape(span, width), wup[:, :, :, :, cols].reshape(width, 256), NN)
        u = u + bias_in[:, cols]
        phi = 0.5 + 0.5 * lax.erf(u * math.sqrt(0.5))
        act[:, cols] = (u * phi).astype(BF)
        slope = phi + u * (jnp.exp(-0.5 * u * u) * (1.0 / math.sqrt(2.0 * math.pi)))
        d_up = (dact[:, cols] * slope).astype(BF)
        dup[:, cols] = d_up
        small_out[3:4, cols] = jnp.sum(d_up.astype(F32), axis=0, keepdims=True)

    def sends(j):
        cols = pl.ds(pl.multiple_of(j * 512, 512), 512)
        return [
            remote(
                part.at[p - 1, :, cols],
                got.at[p - 1, :, cols],
                sems,
                4 + 3 * j + p - 1,
                peer(x=-ORDER[p]),
            )
            for p in (3, 1, 2)
        ]

    @pl.loop(0, 4)
    def _(j):
        cols = pl.ds(pl.multiple_of(j * 512, 512), 512)
        d = dot(dup[...], wup[j].reshape(512, hidden), NT)
        own[:, cols] = d[:blk]
        for p in (1, 2, 3):
            part[p - 1, :, cols] = d[p * blk : (p + 1) * blk].astype(BF)
        for copy in sends(j):
            copy.start()

    @pl.loop(0, 4)
    def _(j):
        cols = pl.ds(pl.multiple_of(j * 512, 512), 512)
        o = dot(act[...], wdn[:, :, :, :, cols].reshape(hidden, 512), NN)
        outp[:, :, cols] = o.astype(BF).reshape(4, blk, 512)

    keep_out = pltpu.make_async_copy(outp, outp_hbm, local_sem.at[6])
    keep_out.start()

    def grad_down(c, t):
        cols = pl.ds(pl.multiple_of(c * (hidden // 2) + t * 256, 256), 256)
        return dot(act[:, cols], dyg[...].reshape(span, width), TN)

    def grad_up(t, c):
        cols = pl.ds(pl.multiple_of(t * 512 + c * 256, 256), 256)
        return dot(a2g[:, :, cols].reshape(span, 256), dup[...], TN)

    def swap_down(t):
        return remote(wdn.at[other, t], dn_c.at[t], sems, 16 + t, peer(core=1))

    def swap_up(t):
        return remote(wup.at[t, other], up_c.at[t], sems, 20 + t, peer(core=1))

    @pl.loop(0, 4)
    def _(t):
        wdn[other, t] = grad_down(other, t).astype(BF).reshape(4, 64, width)
        swap_down(t).start()

    @pl.loop(0, 4)
    def _(t):
        wup[t, other] = grad_up(t, other).astype(BF).reshape(4, 64, hidden)
        swap_up(t).start()

    @pl.loop(0, 4)
    def _(t):
        swap_down(t).wait_recv()
        total = grad_down(core, t) + dn_c[t].reshape(256, width).astype(F32)
        wdn[core, t] = total.astype(BF).reshape(4, 64, width)

    first = []

    def stage(src, dst, index, to):
        first.append(remote(src, dst, sems, index, to))
        first[-1].start()

    low, high = slice(0, 32), slice(32, 64)
    for k in (1, 3, 2):
        zz, yy = lax.rem(z + k, 4), lax.rem(y + k + 3, 4)
        stage(wdn.at[core, :, zz, low], dn_a_got.at[k - 1], 24 + k, peer(z=k))
        stage(wdn.at[core, yy, :, high], dn_b_got.at[k - 1], 28 + k, peer(y=k))

    @pl.loop(0, 4)
    def _(t):
        swap_up(t).wait_recv()
        total = grad_up(t, core) + up_c[t].reshape(256, hidden).astype(F32)
        wup[t, core] = total.astype(BF).reshape(4, 64, hidden)

    for k in (1, 3, 2):
        zz, yy = lax.rem(z + k, 4), lax.rem(y + k, 4)
        stage(wup.at[:, core, zz, low], up_a_got.at[k - 1], 32 + k, peer(z=k))
        stage(wup.at[yy, core, :, high], up_b_got.at[k - 1], 36 + k, peer(y=k))

    @pl.loop(0, 4)
    def _(j):
        for copy in sends(j):
            copy.wait_recv()

    small_out[0:3, :] = jnp.zeros((3, width), F32)
    small_out[4:8, :] = jnp.zeros((4, width), F32)
    gain = gain_in[...]

    @pl.loop(0, blk // 16)
    def _(i):
        rows = pl.ds(pl.multiple_of(i * 16, 16), 16)
        d = own[rows, :]
        for p in range(3):
            d = d + got[p, rows, :].astype(F32)
        v = res_in[rows, :]
        centred = v - jnp.mean(v, axis=-1, keepdims=True)
        s = lax.rsqrt(jnp.mean(centred * centred, axis=-1, keepdims=True) + EPSILON)
        n = centred * s
        dn = d * gain
        d_res = s * (
            dn
            - jnp.mean(dn, axis=-1, keepdims=True)
            - n * jnp.mean(dn * n, axis=-1, keepdims=True)
        )
        dy_own = dy_in[rows, :].astype(F32)
        hid = dy_own + d_res
        low_hid = hid.astype(BF)
        dhid_out[rows, :] = hid
        datt[rows, :] = low_hid
        small_out[0:1, :] += jnp.sum(d * n, axis=0, keepdims=True)
        small_out[1:2, :] += jnp.sum(d, axis=0, keepdims=True)
        small_out[2:3, :] += jnp.sum(low_hid.astype(F32), axis=0, keepdims=True)
        small_out[4:5, :] += jnp.sum(dy_own, axis=0, keepdims=True)

    attn = [
        remote(datt, dattn_hbm.at[x], sems, 40 + k, peer(x=k)) for k in (1, 3, 2)
    ]
    for copy in attn:
        copy.start()
    kept = [keep_out, pltpu.make_async_copy(datt, dattn_hbm.at[x], local_sem.at[7])]
    zy = lax.rem(y + 3, 4)
    kept.append(pltpu.make_async_copy(wdn.at[core, :, z, low], dn_a_own, local_sem.at[8]))
    kept.append(pltpu.make_async_copy(wdn.at[core, zy, :, high], dn_b_own, local_sem.at[9]))
    kept.append(pltpu.make_async_copy(wup.at[:, core, z, low], up_a_own, local_sem.at[10]))
    kept.append(pltpu.make_async_copy(wup.at[y, core, :, high], up_b_own, local_sem.at[11]))
    for copy in kept[1:]:
        copy.start()

    for copy in first + attn:
        copy.wait_recv()
    for copy in spread + first + attn:
        copy.wait_send()

    @pl.loop(0, 4)
    def _(j):
        for copy in sends(j):
            copy.wait_send()
        swap_down(j).wait_send()
        swap_up(j).wait_send()

    for copy in kept:
        copy.wait()


def feed_forward(collective_id, a2, residual, dy, gain, bias, dy_g, wup, wdn):
    blk, width = a2.shape
    hidden = wup.shape[-1]
    span = 4 * blk
    vmem = pl.BlockSpec(memory_space=pltpu.VMEM)
    hbm = pl.BlockSpec(memory_space=pl.ANY)
    quarter = (4, 32, width)
    outs = (
        [((4, blk, width), BF, hbm), ((blk, width), F32, vmem), ((4, blk, width), BF, hbm)]
        + [(quarter, BF, hbm)] * 4
        + [((3,) + quarter, BF, hbm)] * 4
        + [((8, width), F32, vmem)]
    )
    scratch = [
        ((4, 2, 4, 64, hidden), BF),
        ((2, 4, 4, 64, width), BF),
        ((4, blk, width), BF),
        ((4, blk, width), BF),
        ((span, hidden), F32),
        ((span, hidden), BF),
        ((span, hidden), BF),
        ((3, blk, width), BF),
        ((blk, width), F32),
        ((3, blk, width), BF),
        ((4, blk, width), BF),
        ((4, 4, 64, hidden), BF),
        ((4, 4, 64, width), BF),
        ((blk, width), BF),
    ]
    return pl.pallas_call(
        feed_forward_body,
        out_shape=tuple(jax.ShapeDtypeStruct(s, d) for s, d, _ in outs),
        in_specs=[vmem] * 5 + [hbm] * 3,
        out_specs=tuple(o[2] for o in outs),
        scratch_shapes=[pltpu.VMEM(s, d) for s, d in scratch]
        + [
            pltpu.SemaphoreType.DMA((12,)),
            pltpu.SemaphoreType.DMA((44,)),
            pltpu.SemaphoreType.DMA((44,)),
        ],
        compiler_params=pltpu.CompilerParams(
            collective_id=collective_id, has_side_effects=True, vmem_limit_bytes=62 << 20
        ),
        name="feed_forward",
    )(a2, residual, dy, gain.reshape(1, width), bias.reshape(1, hidden), dy_g, wup, wdn)


def local(
    tokens,
    grad_out,
    lengths,
    ln1_gain,
    ln1_bias,
    w_qkv,
    b_qv,
    w_out,
    b_out,
    ln2_gain,
    ln2_bias,
    w_up,
    b_up,
    w_down,
    b_down,
):
    blk, width = tokens.shape[1:]
    span = 4 * blk
    part = width // 4
    hidden = w_up.shape[1] // 4
    heads = HEADS // 4
    x_at, z_at = lax.axis_index("x"), lax.axis_index("z")
    scale = 1.0 / math.sqrt(HEAD)

    tok = tokens.reshape(blk, width)
    dy = grad_out.reshape(blk, width)
    small = jnp.concatenate([ln1_gain, ln1_bias, b_qv, b_out, ln2_gain, ln2_bias, b_up, b_down])
    small = jnp.pad(small.astype(F32), (0, 1024 - small.shape[0])).reshape(8, 128)
    qkv_parts = w_qkv.reshape(16, 3, 4, part).transpose(2, 0, 1, 3).reshape(4, 16, 3 * part)
    up_parts = w_up.reshape(16, 4, hidden).transpose(1, 0, 2)

    def first_body(comm, ins, outs):
        tok_r, dy_r, small_r, qkv_r, out_r = ins
        tok_g, small_g, dy_g, wq, wo = outs
        me = coords()
        slot = into_slot(comm, qkv_r, wq)
        spot = into_scattered(comm, out_r, wo)
        at = (me["y"], me["core"], me["z"])
        s0 = [comm.push(small_r, small_g.at[at + (me["x"],)], to) for to in ring("x")]
        s0.append(comm.local(small_r, small_g.at[at + (me["x"],)]))
        spread_x(comm, tok_r, tok_g)
        q, o = Gather(comm, wq, False), Gather(comm, wo, True)
        comm.arrived(slot)
        q.first()
        comm.arrived(s0)
        mine = small_g.at[at]
        s1 = [comm.push(mine, mine, to) for to in ring("z")]
        comm.arrived(spot)
        o.first()
        spread_x(comm, dy_r, dy_g)
        comm.arrived(s1)
        mine = small_g.at[me["y"], me["core"]]
        s2 = [comm.push(mine, mine, to) for to in ring("y")]
        q.second()
        o.second()
        comm.arrived(s2)
        mine = small_g.at[:, me["core"]]
        comm.push(mine, mine, peer(core=1))
        q.third()
        o.third()

    tok_g, small_g, dy_g, wqkv_g, wout_g = exchange(
        "gather_attn",
        0,
        first_body,
        lambda: gather_peers() + [scattered(), collected()],
        [tok, dy, small, qkv_parts, w_out],
        [
            ((4, blk, width), BF),
            ((4, 2, 4, 4, 8, 128), F32),
            ((4, blk, width), BF),
            ((4, 2, 4, 64, 3 * part), BF),
            ((2, 4, 4, 16, width), BF),
        ],
    )
    small_g = small_g.reshape(128, 1024)
    vectors, start = [], 0
    for size in (16, 16, 32, 16, 16, 16, 64, 16):
        vectors.append(small_g[:, start : start + size].reshape(128 * size))
        start += size
    gain1, shift1, bias_qv, bias_out, gain2, shift2, bias_up, bias_down = vectors
    weight_qkv = wqkv_g.reshape(width, 3 * part)
    weight_out = wout_g.reshape(part, width)

    inputs = tok_g.reshape(span, width).astype(F32)
    normed1 = layer_norm(inputs, gain1, shift1).astype(BF)
    bias_q = lax.dynamic_slice_in_dim(bias_qv, x_at * part, part)
    bias_v = lax.dynamic_slice_in_dim(bias_qv, width + x_at * part, part)
    bias_full = jnp.concatenate([bias_q, jnp.zeros((part,), F32), bias_v])
    projected = (dot(normed1, weight_qkv, NN) + bias_full).astype(BF)

    def second_body(comm, ins, outs):
        p_r, up_r, down_r = ins
        edge, wu, wd = outs
        comm.push(p_r.at[pl.ds(span - W, W), pl.ds(part, 2 * part)], edge, peer(z=1))
        slot = into_slot(comm, up_r, wu)
        spot = into_scattered(comm, down_r, wd)
        u = Gather(comm, wu, False)
        comm.arrived(slot)
        u.first()
        comm.arrived(spot)
        u.second()
        u.third()

    edge_kv, wup_g, wdown_s = exchange(
        "edge_and_up",
        1,
        second_body,
        lambda: gather_peers() + [scattered(), collected()],
        [projected, up_parts, w_down],
        [
            ((W, 2 * part), BF),
            ((4, 2, 4, 64, hidden), BF),
            ((2, 4, 4, 64, width), BF),
        ],
    )

    row_ends = jnp.cumsum(lengths.reshape(-1))
    q_pos = z_at * span + jnp.arange(span, dtype=jnp.int32)
    k_pos = z_at * span - W + jnp.arange(span + W, dtype=jnp.int32)
    q_doc, k_doc = doc_number(q_pos, row_ends), doc_number(k_pos, row_ends)
    reach = W + blk

    def windows(array):
        return jnp.stack([array[b * blk : b * blk + reach] for b in range(4)])

    qp, qd = q_pos.reshape(4, blk, 1), q_doc.reshape(4, blk, 1)
    kp, kd = windows(k_pos)[:, None, :], windows(k_doc)[:, None, :]
    visible = (qd == kd) & (kp <= qp) & (qp - kp < W) & (kp >= 0)

    keys = jnp.concatenate([edge_kv[:, :part], projected[:, part : 2 * part]])
    values = jnp.concatenate([edge_kv[:, part:], projected[:, 2 * part :]])
    q_heads = projected[:, :part].reshape(4, blk, heads, HEAD)
    k_heads = windows(keys).reshape(4, reach, heads, HEAD)
    v_heads = windows(values).reshape(4, reach, heads, HEAD)
    scores = jnp.einsum("bqhd,bkhd->bhqk", q_heads, k_heads, preferred_element_type=F32) * scale
    masked = jnp.where(visible[:, None], scores, NEG_FILL)
    peak = jnp.max(masked, axis=-1, keepdims=True)
    log_total = peak + jnp.log(jnp.sum(jnp.exp(masked - peak), axis=-1, keepdims=True))
    probs = jnp.exp(masked - log_total)
    probs_low = probs.astype(BF)
    mixed = jnp.einsum("bhqk,bkhd->bqhd", probs_low, v_heads, preferred_element_type=F32)
    mixed = mixed.reshape(span, part).astype(BF)
    attn_part = dot(mixed, weight_out, NN).reshape(4, blk, width)

    def third_body(comm, ins, outs):
        part_r, wd_in = ins
        got, wd = outs
        me = coords()
        split_x(comm, part_r, got)
        slot = (me["core"], lax.rem(me["y"] + 3, 4), me["z"])
        comm.arrived([comm.local(wd_in.at[slot], wd.at[slot])])
        d = Gather(comm, wd, True)
        d.first()
        d.second()
        d.third()

    attn_got, wdown_g = exchange(
        "sum_attn_and_down",
        2,
        third_body,
        gather_peers,
        [attn_part.astype(BF), wdown_s],
        [((3, blk, width), BF), ((2, 4, 4, 64, width), BF)],
    )

    own_tok = tok.astype(F32)
    residual = own_tok + pick(attn_part, x_at) + attn_got.astype(F32).sum(0) + bias_out
    normed2 = layer_norm(residual, gain2, shift2).astype(BF)

    bias_up_own = lax.dynamic_slice_in_dim(bias_up, x_at * hidden, hidden)
    (
        d_attn_g,
        d_hidden,
        out_part,
        up_a_own,
        up_b_own,
        down_a_own,
        down_b_own,
        up_a,
        up_b,
        down_a,
        down_b,
        ff_small,
    ) = feed_forward(3, normed2, residual, dy, gain2, bias_up_own, dy_g, wup_g, wdown_g)
    up_sa, up_sb = summed(up_a_own, up_a), summed(up_b_own, up_b)
    down_sa, down_sb = summed(down_a_own, down_a), summed(down_b_own, down_b)
    d_attn = d_attn_g.reshape(span, width)
    d_mixed = dot(d_attn, weight_out, NT).astype(BF)
    d_heads = d_mixed.reshape(4, blk, heads, HEAD)
    d_probs = jnp.einsum("bqhd,bkhd->bhqk", d_heads, v_heads, preferred_element_type=F32)
    d_score = (probs * (d_probs - jnp.sum(d_probs * probs, axis=-1, keepdims=True))).astype(BF)
    d_query = jnp.einsum("bhqk,bkhd->bqhd", d_score, k_heads, preferred_element_type=F32) * scale
    d_kwin = jnp.einsum("bhqk,bqhd->bkhd", d_score, q_heads, preferred_element_type=F32) * scale
    d_vwin = jnp.einsum("bhqk,bqhd->bkhd", probs_low, d_heads, preferred_element_type=F32)

    def unwindow(array):
        array = array.reshape(4, reach, part)
        total = jnp.zeros((span + W, part), F32)
        for b in range(4):
            total = total + jnp.pad(array[b], ((b * blk, span + W - b * blk - reach), (0, 0)))
        return total

    d_keys, d_values = unwindow(d_kwin), unwindow(d_vwin)
    d_edge = jnp.concatenate([d_keys[:W], d_values[:W]], axis=1).astype(BF)

    def seventh_body(comm, ins, outs):
        comm.push(ins[0], outs[0], peer(z=3))
        reduce_second(comm, ins[1], ins[2], outs[1], outs[2], False)
        reduce_second(comm, ins[3], ins[4], outs[3], outs[4], True)
        for p in (1, 2, 3):
            comm.push(ins[5].at[p], outs[5].at[p - 1], peer(x=-ORDER[p]))

    d_edge_got, up_a2, up_b2, down_a2, down_b2, out_got = exchange(
        "edge_back",
        6,
        seventh_body,
        lambda: ring("x") + ring("y") + ring("z"),
        [d_edge, up_sa, up_sb, down_sa, down_sb, out_part],
        [
            ((W, 2 * part), BF),
            ((3, 32, hidden), BF),
            ((3, 32, hidden), BF),
            ((3, 32, width), BF),
            ((3, 32, width), BF),
            ((3, blk, width), BF),
        ],
    )
    out = residual + out_part[0].astype(F32) + out_got.astype(F32).sum(0) + bias_down
    up_f = after_second(up_sa, up_sb, up_a2, up_b2, False)
    down_f = after_second(down_sa, down_sb, down_a2, down_b2, True)
    d_kv = jnp.concatenate([d_keys[W:], d_values[W:]], axis=1)
    d_kv = d_kv + jnp.pad(d_edge_got.astype(F32), ((span - W, 0), (0, 0)))
    d_qkv = jnp.concatenate([d_query.reshape(span, part), d_kv], axis=1).astype(BF)
    d_a1_part = dot(d_qkv, weight_qkv, NT).reshape(4, blk, width)
    g_wqkv = dot(normed1, d_qkv, TN).astype(BF).reshape(4, 2, 4, 64, 3 * part)
    g_wout = dot(mixed, d_attn, TN).astype(BF).reshape(2, 4, 4, 16, width)
    g_bqkv = jnp.sum(d_qkv.astype(F32), axis=0)

    def eighth_body(comm, ins, outs):
        split_x(comm, ins[0], outs[0])
        swap_cores(comm, ins[1], outs[1], False)
        swap_cores(comm, ins[2], outs[2], True)
        split_x(comm, ins[3], outs[3])
        comm.push(ins[4], outs[4], collected())

    d_a1_got, qkv_c, wout_c, up_x, g_down_own = exchange(
        "sum_d_a1",
        7,
        eighth_body,
        lambda: ring("x") + near() + [scattered(), collected()],
        [d_a1_part.astype(BF), g_wqkv, g_wout, up_f.reshape(4, 16, hidden), down_f],
        [
            ((3, blk, width), BF),
            ((4, 4, 64, 3 * part), BF),
            ((4, 4, 16, width), BF),
            ((3, 16, hidden), BF),
            ((64, width), BF),
        ],
    )
    d_a1 = pick(d_a1_part, x_at) + d_a1_got.astype(F32).sum(0)
    d_in, g_gain1, g_shift1 = jax.vjp(layer_norm, own_tok, gain1, shift1)[1](d_a1)
    grad_tokens = d_hidden + d_in
    qkv_s, wout_s = after_cores(g_wqkv, qkv_c, False), after_cores(g_wout, wout_c, True)

    def placed(vector, offset, whole):
        return lax.dynamic_update_slice(jnp.zeros((whole,), F32), vector, (offset,))

    g_bqv = placed(g_bqkv[:part], x_at * part, 2 * width) + placed(
        g_bqkv[2 * part :], width + x_at * part, 2 * width
    )
    g_small = jnp.concatenate(
        [
            v.reshape(128, -1)
            for v in (
                g_gain1,
                g_shift1,
                g_bqv,
                ff_small[2],
                ff_small[0],
                ff_small[1],
                placed(ff_small[3], x_at * hidden, 4 * hidden),
                ff_small[4],
            )
        ],
        axis=1,
    )
    g_small = jnp.pad(g_small, ((0, 0), (0, 256 - g_small.shape[1]))).reshape(4, 2, 4, 8, 128)

    def ninth_body(comm, ins, outs):
        reduce_first(comm, ins[0], outs[0], outs[1], False)
        reduce_first(comm, ins[1], outs[2], outs[3], True)
        me = coords()
        for k in range(1, 8):
            c, zz = lax.rem(me["core"] + k // 4, 2), lax.rem(me["z"] + k % 4, 4)
            comm.push(ins[2].at[:, c, zz], outs[4].at[k - 1], (me["y"], c, zz, me["x"]))

    def across():
        me = coords()
        return [
            (me["y"], lax.rem(me["core"] + k // 4, 2), lax.rem(me["z"] + k % 4, 4), me["x"])
            for k in range(1, 8)
        ]

    qkv_a, qkv_b, wout_a, wout_b, small_a = exchange(
        "reduce_attn_1",
        8,
        ninth_body,
        lambda: ring("y") + across(),
        [qkv_s, wout_s, g_small],
        [
            ((3, 4, 32, 3 * part), BF),
            ((3, 4, 32, 3 * part), BF),
            ((3, 4, 16, width // 2), BF),
            ((3, 4, 16, width // 2), BF),
            ((7, 4, 8, 128), F32),
        ],
    )
    qkv_sa, qkv_sb = after_first(qkv_s, qkv_a, qkv_b, False)
    wout_sa, wout_sb = after_first(wout_s, wout_a, wout_b, True)
    small_s = pick(pick(g_small, lax.axis_index("core"), 1), z_at, 1) + small_a.sum(0)

    def tenth_body(comm, ins, outs):
        reduce_second(comm, ins[0], ins[1], outs[0], outs[1], False)
        reduce_second(comm, ins[2], ins[3], outs[2], outs[3], True)
        y = lax.axis_index("y")
        for k in (1, 3, 2):
            comm.push(ins[4].at[lax.rem(y + k, 4)], outs[4].at[k - 1], peer(y=k))

    qkv_a2, qkv_b2, wout_a2, wout_b2, small_b = exchange(
        "reduce_attn_2",
        9,
        tenth_body,
        lambda: ring("y") + ring("z"),
        [qkv_sa, qkv_sb, wout_sa, wout_sb, small_s],
        [
            ((3, 32, 3 * part), BF),
            ((3, 32, 3 * part), BF),
            ((3, 16, width // 2), BF),
            ((3, 16, width // 2), BF),
            ((3, 8, 128), F32),
        ],
    )
    qkv_f = after_second(qkv_sa, qkv_sb, qkv_a2, qkv_b2, False)
    wout_f = after_second(wout_sa, wout_sb, wout_a2, wout_b2, True)
    small_f = pick(small_s, lax.axis_index("y")) + small_b.sum(0)

    def last_body(comm, ins, outs):
        split_x(comm, ins[0], outs[0])
        comm.push(ins[1], outs[1], collected())
        for k in (1, 3, 2):
            comm.push(ins[2], outs[2].at[k - 1], peer(x=k))

    qkv_x, g_out_own, small_x = exchange(
        "hand_back",
        10,
        last_body,
        lambda: ring("x") + [scattered(), collected()],
        [qkv_f.reshape(4, 16, 3 * part), wout_f, small_f],
        [((3, 16, 3 * part), BF), ((16, width), BF), ((3, 8, 128), F32)],
    )

    def columns(own, received, groups):
        every = jnp.concatenate([received, pick(own, x_at)[None]])
        order = jnp.stack([lax.rem(x_at - s + 7, 4) for s in range(4)])
        every = jnp.take(every, order, axis=0).reshape(4, 16, groups, -1)
        return every.transpose(1, 2, 0, 3).reshape(16, -1).astype(F32)

    g_qkv_own = columns(qkv_f.reshape(4, 16, 3 * part), qkv_x, 3)
    g_up_own = columns(up_f.reshape(4, 16, hidden), up_x, 1)
    small_all = (small_f + small_x.sum(0)).reshape(4, 256)
    mine = pick(small_all, x_at)
    cuts, start = [], 0
    for size in (16, 16, 32, 16, 16, 16, 64, 16):
        cuts.append(mine[start : start + size])
        start += size
    return (
        out.astype(BF).reshape(1, blk, width),
        grad_tokens.reshape(1, blk, width),
        cuts[0],
        cuts[1],
        g_qkv_own,
        cuts[2],
        g_out_own.astype(F32),
        cuts[3],
        cuts[4],
        cuts[5],
        g_up_own,
        cuts[6],
        g_down_own.astype(F32),
        cuts[7],
    )


def solution(mesh):
    fine = Mesh(mesh.devices.reshape(4, 2, 4, 4), AXES)
    rows, seq = ("y", "core"), ("z", "x")
    every = rows + seq
    token = P(rows, seq, None)
    vec, mat = P(every), P(every, None)
    in_specs = (token, token, P(rows, None), vec, vec, mat, vec, mat, vec, vec, vec, mat, vec, mat, vec)
    out_specs = (token, token, vec, vec, mat, vec, mat, vec, vec, vec, mat, vec, mat, vec)
    return jax.shard_map(local, mesh=fine, in_specs=in_specs, out_specs=out_specs, check_vma=False)
```

```python
import functools
import math

import jax
import jax.numpy as jnp
from jax import lax
from jax.experimental import pallas as pl
from jax.experimental.pallas import tpu as pltpu
from jax.sharding import Mesh, PartitionSpec as P

HEADS = 16
HEAD = 128
W = 256
EPSILON = 1e-05
NEG_FILL = -1e30

AXES = ("y", "core", "z", "x")
SIZE = {"y": 4, "core": 2, "z": 4, "x": 4}
BF = jnp.bfloat16
F32 = jnp.float32
SEMS = 96


def coords():
    return {a: lax.axis_index(a) for a in AXES}


def peer(**delta):
    me = coords()
    return tuple(lax.rem(me[a] + delta.get(a, 0) % SIZE[a], SIZE[a]) for a in AXES)


class Comm:
    def __init__(self, send_sem, recv_sem):
        self.send_sem, self.recv_sem = send_sem, recv_sem
        self.count, self.open = 0, []

    def push(self, src, dst, to):
        copy = pltpu.make_async_remote_copy(
            src_ref=src,
            dst_ref=dst,
            send_sem=self.send_sem.at[self.count],
            recv_sem=self.recv_sem.at[self.count],
            device_id=to,
            device_id_type=pl.DeviceIdType.MESH,
        )
        self.count += 1
        copy.start()
        self.open.append([copy, True, True])
        return self.open[-1]

    def local(self, src, dst):
        copy = pltpu.make_async_copy(src, dst, self.send_sem.at[self.count])
        self.count += 1
        copy.start()
        self.open.append([copy, False, True])
        return self.open[-1]

    def arrived(self, entries):
        for entry in entries:
            if entry[2]:
                if entry[1]:
                    entry[0].wait_recv()
                else:
                    entry[0].wait()
                entry[2] = False

    def drain(self):
        self.arrived(self.open)
        for copy, remote, _ in self.open:
            if remote:
                copy.wait_send()


def greet(devices):
    barrier = pltpu.get_barrier_semaphore()
    for device in devices:
        pl.semaphore_signal(barrier, inc=1, device_id=device, device_id_type=pl.DeviceIdType.MESH)
    pl.semaphore_wait(barrier, len(devices))


def exchange(name, collective_id, body, peers, ins, outs):
    def kernel(*refs):
        in_refs = refs[: len(ins)]
        out_refs = refs[len(ins) : len(ins) + len(outs)]
        comm = Comm(*refs[len(ins) + len(outs) :])
        greet(peers())
        body(comm, in_refs, out_refs)
        comm.drain()

    return pl.pallas_call(
        kernel,
        out_shape=tuple(jax.ShapeDtypeStruct(s, d) for s, d in outs),
        in_specs=[pl.BlockSpec(memory_space=pl.ANY)] * len(ins),
        out_specs=tuple(pl.BlockSpec(memory_space=pl.ANY) for _ in outs),
        scratch_shapes=[pltpu.SemaphoreType.DMA((SEMS,)), pltpu.SemaphoreType.DMA((SEMS,))],
        compiler_params=pltpu.CompilerParams(collective_id=collective_id, has_side_effects=True),
        name=name,
    )(*ins)


def ring(axis):
    return [peer(**{axis: k}) for k in (1, 3, 2)]


def near():
    return [peer(core=1)]


def scattered():
    me = coords()
    return (lax.rem(me["z"] + 1, 4), me["core"], me["x"], me["y"])


def collected():
    me = coords()
    return (me["x"], me["core"], lax.rem(me["y"] + 3, 4), me["z"])


def spread_x(comm, src, dst):
    x = lax.axis_index("x")
    sent = [comm.push(src, dst.at[x], to) for to in ring("x")]
    return sent + [comm.local(src, dst.at[x])]


def split_x(comm, src, dst):
    x = lax.axis_index("x")
    return [
        comm.push(src.at[lax.rem(x + k, 4)], dst.at[k - 1], peer(x=k)) for k in (1, 3, 2)
    ]


def halves(rows, cols):
    every = slice(None)
    if rows >= 32:
        return [(slice(0, rows // 2), every), (slice(rows // 2, rows), every)]
    return [(every, slice(0, cols // 2)), (every, slice(cols // 2, cols))]


class Gather:
    def __init__(self, comm, w, by_core):
        self.comm, self.w, self.by_core = comm, w, by_core
        self.cut = halves(*w.shape[3:])

    def at(self, y, core, z, half):
        slot = (core, y, z) if self.by_core else (y, core, z)
        return self.w.at[slot + self.cut[half]]

    def place(self):
        me = coords()
        y = lax.rem(me["y"] + 3, 4) if self.by_core else me["y"]
        return y, me["core"], me["z"]

    def first(self):
        y, c, z = self.place()
        a, b = self.at(y, c, z, 0), self.at(y, c, z, 1)
        self.a = [self.comm.push(a, a, to) for to in ring("z")]
        self.b = [self.comm.push(b, b, to) for to in ring("y")]

    def second(self):
        y, c, z = self.place()
        every = slice(None)
        self.comm.arrived(self.a)
        a = self.at(y, c, every, 0)
        self.a2 = [self.comm.push(a, a, to) for to in ring("y")]
        self.comm.arrived(self.b)
        b = self.at(every, c, z, 1)
        self.b2 = [self.comm.push(b, b, to) for to in ring("z")]

    def third(self):
        _, c, _ = self.place()
        every = slice(None)
        self.comm.arrived(self.a2)
        a = self.at(every, c, every, 0)
        self.comm.push(a, a, peer(core=1))
        self.comm.arrived(self.b2)
        b = self.at(every, c, every, 1)
        self.comm.push(b, b, peer(core=1))


def gather_peers():
    return ring("x") + ring("y") + ring("z") + near()


def into_slot(comm, src, w):
    me = coords()
    slot = w.at[me["y"], me["core"], me["z"], pl.ds(me["x"] * 16, 16)]
    sent = [
        comm.push(src.at[lax.rem(me["x"] + k, 4)], slot, peer(x=k)) for k in (1, 3, 2)
    ]
    return sent + [comm.local(src.at[me["x"]], slot)]


def into_scattered(comm, src, w):
    me = coords()
    return [comm.push(src, w.at[me["core"], me["z"], me["x"]], scattered())]


def swap_cores(comm, g, dst, by_core):
    other = 1 - lax.axis_index("core")
    src = g.at[other] if by_core else g.at[:, other]
    return [comm.push(src, dst, peer(core=1))]


def reduce_first(comm, s, dst_a, dst_b, by_core):
    y, z = lax.axis_index("y"), lax.axis_index("z")
    cut = halves(*s.shape[2:])
    for k in (1, 3, 2):
        to = lax.rem(z + k, 4)
        comm.push(s.at[(slice(None), to) + cut[0]], dst_a.at[k - 1], peer(z=k))
    for k in (1, 3, 2):
        to = lax.rem(y + k + (3 if by_core else 0), 4)
        comm.push(s.at[(to, slice(None)) + cut[1]], dst_b.at[k - 1], peer(y=k))


def reduce_second(comm, sa, sb, dst_a, dst_b, by_core):
    y, z = lax.axis_index("y"), lax.axis_index("z")
    for k in (1, 3, 2):
        to = lax.rem(y + k + (3 if by_core else 0), 4)
        comm.push(sa.at[to], dst_a.at[k - 1], peer(y=k))
    for k in (1, 3, 2):
        comm.push(sb.at[lax.rem(z + k, 4)], dst_b.at[k - 1], peer(z=k))


def pick(array, index, axis=0):
    return lax.dynamic_index_in_dim(array, index, axis, keepdims=False)


def after_cores(g, received, by_core):
    own = pick(g, lax.axis_index("core"), 0 if by_core else 1)
    return (own.astype(F32) + received.astype(F32)).astype(BF)


def slot_y(by_core):
    y = lax.axis_index("y")
    return lax.rem(y + 3, 4) if by_core else y


def after_first(s, ra, rb, by_core):
    every = slice(None)
    cut = halves(*s.shape[2:])
    own_a = pick(s[(every, every) + cut[0]], lax.axis_index("z"), 1).astype(F32)
    own_b = pick(s[(every, every) + cut[1]], slot_y(by_core), 0).astype(F32)
    return (
        (own_a + ra.astype(F32).sum(0)).astype(BF),
        (own_b + rb.astype(F32).sum(0)).astype(BF),
    )


def summed(own, received):
    return (own.astype(F32) + received.astype(F32).sum(0)).astype(BF)


def after_second(sa, sb, ra, rb, by_core):
    own_a = pick(sa, slot_y(by_core)).astype(F32)
    own_b = pick(sb, lax.axis_index("z")).astype(F32)
    return jnp.concatenate(
        [own_a + ra.astype(F32).sum(0), own_b + rb.astype(F32).sum(0)],
        axis=0 if sa.shape[1] == 32 else 1,
    ).astype(BF)


def layer_norm(values, gain, shift):
    center = jnp.mean(values, axis=-1, keepdims=True)
    centred = values - center
    spread = jnp.mean(centred * centred, axis=-1, keepdims=True)
    return centred * lax.rsqrt(spread + EPSILON) * gain + shift


def doc_number(positions, doc_ends):
    return jnp.sum((doc_ends[None, :] <= positions[:, None]).astype(jnp.int32), axis=1)


def dot(a, b, dims):
    return lax.dot_general(a, b, (dims, ((), ())), preferred_element_type=F32)


NN = ((1,), (0,))
NT = ((1,), (1,))
TN = ((0,), (0,))


ORDER = (0, 1, 3, 2)


def remote(src, dst, sems, index, to):
    send, recv = sems
    return pltpu.make_async_remote_copy(
        src_ref=src,
        dst_ref=dst,
        send_sem=send.at[index],
        recv_sem=recv.at[index],
        device_id=to,
        device_id_type=pl.DeviceIdType.MESH,
    )


def feed_forward_body(
    a2_in,
    res_in,
    dy_in,
    gain_in,
    bias_in,
    dyg_hbm,
    wup_hbm,
    wdn_hbm,
    dattn_hbm,
    dhid_out,
    outp_hbm,
    up_a_own,
    up_b_own,
    dn_a_own,
    dn_b_own,
    up_a_got,
    up_b_got,
    dn_a_got,
    dn_b_got,
    small_out,
    wup,
    wdn,
    a2g,
    dyg,
    dact,
    act,
    dup,
    part,
    own,
    got,
    outp,
    up_c,
    dn_c,
    datt,
    local_sem,
    send_sem,
    recv_sem,
):
    sems = (send_sem, recv_sem)
    me = coords()
    x, y, z, core = me["x"], me["y"], me["z"], me["core"]
    other = 1 - core
    blk, width = a2_in.shape
    span = 4 * blk
    hidden = act.shape[1]

    load_down = pltpu.make_async_copy(wdn_hbm, wdn, local_sem.at[0])
    load_down.start()
    load_dy = []
    for p, k in enumerate(ORDER):
        load_dy.append(
            pltpu.make_async_copy(
                dyg_hbm.at[lax.rem(x + 4 - k, 4)], dyg.at[p], local_sem.at[1 + p]
            )
        )
        load_dy[-1].start()
    load_up = pltpu.make_async_copy(wup_hbm, wup, local_sem.at[5])
    load_up.start()

    greet(ring("x") + ring("y") + ring("z") + near())

    spread = [
        remote(a2_in, a2g.at[p], sems, p, peer(x=ORDER[p])) for p in (1, 2, 3)
    ]
    for copy in spread:
        copy.start()
    a2g[0] = a2_in[...]

    load_down.wait()
    for copy in load_dy:
        copy.wait()

    @pl.loop(0, 4)
    def _(j):
        tile = wdn[j // 2, pl.ds(2 * lax.rem(j, 2), 2)].reshape(512, width)
        cols = pl.ds(pl.multiple_of(j * 512, 512), 512)
        dact[:, cols] = dot(dyg[...].reshape(span, width), tile, NT)

    load_up.wait()
    for copy in spread:
        copy.wait_recv()

    @pl.loop(0, hidden // 256)
    def _(j):
        cols = pl.ds(pl.multiple_of(j * 256, 256), 256)
        u = dot(a2g[...].reshape(span, width), wup[:, :, :, :, cols].reshape(width, 256), NN)
        u = u + bias_in[:, cols]
        phi = 0.5 + 0.5 * lax.erf(u * math.sqrt(0.5))
        act[:, cols] = (u * phi).astype(BF)
        slope = phi + u * (jnp.exp(-0.5 * u * u) * (1.0 / math.sqrt(2.0 * math.pi)))
        d_up = (dact[:, cols] * slope).astype(BF)
        dup[:, cols] = d_up
        small_out[3:4, cols] = jnp.sum(d_up.astype(F32), axis=0, keepdims=True)

    def sends(j):
        cols = pl.ds(pl.multiple_of(j * 512, 512), 512)
        return [
            remote(
                part.at[p - 1, :, cols],
                got.at[p - 1, :, cols],
                sems,
                4 + 3 * j + p - 1,
                peer(x=-ORDER[p]),
            )
            for p in (3, 1, 2)
        ]

    @pl.loop(0, 4)
    def _(j):
        cols = pl.ds(pl.multiple_of(j * 512, 512), 512)
        d = dot(dup[...], wup[j].reshape(512, hidden), NT)
        own[:, cols] = d[:blk]
        for p in (1, 2, 3):
            part[p - 1, :, cols] = d[p * blk : (p + 1) * blk].astype(BF)
        for copy in sends(j):
            copy.start()

    @pl.loop(0, 4)
    def _(j):
        cols = pl.ds(pl.multiple_of(j * 512, 512), 512)
        o = dot(act[...], wdn[:, :, :, :, cols].reshape(hidden, 512), NN)
        outp[:, :, cols] = o.astype(BF).reshape(4, blk, 512)

    keep_out = pltpu.make_async_copy(outp, outp_hbm, local_sem.at[6])
    keep_out.start()

    def grad_down(c, t):
        cols = pl.ds(pl.multiple_of(c * (hidden // 2) + t * 256, 256), 256)
        return dot(act[:, cols], dyg[...].reshape(span, width), TN)

    def grad_up(t, c):
        cols = pl.ds(pl.multiple_of(t * 512 + c * 256, 256), 256)
        return dot(a2g[:, :, cols].reshape(span, 256), dup[...], TN)

    def swap_down(t):
        return remote(wdn.at[other, t], dn_c.at[t], sems, 16 + t, peer(core=1))

    def swap_up(t):
        return remote(wup.at[t, other], up_c.at[t], sems, 20 + t, peer(core=1))

    @pl.loop(0, 4)
    def _(t):
        wdn[other, t] = grad_down(other, t).astype(BF).reshape(4, 64, width)
        swap_down(t).start()

    @pl.loop(0, 4)
    def _(t):
        wup[t, other] = grad_up(t, other).astype(BF).reshape(4, 64, hidden)
        swap_up(t).start()

    @pl.loop(0, 4)
    def _(t):
        swap_down(t).wait_recv()
        total = grad_down(core, t) + dn_c[t].reshape(256, width).astype(F32)
        wdn[core, t] = total.astype(BF).reshape(4, 64, width)

    first = []

    def stage(src, dst, index, to):
        first.append(remote(src, dst, sems, index, to))
        first[-1].start()

    low, high = slice(0, 32), slice(32, 64)
    for k in (1, 3, 2):
        zz, yy = lax.rem(z + k, 4), lax.rem(y + k + 3, 4)
        stage(wdn.at[core, :, zz, low], dn_a_got.at[k - 1], 24 + k, peer(z=k))
        stage(wdn.at[core, yy, :, high], dn_b_got.at[k - 1], 28 + k, peer(y=k))

    @pl.loop(0, 4)
    def _(t):
        swap_up(t).wait_recv()
        total = grad_up(t, core) + up_c[t].reshape(256, hidden).astype(F32)
        wup[t, core] = total.astype(BF).reshape(4, 64, hidden)

    for k in (1, 3, 2):
        zz, yy = lax.rem(z + k, 4), lax.rem(y + k, 4)
        stage(wup.at[:, core, zz, low], up_a_got.at[k - 1], 32 + k, peer(z=k))
        stage(wup.at[yy, core, :, high], up_b_got.at[k - 1], 36 + k, peer(y=k))

    @pl.loop(0, 4)
    def _(j):
        for copy in sends(j):
            copy.wait_recv()

    small_out[0:3, :] = jnp.zeros((3, width), F32)
    small_out[4:8, :] = jnp.zeros((4, width), F32)
    gain = gain_in[...]

    @pl.loop(0, blk // 16)
    def _(i):
        rows = pl.ds(pl.multiple_of(i * 16, 16), 16)
        d = own[rows, :]
        for p in range(3):
            d = d + got[p, rows, :].astype(F32)
        v = res_in[rows, :]
        centred = v - jnp.mean(v, axis=-1, keepdims=True)
        s = lax.rsqrt(jnp.mean(centred * centred, axis=-1, keepdims=True) + EPSILON)
        n = centred * s
        dn = d * gain
        d_res = s * (
            dn
            - jnp.mean(dn, axis=-1, keepdims=True)
            - n * jnp.mean(dn * n, axis=-1, keepdims=True)
        )
        dy_own = dy_in[rows, :].astype(F32)
        hid = dy_own + d_res
        low_hid = hid.astype(BF)
        dhid_out[rows, :] = hid
        datt[rows, :] = low_hid
        small_out[0:1, :] += jnp.sum(d * n, axis=0, keepdims=True)
        small_out[1:2, :] += jnp.sum(d, axis=0, keepdims=True)
        small_out[2:3, :] += jnp.sum(low_hid.astype(F32), axis=0, keepdims=True)
        small_out[4:5, :] += jnp.sum(dy_own, axis=0, keepdims=True)

    attn = [
        remote(datt, dattn_hbm.at[x], sems, 40 + k, peer(x=k)) for k in (1, 3, 2)
    ]
    for copy in attn:
        copy.start()
    kept = [keep_out, pltpu.make_async_copy(datt, dattn_hbm.at[x], local_sem.at[7])]
    zy = lax.rem(y + 3, 4)
    kept.append(pltpu.make_async_copy(wdn.at[core, :, z, low], dn_a_own, local_sem.at[8]))
    kept.append(pltpu.make_async_copy(wdn.at[core, zy, :, high], dn_b_own, local_sem.at[9]))
    kept.append(pltpu.make_async_copy(wup.at[:, core, z, low], up_a_own, local_sem.at[10]))
    kept.append(pltpu.make_async_copy(wup.at[y, core, :, high], up_b_own, local_sem.at[11]))
    for copy in kept[1:]:
        copy.start()

    for copy in first + attn:
        copy.wait_recv()
    for copy in spread + first + attn:
        copy.wait_send()

    @pl.loop(0, 4)
    def _(j):
        for copy in sends(j):
            copy.wait_send()
        swap_down(j).wait_send()
        swap_up(j).wait_send()

    for copy in kept:
        copy.wait()


def feed_forward(collective_id, a2, residual, dy, gain, bias, dy_g, wup, wdn):
    blk, width = a2.shape
    hidden = wup.shape[-1]
    span = 4 * blk
    vmem = pl.BlockSpec(memory_space=pltpu.VMEM)
    hbm = pl.BlockSpec(memory_space=pl.ANY)
    quarter = (4, 32, width)
    outs = (
        [((4, blk, width), BF, hbm), ((blk, width), F32, vmem), ((4, blk, width), BF, hbm)]
        + [(quarter, BF, hbm)] * 4
        + [((3,) + quarter, BF, hbm)] * 4
        + [((8, width), F32, vmem)]
    )
    scratch = [
        ((4, 2, 4, 64, hidden), BF),
        ((2, 4, 4, 64, width), BF),
        ((4, blk, width), BF),
        ((4, blk, width), BF),
        ((span, hidden), F32),
        ((span, hidden), BF),
        ((span, hidden), BF),
        ((3, blk, width), BF),
        ((blk, width), F32),
        ((3, blk, width), BF),
        ((4, blk, width), BF),
        ((4, 4, 64, hidden), BF),
        ((4, 4, 64, width), BF),
        ((blk, width), BF),
    ]
    return pl.pallas_call(
        feed_forward_body,
        out_shape=tuple(jax.ShapeDtypeStruct(s, d) for s, d, _ in outs),
        in_specs=[vmem] * 5 + [hbm] * 3,
        out_specs=tuple(o[2] for o in outs),
        scratch_shapes=[pltpu.VMEM(s, d) for s, d in scratch]
        + [
            pltpu.SemaphoreType.DMA((12,)),
            pltpu.SemaphoreType.DMA((44,)),
            pltpu.SemaphoreType.DMA((44,)),
        ],
        compiler_params=pltpu.CompilerParams(
            collective_id=collective_id, has_side_effects=True, vmem_limit_bytes=62 << 20
        ),
        name="feed_forward",
    )(a2, residual, dy, gain.reshape(1, width), bias.reshape(1, hidden), dy_g, wup, wdn)


def norm_backward(d, v, gain):
    centred = v - jnp.mean(v, axis=-1, keepdims=True)
    s = lax.rsqrt(jnp.mean(centred * centred, axis=-1, keepdims=True) + EPSILON)
    n = centred * s
    dn = d * gain
    d_v = s * (
        dn - jnp.mean(dn, axis=-1, keepdims=True) - n * jnp.mean(dn * n, axis=-1, keepdims=True)
    )
    return d_v, n


def attention_backward_body(
    gain_in,
    bdown_in,
    ffsmall_in,
    dattn_hbm,
    wout_hbm,
    proj_hbm,
    edge_hbm,
    bias_hbm,
    a1_hbm,
    mixed_hbm,
    wqkv_hbm,
    tok_hbm,
    dhid_hbm,
    res_hbm,
    outp_hbm,
    ffo0,
    ffo1,
    ffo2,
    ffo3,
    ffg0,
    ffg1,
    ffg2,
    ffg3,
    out_o,
    gtok_o,
    gqkv_o,
    gout_o,
    gup_o,
    gdn_o,
    small_o,
    dattn,
    wout,
    proj,
    kv,
    bias,
    a1,
    mixed,
    wqkv,
    tok,
    dhid,
    res,
    outown,
    outgot,
    fo,
    fg,
    fs,
    fg2,
    fup,
    fdn,
    dmix,
    dkv,
    dqkv,
    dedge,
    dedge_got,
    part,
    got,
    qkv_c,
    out_c,
    qa,
    qb,
    oa,
    ob,
    qs,
    os_,
    qa2,
    qb2,
    oa2,
    ob2,
    fq,
    fout,
    sm,
    smc,
    smz,
    smy,
    local_sem,
    send_sem,
    recv_sem,
):
    sems = (send_sem, recv_sem)
    me = coords()
    x, y, z, core = me["x"], me["y"], me["z"], me["core"]
    other = 1 - core
    zy = lax.rem(y + 3, 4)
    blk, width = tok.shape
    span = 4 * blk
    partw = mixed.shape[1]
    heads = partw // HEAD
    scale = 1.0 / math.sqrt(HEAD)
    reach = W + blk
    used = [0]
    pending = []

    def load(src, dst):
        copy = pltpu.make_async_copy(src, dst, local_sem.at[used[0]])
        used[0] += 1
        copy.start()
        return copy

    def push(src, dst, index, to):
        copy = remote(src, dst, sems, index, to)
        copy.start()
        pending.append(copy)
        return copy

    l_dattn, l_wout = load(dattn_hbm, dattn), load(wout_hbm, wout)
    l_attn = [
        load(proj_hbm, proj),
        load(edge_hbm, kv.at[pl.ds(0, W)]),
        load(proj_hbm.at[:, pl.ds(partw, 2 * partw)], kv.at[pl.ds(W, span)]),
        load(bias_hbm, bias),
    ]
    l_ff = [load(s, fo.at[i]) for i, s in enumerate((ffo0, ffo1, ffo2, ffo3))]
    l_ff += [load(s, fg.at[i]) for i, s in enumerate((ffg0, ffg1, ffg2, ffg3))]
    l_wqkv, l_a1, l_mixed = load(wqkv_hbm, wqkv), load(a1_hbm, a1), load(mixed_hbm, mixed)
    l_end = [load(outp_hbm.at[0], outown), load(res_hbm, res)]
    l_end += [load(tok_hbm, tok), load(dhid_hbm, dhid)]

    greet(ring("x") + ring("y") + ring("z") + near() + [scattered(), collected()])

    p_out = [
        push(outp_hbm.at[p], outgot.at[p - 1], p, peer(x=-ORDER[p])) for p in (1, 2, 3)
    ]

    dkv[...] = jnp.zeros(dkv.shape, F32)
    l_dattn.wait()
    l_wout.wait()
    dmix[...] = dot(
        dattn[...].reshape(span, width), wout[...].reshape(partw, width), NT
    ).astype(BF)
    for copy in l_attn:
        copy.wait()

    def block(b):
        rows = pl.ds(pl.multiple_of(b * blk, blk), blk)
        window = pl.ds(pl.multiple_of(b * blk, blk), reach)
        for h in range(heads):
            cols = pl.ds(h * HEAD, HEAD)
            vcols = pl.ds(partw + h * HEAD, HEAD)
            q, k, v = proj[rows, cols], kv[window, cols], kv[window, vcols]
            s = dot(q, k, NT) * scale + bias[b]
            e = jnp.exp(s - jnp.max(s, axis=-1, keepdims=True))
            p = e * (1.0 / jnp.sum(e, axis=-1, keepdims=True))
            do = dmix[rows, cols]
            dp = dot(do, v, NT)
            ds = (p * (dp - jnp.sum(dp * p, axis=-1, keepdims=True))).astype(BF)
            dqkv[rows, cols] = (dot(ds, k, NN) * scale).astype(BF)
            dkv[window, cols] += dot(ds, q, TN) * scale
            dkv[window, vcols] += dot(p.astype(BF), do, TN)

    pl.loop(0, 2)(block)
    dedge[...] = dkv[0:W, :].astype(BF)
    p_edge = push(dedge, dedge_got, 4, peer(z=3))
    pl.loop(2, 4)(block)

    for copy in l_ff:
        copy.wait()

    @pl.loop(0, 4)
    def _(i):
        for c in range(4):
            total = fo[i, c].astype(F32)
            for g in range(3):
                total = total + fg[i, g, c].astype(F32)
            fs[i, c] = total.astype(BF)

    p_ff = []
    for k in (1, 3, 2):
        tz, ty, tyc = lax.rem(z + k, 4), lax.rem(y + k, 4), lax.rem(y + k + 3, 4)
        p_ff.append(push(fs.at[0, ty], fg2.at[0, k - 1], 4 + k, peer(y=k)))
        p_ff.append(push(fs.at[1, tz], fg2.at[1, k - 1], 7 + k, peer(z=k)))
        p_ff.append(push(fs.at[2, tyc], fg2.at[2, k - 1], 10 + k, peer(y=k)))
        p_ff.append(push(fs.at[3, tz], fg2.at[3, k - 1], 13 + k, peer(z=k)))

    p_edge.wait_recv()
    dqkv[0 : span - W, partw:] = dkv[W:span, :].astype(BF)
    dqkv[span - W :, partw:] = (dkv[span:, :] + dedge_got[...].astype(F32)).astype(BF)
    l_wqkv.wait()

    def sends(j):
        cols = pl.ds(pl.multiple_of(j * 512, 512), 512)
        return [
            remote(
                part.at[lax.rem(x + k, 4), :, cols],
                got.at[k - 1, :, cols],
                sems,
                20 + 3 * j + k - 1,
                peer(x=k),
            )
            for k in (2, 1, 3)
        ]

    @pl.loop(0, 4)
    def _(j):
        cols = pl.ds(pl.multiple_of(j * 512, 512), 512)
        d = dot(dqkv[...], wqkv[j].reshape(512, 3 * partw), NT)
        part[:, :, cols] = d.astype(BF).reshape(4, blk, 512)
        for copy in sends(j):
            copy.start()

    def grad_qkv(t, c):
        cols = pl.ds(pl.multiple_of(t * 512 + c * 256, 256), 256)
        return dot(a1[:, cols], dqkv[...], TN)

    def grad_out(c):
        cols = pl.ds(pl.multiple_of(c * 256, 256), 256)
        return dot(mixed[:, cols], dattn[...].reshape(span, width), TN)

    def swap(t):
        return remote(wqkv.at[t, other], qkv_c.at[t], sems, 32 + t, peer(core=1))

    l_a1.wait()

    @pl.loop(0, 4)
    def _(t):
        wqkv[t, other] = grad_qkv(t, other).astype(BF).reshape(4, 64, 3 * partw)
        swap(t).start()

    l_mixed.wait()
    wout[other] = grad_out(other).astype(BF).reshape(4, 4, 16, width)
    p_oc = push(wout.at[other], out_c, 36, peer(core=1))

    @pl.loop(0, 4)
    def _(t):
        swap(t).wait_recv()
        total = grad_qkv(t, core) + qkv_c[t].reshape(256, 3 * partw).astype(F32)
        wqkv[t, core] = total.astype(BF).reshape(4, 64, 3 * partw)

    low, high = slice(0, 32), slice(32, 64)
    left, right = slice(0, width // 2), slice(width // 2, width)
    p_q1, p_o1 = [], []
    for k in (1, 3, 2):
        tz, ty = lax.rem(z + k, 4), lax.rem(y + k, 4)
        p_q1.append(push(wqkv.at[:, core, tz, low], qa.at[k - 1], 36 + k, peer(z=k)))
        p_q1.append(push(wqkv.at[ty, core, :, high], qb.at[k - 1], 39 + k, peer(y=k)))

    p_oc.wait_recv()
    wout[core] = (
        grad_out(core) + out_c[...].reshape(256, width).astype(F32)
    ).astype(BF).reshape(4, 4, 16, width)
    for k in (1, 3, 2):
        tz, tyc = lax.rem(z + k, 4), lax.rem(y + k + 3, 4)
        p_o1.append(push(wout.at[core, :, tz, :, left], oa.at[k - 1], 42 + k, peer(z=k)))
        p_o1.append(push(wout.at[core, tyc, :, :, right], ob.at[k - 1], 45 + k, peer(y=k)))

    for copy in p_ff:
        copy.wait_recv()
    at = (y, z, zy, z)
    for i in range(4):
        total = fs[i, at[i]].astype(F32)
        for g in range(3):
            total = total + fg2[i, g].astype(F32)
        into, half = (fup, fdn)[i // 2], i % 2
        if i < 2:
            into[2 * half : 2 * half + 2] = total.astype(BF).reshape(2, 16, fup.shape[2])
        else:
            into[32 * half : 32 * half + 32, :] = total.astype(BF)
    p_x = [
        push(fup.at[lax.rem(x + k, 4)], gup_o.at[x], 48 + k, peer(x=k)) for k in (1, 3, 2)
    ]
    p_x.append(push(fdn, gdn_o, 52, collected()))
    kept = [load(fup.at[x], gup_o.at[x])]

    for copy in l_end:
        copy.wait()
    for copy in p_out:
        copy.wait_recv()

    @pl.loop(0, blk // 16)
    def _(i):
        rows = pl.ds(pl.multiple_of(i * 16, 16), 16)
        total = res[rows, :] + bdown_in[...] + outown[rows, :].astype(F32)
        for g in range(3):
            total = total + outgot[g, rows, :].astype(F32)
        out_o[rows, :] = total.astype(BF)

    sm[0, 0:5, :] = ffsmall_in[0:5, :]
    sm[0, 5:7, :] = jnp.zeros((2, width), F32)
    sm[0, 7:8, :] = jnp.zeros((1, width), F32)
    sm[0, 7:8, 0 : 3 * partw] = jnp.sum(dqkv[...].astype(F32), axis=0, keepdims=True)

    @pl.loop(0, 4)
    def _(j):
        for copy in sends(j):
            copy.wait_recv()

    gain = gain_in[...]

    @pl.loop(0, blk // 16)
    def _(i):
        rows = pl.ds(pl.multiple_of(i * 16, 16), 16)
        d = part[x, rows, :].astype(F32)
        for g in range(3):
            d = d + got[g, rows, :].astype(F32)
        d_in, n = norm_backward(d, tok[rows, :].astype(F32), gain)
        gtok_o[rows, :] = dhid[rows, :] + d_in
        sm[0, 5:6, :] += jnp.sum(d * n, axis=0, keepdims=True)
        sm[0, 6:7, :] += jnp.sum(d, axis=0, keepdims=True)

    p_sc = push(sm.at[0], smc, 53, peer(core=1))

    for copy in p_q1:
        copy.wait_recv()
    for c in range(4):
        ta, tb = wqkv[c, core, z, low].astype(F32), wqkv[y, core, c, high].astype(F32)
        for g in range(3):
            ta, tb = ta + qa[g, c].astype(F32), tb + qb[g, c].astype(F32)
        qs[0, c], qs[1, c] = ta.astype(BF), tb.astype(BF)
    p_q2 = []
    for k in (1, 3, 2):
        tz, ty = lax.rem(z + k, 4), lax.rem(y + k, 4)
        p_q2.append(push(qs.at[0, ty], qa2.at[k - 1], 53 + k, peer(y=k)))
        p_q2.append(push(qs.at[1, tz], qb2.at[k - 1], 56 + k, peer(z=k)))

    p_sc.wait_recv()
    sm[1] = sm[0] + smc[...]
    p_sz = [push(sm.at[1], smz.at[k - 1], 59 + k, peer(z=k)) for k in (1, 3, 2)]

    for copy in p_o1:
        copy.wait_recv()
    for c in range(4):
        ta, tb = wout[core, c, z, :, left].astype(F32), wout[core, zy, c, :, right].astype(F32)
        for g in range(3):
            ta, tb = ta + oa[g, c].astype(F32), tb + ob[g, c].astype(F32)
        os_[0, c], os_[1, c] = ta.astype(BF), tb.astype(BF)
    p_o2 = []
    for k in (1, 3, 2):
        tz, tyc = lax.rem(z + k, 4), lax.rem(y + k + 3, 4)
        p_o2.append(push(os_.at[0, tyc], oa2.at[k - 1], 62 + k, peer(y=k)))
        p_o2.append(push(os_.at[1, tz], ob2.at[k - 1], 65 + k, peer(z=k)))

    for copy in p_sz:
        copy.wait_recv()
    sm[2] = sm[1] + smz[0] + smz[1] + smz[2]
    p_sy = [push(sm.at[2], smy.at[k - 1], 68 + k, peer(y=k)) for k in (1, 3, 2)]

    for copy in p_q2:
        copy.wait_recv()
    ta, tb = qs[0, y].astype(F32), qs[1, z].astype(F32)
    for g in range(3):
        ta, tb = ta + qa2[g].astype(F32), tb + qb2[g].astype(F32)
    fq[0:2] = ta.astype(BF).reshape(2, 16, 3 * partw)
    fq[2:4] = tb.astype(BF).reshape(2, 16, 3 * partw)
    p_x += [
        push(fq.at[lax.rem(x + k, 4)], gqkv_o.at[x], 71 + k, peer(x=k)) for k in (1, 3, 2)
    ]
    kept.append(load(fq.at[x], gqkv_o.at[x]))

    for copy in p_o2:
        copy.wait_recv()
    ta, tb = os_[0, zy].astype(F32), os_[1, z].astype(F32)
    for g in range(3):
        ta, tb = ta + oa2[g].astype(F32), tb + ob2[g].astype(F32)
    fout[:, left], fout[:, right] = ta.astype(BF), tb.astype(BF)
    p_x.append(push(fout, gout_o, 75, collected()))

    for copy in p_sy:
        copy.wait_recv()
    sm[3] = sm[2] + smy[0] + smy[1] + smy[2]
    p_x += [push(sm.at[3], small_o.at[x], 75 + k, peer(x=k)) for k in (1, 3, 2)]
    kept.append(load(sm.at[3], small_o.at[x]))

    for copy in p_x:
        copy.wait_recv()
    for copy in pending:
        copy.wait_send()

    @pl.loop(0, 4)
    def _(j):
        for copy in sends(j):
            copy.wait_send()
        swap(j).wait_send()

    for copy in kept:
        copy.wait()


def attention_backward(
    collective_id,
    gain,
    b_down,
    ff_small,
    d_attn,
    wout,
    projected,
    edge,
    bias,
    a1,
    mixed,
    wqkv,
    tok,
    d_hidden,
    residual,
    out_part,
    ff_own,
    ff_got,
):
    blk, width = tok.shape
    span, partw = mixed.shape
    hidden = ff_own[0].shape[-1]
    vmem = pl.BlockSpec(memory_space=pltpu.VMEM)
    hbm = pl.BlockSpec(memory_space=pl.ANY)
    outs = [
        ((blk, width), BF, vmem),
        ((blk, width), F32, vmem),
        ((4, 16, 3 * partw), BF, hbm),
        ((16, width), BF, hbm),
        ((4, 16, hidden), BF, hbm),
        ((64, width), BF, hbm),
        ((4, 8, width), F32, hbm),
    ]
    half = width // 2
    scratch = [
        ((4, blk, width), BF),
        ((2, 4, 4, 16, width), BF),
        ((span, 3 * partw), BF),
        ((span + W, 2 * partw), BF),
        (bias.shape, F32),
        ((span, width), BF),
        ((span, partw), BF),
        ((4, 2, 4, 64, 3 * partw), BF),
        ((blk, width), BF),
        ((blk, width), F32),
        ((blk, width), F32),
        ((blk, width), BF),
        ((3, blk, width), BF),
        ((4, 4, 32, width), BF),
        ((4, 3, 4, 32, width), BF),
        ((4, 4, 32, width), BF),
        ((4, 3, 32, width), BF),
        ((4, 16, hidden), BF),
        ((64, width), BF),
        ((span, partw), BF),
        ((span + W, 2 * partw), F32),
        ((span, 3 * partw), BF),
        ((W, 2 * partw), BF),
        ((W, 2 * partw), BF),
        ((4, blk, width), BF),
        ((3, blk, width), BF),
        ((4, 4, 64, 3 * partw), BF),
        ((4, 4, 16, width), BF),
        ((3, 4, 32, 3 * partw), BF),
        ((3, 4, 32, 3 * partw), BF),
        ((3, 4, 16, half), BF),
        ((3, 4, 16, half), BF),
        ((2, 4, 32, 3 * partw), BF),
        ((2, 4, 16, half), BF),
        ((3, 32, 3 * partw), BF),
        ((3, 32, 3 * partw), BF),
        ((3, 16, half), BF),
        ((3, 16, half), BF),
        ((4, 16, 3 * partw), BF),
        ((16, width), BF),
        ((4, 8, width), F32),
        ((8, width), F32),
        ((3, 8, width), F32),
        ((3, 8, width), F32),
    ]
    return pl.pallas_call(
        attention_backward_body,
        out_shape=tuple(jax.ShapeDtypeStruct(s, d) for s, d, _ in outs),
        in_specs=[vmem] * 3 + [hbm] * 20,
        out_specs=tuple(o[2] for o in outs),
        scratch_shapes=[pltpu.VMEM(s, d) for s, d in scratch]
        + [
            pltpu.SemaphoreType.DMA((32,)),
            pltpu.SemaphoreType.DMA((80,)),
            pltpu.SemaphoreType.DMA((80,)),
        ],
        compiler_params=pltpu.CompilerParams(
            collective_id=collective_id, has_side_effects=True, vmem_limit_bytes=62 << 20
        ),
        name="attention_backward",
    )(
        gain.reshape(1, width),
        b_down.reshape(1, width),
        ff_small,
        d_attn,
        wout,
        projected,
        edge,
        bias,
        a1,
        mixed,
        wqkv,
        tok,
        d_hidden,
        residual,
        out_part,
        *ff_own,
        *ff_got,
    )


def local(
    tokens,
    grad_out,
    lengths,
    ln1_gain,
    ln1_bias,
    w_qkv,
    b_qv,
    w_out,
    b_out,
    ln2_gain,
    ln2_bias,
    w_up,
    b_up,
    w_down,
    b_down,
):
    blk, width = tokens.shape[1:]
    span = 4 * blk
    part = width // 4
    hidden = w_up.shape[1] // 4
    heads = HEADS // 4
    x_at, z_at = lax.axis_index("x"), lax.axis_index("z")
    scale = 1.0 / math.sqrt(HEAD)

    tok = tokens.reshape(blk, width)
    dy = grad_out.reshape(blk, width)
    small = jnp.concatenate([ln1_gain, ln1_bias, b_qv, b_out, ln2_gain, ln2_bias, b_up, b_down])
    small = jnp.pad(small.astype(F32), (0, 1024 - small.shape[0])).reshape(8, 128)
    qkv_parts = w_qkv.reshape(16, 3, 4, part).transpose(2, 0, 1, 3).reshape(4, 16, 3 * part)
    up_parts = w_up.reshape(16, 4, hidden).transpose(1, 0, 2)

    def first_body(comm, ins, outs):
        tok_r, dy_r, small_r, qkv_r, out_r = ins
        tok_g, small_g, dy_g, wq, wo = outs
        me = coords()
        slot = into_slot(comm, qkv_r, wq)
        spot = into_scattered(comm, out_r, wo)
        at = (me["y"], me["core"], me["z"])
        s0 = [comm.push(small_r, small_g.at[at + (me["x"],)], to) for to in ring("x")]
        s0.append(comm.local(small_r, small_g.at[at + (me["x"],)]))
        spread_x(comm, tok_r, tok_g)
        q, o = Gather(comm, wq, False), Gather(comm, wo, True)
        comm.arrived(slot)
        q.first()
        comm.arrived(s0)
        mine = small_g.at[at]
        s1 = [comm.push(mine, mine, to) for to in ring("z")]
        comm.arrived(spot)
        o.first()
        spread_x(comm, dy_r, dy_g)
        comm.arrived(s1)
        mine = small_g.at[me["y"], me["core"]]
        s2 = [comm.push(mine, mine, to) for to in ring("y")]
        q.second()
        o.second()
        comm.arrived(s2)
        mine = small_g.at[:, me["core"]]
        comm.push(mine, mine, peer(core=1))
        q.third()
        o.third()

    tok_g, small_g, dy_g, wqkv_g, wout_g = exchange(
        "gather_attn",
        0,
        first_body,
        lambda: gather_peers() + [scattered(), collected()],
        [tok, dy, small, qkv_parts, w_out],
        [
            ((4, blk, width), BF),
            ((4, 2, 4, 4, 8, 128), F32),
            ((4, blk, width), BF),
            ((4, 2, 4, 64, 3 * part), BF),
            ((2, 4, 4, 16, width), BF),
        ],
    )
    small_g = small_g.reshape(128, 1024)
    vectors, start = [], 0
    for size in (16, 16, 32, 16, 16, 16, 64, 16):
        vectors.append(small_g[:, start : start + size].reshape(128 * size))
        start += size
    gain1, shift1, bias_qv, bias_out, gain2, shift2, bias_up, bias_down = vectors
    weight_qkv = wqkv_g.reshape(width, 3 * part)
    weight_out = wout_g.reshape(part, width)

    inputs = tok_g.reshape(span, width).astype(F32)
    normed1 = layer_norm(inputs, gain1, shift1).astype(BF)
    bias_q = lax.dynamic_slice_in_dim(bias_qv, x_at * part, part)
    bias_v = lax.dynamic_slice_in_dim(bias_qv, width + x_at * part, part)
    bias_full = jnp.concatenate([bias_q, jnp.zeros((part,), F32), bias_v])
    projected = (dot(normed1, weight_qkv, NN) + bias_full).astype(BF)

    def second_body(comm, ins, outs):
        p_r, up_r, down_r = ins
        edge, wu, wd = outs
        comm.push(p_r.at[pl.ds(span - W, W), pl.ds(part, 2 * part)], edge, peer(z=1))
        slot = into_slot(comm, up_r, wu)
        spot = into_scattered(comm, down_r, wd)
        u = Gather(comm, wu, False)
        comm.arrived(slot)
        u.first()
        comm.arrived(spot)
        u.second()
        u.third()

    edge_kv, wup_g, wdown_s = exchange(
        "edge_and_up",
        1,
        second_body,
        lambda: gather_peers() + [scattered(), collected()],
        [projected, up_parts, w_down],
        [
            ((W, 2 * part), BF),
            ((4, 2, 4, 64, hidden), BF),
            ((2, 4, 4, 64, width), BF),
        ],
    )

    row_ends = jnp.cumsum(lengths.reshape(-1))
    q_pos = z_at * span + jnp.arange(span, dtype=jnp.int32)
    k_pos = z_at * span - W + jnp.arange(span + W, dtype=jnp.int32)
    q_doc, k_doc = doc_number(q_pos, row_ends), doc_number(k_pos, row_ends)
    reach = W + blk

    def windows(array):
        return jnp.stack([array[b * blk : b * blk + reach] for b in range(4)])

    qp, qd = q_pos.reshape(4, blk, 1), q_doc.reshape(4, blk, 1)
    kp, kd = windows(k_pos)[:, None, :], windows(k_doc)[:, None, :]
    visible = (qd == kd) & (kp <= qp) & (qp - kp < W) & (kp >= 0)

    keys = jnp.concatenate([edge_kv[:, :part], projected[:, part : 2 * part]])
    values = jnp.concatenate([edge_kv[:, part:], projected[:, 2 * part :]])
    q_heads = projected[:, :part].reshape(4, blk, heads, HEAD)
    k_heads = windows(keys).reshape(4, reach, heads, HEAD)
    v_heads = windows(values).reshape(4, reach, heads, HEAD)
    scores = jnp.einsum("bqhd,bkhd->bhqk", q_heads, k_heads, preferred_element_type=F32) * scale
    masked = jnp.where(visible[:, None], scores, NEG_FILL)
    peak = jnp.max(masked, axis=-1, keepdims=True)
    log_total = peak + jnp.log(jnp.sum(jnp.exp(masked - peak), axis=-1, keepdims=True))
    probs = jnp.exp(masked - log_total)
    probs_low = probs.astype(BF)
    mixed = jnp.einsum("bhqk,bkhd->bqhd", probs_low, v_heads, preferred_element_type=F32)
    mixed = mixed.reshape(span, part).astype(BF)
    attn_part = dot(mixed, weight_out, NN).reshape(4, blk, width)

    def third_body(comm, ins, outs):
        part_r, wd_in = ins
        got, wd = outs
        me = coords()
        split_x(comm, part_r, got)
        slot = (me["core"], lax.rem(me["y"] + 3, 4), me["z"])
        comm.arrived([comm.local(wd_in.at[slot], wd.at[slot])])
        d = Gather(comm, wd, True)
        d.first()
        d.second()
        d.third()

    attn_got, wdown_g = exchange(
        "sum_attn_and_down",
        2,
        third_body,
        gather_peers,
        [attn_part.astype(BF), wdown_s],
        [((3, blk, width), BF), ((2, 4, 4, 64, width), BF)],
    )

    own_tok = tok.astype(F32)
    residual = own_tok + pick(attn_part, x_at) + attn_got.astype(F32).sum(0) + bias_out
    normed2 = layer_norm(residual, gain2, shift2).astype(BF)

    bias_up_own = lax.dynamic_slice_in_dim(bias_up, x_at * hidden, hidden)
    (
        d_attn_g,
        d_hidden,
        out_part,
        up_a_own,
        up_b_own,
        down_a_own,
        down_b_own,
        up_a,
        up_b,
        down_a,
        down_b,
        ff_small,
    ) = feed_forward(3, normed2, residual, dy, gain2, bias_up_own, dy_g, wup_g, wdown_g)
    bias = jnp.where(visible, 0.0, NEG_FILL).astype(F32)
    out, grad_tokens, qkv_x, g_out_own, up_x, g_down_own, small_x = attention_backward(
        4,
        gain1,
        bias_down,
        ff_small,
        d_attn_g,
        wout_g,
        projected,
        edge_kv,
        bias,
        normed1,
        mixed,
        wqkv_g,
        tok,
        d_hidden,
        residual,
        out_part,
        (up_a_own, up_b_own, down_a_own, down_b_own),
        (up_a, up_b, down_a, down_b),
    )

    def columns(parts, groups):
        parts = parts.reshape(4, 16, groups, -1)
        return parts.transpose(1, 2, 0, 3).reshape(16, -1).astype(F32)

    me = coords()
    device = ((me["y"] * 2 + me["core"]) * 4 + me["z"]) * 4 + me["x"]
    shared = small_x.sum(0)

    def mine(vector, size):
        return lax.dynamic_slice_in_dim(vector, device * size, size)

    g_bqv = jnp.concatenate(
        [small_x[:, 7, :part].reshape(width), small_x[:, 7, 2 * part : 3 * part].reshape(width)]
    )
    return (
        out.reshape(1, blk, width),
        grad_tokens.reshape(1, blk, width),
        mine(shared[5], 16),
        mine(shared[6], 16),
        columns(qkv_x, 3),
        mine(g_bqv, 32),
        g_out_own.astype(F32),
        mine(shared[2], 16),
        mine(shared[0], 16),
        mine(shared[1], 16),
        columns(up_x, 1),
        mine(small_x[:, 3].reshape(4 * hidden), 64),
        g_down_own.astype(F32),
        mine(shared[4], 16),
    )


def solution(mesh):
    fine = Mesh(mesh.devices.reshape(4, 2, 4, 4), AXES)
    rows, seq = ("y", "core"), ("z", "x")
    every = rows + seq
    token = P(rows, seq, None)
    vec, mat = P(every), P(every, None)
    in_specs = (token, token, P(rows, None), vec, vec, mat, vec, mat, vec, vec, vec, mat, vec, mat, vec)
    out_specs = (token, token, vec, vec, mat, vec, mat, vec, vec, vec, mat, vec, mat, vec)
    return jax.shard_map(local, mesh=fine, in_specs=in_specs, out_specs=out_specs, check_vma=False)
```

```python
import functools
import math

import jax
import jax.numpy as jnp
from jax import lax
from jax.experimental import pallas as pl
from jax.experimental.pallas import tpu as pltpu
from jax.sharding import Mesh, PartitionSpec as P

HEADS = 16
HEAD = 128
W = 256
EPSILON = 1e-05
NEG_FILL = -1e30

AXES = ("y", "core", "z", "x")
SIZE = {"y": 4, "core": 2, "z": 4, "x": 4}
BF = jnp.bfloat16
F32 = jnp.float32
SEMS = 160


def coords():
    return {a: lax.axis_index(a) for a in AXES}


def peer(**delta):
    me = coords()
    return tuple(lax.rem(me[a] + delta.get(a, 0) % SIZE[a], SIZE[a]) for a in AXES)


class Comm:
    def __init__(self, send_sem, recv_sem):
        self.send_sem, self.recv_sem = send_sem, recv_sem
        self.count, self.open = 0, []

    def push(self, src, dst, to):
        copy = pltpu.make_async_remote_copy(
            src_ref=src,
            dst_ref=dst,
            send_sem=self.send_sem.at[self.count],
            recv_sem=self.recv_sem.at[self.count],
            device_id=to,
            device_id_type=pl.DeviceIdType.MESH,
        )
        self.count += 1
        copy.start()
        self.open.append([copy, True, True])
        return self.open[-1]

    def local(self, src, dst):
        copy = pltpu.make_async_copy(src, dst, self.send_sem.at[self.count])
        self.count += 1
        copy.start()
        self.open.append([copy, False, True])
        return self.open[-1]

    def arrived(self, entries):
        for entry in entries:
            if entry[2]:
                if entry[1]:
                    entry[0].wait_recv()
                else:
                    entry[0].wait()
                entry[2] = False

    def drain(self):
        self.arrived(self.open)
        for copy, remote_copy, _ in self.open:
            if remote_copy:
                copy.wait_send()
        self.open = []


def greet(devices):
    barrier = pltpu.get_barrier_semaphore()
    for device in devices:
        pl.semaphore_signal(barrier, inc=1, device_id=device, device_id_type=pl.DeviceIdType.MESH)
    pl.semaphore_wait(barrier, len(devices))


def ring(axis):
    return [peer(**{axis: k}) for k in (1, 3, 2)]


def near():
    return [peer(core=1)]


def everyone():
    return ring("x") + ring("y") + ring("z") + near()


def scattered():
    me = coords()
    return (lax.rem(me["z"] + 1, 4), me["core"], me["x"], me["y"])


def collected():
    me = coords()
    return (me["x"], me["core"], lax.rem(me["y"] + 3, 4), me["z"])


class Relay:
    def __init__(self, comm, axis, full, half):
        self.comm, self.axis, self.full, self.half = comm, axis, full, half
        self.me = lax.axis_index(axis)

    def to(self, k):
        return peer(**{self.axis: k})

    def start(self, src=None):
        own = self.full(self.me)
        src = own if src is None else src
        self.sent = [self.comm.push(src, own, self.to(1)), self.comm.push(src, own, self.to(3))]

    def near(self):
        self.comm.arrived(self.sent)
        before, after = lax.rem(self.me + 3, 4), lax.rem(self.me + 1, 4)
        up, down = self.half(before, 0), self.half(after, 1)
        self.passed = [self.comm.push(up, up, self.to(1)), self.comm.push(down, down, self.to(3))]

    def far(self):
        self.comm.arrived(self.passed)


class Gather:
    def __init__(self, comm, w, by_core, cut):
        self.comm, self.w, self.by_core, self.cut = comm, w, by_core, cut
        me = coords()
        self.y, self.core, self.z = me["y"], me["core"], me["z"]

    def slot(self, y, z, cut):
        place = (self.core, y, z) if self.by_core else (y, self.core, z)
        return self.w.at[place + self.cut[cut]]

    def row(self, y):
        return lax.rem(y + 3, 4) if self.by_core else y

    def first(self):
        a = self.slot(self.row(self.y), self.z, 0)
        b = self.slot(self.row(self.y), self.z, 1)
        self.one = [self.comm.push(a, a, to) for to in ring("z")]
        self.one += [self.comm.push(b, b, to) for to in ring("y")]

    def second(self, src_a=None, src_b=None):
        every = slice(None)
        self.a = Relay(
            self.comm,
            "y",
            lambda o: self.slot(self.row(o), every, 0),
            lambda o, h: self.slot(self.row(o), pl.ds(2 * h, 2), 0),
        )
        self.b = Relay(
            self.comm,
            "z",
            lambda o: self.slot(every, o, 1),
            lambda o, h: self.slot(pl.ds(2 * h, 2), o, 1),
        )
        self.a.start(src_a)
        self.b.start(src_b)

    def across(self, k):
        a, b = self.a.full(lax.rem(self.y + k, 4)), self.b.full(lax.rem(self.z + k, 4))
        return [self.comm.push(a, a, peer(core=1)), self.comm.push(b, b, peer(core=1))]

    def near(self):
        self.a.near()
        self.b.near()
        self.two = self.across(0) + self.across(1) + self.across(3)

    def far(self):
        self.a.far()
        self.b.far()
        self.two += self.across(2)

    def done(self):
        self.comm.arrived(self.two)


def by_rows(rows):
    return [(slice(0, rows // 2),), (slice(rows // 2, rows),)]


def by_columns(columns):
    every = slice(None)
    return [(every, slice(0, columns // 2)), (every, slice(columns // 2, columns))]


def dot(a, b, dims):
    return lax.dot_general(a, b, (dims, ((), ())), preferred_element_type=F32)


NN = ((1,), (0,))
NT = ((1,), (1,))
TN = ((0,), (0,))


def mask_of(lengths, first, blk, reach):
    q = first + lax.broadcasted_iota(jnp.int32, (blk, reach), 0)
    k = first - W + lax.broadcasted_iota(jnp.int32, (blk, reach), 1)
    q_doc, k_doc = jnp.zeros((blk, reach), jnp.int32), jnp.zeros((blk, reach), jnp.int32)
    end = 0
    for i in range(lengths.shape[1]):
        end = end + lengths[0, i]
        q_doc = q_doc + jnp.where(q >= end, 1, 0)
        k_doc = k_doc + jnp.where(k >= end, 1, 0)
    seen = (q_doc == k_doc) & (k <= q) & (q - k < W) & (k >= 0)
    return jnp.where(seen, 0.0, NEG_FILL).astype(F32)


SIZES = (16, 16, 32, 16, 16, 16, 64, 16)


def whole_vector(table, index, offset, count):
    size = SIZES[index]
    shift = size.bit_length() - 1
    row = lax.broadcasted_iota(jnp.int32, (128, 1024), 0)
    tile = lax.broadcasted_iota(jnp.int32, (128, 1024), 1)
    chosen = jnp.where(tile == row * 8 + index, 1.0, 0.0).astype(BF)
    share = dot(chosen, table, NN).astype(BF)
    row = lax.broadcasted_iota(jnp.int32, (128, count), 0)
    column = lax.broadcasted_iota(jnp.int32, (128, count), 1) + offset
    spread = jnp.where((column & (size - 1)) == row, 1.0, 0.0).astype(BF)
    values = jnp.where((column >> shift) == row, dot(share, spread, NN), 0.0)
    return jnp.sum(values, axis=0, keepdims=True)


def forward_body(
    lengths,
    tok_in,
    small_in,
    dy_hbm,
    wqkv_hbm,
    wout_hbm,
    wup_hbm,
    wdn_hbm,
    a2_o,
    res_o,
    vec_o,
    dyg_h,
    wq_h,
    wo_h,
    a1_h,
    q_h,
    kv_h,
    mixed_h,
    ua_h,
    ub_h,
    wd_h,
    wq,
    wo,
    tokg,
    a1,
    q,
    kv,
    mixed,
    part,
    got,
    own,
    tmp,
    smalls,
    uslot,
    rs_send,
    rs_recv,
    send_sem,
    recv_sem,
):
    comm = Comm(send_sem, recv_sem)
    me = coords()
    x, y, z, core = me["x"], me["y"], me["z"], me["core"]
    blk, width = tok_in.shape
    span = 4 * blk
    partw = q.shape[1]
    hidden = uslot.shape[1]
    heads = partw // HEAD
    reach = W + blk
    scale = 1.0 / math.sqrt(HEAD)
    mine16 = pl.ds(x * 16, 16)

    greet(everyone() + [scattered(), collected()])

    s_q = []
    for k in (1, 3, 2):
        for g in range(3):
            src = wqkv_hbm.at[:, pl.ds(g * width + lax.rem(x + k, 4) * partw, partw)]
            dst = wq.at[y, core, z, mine16, pl.ds(g * partw, partw)]
            s_q.append(comm.push(src, dst, peer(x=k)))
    for g in range(3):
        src = wqkv_hbm.at[:, pl.ds(g * width + x * partw, partw)]
        s_q.append(comm.local(src, wq.at[y, core, z, mine16, pl.ds(g * partw, partw)]))
    spot = smalls.at[y, core, pl.ds((z * 4 + x) * 8, 8)]
    s_small = [comm.push(small_in, spot, to) for to in ring("x")] + [comm.local(small_in, spot)]
    s_o = [comm.push(wout_hbm, wo.at[core, z, x], scattered())]
    tokens = Relay(
        comm, "x", lambda o: tokg.at[o], lambda o, h: tokg.at[o, pl.ds(h * blk // 2, blk // 2)]
    )
    tokens.start(tok_in)
    tokg[x] = tok_in[...]
    s_u = []
    for k in (1, 3, 2):
        src = wup_hbm.at[:, pl.ds(lax.rem(x + k, 4) * hidden, hidden)]
        s_u.append(comm.push(src, uslot.at[mine16], peer(x=k)))
    s_u.append(comm.local(wup_hbm.at[:, pl.ds(x * hidden, hidden)], uslot.at[mine16]))
    s_d = [comm.push(wdn_hbm, wd_h.at[core, z, x], scattered())]

    qkv_g = Gather(comm, wq, False, by_rows(64))
    out_g = Gather(comm, wo, True, by_columns(width))
    down_g = Gather(comm, wd_h, True, by_rows(64))

    comm.arrived(s_small)
    block = smalls.at[y, core, pl.ds(z * 32, 32)]
    s_small = [comm.push(block, block, to) for to in ring("z")]
    comm.arrived(s_q)
    qkv_g.first()
    comm.arrived(s_o)
    out_g.first()
    comm.arrived(s_small)
    block = smalls.at[y, core]
    s_small = [comm.push(block, block, to) for to in ring("y")]
    comm.arrived(qkv_g.one)
    qkv_g.second()
    comm.arrived(s_small)
    s_small = []
    for other_y in range(4):
        block = smalls.at[other_y, core]
        s_small.append(comm.push(block, block, peer(core=1)))
    comm.arrived(out_g.one)
    out_g.second()
    tokens.near()

    comm.arrived(s_small)
    table = smalls[...].reshape(1024, 128).astype(BF)
    vec_o[0:1, :] = whole_vector(table, 0, 0, width)
    vec_o[1:2, :] = whole_vector(table, 1, 0, width)
    gain, shift = vec_o[0:1, :], vec_o[1:2, :]

    def norm_block(o):
        @pl.loop(0, blk // 16)
        def _(i):
            rows = pl.ds(pl.multiple_of(i * 16, 16), 16)
            v = tokg[o, rows, :].astype(F32)
            centred = v - jnp.mean(v, axis=-1, keepdims=True)
            s = lax.rsqrt(jnp.mean(centred * centred, axis=-1, keepdims=True) + EPSILON)
            at = pl.ds(pl.multiple_of(o * blk + i * 16, 16), 16)
            a1[at, :] = (centred * s * gain + shift).astype(BF)

    norm_block(x)
    norm_block(lax.rem(x + 1, 4))
    qkv_g.near()
    norm_block(lax.rem(x + 3, 4))
    tokens.far()
    cotangent = Relay(
        comm, "x", lambda o: dyg_h.at[o], lambda o, h: dyg_h.at[o, pl.ds(h * blk // 2, blk // 2)]
    )
    cotangent.start(dy_hbm)
    comm.local(dy_hbm, dyg_h.at[x])
    norm_block(lax.rem(x + 2, 4))
    comm.local(a1, a1_h)
    qkv_g.far()
    out_g.near()
    comm.arrived(s_d)
    down_g.first()
    comm.arrived(s_u)
    low, high = uslot.at[0:32], uslot.at[32:64]
    for to in ring("z"):
        comm.push(low, ua_h.at[z], to)
    for to in ring("y"):
        comm.push(high, ub_h.at[y], to)
    comm.local(low, ua_h.at[z])
    comm.local(high, ub_h.at[y])

    vec_o[2:3, :] = jnp.zeros((1, width), F32)
    vec_o[2:3, 0:partw] = whole_vector(table, 2, x * partw, partw)
    vec_o[2:3, 2 * partw : 3 * partw] = whole_vector(table, 2, width + x * partw, partw)
    for i in (3, 4, 5, 7):
        vec_o[i : i + 1, :] = whole_vector(table, i, 0, width)
    vec_o[6:7, :] = whole_vector(table, 6, x * hidden, hidden)

    out_g.far()
    qkv_g.done()

    def project(cols, at):
        r = dot(a1[...], wq[:, :, :, :, cols].reshape(width, at), NN)
        return (r + vec_o[2:3, cols]).astype(BF)

    kv[W:, 0:partw] = project(slice(partw, 2 * partw), partw)
    kv[W:, partw:] = project(slice(2 * partw, 3 * partw), partw)
    s_edge = [comm.push(kv.at[pl.ds(span, W)], kv.at[pl.ds(0, W)], peer(z=1))]
    q[...] = project(slice(0, partw), partw)
    comm.local(wq, wq_h)
    comm.local(q, q_h)
    comm.arrived(down_g.one)
    down_g.second()
    cotangent.near()

    def attend(b):
        rows = pl.ds(pl.multiple_of(b * blk, blk), blk)
        window = pl.ds(pl.multiple_of(b * blk, blk), reach)
        mask = mask_of(lengths, z * span + b * blk, blk, reach)
        for h in range(heads):
            cols, vcols = pl.ds(h * HEAD, HEAD), pl.ds(partw + h * HEAD, HEAD)
            s = dot(q[rows, cols], kv[window, cols], NT) * scale + mask
            e = jnp.exp(s - jnp.max(s, axis=-1, keepdims=True))
            p = (e * (1.0 / jnp.sum(e, axis=-1, keepdims=True))).astype(BF)
            mixed[rows, cols] = dot(p, kv[window, vcols], NN).astype(BF)

    pl.loop(2, 4)(attend)
    comm.arrived(s_edge)
    pl.loop(0, 2)(attend)
    comm.local(kv, kv_h)
    comm.local(mixed, mixed_h)
    down_g.near()
    cotangent.far()
    out_g.done()
    comm.local(wo, wo_h)

    def sends(j):
        cols = pl.ds(pl.multiple_of(j * 512, 512), 512)
        return [
            remote(
                part.at[lax.rem(x + k, 4), :, cols],
                got.at[k - 1, :, cols],
                (rs_send, rs_recv),
                3 * j + k - 1,
                peer(x=k),
            )
            for k in (2, 1, 3)
        ]

    @pl.loop(0, 4)
    def _(j):
        cols = pl.ds(pl.multiple_of(j * 512, 512), 512)
        d = dot(mixed[...], wo[:, :, :, :, cols].reshape(partw, 512), NN)
        part[:, :, cols] = d.astype(BF).reshape(4, blk, 512)
        tmp[...] = d.reshape(4, blk, 512)
        own[:, cols] = tmp[x]
        for copy in sends(j):
            copy.start()

    down_g.far()

    @pl.loop(0, 4)
    def _(j):
        for copy in sends(j):
            copy.wait_recv()

    b_out, gain2, shift2 = vec_o[3:4, :], vec_o[4:5, :], vec_o[5:6, :]

    @pl.loop(0, blk // 16)
    def _(i):
        rows = pl.ds(pl.multiple_of(i * 16, 16), 16)
        v = tok_in[rows, :].astype(F32) + own[rows, :] + b_out
        for g in range(3):
            v = v + got[g, rows, :].astype(F32)
        res_o[rows, :] = v
        centred = v - jnp.mean(v, axis=-1, keepdims=True)
        s = lax.rsqrt(jnp.mean(centred * centred, axis=-1, keepdims=True) + EPSILON)
        a2_o[rows, :] = (centred * s * gain2 + shift2).astype(BF)

    @pl.loop(0, 4)
    def _(j):
        for copy in sends(j):
            copy.wait_send()

    comm.drain()


def forward(collective_id, lengths, tok, small, dy, w_qkv, w_out, w_up, w_down):
    blk, width = tok.shape
    span, partw, hidden = 4 * blk, width // 4, w_up.shape[1] // 4
    vmem = pl.BlockSpec(memory_space=pltpu.VMEM)
    hbm = pl.BlockSpec(memory_space=pl.ANY)
    outs = [
        ((blk, width), BF, vmem),
        ((blk, width), F32, vmem),
        ((8, width), F32, vmem),
        ((4, blk, width), BF, hbm),
        ((4, 2, 4, 64, 3 * partw), BF, hbm),
        ((2, 4, 4, 16, width), BF, hbm),
        ((span, width), BF, hbm),
        ((span, partw), BF, hbm),
        ((span + W, 2 * partw), BF, hbm),
        ((span, partw), BF, hbm),
        ((4, 32, hidden), BF, hbm),
        ((4, 32, hidden), BF, hbm),
        ((2, 4, 4, 64, width), BF, hbm),
    ]
    scratch = [
        ((4, 2, 4, 64, 3 * partw), BF),
        ((2, 4, 4, 16, width), BF),
        ((4, blk, width), BF),
        ((span, width), BF),
        ((span, partw), BF),
        ((span + W, 2 * partw), BF),
        ((span, partw), BF),
        ((4, blk, width), BF),
        ((3, blk, width), BF),
        ((blk, width), F32),
        ((4, blk, 512), F32),
        ((4, 2, 128, 128), F32),
        ((64, hidden), BF),
    ]
    return pl.pallas_call(
        forward_body,
        out_shape=tuple(jax.ShapeDtypeStruct(s, d) for s, d, _ in outs),
        in_specs=[pl.BlockSpec(memory_space=pltpu.SMEM)] + [vmem] * 2 + [hbm] * 5,
        out_specs=tuple(o[2] for o in outs),
        scratch_shapes=[pltpu.VMEM(s, d) for s, d in scratch]
        + [pltpu.SemaphoreType.DMA((n,)) for n in (12, 12, SEMS, SEMS)],
        compiler_params=pltpu.CompilerParams(
            collective_id=collective_id, has_side_effects=True, vmem_limit_bytes=62 << 20
        ),
        name="forward",
    )(lengths, tok, small, dy, w_qkv, w_out, w_up, w_down)


ORDER = (0, 1, 3, 2)


def remote(src, dst, sems, index, to):
    send, recv = sems
    return pltpu.make_async_remote_copy(
        src_ref=src,
        dst_ref=dst,
        send_sem=send.at[index],
        recv_sem=recv.at[index],
        device_id=to,
        device_id_type=pl.DeviceIdType.MESH,
    )


def feed_forward_body(
    a2_in,
    res_in,
    dy_in,
    vec_in,
    dyg_hbm,
    ua_hbm,
    ub_hbm,
    wdn_hbm,
    dattn_hbm,
    dhid_out,
    outp_hbm,
    up_a_own,
    up_b_own,
    dn_a_own,
    dn_b_own,
    up_a_got,
    up_b_got,
    dn_a_got,
    dn_b_got,
    small_out,
    wup,
    wdn,
    a2g,
    dyg,
    dact,
    act,
    dup,
    part,
    own,
    got,
    outp,
    up_c,
    dn_c,
    datt,
    local_sem,
    send_sem,
    recv_sem,
    comm_send,
    comm_recv,
):
    sems = (send_sem, recv_sem)
    comm = Comm(comm_send, comm_recv)
    me = coords()
    x, y, z, core = me["x"], me["y"], me["z"], me["core"]
    other = 1 - core
    blk, width = a2_in.shape
    span = 4 * blk
    hidden = act.shape[1]

    load_down = pltpu.make_async_copy(wdn_hbm, wdn, local_sem.at[0])
    load_down.start()
    load_dy = []
    for p, k in enumerate(ORDER):
        load_dy.append(
            pltpu.make_async_copy(
                dyg_hbm.at[lax.rem(x + 4 - k, 4)], dyg.at[p], local_sem.at[1 + p]
            )
        )
        load_dy[-1].start()
    low, high = slice(0, 32), slice(32, 64)
    load_up = [
        pltpu.make_async_copy(ua_hbm, wup.at[y, core, :, low], local_sem.at[5]),
        pltpu.make_async_copy(ub_hbm, wup.at[:, core, z, high], local_sem.at[7]),
    ]
    for copy in load_up:
        copy.start()

    greet(everyone())

    spread = [comm.push(a2_in, a2g.at[1], peer(x=1)), comm.push(a2_in, a2g.at[2], peer(x=3))]
    up_g = Gather(comm, wup, False, by_rows(64))
    up_g.second(ua_hbm, ub_hbm)
    a2g[0] = a2_in[...]

    load_down.wait()
    for copy in load_dy:
        copy.wait()

    @pl.loop(0, 4)
    def _(j):
        tile = wdn[j // 2, pl.ds(2 * lax.rem(j, 2), 2)].reshape(512, width)
        cols = pl.ds(pl.multiple_of(j * 512, 512), 512)
        dact[:, cols] = dot(dyg[...].reshape(span, width), tile, NT)

    comm.arrived(spread)
    top, bottom = pl.ds(0, blk // 2), pl.ds(blk // 2, blk // 2)
    passed = [
        comm.push(a2g.at[1, top], a2g.at[3, top], peer(x=1)),
        comm.push(a2g.at[2, bottom], a2g.at[3, bottom], peer(x=3)),
    ]
    for copy in load_up:
        copy.wait()
    up_g.near()
    comm.arrived(passed)
    up_g.far()
    up_g.done()

    @pl.loop(0, hidden // 256)
    def _(j):
        cols = pl.ds(pl.multiple_of(j * 256, 256), 256)
        u = dot(a2g[...].reshape(span, width), wup[:, :, :, :, cols].reshape(width, 256), NN)
        u = u + vec_in[6:7, cols]
        phi = 0.5 + 0.5 * lax.erf(u * math.sqrt(0.5))
        act[:, cols] = (u * phi).astype(BF)
        slope = phi + u * (jnp.exp(-0.5 * u * u) * (1.0 / math.sqrt(2.0 * math.pi)))
        d_up = (dact[:, cols] * slope).astype(BF)
        dup[:, cols] = d_up
        small_out[3:4, cols] = jnp.sum(d_up.astype(F32), axis=0, keepdims=True)

    def sends(j):
        cols = pl.ds(pl.multiple_of(j * 512, 512), 512)
        return [
            remote(
                part.at[p - 1, :, cols],
                got.at[p - 1, :, cols],
                sems,
                4 + 3 * j + p - 1,
                peer(x=-ORDER[p]),
            )
            for p in (3, 1, 2)
        ]

    @pl.loop(0, 4)
    def _(j):
        cols = pl.ds(pl.multiple_of(j * 512, 512), 512)
        d = dot(dup[...], wup[j].reshape(512, hidden), NT)
        own[:, cols] = d[:blk]
        for p in (1, 2, 3):
            part[p - 1, :, cols] = d[p * blk : (p + 1) * blk].astype(BF)
        for copy in sends(j):
            copy.start()

    @pl.loop(0, 4)
    def _(j):
        cols = pl.ds(pl.multiple_of(j * 512, 512), 512)
        o = dot(act[...], wdn[:, :, :, :, cols].reshape(hidden, 512), NN)
        outp[:, :, cols] = o.astype(BF).reshape(4, blk, 512)

    keep_out = pltpu.make_async_copy(outp, outp_hbm, local_sem.at[6])
    keep_out.start()

    def grad_down(c, t):
        cols = pl.ds(pl.multiple_of(c * (hidden // 2) + t * 256, 256), 256)
        return dot(act[:, cols], dyg[...].reshape(span, width), TN)

    def grad_up(t, c):
        cols = pl.ds(pl.multiple_of(t * 512 + c * 256, 256), 256)
        return dot(a2g[:, :, cols].reshape(span, 256), dup[...], TN)

    def swap_down(t):
        return remote(wdn.at[other, t], dn_c.at[t], sems, 16 + t, peer(core=1))

    def swap_up(t):
        return remote(wup.at[t, other], up_c.at[t], sems, 20 + t, peer(core=1))

    @pl.loop(0, 4)
    def _(t):
        wdn[other, t] = grad_down(other, t).astype(BF).reshape(4, 64, width)
        swap_down(t).start()

    comm.drain()

    @pl.loop(0, 4)
    def _(t):
        wup[t, other] = grad_up(t, other).astype(BF).reshape(4, 64, hidden)
        swap_up(t).start()

    @pl.loop(0, 4)
    def _(t):
        swap_down(t).wait_recv()
        total = grad_down(core, t) + dn_c[t].reshape(256, width).astype(F32)
        wdn[core, t] = total.astype(BF).reshape(4, 64, width)

    first = []

    def stage(src, dst, index, to):
        first.append(remote(src, dst, sems, index, to))
        first[-1].start()

    for k in (1, 3, 2):
        zz, yy = lax.rem(z + k, 4), lax.rem(y + k + 3, 4)
        stage(wdn.at[core, :, zz, low], dn_a_got.at[k - 1], 24 + k, peer(z=k))
        stage(wdn.at[core, yy, :, high], dn_b_got.at[k - 1], 28 + k, peer(y=k))

    @pl.loop(0, 4)
    def _(t):
        swap_up(t).wait_recv()
        total = grad_up(t, core) + up_c[t].reshape(256, hidden).astype(F32)
        wup[t, core] = total.astype(BF).reshape(4, 64, hidden)

    for k in (1, 3, 2):
        zz, yy = lax.rem(z + k, 4), lax.rem(y + k, 4)
        stage(wup.at[:, core, zz, low], up_a_got.at[k - 1], 32 + k, peer(z=k))
        stage(wup.at[yy, core, :, high], up_b_got.at[k - 1], 36 + k, peer(y=k))

    @pl.loop(0, 4)
    def _(j):
        for copy in sends(j):
            copy.wait_recv()

    small_out[0:3, :] = jnp.zeros((3, width), F32)
    small_out[4:8, :] = jnp.zeros((4, width), F32)
    gain = vec_in[4:5, :]

    @pl.loop(0, blk // 16)
    def _(i):
        rows = pl.ds(pl.multiple_of(i * 16, 16), 16)
        d = own[rows, :]
        for p in range(3):
            d = d + got[p, rows, :].astype(F32)
        v = res_in[rows, :]
        centred = v - jnp.mean(v, axis=-1, keepdims=True)
        s = lax.rsqrt(jnp.mean(centred * centred, axis=-1, keepdims=True) + EPSILON)
        n = centred * s
        dn = d * gain
        d_res = s * (
            dn
            - jnp.mean(dn, axis=-1, keepdims=True)
            - n * jnp.mean(dn * n, axis=-1, keepdims=True)
        )
        dy_own = dy_in[rows, :].astype(F32)
        hid = dy_own + d_res
        low_hid = hid.astype(BF)
        dhid_out[rows, :] = hid
        datt[rows, :] = low_hid
        small_out[0:1, :] += jnp.sum(d * n, axis=0, keepdims=True)
        small_out[1:2, :] += jnp.sum(d, axis=0, keepdims=True)
        small_out[2:3, :] += jnp.sum(low_hid.astype(F32), axis=0, keepdims=True)
        small_out[4:5, :] += jnp.sum(dy_own, axis=0, keepdims=True)

    attn = Relay(
        comm, "x", lambda o: dattn_hbm.at[o], lambda o, h: dattn_hbm.at[o, pl.ds(h * blk // 2, blk // 2)]
    )
    attn.start(datt)
    kept = [keep_out, pltpu.make_async_copy(datt, dattn_hbm.at[x], local_sem.at[7])]
    zy = lax.rem(y + 3, 4)
    kept.append(pltpu.make_async_copy(wdn.at[core, :, z, low], dn_a_own, local_sem.at[8]))
    kept.append(pltpu.make_async_copy(wdn.at[core, zy, :, high], dn_b_own, local_sem.at[9]))
    kept.append(pltpu.make_async_copy(wup.at[:, core, z, low], up_a_own, local_sem.at[10]))
    kept.append(pltpu.make_async_copy(wup.at[y, core, :, high], up_b_own, local_sem.at[11]))
    for copy in kept[1:]:
        copy.start()

    attn.near()
    for copy in first:
        copy.wait_recv()
    for copy in first:
        copy.wait_send()

    @pl.loop(0, 4)
    def _(j):
        for copy in sends(j):
            copy.wait_send()
        swap_down(j).wait_send()
        swap_up(j).wait_send()

    for copy in kept:
        copy.wait()
    comm.drain()


def feed_forward(collective_id, a2, residual, dy, vectors, dy_g, up_a, up_b, wdn):
    blk, width = a2.shape
    hidden = up_a.shape[-1]
    span = 4 * blk
    vmem = pl.BlockSpec(memory_space=pltpu.VMEM)
    hbm = pl.BlockSpec(memory_space=pl.ANY)
    quarter = (4, 32, width)
    outs = (
        [((4, blk, width), BF, hbm), ((blk, width), F32, vmem), ((4, blk, width), BF, hbm)]
        + [(quarter, BF, hbm)] * 4
        + [((3,) + quarter, BF, hbm)] * 4
        + [((8, width), F32, vmem)]
    )
    scratch = [
        ((4, 2, 4, 64, hidden), BF),
        ((2, 4, 4, 64, width), BF),
        ((4, blk, width), BF),
        ((4, blk, width), BF),
        ((span, hidden), F32),
        ((span, hidden), BF),
        ((span, hidden), BF),
        ((3, blk, width), BF),
        ((blk, width), F32),
        ((3, blk, width), BF),
        ((4, blk, width), BF),
        ((4, 4, 64, hidden), BF),
        ((4, 4, 64, width), BF),
        ((blk, width), BF),
    ]
    return pl.pallas_call(
        feed_forward_body,
        out_shape=tuple(jax.ShapeDtypeStruct(s, d) for s, d, _ in outs),
        in_specs=[vmem] * 4 + [hbm] * 4,
        out_specs=tuple(o[2] for o in outs),
        scratch_shapes=[pltpu.VMEM(s, d) for s, d in scratch]
        + [
            pltpu.SemaphoreType.DMA((12,)),
            pltpu.SemaphoreType.DMA((40,)),
            pltpu.SemaphoreType.DMA((40,)),
            pltpu.SemaphoreType.DMA((40,)),
            pltpu.SemaphoreType.DMA((40,)),
        ],
        compiler_params=pltpu.CompilerParams(
            collective_id=collective_id, has_side_effects=True, vmem_limit_bytes=62 << 20
        ),
        name="feed_forward",
    )(a2, residual, dy, vectors, dy_g, up_a, up_b, wdn)


def norm_backward(d, v, gain):
    centred = v - jnp.mean(v, axis=-1, keepdims=True)
    s = lax.rsqrt(jnp.mean(centred * centred, axis=-1, keepdims=True) + EPSILON)
    n = centred * s
    dn = d * gain
    d_v = s * (
        dn - jnp.mean(dn, axis=-1, keepdims=True) - n * jnp.mean(dn * n, axis=-1, keepdims=True)
    )
    return d_v, n


def attention_backward_body(
    lengths,
    vec_in,
    ffsmall_in,
    dattn_hbm,
    wout_hbm,
    q_hbm,
    kv_hbm,
    a1_hbm,
    mixed_hbm,
    wqkv_hbm,
    tok_hbm,
    dhid_hbm,
    res_hbm,
    outp_hbm,
    ffo0,
    ffo1,
    ffo2,
    ffo3,
    ffg0,
    ffg1,
    ffg2,
    ffg3,
    out_o,
    gtok_o,
    gqkv_o,
    gout_o,
    gup_o,
    gdn_o,
    small_o,
    dattn,
    wout,
    q_all,
    kv,
    a1,
    mixed,
    wqkv,
    tok,
    dhid,
    res,
    outown,
    outgot,
    fo,
    fg,
    fs,
    fg2,
    fup,
    fdn,
    dmix,
    dkv,
    dqkv,
    dedge,
    dedge_got,
    part,
    got,
    qkv_c,
    out_c,
    qa,
    qb,
    oa,
    ob,
    qs,
    os_,
    qa2,
    qb2,
    oa2,
    ob2,
    fq,
    fout,
    sm,
    smc,
    smz,
    smy,
    local_sem,
    send_sem,
    recv_sem,
):
    sems = (send_sem, recv_sem)
    me = coords()
    x, y, z, core = me["x"], me["y"], me["z"], me["core"]
    other = 1 - core
    zy = lax.rem(y + 3, 4)
    blk, width = tok.shape
    span = 4 * blk
    partw = mixed.shape[1]
    heads = partw // HEAD
    scale = 1.0 / math.sqrt(HEAD)
    reach = W + blk
    used = [0]
    pending = []

    def load(src, dst):
        copy = pltpu.make_async_copy(src, dst, local_sem.at[used[0]])
        used[0] += 1
        copy.start()
        return copy

    def push(src, dst, index, to):
        copy = remote(src, dst, sems, index, to)
        copy.start()
        pending.append(copy)
        return copy

    l_dattn, l_wout = load(dattn_hbm, dattn), load(wout_hbm, wout)
    l_attn = [load(q_hbm, q_all), load(kv_hbm, kv)]
    l_ff = [load(s, fo.at[i]) for i, s in enumerate((ffo0, ffo1, ffo2, ffo3))]
    l_ff += [load(s, fg.at[i]) for i, s in enumerate((ffg0, ffg1, ffg2, ffg3))]
    l_wqkv, l_a1, l_mixed = load(wqkv_hbm, wqkv), load(a1_hbm, a1), load(mixed_hbm, mixed)
    l_end = [load(outp_hbm.at[0], outown), load(res_hbm, res)]
    l_end += [load(tok_hbm, tok), load(dhid_hbm, dhid)]

    greet(ring("x") + ring("y") + ring("z") + near() + [scattered(), collected()])

    p_out = [
        push(outp_hbm.at[p], outgot.at[p - 1], p, peer(x=-ORDER[p])) for p in (1, 2, 3)
    ]

    dkv[...] = jnp.zeros(dkv.shape, F32)
    l_dattn.wait()
    l_wout.wait()
    dmix[...] = dot(
        dattn[...].reshape(span, width), wout[...].reshape(partw, width), NT
    ).astype(BF)
    for copy in l_attn:
        copy.wait()

    def block(b):
        rows = pl.ds(pl.multiple_of(b * blk, blk), blk)
        window = pl.ds(pl.multiple_of(b * blk, blk), reach)
        mask = mask_of(lengths, z * span + b * blk, blk, reach)
        for h in range(heads):
            cols = pl.ds(h * HEAD, HEAD)
            vcols = pl.ds(partw + h * HEAD, HEAD)
            q, k, v = q_all[rows, cols], kv[window, cols], kv[window, vcols]
            s = dot(q, k, NT) * scale + mask
            e = jnp.exp(s - jnp.max(s, axis=-1, keepdims=True))
            p = e * (1.0 / jnp.sum(e, axis=-1, keepdims=True))
            do = dmix[rows, cols]
            dp = dot(do, v, NT)
            ds = (p * (dp - jnp.sum(dp * p, axis=-1, keepdims=True))).astype(BF)
            dqkv[rows, cols] = (dot(ds, k, NN) * scale).astype(BF)
            dkv[window, cols] += dot(ds, q, TN) * scale
            dkv[window, vcols] += dot(p.astype(BF), do, TN)

    pl.loop(0, 2)(block)
    dedge[...] = dkv[0:W, :].astype(BF)
    p_edge = push(dedge, dedge_got, 4, peer(z=3))
    pl.loop(2, 4)(block)

    for copy in l_ff:
        copy.wait()

    @pl.loop(0, 4)
    def _(i):
        for c in range(4):
            total = fo[i, c].astype(F32)
            for g in range(3):
                total = total + fg[i, g, c].astype(F32)
            fs[i, c] = total.astype(BF)

    p_ff = []
    for k in (1, 3, 2):
        tz, ty, tyc = lax.rem(z + k, 4), lax.rem(y + k, 4), lax.rem(y + k + 3, 4)
        p_ff.append(push(fs.at[0, ty], fg2.at[0, k - 1], 4 + k, peer(y=k)))
        p_ff.append(push(fs.at[1, tz], fg2.at[1, k - 1], 7 + k, peer(z=k)))
        p_ff.append(push(fs.at[2, tyc], fg2.at[2, k - 1], 10 + k, peer(y=k)))
        p_ff.append(push(fs.at[3, tz], fg2.at[3, k - 1], 13 + k, peer(z=k)))

    p_edge.wait_recv()
    dqkv[0 : span - W, partw:] = dkv[W:span, :].astype(BF)
    dqkv[span - W :, partw:] = (dkv[span:, :] + dedge_got[...].astype(F32)).astype(BF)
    l_wqkv.wait()

    def sends(j):
        cols = pl.ds(pl.multiple_of(j * 512, 512), 512)
        return [
            remote(
                part.at[lax.rem(x + k, 4), :, cols],
                got.at[k - 1, :, cols],
                sems,
                20 + 3 * j + k - 1,
                peer(x=k),
            )
            for k in (2, 1, 3)
        ]

    @pl.loop(0, 4)
    def _(j):
        cols = pl.ds(pl.multiple_of(j * 512, 512), 512)
        d = dot(dqkv[...], wqkv[j].reshape(512, 3 * partw), NT)
        part[:, :, cols] = d.astype(BF).reshape(4, blk, 512)
        for copy in sends(j):
            copy.start()

    def grad_qkv(t, c):
        cols = pl.ds(pl.multiple_of(t * 512 + c * 256, 256), 256)
        return dot(a1[:, cols], dqkv[...], TN)

    def grad_out(c):
        cols = pl.ds(pl.multiple_of(c * 256, 256), 256)
        return dot(mixed[:, cols], dattn[...].reshape(span, width), TN)

    def swap(t):
        return remote(wqkv.at[t, other], qkv_c.at[t], sems, 32 + t, peer(core=1))

    l_a1.wait()

    @pl.loop(0, 4)
    def _(t):
        wqkv[t, other] = grad_qkv(t, other).astype(BF).reshape(4, 64, 3 * partw)
        swap(t).start()

    l_mixed.wait()
    wout[other] = grad_out(other).astype(BF).reshape(4, 4, 16, width)
    p_oc = push(wout.at[other], out_c, 36, peer(core=1))

    @pl.loop(0, 4)
    def _(t):
        swap(t).wait_recv()
        total = grad_qkv(t, core) + qkv_c[t].reshape(256, 3 * partw).astype(F32)
        wqkv[t, core] = total.astype(BF).reshape(4, 64, 3 * partw)

    low, high = slice(0, 32), slice(32, 64)
    left, right = slice(0, width // 2), slice(width // 2, width)
    p_q1, p_o1 = [], []
    for k in (1, 3, 2):
        tz, ty = lax.rem(z + k, 4), lax.rem(y + k, 4)
        p_q1.append(push(wqkv.at[:, core, tz, low], qa.at[k - 1], 36 + k, peer(z=k)))
        p_q1.append(push(wqkv.at[ty, core, :, high], qb.at[k - 1], 39 + k, peer(y=k)))

    p_oc.wait_recv()
    wout[core] = (
        grad_out(core) + out_c[...].reshape(256, width).astype(F32)
    ).astype(BF).reshape(4, 4, 16, width)
    for k in (1, 3, 2):
        tz, tyc = lax.rem(z + k, 4), lax.rem(y + k + 3, 4)
        p_o1.append(push(wout.at[core, :, tz, :, left], oa.at[k - 1], 42 + k, peer(z=k)))
        p_o1.append(push(wout.at[core, tyc, :, :, right], ob.at[k - 1], 45 + k, peer(y=k)))

    for copy in p_ff:
        copy.wait_recv()
    at = (y, z, zy, z)
    for i in range(4):
        total = fs[i, at[i]].astype(F32)
        for g in range(3):
            total = total + fg2[i, g].astype(F32)
        into, half = (fup, fdn)[i // 2], i % 2
        if i < 2:
            into[2 * half : 2 * half + 2] = total.astype(BF).reshape(2, 16, fup.shape[2])
        else:
            into[32 * half : 32 * half + 32, :] = total.astype(BF)
    p_x = [
        push(fup.at[lax.rem(x + k, 4)], gup_o.at[x], 48 + k, peer(x=k)) for k in (1, 3, 2)
    ]
    p_x.append(push(fdn, gdn_o, 52, collected()))
    kept = [load(fup.at[x], gup_o.at[x])]

    for copy in l_end:
        copy.wait()
    for copy in p_out:
        copy.wait_recv()

    @pl.loop(0, blk // 16)
    def _(i):
        rows = pl.ds(pl.multiple_of(i * 16, 16), 16)
        total = res[rows, :] + vec_in[7:8, :] + outown[rows, :].astype(F32)
        for g in range(3):
            total = total + outgot[g, rows, :].astype(F32)
        out_o[rows, :] = total.astype(BF)

    sm[0, 0:5, :] = ffsmall_in[0:5, :]
    sm[0, 5:7, :] = jnp.zeros((2, width), F32)
    sm[0, 7:8, :] = jnp.zeros((1, width), F32)
    sm[0, 7:8, 0 : 3 * partw] = jnp.sum(dqkv[...].astype(F32), axis=0, keepdims=True)

    @pl.loop(0, 4)
    def _(j):
        for copy in sends(j):
            copy.wait_recv()

    gain = vec_in[0:1, :]

    @pl.loop(0, blk // 16)
    def _(i):
        rows = pl.ds(pl.multiple_of(i * 16, 16), 16)
        d = part[x, rows, :].astype(F32)
        for g in range(3):
            d = d + got[g, rows, :].astype(F32)
        d_in, n = norm_backward(d, tok[rows, :].astype(F32), gain)
        gtok_o[rows, :] = dhid[rows, :] + d_in
        sm[0, 5:6, :] += jnp.sum(d * n, axis=0, keepdims=True)
        sm[0, 6:7, :] += jnp.sum(d, axis=0, keepdims=True)

    p_sc = push(sm.at[0], smc, 53, peer(core=1))

    for copy in p_q1:
        copy.wait_recv()
    for c in range(4):
        ta, tb = wqkv[c, core, z, low].astype(F32), wqkv[y, core, c, high].astype(F32)
        for g in range(3):
            ta, tb = ta + qa[g, c].astype(F32), tb + qb[g, c].astype(F32)
        qs[0, c], qs[1, c] = ta.astype(BF), tb.astype(BF)
    p_q2 = []
    for k in (1, 3, 2):
        tz, ty = lax.rem(z + k, 4), lax.rem(y + k, 4)
        p_q2.append(push(qs.at[0, ty], qa2.at[k - 1], 53 + k, peer(y=k)))
        p_q2.append(push(qs.at[1, tz], qb2.at[k - 1], 56 + k, peer(z=k)))

    p_sc.wait_recv()
    sm[1] = sm[0] + smc[...]
    p_sz = [push(sm.at[1], smz.at[k - 1], 59 + k, peer(z=k)) for k in (1, 3, 2)]

    for copy in p_o1:
        copy.wait_recv()
    for c in range(4):
        ta, tb = wout[core, c, z, :, left].astype(F32), wout[core, zy, c, :, right].astype(F32)
        for g in range(3):
            ta, tb = ta + oa[g, c].astype(F32), tb + ob[g, c].astype(F32)
        os_[0, c], os_[1, c] = ta.astype(BF), tb.astype(BF)
    p_o2 = []
    for k in (1, 3, 2):
        tz, tyc = lax.rem(z + k, 4), lax.rem(y + k + 3, 4)
        p_o2.append(push(os_.at[0, tyc], oa2.at[k - 1], 62 + k, peer(y=k)))
        p_o2.append(push(os_.at[1, tz], ob2.at[k - 1], 65 + k, peer(z=k)))

    for copy in p_sz:
        copy.wait_recv()
    sm[2] = sm[1] + smz[0] + smz[1] + smz[2]
    p_sy = [push(sm.at[2], smy.at[k - 1], 68 + k, peer(y=k)) for k in (1, 3, 2)]

    for copy in p_q2:
        copy.wait_recv()
    ta, tb = qs[0, y].astype(F32), qs[1, z].astype(F32)
    for g in range(3):
        ta, tb = ta + qa2[g].astype(F32), tb + qb2[g].astype(F32)
    fq[0:2] = ta.astype(BF).reshape(2, 16, 3 * partw)
    fq[2:4] = tb.astype(BF).reshape(2, 16, 3 * partw)
    p_x += [
        push(fq.at[lax.rem(x + k, 4)], gqkv_o.at[x], 71 + k, peer(x=k)) for k in (1, 3, 2)
    ]
    kept.append(load(fq.at[x], gqkv_o.at[x]))

    for copy in p_o2:
        copy.wait_recv()
    ta, tb = os_[0, zy].astype(F32), os_[1, z].astype(F32)
    for g in range(3):
        ta, tb = ta + oa2[g].astype(F32), tb + ob2[g].astype(F32)
    fout[:, left], fout[:, right] = ta.astype(BF), tb.astype(BF)
    p_x.append(push(fout, gout_o, 75, collected()))

    for copy in p_sy:
        copy.wait_recv()
    sm[3] = sm[2] + smy[0] + smy[1] + smy[2]
    p_x += [push(sm.at[3], small_o.at[x], 75 + k, peer(x=k)) for k in (1, 3, 2)]
    kept.append(load(sm.at[3], small_o.at[x]))

    for copy in p_x:
        copy.wait_recv()
    for copy in pending:
        copy.wait_send()

    @pl.loop(0, 4)
    def _(j):
        for copy in sends(j):
            copy.wait_send()
        swap(j).wait_send()

    for copy in kept:
        copy.wait()


def attention_backward(
    collective_id,
    lengths,
    vectors,
    ff_small,
    d_attn,
    wout,
    q,
    kv,
    a1,
    mixed,
    wqkv,
    tok,
    d_hidden,
    residual,
    out_part,
    ff_own,
    ff_got,
):
    blk, width = tok.shape
    span, partw = mixed.shape
    hidden = ff_own[0].shape[-1]
    vmem = pl.BlockSpec(memory_space=pltpu.VMEM)
    hbm = pl.BlockSpec(memory_space=pl.ANY)
    outs = [
        ((blk, width), BF, vmem),
        ((blk, width), F32, vmem),
        ((4, 16, 3 * partw), BF, hbm),
        ((16, width), BF, hbm),
        ((4, 16, hidden), BF, hbm),
        ((64, width), BF, hbm),
        ((4, 8, width), F32, hbm),
    ]
    half = width // 2
    scratch = [
        ((4, blk, width), BF),
        ((2, 4, 4, 16, width), BF),
        ((span, partw), BF),
        ((span + W, 2 * partw), BF),
        ((span, width), BF),
        ((span, partw), BF),
        ((4, 2, 4, 64, 3 * partw), BF),
        ((blk, width), BF),
        ((blk, width), F32),
        ((blk, width), F32),
        ((blk, width), BF),
        ((3, blk, width), BF),
        ((4, 4, 32, width), BF),
        ((4, 3, 4, 32, width), BF),
        ((4, 4, 32, width), BF),
        ((4, 3, 32, width), BF),
        ((4, 16, hidden), BF),
        ((64, width), BF),
        ((span, partw), BF),
        ((span + W, 2 * partw), F32),
        ((span, 3 * partw), BF),
        ((W, 2 * partw), BF),
        ((W, 2 * partw), BF),
        ((4, blk, width), BF),
        ((3, blk, width), BF),
        ((4, 4, 64, 3 * partw), BF),
        ((4, 4, 16, width), BF),
        ((3, 4, 32, 3 * partw), BF),
        ((3, 4, 32, 3 * partw), BF),
        ((3, 4, 16, half), BF),
        ((3, 4, 16, half), BF),
        ((2, 4, 32, 3 * partw), BF),
        ((2, 4, 16, half), BF),
        ((3, 32, 3 * partw), BF),
        ((3, 32, 3 * partw), BF),
        ((3, 16, half), BF),
        ((3, 16, half), BF),
        ((4, 16, 3 * partw), BF),
        ((16, width), BF),
        ((4, 8, width), F32),
        ((8, width), F32),
        ((3, 8, width), F32),
        ((3, 8, width), F32),
    ]
    return pl.pallas_call(
        attention_backward_body,
        out_shape=tuple(jax.ShapeDtypeStruct(s, d) for s, d, _ in outs),
        in_specs=[pl.BlockSpec(memory_space=pltpu.SMEM)] + [vmem] * 2 + [hbm] * 19,
        out_specs=tuple(o[2] for o in outs),
        scratch_shapes=[pltpu.VMEM(s, d) for s, d in scratch]
        + [
            pltpu.SemaphoreType.DMA((32,)),
            pltpu.SemaphoreType.DMA((80,)),
            pltpu.SemaphoreType.DMA((80,)),
        ],
        compiler_params=pltpu.CompilerParams(
            collective_id=collective_id, has_side_effects=True, vmem_limit_bytes=62 << 20
        ),
        name="attention_backward",
    )(
        lengths,
        vectors,
        ff_small,
        d_attn,
        wout,
        q,
        kv,
        a1,
        mixed,
        wqkv,
        tok,
        d_hidden,
        residual,
        out_part,
        *ff_own,
        *ff_got,
    )


def local(
    tokens,
    grad_out,
    lengths,
    ln1_gain,
    ln1_bias,
    w_qkv,
    b_qv,
    w_out,
    b_out,
    ln2_gain,
    ln2_bias,
    w_up,
    b_up,
    w_down,
    b_down,
):
    blk, width = tokens.shape[1:]
    part = width // 4
    hidden = w_up.shape[1] // 4
    tok = tokens.reshape(blk, width)
    dy = grad_out.reshape(blk, width)
    small = jnp.zeros((1024,), F32)
    vectors = (ln1_gain, ln1_bias, b_qv, b_out, ln2_gain, ln2_bias, b_up, b_down)
    for i, vector in enumerate(vectors):
        size = vector.shape[0]
        small = small + jnp.pad(vector.astype(F32), (i * 128, 1024 - i * 128 - size))
    (
        a2,
        residual,
        vectors,
        dy_g,
        wqkv_g,
        wout_g,
        a1,
        query,
        kv,
        mixed,
        up_a,
        up_b,
        wdown_g,
    ) = forward(0, lengths, tok, small.reshape(8, 128), dy, w_qkv, w_out, w_up, w_down)
    (
        d_attn_g,
        d_hidden,
        out_part,
        up_a_own,
        up_b_own,
        down_a_own,
        down_b_own,
        up_a_got,
        up_b_got,
        down_a_got,
        down_b_got,
        ff_small,
    ) = feed_forward(1, a2, residual, dy, vectors, dy_g, up_a, up_b, wdown_g)
    out, grad_tokens, qkv_x, g_out_own, up_x, g_down_own, small_x = attention_backward(
        2,
        lengths,
        vectors,
        ff_small,
        d_attn_g,
        wout_g,
        query,
        kv,
        a1,
        mixed,
        wqkv_g,
        tok,
        d_hidden,
        residual,
        out_part,
        (up_a_own, up_b_own, down_a_own, down_b_own),
        (up_a_got, up_b_got, down_a_got, down_b_got),
    )

    def columns(parts, groups):
        parts = parts.reshape(4, 16, groups, -1)
        return parts.transpose(1, 2, 0, 3).reshape(16, -1).astype(F32)

    me = coords()
    device = ((me["y"] * 2 + me["core"]) * 4 + me["z"]) * 4 + me["x"]
    shared = small_x.sum(0)

    def mine(vector, size):
        return lax.dynamic_slice_in_dim(vector, device * size, size)

    g_bqv = jnp.concatenate(
        [small_x[:, 7, :part].reshape(width), small_x[:, 7, 2 * part : 3 * part].reshape(width)]
    )
    return (
        out.reshape(1, blk, width),
        grad_tokens.reshape(1, blk, width),
        mine(shared[5], 16),
        mine(shared[6], 16),
        columns(qkv_x, 3),
        mine(g_bqv, 32),
        g_out_own.astype(F32),
        mine(shared[2], 16),
        mine(shared[0], 16),
        mine(shared[1], 16),
        columns(up_x, 1),
        mine(small_x[:, 3].reshape(4 * hidden), 64),
        g_down_own.astype(F32),
        mine(shared[4], 16),
    )


def solution(mesh):
    fine = Mesh(mesh.devices.reshape(4, 2, 4, 4), AXES)
    rows, seq = ("y", "core"), ("z", "x")
    every = rows + seq
    token = P(rows, seq, None)
    vec, mat = P(every), P(every, None)
    in_specs = (token, token, P(rows, None), vec, vec, mat, vec, mat, vec, vec, vec, mat, vec, mat, vec)
    out_specs = (token, token, vec, vec, mat, vec, mat, vec, vec, vec, mat, vec, mat, vec)
    return jax.shard_map(local, mesh=fine, in_specs=in_specs, out_specs=out_specs, check_vma=False)
```

```python
import functools
import math

import jax
import jax.numpy as jnp
from jax import lax
from jax.experimental import pallas as pl
from jax.experimental.pallas import tpu as pltpu
from jax.sharding import Mesh, PartitionSpec as P

HEADS = 16
HEAD = 128
W = 256
EPSILON = 1e-05
NEG_FILL = -1e30

AXES = ("y", "core", "z", "x")
SIZE = {"y": 4, "core": 2, "z": 4, "x": 4}
BF = jnp.bfloat16
F32 = jnp.float32
SEMS = 180


def coords():
    return {a: lax.axis_index(a) for a in AXES}


def peer(**delta):
    me = coords()
    return tuple(lax.rem(me[a] + delta.get(a, 0) % SIZE[a], SIZE[a]) for a in AXES)


class Comm:
    def __init__(self, send_sem, recv_sem, base=0, room=SEMS):
        self.send_sem, self.recv_sem = send_sem, recv_sem
        self.count, self.last, self.open = base, base + room, []

    def push(self, src, dst, to):
        copy = pltpu.make_async_remote_copy(
            src_ref=src,
            dst_ref=dst,
            send_sem=self.send_sem.at[self.count],
            recv_sem=self.recv_sem.at[self.count],
            device_id=to,
            device_id_type=pl.DeviceIdType.MESH,
        )
        assert self.count < self.last
        self.count += 1
        copy.start()
        self.open.append([copy, True, True])
        return self.open[-1]

    def local(self, src, dst):
        copy = pltpu.make_async_copy(src, dst, self.send_sem.at[self.count])
        self.count += 1
        copy.start()
        self.open.append([copy, False, True])
        return self.open[-1]

    def arrived(self, entries):
        for entry in entries:
            if entry[2]:
                if entry[1]:
                    entry[0].wait_recv()
                else:
                    entry[0].wait()
                entry[2] = False

    def drain(self):
        self.arrived(self.open)
        for copy, remote_copy, _ in self.open:
            if remote_copy:
                copy.wait_send()
        self.open = []


def greet(devices):
    barrier = pltpu.get_barrier_semaphore()
    for device in devices:
        pl.semaphore_signal(barrier, inc=1, device_id=device, device_id_type=pl.DeviceIdType.MESH)
    pl.semaphore_wait(barrier, len(devices))


def ring(axis):
    return [peer(**{axis: k}) for k in (1, 3, 2)]


def near():
    return [peer(core=1)]


def plane():
    return [peer(y=i // 4, z=i % 4) for i in range(1, 16)]


def everyone():
    return ring("x") + ring("y") + ring("z") + near()


def scattered():
    me = coords()
    return (lax.rem(me["z"] + 1, 4), me["core"], me["x"], me["y"])


def collected():
    me = coords()
    return (me["x"], me["core"], lax.rem(me["y"] + 3, 4), me["z"])


class Relay:
    def __init__(self, comm, axis, full, half):
        self.comm, self.axis, self.full, self.half = comm, axis, full, half
        self.me = lax.axis_index(axis)

    def to(self, k):
        return peer(**{self.axis: k})

    def start(self, src=None):
        own = self.full(self.me)
        src = own if src is None else src
        self.sent = [self.comm.push(src, own, self.to(1)), self.comm.push(src, own, self.to(3))]

    def near(self):
        self.comm.arrived(self.sent)
        before, after = lax.rem(self.me + 3, 4), lax.rem(self.me + 1, 4)
        up, down = self.half(before, 0), self.half(after, 1)
        self.passed = [self.comm.push(up, up, self.to(1)), self.comm.push(down, down, self.to(3))]

    def far(self):
        self.comm.arrived(self.passed)


class Gather:
    def __init__(self, comm, w, by_core, cut, shift=0):
        self.comm, self.w, self.by_core, self.cut = comm, w, by_core, cut
        self.shift = shift
        me = coords()
        self.y, self.core, self.z = me["y"], me["core"], me["z"]

    def slot(self, y, z, cut):
        place = (self.core, y, z) if self.by_core else (y, self.core, z)
        return self.w.at[place + self.cut[cut]]

    def row(self, y):
        return lax.rem(y + self.shift, 4)

    def first(self):
        self.first_a()
        self.first_b()
        self.one = self.one_a + self.one_b

    def first_a(self):
        a = self.slot(self.row(self.y), self.z, 0)
        self.one_a = [self.comm.push(a, a, to) for to in ring("z")]

    def first_b(self):
        b = self.slot(self.row(self.y), self.z, 1)
        self.one_b = [self.comm.push(b, b, to) for to in ring("y")]

    def second(self):
        self.second_a()
        self.second_b()

    def second_a(self):
        every = slice(None)
        self.a = Relay(
            self.comm,
            "y",
            lambda o: self.slot(self.row(o), every, 0),
            lambda o, h: self.slot(self.row(o), pl.ds(2 * h, 2), 0),
        )
        self.a.start()

    def second_b(self):
        every = slice(None)
        self.b = Relay(
            self.comm,
            "z",
            lambda o: self.slot(every, o, 1),
            lambda o, h: self.slot(pl.ds(2 * h, 2), o, 1),
        )
        self.b.start()

    def across(self, relay, k):
        block = relay.full(lax.rem(relay.me + k, 4))
        self.two.append(self.comm.push(block, block, peer(core=1)))

    def near_a(self):
        self.two = []
        self.a.near()
        for k in (0, 1, 3):
            self.across(self.a, k)

    def near_b(self):
        self.b.near()
        for k in (0, 1, 3):
            self.across(self.b, k)

    def near(self):
        self.near_a()
        self.near_b()

    def far_a(self):
        self.a.far()
        self.across(self.a, 2)

    def far_b(self):
        self.b.far()
        self.across(self.b, 2)

    def far(self):
        self.far_a()
        self.far_b()

    def done(self):
        self.comm.arrived(self.two)


def by_rows(rows):
    return [(slice(0, rows // 2),), (slice(rows // 2, rows),)]


def by_columns(columns):
    every = slice(None)
    return [(every, slice(0, columns // 2)), (every, slice(columns // 2, columns))]


def dot(a, b, dims):
    return lax.dot_general(a, b, (dims, ((), ())), preferred_element_type=F32)


NN = ((1,), (0,))
NT = ((1,), (1,))
TN = ((0,), (0,))


def mask_of(lengths, first, blk, reach):
    q = first + lax.broadcasted_iota(jnp.int32, (blk, reach), 0)
    k = first - W + lax.broadcasted_iota(jnp.int32, (blk, reach), 1)
    q_doc, k_doc = jnp.zeros((blk, reach), jnp.int32), jnp.zeros((blk, reach), jnp.int32)
    end = 0
    for i in range(lengths.shape[1]):
        end = end + lengths[0, i]
        q_doc = q_doc + jnp.where(q >= end, 1, 0)
        k_doc = k_doc + jnp.where(k >= end, 1, 0)
    seen = (q_doc == k_doc) & (k <= q) & (q - k < W) & (k >= 0)
    return jnp.where(seen, 0.0, NEG_FILL).astype(F32)


def shuffle():
    row = lax.broadcasted_iota(jnp.int32, (512, 512), 0)
    column = lax.broadcasted_iota(jnp.int32, (512, 512), 1)
    source = 64 * ((column >> 4) & 7) + 16 * (column >> 7) + (column & 15)
    return jnp.where(source == row, 1.0, 0.0).astype(BF)


def whole_vector(table, index, offset, count, size, lane):
    shift = size.bit_length() - 1
    row = lax.broadcasted_iota(jnp.int32, (128, 1024), 0)
    tile = lax.broadcasted_iota(jnp.int32, (128, 1024), 1)
    chosen = jnp.where(tile == row * 8 + index, 1.0, 0.0).astype(BF)
    share = dot(chosen, table, NN).astype(BF)
    row = lax.broadcasted_iota(jnp.int32, (128, count), 0)
    column = lax.broadcasted_iota(jnp.int32, (128, count), 1) + offset
    spread = jnp.where((column & (size - 1)) + lane == row, 1.0, 0.0).astype(BF)
    values = jnp.where((column >> shift) == row, dot(share, spread, NN), 0.0)
    return jnp.sum(values, axis=0, keepdims=True)


ORDER = (0, 1, 3, 2)


def remote(src, dst, sems, index, to):
    send, recv = sems
    return pltpu.make_async_remote_copy(
        src_ref=src,
        dst_ref=dst,
        send_sem=send.at[index],
        recv_sem=recv.at[index],
        device_id=to,
        device_id_type=pl.DeviceIdType.MESH,
    )


def forward_body(
    lengths,
    tok_in,
    small_in,
    wup_in,
    dy_in,
    wdn_in,
    wqkv_hbm,
    wout_hbm,
    vec_o,
    res_o,
    dhid_out,
    small_out,
    wq_h,
    wo_h,
    a1_h,
    q_h,
    kv_h,
    mixed_h,
    dattn_hbm,
    outp_hbm,
    up_a_own,
    up_b_own,
    dn_a_own,
    dn_b_own,
    up_a_got,
    up_b_got,
    dn_a_got,
    dn_b_got,
    wup,
    wdn,
    cc,
    wo,
    tokg,
    act,
    dup,
    dact,
    q,
    kv,
    mixed,
    dyg,
    part,
    got,
    own,
    outp,
    dattn,
    smalls,
    stack,
    uparts,
    local_sem,
    free_sem,
    rs_send,
    rs_recv,
    ff_send,
    ff_recv,
    send_sem,
    recv_sem,
):
    groups, taken = [], [0]

    def group(room):
        comm = Comm(send_sem, recv_sem, taken[0], room)
        taken[0] += room
        groups.append(comm)
        return comm

    c_q, c_o, c_u, c_d = group(36), group(26), group(26), group(26)
    c_small, c_tok, comm = group(28), group(4), group(32)
    sems = (ff_send, ff_recv)
    me = coords()
    x, y, z, core = me["x"], me["y"], me["z"], me["core"]
    other = 1 - core
    blk, width = tok_in.shape
    span = 4 * blk
    partw = q.shape[1]
    hidden = act.shape[1]
    heads = partw // HEAD
    reach = W + blk
    scale = 1.0 / math.sqrt(HEAD)
    mine16 = pl.ds(x * 16, 16)
    low, high = slice(0, 32), slice(32, 64)
    a1, up_c, dn_c, a2g = act, cc.at[0], cc.at[1], tokg
    wide = slice(0, 3 * partw)

    greet(ring("x") + plane() + near() + [scattered(), collected()])

    s_q = []
    for k in (1, 3, 2):
        for g in range(3):
            src = wqkv_hbm.at[:, pl.ds(g * width + lax.rem(x + k, 4) * partw, partw)]
            dst = cc.at[core, y, z, mine16, pl.ds(g * partw, partw)]
            s_q.append(c_q.push(src, dst, peer(x=k)))
    for g in range(3):
        src = wqkv_hbm.at[:, pl.ds(g * width + x * partw, partw)]
        s_q.append(c_q.local(src, cc.at[core, y, z, mine16, pl.ds(g * partw, partw)]))
    spot = smalls.at[y, core, pl.ds((z * 4 + x) * 8, 8)]
    s_small = [c_small.push(small_in, spot, to) for to in ring("x")]
    s_small.append(c_small.local(small_in, spot))
    s_o = [c_o.push(wout_hbm, wo.at[core, z, x], scattered())]
    tokens = Relay(
        c_tok, "x", lambda o: tokg.at[o], lambda o, h: tokg.at[o, pl.ds(h * blk // 2, blk // 2)]
    )
    tokens.start(tok_in)
    tokg[x] = tok_in[...]

    qkv_g = Gather(c_q, cc, True, [cut + (wide,) for cut in by_rows(64)])
    out_g = Gather(c_o, wo, True, by_columns(width), 3)
    down_g = Gather(c_d, wdn, False, by_rows(64))
    up_g = Gather(c_u, wup, False, by_rows(64))

    c_q.arrived(s_q)
    qkv_g.first()
    c_small.arrived(s_small)
    block = smalls.at[y, core, pl.ds(z * 32, 32)]
    s_small = [c_small.push(block, block, to) for to in plane()]

    slabs = 4 * hidden // 512
    for i in range(slabs):
        stack[16 * i : 16 * i + 16, :] = wup_in[:, 512 * i : 512 * i + 512]
    mixed_up = dot(stack[...], shuffle(), NN).astype(BF)
    for i in range(slabs):
        for to in range(4):
            uparts[to, :, 128 * i : 128 * i + 128] = mixed_up[
                16 * i : 16 * i + 16, 128 * to : 128 * to + 128
            ]

    c_q.arrived(qkv_g.one)
    qkv_g.second()
    c_o.arrived(s_o)
    out_g.first()
    c_small.arrived(s_small)
    s_small = []
    for other_y in range(4):
        block = smalls.at[other_y, core]
        s_small.append(c_small.push(block, block, peer(core=1)))
    tokens.near()
    s_u, s_d = [], []
    for k in (1, 3, 2):
        to = lax.rem(x + k, 4)
        s_d.append(
            c_d.push(wdn_in.at[pl.ds(to * 16, 16)], wdn.at[y, core, z, mine16], peer(x=k))
        )
        s_u.append(c_u.push(uparts.at[to], wup.at[y, core, z, mine16], peer(x=k)))
    s_d.append(c_d.local(wdn_in.at[mine16], wdn.at[y, core, z, mine16]))
    s_u.append(c_u.local(uparts.at[x], wup.at[y, core, z, mine16]))

    c_small.arrived(s_small)
    table = smalls[...].reshape(1024, 128).astype(BF)
    vec_o[0:1, :] = whole_vector(table, 0, 0, width, 16, 0)
    vec_o[1:2, :] = whole_vector(table, 1, 0, width, 16, 0)
    gain, shift = vec_o[0:1, :], vec_o[1:2, :]

    def norm_block(o):
        @pl.loop(0, blk // 16)
        def _(i):
            rows = pl.ds(pl.multiple_of(i * 16, 16), 16)
            v = tokg[o, rows, :].astype(F32)
            centred = v - jnp.mean(v, axis=-1, keepdims=True)
            s = lax.rsqrt(jnp.mean(centred * centred, axis=-1, keepdims=True) + EPSILON)
            at = pl.ds(pl.multiple_of(o * blk + i * 16, 16), 16)
            a1[at, :] = (centred * s * gain + shift).astype(BF)

    norm_block(x)
    qkv_g.near()
    c_o.arrived(out_g.one)
    out_g.second()
    norm_block(lax.rem(x + 1, 4))
    norm_block(lax.rem(x + 3, 4))
    qkv_g.far()
    out_g.near()
    c_d.arrived(s_d)
    down_g.first()
    c_u.arrived(s_u)
    up_g.first()
    tokens.far()
    s_dy = [comm.push(dy_in, dyg.at[p], peer(x=ORDER[p])) for p in (1, 2, 3)]
    dyg[0] = dy_in[...]
    norm_block(lax.rem(x + 2, 4))
    keep_a1 = [comm.local(a1, a1_h)]
    vec_o[2:3, :] = jnp.zeros((1, width), F32)
    vec_o[2:3, 0:partw] = whole_vector(table, 2, x * partw, partw, 32, 0)
    vec_o[2:3, 2 * partw : 3 * partw] = whole_vector(table, 2, width + x * partw, partw, 32, 0)
    qkv_g.done()

    def project(first):
        cols = slice(first, first + partw)
        total = vec_o[2:3, cols]
        rows = [
            jnp.concatenate([cc[0, j, :, :, cols], cc[1, j, :, :, cols]]).reshape(512, partw)
            for j in range(4)
        ]
        w = jnp.concatenate(rows)
        return (dot(a1[...], w, NN) + total).astype(BF)

    kv[W:, 0:partw] = project(partw)
    kv[W:, partw:] = project(2 * partw)
    s_edge = [comm.push(kv.at[pl.ds(span, W)], kv.at[pl.ds(0, W)], peer(z=1))]
    q[...] = project(0)
    keep_q = [c_q.local(cc.at[:, :, :, :, wide], wq_h)]
    comm.local(q, q_h)

    def attend(b):
        rows = pl.ds(pl.multiple_of(b * blk, blk), blk)
        window = pl.ds(pl.multiple_of(b * blk, blk), reach)
        mask = mask_of(lengths, z * span + b * blk, blk, reach)
        for h in range(heads):
            cols, vcols = pl.ds(h * HEAD, HEAD), pl.ds(partw + h * HEAD, HEAD)
            s = dot(q[rows, cols], kv[window, cols], NT) * scale + mask
            e = jnp.exp(s - jnp.max(s, axis=-1, keepdims=True))
            p = (e * (1.0 / jnp.sum(e, axis=-1, keepdims=True))).astype(BF)
            mixed[rows, cols] = dot(p, kv[window, vcols], NN).astype(BF)

    pl.loop(2, 4)(attend)
    out_g.far()
    c_d.arrived(down_g.one)
    down_g.second_a()
    c_u.arrived(up_g.one)
    up_g.second_a()
    for i in (3, 4, 5, 7):
        vec_o[i : i + 1, :] = whole_vector(table, i, 0, width, 16, 0)
    vec_o[6:7, :] = whole_vector(table, 6, 0, hidden, 16, x * 16)
    comm.arrived(s_edge)
    down_g.second_b()
    up_g.second_b()
    pl.loop(0, 2)(attend)
    comm.local(kv, kv_h)
    comm.local(mixed, mixed_h)
    out_g.done()
    c_o.local(wo, wo_h)
    c_tok.drain()

    def sends_attn(j):
        cols = pl.ds(pl.multiple_of(j * 512, 512), 512)
        return [
            remote(
                part.at[lax.rem(x + k, 4), :, cols],
                got.at[k - 1, :, cols],
                (rs_send, rs_recv),
                3 * j + k - 1,
                peer(x=k),
            )
            for k in (2, 1, 3)
        ]

    @pl.loop(0, 4)
    def _(j):
        cols = pl.ds(pl.multiple_of(j * 512, 512), 512)
        d = dot(mixed[...], wo[:, :, :, :, cols].reshape(partw, 512), NN)
        part[:, :, cols] = d.astype(BF).reshape(4, blk, 512)
        dact[:, 0:512] = d
        own[:, cols] = dact[pl.ds(pl.multiple_of(x * blk, blk), blk), 0:512]
        for copy in sends_attn(j):
            copy.start()

    c_q.drain()
    pl.semaphore_signal(
        free_sem, inc=1, device_id=peer(core=1), device_id_type=pl.DeviceIdType.MESH
    )

    down_g.near_a()
    up_g.near_a()
    down_g.near_b()
    down_g.far_a()
    up_g.near_b()
    up_g.far_a()

    @pl.loop(0, 4)
    def _(j):
        for copy in sends_attn(j):
            copy.wait_recv()

    b_out, gain2, shift2 = vec_o[3:4, :], vec_o[4:5, :], vec_o[5:6, :]

    @pl.loop(0, blk // 16)
    def _(i):
        rows = pl.ds(pl.multiple_of(i * 16, 16), 16)
        v = tok_in[rows, :].astype(F32) + own[rows, :] + b_out
        for g in range(3):
            v = v + got[g, rows, :].astype(F32)
        res_o[rows, :] = v
        centred = v - jnp.mean(v, axis=-1, keepdims=True)
        s = lax.rsqrt(jnp.mean(centred * centred, axis=-1, keepdims=True) + EPSILON)
        a2g[0, rows, :] = (centred * s * gain2 + shift2).astype(BF)

    spread = [comm.push(a2g.at[0], a2g.at[p], peer(x=ORDER[p])) for p in (1, 2)]
    down_g.far_b()
    up_g.far_b()

    @pl.loop(0, 4)
    def _(j):
        for copy in sends_attn(j):
            copy.wait_send()

    comm.arrived(keep_a1 + s_dy)
    down_g.done()

    @pl.loop(0, 4)
    def _(j):
        tile = wdn[j].reshape(512, width)
        cols = pl.ds(pl.multiple_of(j * 512, 512), 512)
        dact[:, cols] = dot(dyg[...].reshape(span, width), tile, NT)

    comm.arrived(spread)
    top, bottom = pl.ds(0, blk // 2), pl.ds(blk // 2, blk // 2)
    passed = [
        comm.push(a2g.at[1, top], a2g.at[3, top], peer(x=1)),
        comm.push(a2g.at[2, bottom], a2g.at[3, bottom], peer(x=3)),
    ]
    up_g.done()
    comm.arrived(passed)

    @pl.loop(0, hidden // 256)
    def _(j):
        cols = pl.ds(pl.multiple_of(j * 256, 256), 256)
        u = dot(a2g[...].reshape(span, width), wup[:, :, :, :, cols].reshape(width, 256), NN)
        u = u + vec_o[6:7, cols]
        phi = 0.5 + 0.5 * lax.erf(u * math.sqrt(0.5))
        act[:, cols] = (u * phi).astype(BF)
        slope = phi + u * (jnp.exp(-0.5 * u * u) * (1.0 / math.sqrt(2.0 * math.pi)))
        d_up = (dact[:, cols] * slope).astype(BF)
        dup[:, cols] = d_up
        small_out[3:4, cols] = jnp.sum(d_up.astype(F32), axis=0, keepdims=True)

    def sends(j):
        cols = pl.ds(pl.multiple_of(j * 512, 512), 512)
        return [
            remote(
                part.at[p - 1, :, cols],
                got.at[p - 1, :, cols],
                sems,
                4 + 3 * j + p - 1,
                peer(x=-ORDER[p]),
            )
            for p in (3, 1, 2)
        ]

    @pl.loop(0, 4)
    def _(j):
        cols = pl.ds(pl.multiple_of(j * 512, 512), 512)
        d = dot(dup[...], wup[j].reshape(512, hidden), NT)
        own[:, cols] = d[:blk]
        for p in (1, 2, 3):
            part[p - 1, :, cols] = d[p * blk : (p + 1) * blk].astype(BF)
        for copy in sends(j):
            copy.start()

    def grad_down(t, c):
        cols = pl.ds(pl.multiple_of(t * 512 + c * 256, 256), 256)
        return dot(act[:, cols], dyg[...].reshape(span, width), TN)

    def grad_up(t, c):
        cols = pl.ds(pl.multiple_of(t * 512 + c * 256, 256), 256)
        return dot(a2g[:, :, cols].reshape(span, 256), dup[...], TN)

    def swap_down(t):
        return remote(wdn.at[t, other], dn_c.at[t], sems, 16 + t, peer(core=1))

    def swap_up(t):
        return remote(wup.at[t, other], up_c.at[t], sems, 20 + t, peer(core=1))

    c_u.drain()
    pl.semaphore_wait(free_sem, 1)

    @pl.loop(0, 4)
    def _(t):
        wup[t, other] = grad_up(t, other).astype(BF).reshape(4, 64, hidden)
        swap_up(t).start()

    first = []

    def stage(src, dst, index, to):
        first.append(remote(src, dst, sems, index, to))
        first[-1].start()

    @pl.loop(0, 4)
    def _(t):
        swap_up(t).wait_recv()
        total = grad_up(t, core) + up_c[t].reshape(256, hidden).astype(F32)
        wup[t, core] = total.astype(BF).reshape(4, 64, hidden)

    for k in (1, 3, 2):
        zz, yy = lax.rem(z + k, 4), lax.rem(y + k, 4)
        stage(wup.at[:, core, zz, low], up_a_got.at[k - 1], 32 + k, peer(z=k))
        stage(wup.at[yy, core, :, high], up_b_got.at[k - 1], 36 + k, peer(y=k))

    @pl.loop(0, 4)
    def _(j):
        cols = pl.ds(pl.multiple_of(j * 512, 512), 512)
        o = dot(act[...], wdn[:, :, :, :, cols].reshape(hidden, 512), NN)
        outp[:, :, cols] = o.astype(BF).reshape(4, blk, 512)

    keep_out = pltpu.make_async_copy(outp, outp_hbm, local_sem.at[0])
    keep_out.start()

    c_d.drain()

    @pl.loop(0, 4)
    def _(t):
        wdn[t, other] = grad_down(t, other).astype(BF).reshape(4, 64, width)
        swap_down(t).start()

    @pl.loop(0, 4)
    def _(t):
        swap_down(t).wait_recv()
        total = grad_down(t, core) + dn_c[t].reshape(256, width).astype(F32)
        wdn[t, core] = total.astype(BF).reshape(4, 64, width)

    for k in (1, 3, 2):
        zz, yy = lax.rem(z + k, 4), lax.rem(y + k, 4)
        stage(wdn.at[:, core, zz, low], dn_a_got.at[k - 1], 24 + k, peer(z=k))
        stage(wdn.at[yy, core, :, high], dn_b_got.at[k - 1], 28 + k, peer(y=k))

    @pl.loop(0, 4)
    def _(j):
        for copy in sends(j):
            copy.wait_recv()

    small_out[0:3, :] = jnp.zeros((3, width), F32)
    small_out[4:8, :] = jnp.zeros((4, width), F32)
    gain = vec_o[4:5, :]

    @pl.loop(0, blk // 16)
    def _(i):
        rows = pl.ds(pl.multiple_of(i * 16, 16), 16)
        d = own[rows, :]
        for p in range(3):
            d = d + got[p, rows, :].astype(F32)
        v = res_o[rows, :]
        centred = v - jnp.mean(v, axis=-1, keepdims=True)
        s = lax.rsqrt(jnp.mean(centred * centred, axis=-1, keepdims=True) + EPSILON)
        n = centred * s
        dn = d * gain
        d_res = s * (
            dn
            - jnp.mean(dn, axis=-1, keepdims=True)
            - n * jnp.mean(dn * n, axis=-1, keepdims=True)
        )
        dy_own = dy_in[rows, :].astype(F32)
        hid = dy_own + d_res
        low_hid = hid.astype(BF)
        dhid_out[rows, :] = hid
        dattn[x, rows, :] = low_hid
        small_out[0:1, :] += jnp.sum(d * n, axis=0, keepdims=True)
        small_out[1:2, :] += jnp.sum(d, axis=0, keepdims=True)
        small_out[2:3, :] += jnp.sum(low_hid.astype(F32), axis=0, keepdims=True)
        small_out[4:5, :] += jnp.sum(dy_own, axis=0, keepdims=True)

    attn = Relay(
        comm, "x", lambda o: dattn.at[o], lambda o, h: dattn.at[o, pl.ds(h * blk // 2, blk // 2)]
    )
    attn.start()
    kept = [keep_out]
    kept.append(pltpu.make_async_copy(wdn.at[:, core, z, low], dn_a_own, local_sem.at[2]))
    kept.append(pltpu.make_async_copy(wdn.at[y, core, :, high], dn_b_own, local_sem.at[3]))
    kept.append(pltpu.make_async_copy(wup.at[:, core, z, low], up_a_own, local_sem.at[4]))
    kept.append(pltpu.make_async_copy(wup.at[y, core, :, high], up_b_own, local_sem.at[5]))
    for copy in kept[1:]:
        copy.start()
    attn.near()
    attn.far()
    kept.append(pltpu.make_async_copy(dattn, dattn_hbm, local_sem.at[1]))
    kept[-1].start()

    for copy in first:
        copy.wait_recv()
    for copy in first:
        copy.wait_send()

    @pl.loop(0, 4)
    def _(j):
        for copy in sends(j):
            copy.wait_send()
        swap_down(j).wait_send()
        swap_up(j).wait_send()

    for copy in kept:
        copy.wait()
    for done in groups:
        done.drain()


def forward(collective_id, lengths, tok, small, w_up, dy, w_down, w_qkv, w_out):
    blk, width = tok.shape
    span, partw, hidden = 4 * blk, width // 4, w_up.shape[1] // 4
    vmem = pl.BlockSpec(memory_space=pltpu.VMEM)
    hbm = pl.BlockSpec(memory_space=pl.ANY)
    quarter = (4, 32, width)
    outs = [
        ((8, width), F32, vmem),
        ((blk, width), F32, vmem),
        ((blk, width), F32, vmem),
        ((8, width), F32, vmem),
        ((2, 4, 4, 64, 3 * partw), BF, hbm),
        ((2, 4, 4, 16, width), BF, hbm),
        ((span, width), BF, hbm),
        ((span, partw), BF, hbm),
        ((span + W, 2 * partw), BF, hbm),
        ((span, partw), BF, hbm),
        ((4, blk, width), BF, hbm),
        ((4, blk, width), BF, hbm),
    ]
    outs += [(quarter, BF, hbm)] * 4 + [((3,) + quarter, BF, hbm)] * 4
    scratch = [
        ((4, 2, 4, 64, hidden), BF),
        ((4, 2, 4, 64, width), BF),
        ((2, 4, 4, 64, width), BF),
        ((2, 4, 4, 16, width), BF),
        ((4, blk, width), BF),
        ((span, hidden), BF),
        ((span, hidden), BF),
        ((span, hidden), F32),
        ((span, partw), BF),
        ((span + W, 2 * partw), BF),
        ((span, partw), BF),
        ((4, blk, width), BF),
        ((4, blk, width), BF),
        ((3, blk, width), BF),
        ((blk, width), F32),
        ((4, blk, width), BF),
        ((4, blk, width), BF),
        ((4, 2, 128, 128), F32),
        ((hidden // 8, 512), BF),
        ((4, 16, hidden), BF),
    ]
    return pl.pallas_call(
        forward_body,
        out_shape=tuple(jax.ShapeDtypeStruct(s, d) for s, d, _ in outs),
        in_specs=[pl.BlockSpec(memory_space=pltpu.SMEM)] + [vmem] * 5 + [hbm] * 2,
        out_specs=tuple(o[2] for o in outs),
        scratch_shapes=[pltpu.VMEM(s, d) for s, d in scratch]
        + [pltpu.SemaphoreType.DMA((8,)), pltpu.SemaphoreType.REGULAR]
        + [pltpu.SemaphoreType.DMA((n,)) for n in (12, 12, 40, 40, SEMS, SEMS)],
        compiler_params=pltpu.CompilerParams(
            collective_id=collective_id, has_side_effects=True, vmem_limit_bytes=63 << 20
        ),
        name="forward",
    )(lengths, tok, small, w_up, dy, w_down, w_qkv, w_out)


def norm_backward(d, v, gain):
    centred = v - jnp.mean(v, axis=-1, keepdims=True)
    s = lax.rsqrt(jnp.mean(centred * centred, axis=-1, keepdims=True) + EPSILON)
    n = centred * s
    dn = d * gain
    d_v = s * (
        dn - jnp.mean(dn, axis=-1, keepdims=True) - n * jnp.mean(dn * n, axis=-1, keepdims=True)
    )
    return d_v, n


def attention_backward_body(
    lengths,
    vec_in,
    ffsmall_in,
    dattn_hbm,
    wout_hbm,
    q_hbm,
    kv_hbm,
    a1_hbm,
    mixed_hbm,
    wqkv_hbm,
    tok_hbm,
    dhid_hbm,
    res_hbm,
    outp_hbm,
    ffo0,
    ffo1,
    ffo2,
    ffo3,
    ffg0,
    ffg1,
    ffg2,
    ffg3,
    out_o,
    gtok_o,
    gqkv_o,
    gout_o,
    gup_o,
    gdn_o,
    small_o,
    late_o,
    dattn,
    wout,
    q_all,
    kv,
    a1,
    mixed,
    wqkv,
    tok,
    dhid,
    res,
    outown,
    outgot,
    fo,
    fg,
    fs,
    fg2,
    fup,
    fdn,
    dmix,
    dkv,
    dqkv,
    dedge,
    dedge_got,
    part,
    got,
    qkv_c,
    out_c,
    qa,
    qb,
    oa,
    ob,
    qs,
    os_,
    qa2,
    qb2,
    oa2,
    ob2,
    fq,
    fout,
    sm,
    smc,
    smz,
    smy,
    late,
    late_c,
    late_p,
    late_sum,
    gux,
    stack,
    gq,
    local_sem,
    send_sem,
    recv_sem,
):
    sems = (send_sem, recv_sem)
    me = coords()
    x, y, z, core = me["x"], me["y"], me["z"], me["core"]
    other = 1 - core
    zy = lax.rem(y + 3, 4)
    blk, width = tok.shape
    span = 4 * blk
    partw = mixed.shape[1]
    heads = partw // HEAD
    scale = 1.0 / math.sqrt(HEAD)
    reach = W + blk
    used = [0]
    pending = []

    def load(src, dst):
        copy = pltpu.make_async_copy(src, dst, local_sem.at[used[0]])
        used[0] += 1
        copy.start()
        return copy

    def push(src, dst, index, to):
        copy = remote(src, dst, sems, index, to)
        copy.start()
        pending.append(copy)
        return copy

    l_dattn, l_wout = load(dattn_hbm, dattn), load(wout_hbm, wout)
    l_attn = [load(q_hbm, q_all), load(kv_hbm, kv)]
    low, high = slice(0, 32), slice(32, 64)
    l_ff = [load(s, fo.at[i]) for i, s in enumerate((ffo0, ffo1, ffo2, ffo3))]
    l_ff += [load(s, fg.at[i]) for i, s in enumerate((ffg0, ffg1, ffg2, ffg3))]
    l_wqkv, l_a1, l_mixed = load(wqkv_hbm, wqkv), load(a1_hbm, a1), load(mixed_hbm, mixed)
    l_end = [load(outp_hbm.at[0], outown), load(res_hbm, res)]
    l_end += [load(tok_hbm, tok), load(dhid_hbm, dhid)]

    greet(ring("x") + plane() + near() + [scattered(), collected()])

    p_out = [
        push(outp_hbm.at[p], outgot.at[p - 1], p, peer(x=-ORDER[p])) for p in (1, 2, 3)
    ]

    dkv[...] = jnp.zeros(dkv.shape, F32)
    l_dattn.wait()
    l_wout.wait()
    dmix[...] = dot(
        dattn[...].reshape(span, width), wout[...].reshape(partw, width), NT
    ).astype(BF)
    for copy in l_attn:
        copy.wait()

    def block(b):
        rows = pl.ds(pl.multiple_of(b * blk, blk), blk)
        window = pl.ds(pl.multiple_of(b * blk, blk), reach)
        mask = mask_of(lengths, z * span + b * blk, blk, reach)
        for h in range(heads):
            cols = pl.ds(h * HEAD, HEAD)
            vcols = pl.ds(partw + h * HEAD, HEAD)
            q, k, v = q_all[rows, cols], kv[window, cols], kv[window, vcols]
            s = dot(q, k, NT) * scale + mask
            e = jnp.exp(s - jnp.max(s, axis=-1, keepdims=True))
            p = e * (1.0 / jnp.sum(e, axis=-1, keepdims=True))
            do = dmix[rows, cols]
            dp = dot(do, v, NT)
            ds = (p * (dp - jnp.sum(dp * p, axis=-1, keepdims=True))).astype(BF)
            dqkv[rows, cols] = (dot(ds, k, NN) * scale).astype(BF)
            dkv[window, cols] += dot(ds, q, TN) * scale
            dkv[window, vcols] += dot(p.astype(BF), do, TN)

    pl.loop(0, 2)(block)
    dedge[...] = dkv[0:W, :].astype(BF)
    p_edge = push(dedge, dedge_got, 4, peer(z=3))

    def ff_sum(i):
        for c in range(4):
            total = fo[i, c].astype(F32)
            for g in range(3):
                total = total + fg[i, g, c].astype(F32)
            fs[i, c] = total.astype(BF)

    p_ff = []

    def ff_second(i):
        axis, here = ("y", y) if i % 2 == 0 else ("z", z)
        for k in (1, 3, 2):
            src = fs.at[i, lax.rem(here + k, 4)]
            p_ff.append(push(src, fg2.at[i, k - 1], 4 + 3 * i + k, peer(**{axis: k})))

    for copy in l_ff:
        copy.wait()
    for i in range(4):
        ff_sum(i)
    ff_second(0)
    ff_second(2)
    pl.loop(2, 4)(block)

    p_edge.wait_recv()
    ff_second(1)
    ff_second(3)
    dqkv[0 : span - W, partw:] = dkv[W:span, :].astype(BF)
    dqkv[span - W :, partw:] = (dkv[span:, :] + dedge_got[...].astype(F32)).astype(BF)
    sm[0, 0:5, :] = ffsmall_in[0:5, :]
    sm[0, 5:8, :] = jnp.zeros((3, width), F32)
    sm[0, 7:8, 0 : 3 * partw] = jnp.sum(dqkv[...].astype(F32), axis=0, keepdims=True)
    p_sc = push(sm.at[0], smc, 53, peer(core=1))

    def sends(j):
        cols = pl.ds(pl.multiple_of(j * 512, 512), 512)
        return [
            remote(
                part.at[lax.rem(x + k, 4), :, cols],
                got.at[k - 1, :, cols],
                sems,
                20 + 3 * j + k - 1,
                peer(x=k),
            )
            for k in (2, 1, 3)
        ]

    def grad_qkv(t, c):
        cols = pl.ds(pl.multiple_of(t * 512 + c * 256, 256), 256)
        return dot(a1[:, cols], dqkv[...], TN)

    def grad_out(c):
        cols = pl.ds(pl.multiple_of(c * 256, 256), 256)
        return dot(mixed[:, cols], dattn[...].reshape(span, width), TN)

    def swap(t):
        return remote(gq.at[t, 1], qkv_c.at[t], sems, 32 + t, peer(core=1))

    l_a1.wait()

    @pl.loop(0, 4)
    def _(t):
        gq[t, 1] = grad_qkv(t, other).astype(BF).reshape(4, 64, 3 * partw)
        swap(t).start()

    l_mixed.wait()
    wout[other] = grad_out(other).astype(BF).reshape(4, 4, 16, width)
    p_oc = push(wout.at[other], out_c, 36, peer(core=1))

    @pl.loop(0, 4)
    def _(t):
        swap(t).wait_recv()
        total = grad_qkv(t, core) + qkv_c[t].reshape(256, 3 * partw).astype(F32)
        gq[t, 0] = total.astype(BF).reshape(4, 64, 3 * partw)

    left, right = slice(0, width // 2), slice(width // 2, width)
    p_q1, p_o1 = [], []
    for k in (1, 3, 2):
        tz, ty = lax.rem(z + k, 4), lax.rem(y + k, 4)
        p_q1.append(push(gq.at[:, 0, tz, low], qa.at[k - 1], 36 + k, peer(z=k)))
        p_q1.append(push(gq.at[ty, 0, :, high], qb.at[k - 1], 39 + k, peer(y=k)))

    l_wqkv.wait()

    @pl.loop(0, 4)
    def _(j):
        cols = pl.ds(pl.multiple_of(j * 512, 512), 512)
        d = dot(dqkv[...], wqkv[:, j].reshape(512, 3 * partw), NT)
        part[:, :, cols] = d.astype(BF).reshape(4, blk, 512)
        for copy in sends(j):
            copy.start()

    p_sc.wait_recv()
    sm[1] = sm[0] + smc[...]
    p_sz = [push(sm.at[1], smz.at[k - 1], 59 + k, peer(z=k)) for k in (1, 3, 2)]
    p_oc.wait_recv()
    wout[core] = (
        grad_out(core) + out_c[...].reshape(256, width).astype(F32)
    ).astype(BF).reshape(4, 4, 16, width)
    for k in (1, 3, 2):
        tz, tyc = lax.rem(z + k, 4), lax.rem(y + k + 3, 4)
        p_o1.append(push(wout.at[core, :, tz, :, left], oa.at[k - 1], 42 + k, peer(z=k)))
        p_o1.append(push(wout.at[core, tyc, :, :, right], ob.at[k - 1], 45 + k, peer(y=k)))

    for copy in l_end:
        copy.wait()
    for copy in p_out:
        copy.wait_recv()

    @pl.loop(0, blk // 16)
    def _(i):
        rows = pl.ds(pl.multiple_of(i * 16, 16), 16)
        total = res[rows, :] + vec_in[7:8, :] + outown[rows, :].astype(F32)
        for g in range(3):
            total = total + outgot[g, rows, :].astype(F32)
        out_o[rows, :] = total.astype(BF)

    for copy in p_q1:
        copy.wait_recv()
    for c in range(4):
        ta, tb = gq[c, 0, z, low].astype(F32), gq[y, 0, c, high].astype(F32)
        for g in range(3):
            ta, tb = ta + qa[g, c].astype(F32), tb + qb[g, c].astype(F32)
        qs[0, c], qs[1, c] = ta.astype(BF), tb.astype(BF)
    p_q2 = []
    for k in (1, 3, 2):
        tz, ty = lax.rem(z + k, 4), lax.rem(y + k, 4)
        p_q2.append(push(qs.at[0, ty], qa2.at[k - 1], 53 + k, peer(y=k)))
        p_q2.append(push(qs.at[1, tz], qb2.at[k - 1], 56 + k, peer(z=k)))

    for copy in p_sz:
        copy.wait_recv()
    sm[2] = sm[1] + smz[0] + smz[1] + smz[2]
    p_sy = [push(sm.at[2], smy.at[k - 1], 68 + k, peer(y=k)) for k in (1, 3, 2)]
    for copy in p_o1:
        copy.wait_recv()
    for c in range(4):
        ta, tb = wout[core, c, z, :, left].astype(F32), wout[core, zy, c, :, right].astype(F32)
        for g in range(3):
            ta, tb = ta + oa[g, c].astype(F32), tb + ob[g, c].astype(F32)
        os_[0, c], os_[1, c] = ta.astype(BF), tb.astype(BF)
    p_o2 = []
    for k in (1, 3, 2):
        tz, tyc = lax.rem(z + k, 4), lax.rem(y + k + 3, 4)
        p_o2.append(push(os_.at[0, tyc], oa2.at[k - 1], 62 + k, peer(y=k)))
        p_o2.append(push(os_.at[1, tz], ob2.at[k - 1], 65 + k, peer(z=k)))

    late_sum[...] = jnp.zeros(late_sum.shape, F32)

    @pl.loop(0, 4)
    def _(j):
        for copy in sends(j):
            copy.wait_recv()

    gain = vec_in[0:1, :]

    @pl.loop(0, blk // 16)
    def _(i):
        rows = pl.ds(pl.multiple_of(i * 16, 16), 16)
        d = part[x, rows, :].astype(F32)
        for g in range(3):
            d = d + got[g, rows, :].astype(F32)
        d_in, n = norm_backward(d, tok[rows, :].astype(F32), gain)
        gtok_o[rows, :] = dhid[rows, :] + d_in
        late_sum[0:1, :] += jnp.sum(d * n, axis=0, keepdims=True)
        late_sum[1:2, :] += jnp.sum(d, axis=0, keepdims=True)

    for i in range(8):
        at = (i % 4) * (width // 4)
        late[0, i : i + 1, :] = late_sum[i // 4 : i // 4 + 1, at : at + width // 4]
    p_lc = push(late.at[0], late_c, 52, peer(core=1))
    p_lc.wait_recv()
    late[1] = late[0] + late_c[...]
    p_lz = [push(late.at[1], late_p.at[i], 98 + i, to) for i, to in enumerate(plane())]

    for copy in p_sy:
        copy.wait_recv()
    sm[3] = sm[2] + smy[0] + smy[1] + smy[2]
    p_x = [push(sm.at[3], small_o.at[x], 71 + k, peer(x=k)) for k in (1, 3, 2)]
    kept = [load(sm.at[3], small_o.at[x])]


    for copy in p_ff:
        copy.wait_recv()
    at = (y, z, y, z)
    for i in range(4):
        total = fs[i, at[i]].astype(F32)
        for g in range(3):
            total = total + fg2[i, g].astype(F32)
        into, half = (fup, fdn)[i // 2], i % 2
        into[2 * half : 2 * half + 2] = total.astype(BF).reshape(2, 16, width)
    p_u = []
    for k in (1, 3, 2):
        p_u.append(push(fup.at[lax.rem(x + k, 4)], gux.at[x], 48 + k, peer(x=k)))
        p_x.append(push(fdn.at[lax.rem(x + k, 4)], gdn_o.at[x], 76 + k, peer(x=k)))
    gux[x] = fup[x]
    kept.append(load(fdn.at[x], gdn_o.at[x]))

    for copy in p_q2:
        copy.wait_recv()
    ta, tb = qs[0, y].astype(F32), qs[1, z].astype(F32)
    for g in range(3):
        ta, tb = ta + qa2[g].astype(F32), tb + qb2[g].astype(F32)
    fq[0:2] = ta.astype(BF).reshape(2, 16, 3 * partw)
    fq[2:4] = tb.astype(BF).reshape(2, 16, 3 * partw)
    for g in range(3):
        block_cols, own_cols = pl.ds(g * partw, partw), pl.ds(g * width + x * partw, partw)
        for k in (1, 3, 2):
            src = fq.at[lax.rem(x + k, 4), :, block_cols]
            p_x.append(push(src, gqkv_o.at[:, own_cols], 83 + 3 * g + k - 1, peer(x=k)))
        kept.append(load(fq.at[x, :, block_cols], gqkv_o.at[:, own_cols]))

    for copy in p_o2:
        copy.wait_recv()
    ta, tb = os_[0, zy].astype(F32), os_[1, z].astype(F32)
    for g in range(3):
        ta, tb = ta + oa2[g].astype(F32), tb + ob2[g].astype(F32)
    fout[:, left], fout[:, right] = ta.astype(BF), tb.astype(BF)
    p_x.append(push(fout, gout_o, 75, collected()))

    for copy in p_lz:
        copy.wait_recv()
    total = late[1]
    for i in range(15):
        total = total + late_p[i]
    late[2] = total
    p_x += [push(late.at[2], late_o.at[x], 79 + k, peer(x=k)) for k in (1, 3, 2)]
    kept.append(load(late.at[2], late_o.at[x]))

    for copy in p_u:
        copy.wait_recv()
    slabs = width // 128
    for i in range(slabs):
        for c in range(4):
            stack[16 * i : 16 * i + 16, 128 * c : 128 * c + 128] = gux[
                c, :, 128 * i : 128 * i + 128
            ]
    spread_up = dot(stack[...], shuffle(), NT)
    for i in range(slabs):
        gup_o[:, 512 * i : 512 * i + 512] = spread_up[16 * i : 16 * i + 16, :]

    for copy in p_x:
        copy.wait_recv()
    for copy in pending:
        copy.wait_send()

    @pl.loop(0, 4)
    def _(j):
        for copy in sends(j):
            copy.wait_send()
        swap(j).wait_send()

    for copy in kept:
        copy.wait()


def attention_backward(
    collective_id,
    lengths,
    vectors,
    ff_small,
    d_attn,
    wout,
    q,
    kv,
    a1,
    mixed,
    wqkv,
    tok,
    d_hidden,
    residual,
    out_part,
    ff_own,
    ff_got,
):
    blk, width = tok.shape
    span, partw = mixed.shape
    hidden = ff_own[0].shape[-1]
    vmem = pl.BlockSpec(memory_space=pltpu.VMEM)
    hbm = pl.BlockSpec(memory_space=pl.ANY)
    outs = [
        ((blk, width), BF, vmem),
        ((blk, width), F32, vmem),
        ((16, 3 * width), BF, hbm),
        ((16, width), BF, hbm),
        ((16, 4 * hidden), F32, vmem),
        ((4, 16, width), BF, hbm),
        ((4, 8, width), F32, hbm),
        ((4, 8, width // 4), F32, hbm),
    ]
    half = width // 2
    scratch = [
        ((4, blk, width), BF),
        ((2, 4, 4, 16, width), BF),
        ((span, partw), BF),
        ((span + W, 2 * partw), BF),
        ((span, width), BF),
        ((span, partw), BF),
        ((2, 4, 4, 64, 3 * partw), BF),
        ((blk, width), BF),
        ((blk, width), F32),
        ((blk, width), F32),
        ((blk, width), BF),
        ((3, blk, width), BF),
        ((4, 4, 32, width), BF),
        ((4, 3, 4, 32, width), BF),
        ((4, 4, 32, width), BF),
        ((4, 3, 32, width), BF),
        ((4, 16, hidden), BF),
        ((4, 16, width), BF),
        ((span, partw), BF),
        ((span + W, 2 * partw), F32),
        ((span, 3 * partw), BF),
        ((W, 2 * partw), BF),
        ((W, 2 * partw), BF),
        ((4, blk, width), BF),
        ((3, blk, width), BF),
        ((4, 4, 64, 3 * partw), BF),
        ((4, 4, 16, width), BF),
        ((3, 4, 32, 3 * partw), BF),
        ((3, 4, 32, 3 * partw), BF),
        ((3, 4, 16, half), BF),
        ((3, 4, 16, half), BF),
        ((2, 4, 32, 3 * partw), BF),
        ((2, 4, 16, half), BF),
        ((3, 32, 3 * partw), BF),
        ((3, 32, 3 * partw), BF),
        ((3, 16, half), BF),
        ((3, 16, half), BF),
        ((4, 16, 3 * partw), BF),
        ((16, width), BF),
        ((4, 8, width), F32),
        ((8, width), F32),
        ((3, 8, width), F32),
        ((3, 8, width), F32),
        ((3, 8, width // 4), F32),
        ((8, width // 4), F32),
        ((15, 8, width // 4), F32),
        ((2, width), F32),
        ((4, 16, hidden), BF),
        ((hidden // 8, 512), BF),
        ((4, 2, 4, 64, 3 * partw), BF),
    ]
    return pl.pallas_call(
        attention_backward_body,
        out_shape=tuple(jax.ShapeDtypeStruct(s, d) for s, d, _ in outs),
        in_specs=[pl.BlockSpec(memory_space=pltpu.SMEM)] + [vmem] * 2 + [hbm] * 19,
        out_specs=tuple(o[2] for o in outs),
        scratch_shapes=[pltpu.VMEM(s, d) for s, d in scratch]
        + [
            pltpu.SemaphoreType.DMA((32,)),
            pltpu.SemaphoreType.DMA((114,)),
            pltpu.SemaphoreType.DMA((114,)),
        ],
        compiler_params=pltpu.CompilerParams(
            collective_id=collective_id, has_side_effects=True, vmem_limit_bytes=62 << 20
        ),
        name="attention_backward",
    )(
        lengths,
        vectors,
        ff_small,
        d_attn,
        wout,
        q,
        kv,
        a1,
        mixed,
        wqkv,
        tok,
        d_hidden,
        residual,
        out_part,
        *ff_own,
        *ff_got,
    )


def results_body(
    out,
    gtok,
    gqkv,
    gout,
    gup,
    gdn,
    small,
    late,
    out_o,
    gtok_o,
    gain1_o,
    shift1_o,
    gqkv_o,
    bqv_o,
    gout_o,
    bout_o,
    gain2_o,
    shift2_o,
    gup_o,
    bup_o,
    gdn_o,
    bdown_o,
    sums,
):
    me = coords()
    device = ((me["y"] * 2 + me["core"]) * 4 + me["z"]) * 4 + me["x"]
    out_o[...] = out[...]
    gtok_o[...] = gtok[...]
    gqkv_o[...] = gqkv[...].astype(F32)
    gout_o[...] = gout[...].astype(F32)
    gup_o[...] = gup[...]
    gdn_o[...] = gdn[...].reshape(gdn_o.shape).astype(F32)

    tile = pl.ds(pl.multiple_of(device // 8 * 128, 128), 128)
    turn = lax.rem(128 - 16 * lax.rem(device, 8), 128)
    shares = [pltpu.roll(small[i, :, tile], turn, 1) for i in range(4)]
    total = shares[0] + shares[1] + shares[2] + shares[3]
    gain2_o[...] = total[0:1, 0:16]
    shift2_o[...] = total[1:2, 0:16]
    bout_o[...] = total[2:3, 0:16]
    bdown_o[...] = total[4:5, 0:16]
    for i in range(4):
        bup_o[:, 16 * i : 16 * i + 16] = shares[i][3:4, 0:16]

    sums[...] = late[0] + late[1] + late[2] + late[3]
    place = lax.rem(device, 32)
    tile = pl.ds(pl.multiple_of(place // 8 * 128, 128), 128)
    turned = pltpu.roll(sums[:, tile], turn, 1)
    row = lax.broadcasted_iota(jnp.int32, turned.shape, 0)

    def only(i):
        return jnp.sum(jnp.where(row == i, turned, 0.0), axis=0, keepdims=True)[:, 0:16]

    gain1_o[...] = only(device // 32)
    shift1_o[...] = only(4 + device // 32)

    half, place = device // 64, lax.rem(device, 16)
    tile = pl.ds(pl.multiple_of(half * 1024 + place // 4 * 128, 128), 128)
    turn = lax.rem(128 - 32 * lax.rem(device, 4), 128)
    bqv_o[...] = pltpu.roll(small[lax.rem(device, 64) // 16, :, tile], turn, 1)[7:8, 0:32]


def results(*arrays):
    out, gtok, gqkv, gout, gup, gdn = arrays[:6]
    vmem = pl.BlockSpec(memory_space=pltpu.VMEM)
    rows, vector = gdn.shape[0] * gdn.shape[1], lambda n: ((1, n), F32)
    outs = [
        (out.shape, BF),
        (gtok.shape, F32),
        vector(16),
        vector(16),
        (gqkv.shape, F32),
        vector(32),
        (gout.shape, F32),
        vector(16),
        vector(16),
        vector(16),
        (gup.shape, F32),
        vector(64),
        ((rows, gdn.shape[2]), F32),
        vector(16),
    ]
    return pl.pallas_call(
        results_body,
        out_shape=tuple(jax.ShapeDtypeStruct(s, d) for s, d in outs),
        in_specs=[vmem] * 8,
        out_specs=(vmem,) * 14,
        scratch_shapes=[pltpu.VMEM(arrays[7].shape[1:], F32)],
        compiler_params=pltpu.CompilerParams(vmem_limit_bytes=40 << 20),
        name="results",
    )(*arrays)


def local(
    tokens,
    grad_out,
    lengths,
    ln1_gain,
    ln1_bias,
    w_qkv,
    b_qv,
    w_out,
    b_out,
    ln2_gain,
    ln2_bias,
    w_up,
    b_up,
    w_down,
    b_down,
):
    blk, width = tokens.shape[1:]
    part = width // 4
    hidden = w_up.shape[1] // 4
    tok = tokens.reshape(blk, width)
    dy = grad_out.reshape(blk, width)
    small = jnp.zeros((1024,), F32)
    vectors = (ln1_gain, ln1_bias, b_qv, b_out, ln2_gain, ln2_bias, b_up, b_down)
    for i, vector in enumerate(vectors):
        size = vector.shape[0]
        small = small + jnp.pad(vector.astype(F32), (i * 128, 1024 - i * 128 - size))
    (
        vectors,
        residual,
        d_hidden,
        ff_small,
        wqkv_g,
        wout_g,
        a1,
        query,
        kv,
        mixed,
        d_attn_g,
        out_part,
        up_a_own,
        up_b_own,
        down_a_own,
        down_b_own,
        up_a_got,
        up_b_got,
        down_a_got,
        down_b_got,
    ) = forward(0, lengths, tok, small.reshape(8, 128), w_up, dy, w_down, w_qkv, w_out)
    last = attention_backward(
        1,
        lengths,
        vectors,
        ff_small,
        d_attn_g,
        wout_g,
        query,
        kv,
        a1,
        mixed,
        wqkv_g,
        tok,
        d_hidden,
        residual,
        out_part,
        (up_a_own, up_b_own, down_a_own, down_b_own),
        (up_a_got, up_b_got, down_a_got, down_b_got),
    )

    final = list(results(*last))
    final[0] = final[0].reshape(1, blk, width)
    final[1] = final[1].reshape(1, blk, width)
    for i in (2, 3, 5, 7, 8, 9, 11, 13):
        final[i] = final[i].reshape(-1)
    return tuple(final)


def solution(mesh):
    fine = Mesh(mesh.devices.reshape(4, 2, 4, 4), AXES)
    rows, seq = ("y", "core"), ("z", "x")
    every = rows + seq
    token = P(rows, seq, None)
    vec, mat = P(every), P(every, None)
    in_specs = (token, token, P(rows, None), vec, vec, mat, vec, mat, vec, vec, vec, mat, vec, mat, vec)
    out_specs = (token, token, vec, vec, mat, vec, mat, vec, vec, vec, mat, vec, mat, vec)
    return jax.shard_map(local, mesh=fine, in_specs=in_specs, out_specs=out_specs, check_vma=False)
```

```python
import functools
import math

import jax
import jax.numpy as jnp
from jax import lax
from jax.experimental import pallas as pl
from jax.experimental.pallas import tpu as pltpu
from jax.sharding import Mesh, PartitionSpec as P

HEADS = 16
HEAD = 128
W = 256
EPSILON = 1e-05
NEG_FILL = -1e30

AXES = ("y", "core", "z", "x")
SIZE = {"y": 4, "core": 2, "z": 4, "x": 4}
BF = jnp.bfloat16
F32 = jnp.float32
SEMS = 212


def coords():
    return {a: lax.axis_index(a) for a in AXES}


def peer(**delta):
    me = coords()
    return tuple(lax.rem(me[a] + delta.get(a, 0) % SIZE[a], SIZE[a]) for a in AXES)


class Comm:
    def __init__(self, send_sem, recv_sem, base=0, room=SEMS):
        self.send_sem, self.recv_sem = send_sem, recv_sem
        self.count, self.last, self.open = base, base + room, []

    def push(self, src, dst, to):
        copy = pltpu.make_async_remote_copy(
            src_ref=src,
            dst_ref=dst,
            send_sem=self.send_sem.at[self.count],
            recv_sem=self.recv_sem.at[self.count],
            device_id=to,
            device_id_type=pl.DeviceIdType.MESH,
        )
        assert self.count < self.last
        self.count += 1
        copy.start()
        self.open.append([copy, True, True])
        return self.open[-1]

    def local(self, src, dst):
        copy = pltpu.make_async_copy(src, dst, self.send_sem.at[self.count])
        self.count += 1
        copy.start()
        self.open.append([copy, False, True])
        return self.open[-1]

    def arrived(self, entries):
        for entry in entries:
            if entry[2]:
                if entry[1]:
                    entry[0].wait_recv()
                else:
                    entry[0].wait()
                entry[2] = False

    def drain(self):
        self.arrived(self.open)
        for copy, remote_copy, _ in self.open:
            if remote_copy:
                copy.wait_send()
        self.open = []


def greet(devices):
    barrier = pltpu.get_barrier_semaphore()
    for device in devices:
        pl.semaphore_signal(barrier, inc=1, device_id=device, device_id_type=pl.DeviceIdType.MESH)
    pl.semaphore_wait(barrier, len(devices))


def ring(axis):
    return [peer(**{axis: k}) for k in (1, 3, 2)]


def near():
    return [peer(core=1)]


def plane():
    return [peer(y=i // 4, z=i % 4) for i in range(1, 16)]


def everyone():
    return ring("x") + ring("y") + ring("z") + near()


def scattered():
    me = coords()
    return (lax.rem(me["z"] + 1, 4), me["core"], me["x"], me["y"])


def collected():
    me = coords()
    return (me["x"], me["core"], lax.rem(me["y"] + 3, 4), me["z"])


class Relay:
    def __init__(self, comm, axis, full, half):
        self.comm, self.axis, self.full, self.half = comm, axis, full, half
        self.me = lax.axis_index(axis)

    def to(self, k):
        return peer(**{self.axis: k})

    def start(self, src=None):
        own = self.full(self.me)
        src = own if src is None else src
        self.sent = [self.comm.push(src, own, self.to(1)), self.comm.push(src, own, self.to(3))]

    def near(self):
        self.comm.arrived(self.sent)
        before, after = lax.rem(self.me + 3, 4), lax.rem(self.me + 1, 4)
        up, down = self.half(before, 0), self.half(after, 1)
        self.passed = [self.comm.push(up, up, self.to(1)), self.comm.push(down, down, self.to(3))]

    def far(self):
        self.comm.arrived(self.passed)


class RingSum:
    def __init__(self, comm, axis, ref, tmp, got):
        self.comm, self.axis, self.ref, self.tmp, self.got = comm, axis, ref, tmp, got
        self.me = lax.axis_index(axis)

    def at(self, k):
        return lax.rem(self.me + k, 4)

    def push(self, src, dst, k):
        return self.comm.push(src, dst, peer(**{self.axis: k}))

    def start(self):
        self.up = self.push(self.ref(self.at(2), 0), self.tmp.at[0], 1)
        self.down = self.push(self.ref(self.at(2), 1), self.tmp.at[1], 3)
        self.end = [
            self.push(self.ref(self.at(1), 1), self.got.at[0, pl.ds(2, 2)], 1),
            self.push(self.ref(self.at(3), 0), self.got.at[1, pl.ds(0, 2)], 3),
        ]

    def middle(self):
        for arrived, k, h, back in ((self.up, 1, 0, 0), (self.down, 3, 1, 2)):
            self.comm.arrived([arrived])
            block = self.ref(self.at(k), h)
            for c in range(2):
                total = block[c].astype(F32) + self.tmp[h, c].astype(F32)
                block[c] = total.astype(BF)
            self.end.append(self.push(block, self.got.at[h, pl.ds(back, 2)], k))

    def finish(self):
        self.comm.arrived(self.end)


class Gather:
    def __init__(self, comm, w, by_core, cut, shift=0):
        self.comm, self.w, self.by_core, self.cut = comm, w, by_core, cut
        self.shift = shift
        me = coords()
        self.y, self.core, self.z = me["y"], me["core"], me["z"]

    def slot(self, y, z, cut):
        place = (self.core, y, z) if self.by_core else (y, self.core, z)
        return self.w.at[place + self.cut[cut]]

    def row(self, y):
        return lax.rem(y + self.shift, 4)

    def first(self):
        self.first_a()
        self.first_b()
        self.one = self.one_a + self.one_b

    def first_a(self):
        a = self.slot(self.row(self.y), self.z, 0)
        self.one_a = [self.comm.push(a, a, to) for to in ring("z")]

    def first_b(self):
        b = self.slot(self.row(self.y), self.z, 1)
        self.one_b = [self.comm.push(b, b, to) for to in ring("y")]

    def second(self):
        self.second_a()
        self.second_b()

    def second_a(self):
        every = slice(None)
        self.a = Relay(
            self.comm,
            "y",
            lambda o: self.slot(self.row(o), every, 0),
            lambda o, h: self.slot(self.row(o), pl.ds(2 * h, 2), 0),
        )
        self.a.start()

    def second_b(self):
        every = slice(None)
        self.b = Relay(
            self.comm,
            "z",
            lambda o: self.slot(every, o, 1),
            lambda o, h: self.slot(pl.ds(2 * h, 2), o, 1),
        )
        self.b.start()

    def across(self, relay, k):
        block = relay.full(lax.rem(relay.me + k, 4))
        self.two.append(self.comm.push(block, block, peer(core=1)))

    def near_a(self):
        self.two = []
        self.a.near()
        for k in (0, 1, 3):
            self.across(self.a, k)

    def near_b(self):
        self.b.near()
        for k in (0, 1, 3):
            self.across(self.b, k)

    def near(self):
        self.near_a()
        self.near_b()

    def far_a(self):
        self.a.far()
        self.across(self.a, 2)

    def far_b(self):
        self.b.far()
        self.across(self.b, 2)

    def far(self):
        self.far_a()
        self.far_b()

    def done(self):
        self.comm.arrived(self.two)


def by_rows(rows):
    return [(slice(0, rows // 2),), (slice(rows // 2, rows),)]


def by_columns(columns):
    every = slice(None)
    return [(every, slice(0, columns // 2)), (every, slice(columns // 2, columns))]


def dot(a, b, dims):
    return lax.dot_general(a, b, (dims, ((), ())), preferred_element_type=F32)


NN = ((1,), (0,))
NT = ((1,), (1,))
TN = ((0,), (0,))


def mask_of(lengths, first, blk, reach):
    q = first + lax.broadcasted_iota(jnp.int32, (blk, reach), 0)
    k = first - W + lax.broadcasted_iota(jnp.int32, (blk, reach), 1)
    q_doc, k_doc = jnp.zeros((blk, reach), jnp.int32), jnp.zeros((blk, reach), jnp.int32)
    end = 0
    for i in range(lengths.shape[1]):
        end = end + lengths[0, i]
        q_doc = q_doc + jnp.where(q >= end, 1, 0)
        k_doc = k_doc + jnp.where(k >= end, 1, 0)
    seen = (q_doc == k_doc) & (k <= q) & (q - k < W) & (k >= 0)
    return jnp.where(seen, 0.0, NEG_FILL).astype(F32)


def shuffle():
    row = lax.broadcasted_iota(jnp.int32, (512, 512), 0)
    column = lax.broadcasted_iota(jnp.int32, (512, 512), 1)
    source = 64 * ((column >> 4) & 7) + 16 * (column >> 7) + (column & 15)
    return jnp.where(source == row, 1.0, 0.0).astype(BF)


def whole_vector(table, index, offset, count, size, lane):
    shift = size.bit_length() - 1
    row = lax.broadcasted_iota(jnp.int32, (128, 1024), 0)
    tile = lax.broadcasted_iota(jnp.int32, (128, 1024), 1)
    chosen = jnp.where(tile == row * 8 + index, 1.0, 0.0).astype(BF)
    share = dot(chosen, table, NN).astype(BF)
    row = lax.broadcasted_iota(jnp.int32, (128, count), 0)
    column = lax.broadcasted_iota(jnp.int32, (128, count), 1) + offset
    spread = jnp.where((column & (size - 1)) + lane == row, 1.0, 0.0).astype(BF)
    values = jnp.where((column >> shift) == row, dot(share, spread, NN), 0.0)
    return jnp.sum(values, axis=0, keepdims=True)


ORDER = (0, 1, 3, 2)


def remote(src, dst, sems, index, to):
    send, recv = sems
    return pltpu.make_async_remote_copy(
        src_ref=src,
        dst_ref=dst,
        send_sem=send.at[index],
        recv_sem=recv.at[index],
        device_id=to,
        device_id_type=pl.DeviceIdType.MESH,
    )


def forward_body(
    lengths,
    tok_in,
    small_in,
    wup_in,
    dy_in,
    wdn_in,
    wqkv_hbm,
    wout_hbm,
    vec_o,
    res_o,
    dhid_out,
    small_out,
    wq_h,
    wo_h,
    a1_h,
    q_h,
    kv_h,
    mixed_h,
    dattn_hbm,
    outp_hbm,
    up_a_own,
    up_b_own,
    dn_a_own,
    dn_b_own,
    up_a_got,
    up_b_got,
    dn_a_got,
    dn_b_got,
    wup,
    wdn,
    cc,
    wo,
    tokg,
    act,
    dup,
    dact,
    q,
    kv,
    mixed,
    dyg,
    part,
    got,
    own,
    outp,
    dattn,
    smalls,
    stack,
    uparts,
    ring_tmp,
    local_sem,
    free_sem,
    rs_send,
    rs_recv,
    ff_send,
    ff_recv,
    send_sem,
    recv_sem,
):
    groups, taken = [], [0]

    def group(room):
        comm = Comm(send_sem, recv_sem, taken[0], room)
        taken[0] += room
        groups.append(comm)
        return comm

    c_q, c_o, c_u, c_d = group(36), group(26), group(26), group(26)
    c_small, c_tok, comm = group(28), group(4), group(32)
    sems = (ff_send, ff_recv)
    me = coords()
    x, y, z, core = me["x"], me["y"], me["z"], me["core"]
    other = 1 - core
    blk, width = tok_in.shape
    span = 4 * blk
    partw = q.shape[1]
    hidden = act.shape[1]
    heads = partw // HEAD
    reach = W + blk
    scale = 1.0 / math.sqrt(HEAD)
    mine16 = pl.ds(x * 16, 16)
    low, high = slice(0, 32), slice(32, 64)
    a1, up_c, dn_c, a2g = act, cc.at[0], cc.at[1], tokg
    wide = slice(0, 3 * partw)

    greet(ring("x") + plane() + near() + [scattered(), collected()])

    s_q = []
    for k in (1, 3, 2):
        for g in range(3):
            src = wqkv_hbm.at[:, pl.ds(g * width + lax.rem(x + k, 4) * partw, partw)]
            dst = cc.at[core, y, z, mine16, pl.ds(g * partw, partw)]
            s_q.append(c_q.push(src, dst, peer(x=k)))
    for g in range(3):
        src = wqkv_hbm.at[:, pl.ds(g * width + x * partw, partw)]
        s_q.append(c_q.local(src, cc.at[core, y, z, mine16, pl.ds(g * partw, partw)]))
    spot = smalls.at[y, core, pl.ds((z * 4 + x) * 8, 8)]
    s_small = [c_small.push(small_in, spot, to) for to in ring("x")]
    s_small.append(c_small.local(small_in, spot))
    s_o = [c_o.push(wout_hbm, wo.at[core, z, x], scattered())]
    tokens = Relay(
        c_tok, "x", lambda o: tokg.at[o], lambda o, h: tokg.at[o, pl.ds(h * blk // 2, blk // 2)]
    )
    tokens.start(tok_in)
    tokg[x] = tok_in[...]

    qkv_g = Gather(c_q, cc, True, [cut + (wide,) for cut in by_rows(64)])
    out_g = Gather(c_o, wo, True, by_columns(width), 3)
    down_g = Gather(c_d, wdn, False, by_rows(64))
    up_g = Gather(c_u, wup, False, by_rows(64))

    c_q.arrived(s_q)
    qkv_g.first()
    c_small.arrived(s_small)
    block = smalls.at[y, core, pl.ds(z * 32, 32)]
    s_small = [c_small.push(block, block, to) for to in plane()]

    slabs = 4 * hidden // 512
    for i in range(slabs):
        stack[16 * i : 16 * i + 16, :] = wup_in[:, 512 * i : 512 * i + 512]
    mixed_up = dot(stack[...], shuffle(), NN).astype(BF)
    for i in range(slabs):
        for to in range(4):
            uparts[to, :, 128 * i : 128 * i + 128] = mixed_up[
                16 * i : 16 * i + 16, 128 * to : 128 * to + 128
            ]

    c_q.arrived(qkv_g.one)
    qkv_g.second()
    c_o.arrived(s_o)
    out_g.first()
    c_small.arrived(s_small)
    s_small = []
    for other_y in range(4):
        block = smalls.at[other_y, core]
        s_small.append(c_small.push(block, block, peer(core=1)))
    tokens.near()
    s_u, s_d = [], []
    for k in (1, 3, 2):
        to = lax.rem(x + k, 4)
        s_d.append(
            c_d.push(wdn_in.at[pl.ds(to * 16, 16)], wdn.at[y, core, z, mine16], peer(x=k))
        )
        s_u.append(c_u.push(uparts.at[to], wup.at[y, core, z, mine16], peer(x=k)))
    s_d.append(c_d.local(wdn_in.at[mine16], wdn.at[y, core, z, mine16]))
    s_u.append(c_u.local(uparts.at[x], wup.at[y, core, z, mine16]))
    s_dy = [comm.push(dy_in, dyg.at[p], peer(x=ORDER[p])) for p in (1, 2, 3)]
    dyg[0] = dy_in[...]

    c_small.arrived(s_small)
    table = smalls[...].reshape(1024, 128).astype(BF)
    vec_o[0:1, :] = whole_vector(table, 0, 0, width, 16, 0)
    vec_o[1:2, :] = whole_vector(table, 1, 0, width, 16, 0)
    gain, shift = vec_o[0:1, :], vec_o[1:2, :]

    def norm_block(o):
        @pl.loop(0, blk // 16)
        def _(i):
            rows = pl.ds(pl.multiple_of(i * 16, 16), 16)
            v = tokg[o, rows, :].astype(F32)
            centred = v - jnp.mean(v, axis=-1, keepdims=True)
            s = lax.rsqrt(jnp.mean(centred * centred, axis=-1, keepdims=True) + EPSILON)
            at = pl.ds(pl.multiple_of(o * blk + i * 16, 16), 16)
            a1[at, :] = (centred * s * gain + shift).astype(BF)

    norm_block(x)
    qkv_g.near()
    c_o.arrived(out_g.one)
    out_g.second()
    norm_block(lax.rem(x + 1, 4))
    norm_block(lax.rem(x + 3, 4))
    qkv_g.far()
    tokens.far()
    norm_block(lax.rem(x + 2, 4))
    out_g.near()
    c_d.arrived(s_d)
    down_g.first()
    c_u.arrived(s_u)
    up_g.first_b()
    keep_a1 = [comm.local(a1, a1_h)]
    vec_o[2:3, :] = jnp.zeros((1, width), F32)
    vec_o[2:3, 0:partw] = whole_vector(table, 2, x * partw, partw, 32, 0)
    vec_o[2:3, 2 * partw : 3 * partw] = whole_vector(table, 2, width + x * partw, partw, 32, 0)
    qkv_g.done()

    def project(first):
        cols = slice(first, first + partw)
        total = vec_o[2:3, cols]
        rows = [
            jnp.concatenate([cc[0, j, :, :, cols], cc[1, j, :, :, cols]]).reshape(512, partw)
            for j in range(4)
        ]
        w = jnp.concatenate(rows)
        return (dot(a1[...], w, NN) + total).astype(BF)

    kv[W:, 0:partw] = project(partw)
    kv[W:, partw:] = project(2 * partw)
    s_edge = [comm.push(kv.at[pl.ds(span, W)], kv.at[pl.ds(0, W)], peer(z=1))]
    q[...] = project(0)
    keep_q = [c_q.local(cc.at[:, :, :, :, wide], wq_h)]
    comm.local(q, q_h)

    def attend(b):
        rows = pl.ds(pl.multiple_of(b * blk, blk), blk)
        window = pl.ds(pl.multiple_of(b * blk, blk), reach)
        mask = mask_of(lengths, z * span + b * blk, blk, reach)
        for h in range(heads):
            cols, vcols = pl.ds(h * HEAD, HEAD), pl.ds(partw + h * HEAD, HEAD)
            s = dot(q[rows, cols], kv[window, cols], NT) * scale + mask
            e = jnp.exp(s - jnp.max(s, axis=-1, keepdims=True))
            p = (e * (1.0 / jnp.sum(e, axis=-1, keepdims=True))).astype(BF)
            mixed[rows, cols] = dot(p, kv[window, vcols], NN).astype(BF)

    def sends_attn(j):
        cols = pl.ds(pl.multiple_of(j * 512, 512), 512)
        return [
            remote(
                part.at[lax.rem(x + k, 4), :, cols],
                got.at[k - 1, :, cols],
                (rs_send, rs_recv),
                3 * j + k - 1,
                peer(x=k),
            )
            for k in (2, 1, 3)
        ]

    def project_out(o):
        rows = slice(o * blk, (o + 2) * blk)

        @pl.loop(0, 4)
        def _(j):
            cols = pl.ds(pl.multiple_of(j * 512, 512), 512)
            d = dot(mixed[rows, :], wo[:, :, :, :, cols].reshape(partw, 512), NN)
            part[o : o + 2, :, cols] = d.astype(BF).reshape(2, blk, 512)
            dact[rows, cols] = d
            for to in (o, o + 1):
                k = lax.rem(to - x + 4, 4)

                @pl.when(k != 0)
                def _():
                    remote(
                        part.at[to, :, cols],
                        got.at[k - 1, :, cols],
                        (rs_send, rs_recv),
                        3 * j + k - 1,
                        (y, core, z, to),
                    ).start()

    pl.loop(2, 4)(attend)
    out_g.far()
    c_d.arrived(down_g.one)
    down_g.second_a()
    for i in (3, 4, 5, 7):
        vec_o[i : i + 1, :] = whole_vector(table, i, 0, width, 16, 0)
    vec_o[6:7, :] = whole_vector(table, 6, 0, hidden, 16, x * 16)
    out_g.done()
    c_tok.drain()
    project_out(2)
    comm.arrived(s_edge)
    up_g.first_a()
    down_g.second_b()
    pl.loop(0, 2)(attend)
    project_out(0)
    down_g.near_a()
    c_u.arrived(up_g.one_a + up_g.one_b)
    up_g.second_a()
    comm.local(kv, kv_h)
    comm.local(mixed, mixed_h)
    c_o.local(wo, wo_h)
    c_q.drain()
    pl.semaphore_signal(
        free_sem, inc=1, device_id=peer(core=1), device_id_type=pl.DeviceIdType.MESH
    )
    down_g.near_b()
    up_g.second_b()
    down_g.far_a()

    @pl.loop(0, 4)
    def _(j):
        for copy in sends_attn(j):
            copy.wait_recv()

    b_out, gain2, shift2 = vec_o[3:4, :], vec_o[4:5, :], vec_o[5:6, :]

    @pl.loop(0, blk // 16)
    def _(i):
        rows = pl.ds(pl.multiple_of(i * 16, 16), 16)
        own_rows = pl.ds(pl.multiple_of(x * blk + i * 16, 16), 16)
        v = tok_in[rows, :].astype(F32) + dact[own_rows, :] + b_out
        for g in range(3):
            v = v + got[g, rows, :].astype(F32)
        res_o[rows, :] = v
        centred = v - jnp.mean(v, axis=-1, keepdims=True)
        s = lax.rsqrt(jnp.mean(centred * centred, axis=-1, keepdims=True) + EPSILON)
        a2g[0, rows, :] = (centred * s * gain2 + shift2).astype(BF)

    spread = [comm.push(a2g.at[0], a2g.at[p], peer(x=ORDER[p])) for p in (1, 2)]
    down_g.far_b()
    up_g.near_a()
    up_g.near_b()

    @pl.loop(0, 4)
    def _(j):
        for copy in sends_attn(j):
            copy.wait_send()

    comm.arrived(keep_a1 + s_dy)
    down_g.done()

    @pl.loop(0, 4)
    def _(j):
        tile = wdn[j].reshape(512, width)
        cols = pl.ds(pl.multiple_of(j * 512, 512), 512)
        dact[:, cols] = dot(dyg[...].reshape(span, width), tile, NT)

    comm.arrived(spread)
    top, bottom = pl.ds(0, blk // 2), pl.ds(blk // 2, blk // 2)
    passed = [
        comm.push(a2g.at[1, top], a2g.at[3, top], peer(x=1)),
        comm.push(a2g.at[2, bottom], a2g.at[3, bottom], peer(x=3)),
    ]
    up_g.far_a()
    up_g.far_b()
    up_g.done()
    comm.arrived(passed)

    @pl.loop(0, hidden // 256)
    def _(j):
        cols = pl.ds(pl.multiple_of(j * 256, 256), 256)
        u = dot(a2g[...].reshape(span, width), wup[:, :, :, :, cols].reshape(width, 256), NN)
        u = u + vec_o[6:7, cols]
        phi = 0.5 + 0.5 * lax.erf(u * math.sqrt(0.5))
        act[:, cols] = (u * phi).astype(BF)
        slope = phi + u * (jnp.exp(-0.5 * u * u) * (1.0 / math.sqrt(2.0 * math.pi)))
        d_up = (dact[:, cols] * slope).astype(BF)
        dup[:, cols] = d_up
        small_out[3:4, cols] = jnp.sum(d_up.astype(F32), axis=0, keepdims=True)

    def sends(j):
        cols = pl.ds(pl.multiple_of(j * 512, 512), 512)
        return [
            remote(
                part.at[p - 1, :, cols],
                got.at[p - 1, :, cols],
                sems,
                4 + 3 * j + p - 1,
                peer(x=-ORDER[p]),
            )
            for p in (3, 1, 2)
        ]

    @pl.loop(0, 4)
    def _(j):
        cols = pl.ds(pl.multiple_of(j * 512, 512), 512)
        d = dot(dup[...], wup[j].reshape(512, hidden), NT)
        own[:, cols] = d[:blk]
        for p in (1, 2, 3):
            part[p - 1, :, cols] = d[p * blk : (p + 1) * blk].astype(BF)
        for copy in sends(j):
            copy.start()

    def grad_down(t, c):
        cols = pl.ds(pl.multiple_of(t * 512 + c * 256, 256), 256)
        return dot(act[:, cols], dyg[...].reshape(span, width), TN)

    def grad_up(t, c):
        cols = pl.ds(pl.multiple_of(t * 512 + c * 256, 256), 256)
        return dot(a2g[:, :, cols].reshape(span, 256), dup[...], TN)

    def swap_down(t):
        return remote(wdn.at[t, other], dn_c.at[t], sems, 16 + t, peer(core=1))

    def swap_up(t):
        return remote(wup.at[t, other], up_c.at[t], sems, 20 + t, peer(core=1))

    c_u.drain()
    pl.semaphore_wait(free_sem, 1)

    @pl.loop(0, 4)
    def _(t):
        wup[t, other] = grad_up(t, other).astype(BF).reshape(4, 64, hidden)
        swap_up(t).start()

    c_ring = group(32)

    def ring_sums(w, tmp_a, tmp_b, got_a, got_b):
        return (
            RingSum(c_ring, "z", lambda o, h: w.at[pl.ds(2 * h, 2), core, o, low], tmp_a, got_a),
            RingSum(c_ring, "y", lambda o, h: w.at[o, core, pl.ds(2 * h, 2), high], tmp_b, got_b),
        )

    up_sums = ring_sums(wup, ring_tmp.at[0], ring_tmp.at[1], up_a_got, up_b_got)
    down_sums = ring_sums(wdn, ring_tmp.at[2], ring_tmp.at[3], dn_a_got, dn_b_got)

    @pl.loop(0, 4)
    def _(t):
        swap_up(t).wait_recv()
        total = grad_up(t, core) + up_c[t].reshape(256, hidden).astype(F32)
        wup[t, core] = total.astype(BF).reshape(4, 64, hidden)

    for total in up_sums:
        total.start()

    @pl.loop(0, 4)
    def _(j):
        cols = pl.ds(pl.multiple_of(j * 512, 512), 512)
        o = dot(act[...], wdn[:, :, :, :, cols].reshape(hidden, 512), NN)
        outp[:, :, cols] = o.astype(BF).reshape(4, blk, 512)

    keep_out = pltpu.make_async_copy(outp, outp_hbm, local_sem.at[0])
    keep_out.start()

    c_d.drain()

    @pl.loop(0, 4)
    def _(t):
        wdn[t, other] = grad_down(t, other).astype(BF).reshape(4, 64, width)
        swap_down(t).start()

    for total in up_sums:
        total.middle()

    @pl.loop(0, 4)
    def _(t):
        swap_down(t).wait_recv()
        total = grad_down(t, core) + dn_c[t].reshape(256, width).astype(F32)
        wdn[t, core] = total.astype(BF).reshape(4, 64, width)

    for total in down_sums:
        total.start()

    @pl.loop(0, 4)
    def _(j):
        for copy in sends(j):
            copy.wait_recv()

    small_out[0:3, :] = jnp.zeros((3, width), F32)
    small_out[4:8, :] = jnp.zeros((4, width), F32)
    gain = vec_o[4:5, :]

    @pl.loop(0, blk // 16)
    def _(i):
        rows = pl.ds(pl.multiple_of(i * 16, 16), 16)
        d = own[rows, :]
        for p in range(3):
            d = d + got[p, rows, :].astype(F32)
        v = res_o[rows, :]
        centred = v - jnp.mean(v, axis=-1, keepdims=True)
        s = lax.rsqrt(jnp.mean(centred * centred, axis=-1, keepdims=True) + EPSILON)
        n = centred * s
        dn = d * gain
        d_res = s * (
            dn
            - jnp.mean(dn, axis=-1, keepdims=True)
            - n * jnp.mean(dn * n, axis=-1, keepdims=True)
        )
        dy_own = dy_in[rows, :].astype(F32)
        hid = dy_own + d_res
        low_hid = hid.astype(BF)
        dhid_out[rows, :] = hid
        dattn[x, rows, :] = low_hid
        small_out[0:1, :] += jnp.sum(d * n, axis=0, keepdims=True)
        small_out[1:2, :] += jnp.sum(d, axis=0, keepdims=True)
        small_out[2:3, :] += jnp.sum(low_hid.astype(F32), axis=0, keepdims=True)
        small_out[4:5, :] += jnp.sum(dy_own, axis=0, keepdims=True)

    attn = Relay(
        comm, "x", lambda o: dattn.at[o], lambda o, h: dattn.at[o, pl.ds(h * blk // 2, blk // 2)]
    )
    attn.start()
    kept = [keep_out]
    kept.append(pltpu.make_async_copy(wdn.at[:, core, z, low], dn_a_own, local_sem.at[2]))
    kept.append(pltpu.make_async_copy(wdn.at[y, core, :, high], dn_b_own, local_sem.at[3]))
    kept.append(pltpu.make_async_copy(wup.at[:, core, z, low], up_a_own, local_sem.at[4]))
    kept.append(pltpu.make_async_copy(wup.at[y, core, :, high], up_b_own, local_sem.at[5]))
    for copy in kept[1:]:
        copy.start()
    for total in down_sums:
        total.middle()
    attn.near()
    attn.far()
    kept.append(pltpu.make_async_copy(dattn, dattn_hbm, local_sem.at[1]))
    kept[-1].start()

    for total in up_sums + down_sums:
        total.finish()

    @pl.loop(0, 4)
    def _(j):
        for copy in sends(j):
            copy.wait_send()
        swap_down(j).wait_send()
        swap_up(j).wait_send()

    for copy in kept:
        copy.wait()
    for done in groups:
        done.drain()


def forward(collective_id, lengths, tok, small, w_up, dy, w_down, w_qkv, w_out):
    blk, width = tok.shape
    span, partw, hidden = 4 * blk, width // 4, w_up.shape[1] // 4
    vmem = pl.BlockSpec(memory_space=pltpu.VMEM)
    hbm = pl.BlockSpec(memory_space=pl.ANY)
    quarter = (4, 32, width)
    outs = [
        ((8, width), F32, vmem),
        ((blk, width), F32, vmem),
        ((blk, width), F32, vmem),
        ((8, width), F32, vmem),
        ((2, 4, 4, 64, 3 * partw), BF, hbm),
        ((2, 4, 4, 16, width), BF, hbm),
        ((span, width), BF, hbm),
        ((span, partw), BF, hbm),
        ((span + W, 2 * partw), BF, hbm),
        ((span, partw), BF, hbm),
        ((4, blk, width), BF, hbm),
        ((4, blk, width), BF, hbm),
    ]
    outs += [(quarter, BF, hbm)] * 4 + [((2,) + quarter, BF, hbm)] * 4
    scratch = [
        ((4, 2, 4, 64, hidden), BF),
        ((4, 2, 4, 64, width), BF),
        ((2, 4, 4, 64, width), BF),
        ((2, 4, 4, 16, width), BF),
        ((4, blk, width), BF),
        ((span, hidden), BF),
        ((span, hidden), BF),
        ((span, hidden), F32),
        ((span, partw), BF),
        ((span + W, 2 * partw), BF),
        ((span, partw), BF),
        ((4, blk, width), BF),
        ((4, blk, width), BF),
        ((3, blk, width), BF),
        ((blk, width), F32),
        ((4, blk, width), BF),
        ((4, blk, width), BF),
        ((4, 2, 128, 128), F32),
        ((hidden // 8, 512), BF),
        ((4, 16, hidden), BF),
        ((4, 2, 2, 32, width), BF),
    ]
    return pl.pallas_call(
        forward_body,
        out_shape=tuple(jax.ShapeDtypeStruct(s, d) for s, d, _ in outs),
        in_specs=[pl.BlockSpec(memory_space=pltpu.SMEM)] + [vmem] * 5 + [hbm] * 2,
        out_specs=tuple(o[2] for o in outs),
        scratch_shapes=[pltpu.VMEM(s, d) for s, d in scratch]
        + [pltpu.SemaphoreType.DMA((8,)), pltpu.SemaphoreType.REGULAR]
        + [pltpu.SemaphoreType.DMA((n,)) for n in (12, 12, 40, 40, SEMS, SEMS)],
        compiler_params=pltpu.CompilerParams(
            collective_id=collective_id, has_side_effects=True, vmem_limit_bytes=63 << 20
        ),
        name="forward",
    )(lengths, tok, small, w_up, dy, w_down, w_qkv, w_out)


def norm_backward(d, v, gain):
    centred = v - jnp.mean(v, axis=-1, keepdims=True)
    s = lax.rsqrt(jnp.mean(centred * centred, axis=-1, keepdims=True) + EPSILON)
    n = centred * s
    dn = d * gain
    d_v = s * (
        dn - jnp.mean(dn, axis=-1, keepdims=True) - n * jnp.mean(dn * n, axis=-1, keepdims=True)
    )
    return d_v, n


def attention_backward_body(
    lengths,
    vec_in,
    ffsmall_in,
    dattn_hbm,
    wout_hbm,
    q_hbm,
    kv_hbm,
    a1_hbm,
    mixed_hbm,
    wqkv_hbm,
    tok_hbm,
    dhid_hbm,
    res_hbm,
    outp_hbm,
    ffo0,
    ffo1,
    ffo2,
    ffo3,
    ffg0,
    ffg1,
    ffg2,
    ffg3,
    out_o,
    gtok_o,
    gqkv_o,
    gout_o,
    gup_o,
    gdn_o,
    small_o,
    late_o,
    dattn,
    wout,
    q_all,
    kv,
    a1,
    mixed,
    wqkv,
    tok,
    dhid,
    res,
    outown,
    outgot,
    fo,
    fg,
    fs,
    fg2,
    fup,
    fdn,
    dmix,
    dkv,
    dqkv,
    dedge,
    dedge_got,
    part,
    got,
    qkv_c,
    out_c,
    qa,
    qb,
    oa,
    ob,
    qs,
    os_,
    qa2,
    qb2,
    oa2,
    ob2,
    fq,
    fout,
    sm,
    smc,
    smz,
    smy,
    late,
    late_c,
    late_p,
    late_sum,
    gux,
    stack,
    gq,
    part_tmp,
    q_tmp,
    o_tmp,
    local_sem,
    send_sem,
    recv_sem,
    comm_send,
    comm_recv,
):
    sems = (send_sem, recv_sem)
    comm = Comm(comm_send, comm_recv, 0, 32)
    me = coords()
    x, y, z, core = me["x"], me["y"], me["z"], me["core"]
    other = 1 - core
    zy = lax.rem(y + 3, 4)
    blk, width = tok.shape
    span = 4 * blk
    partw = mixed.shape[1]
    heads = partw // HEAD
    scale = 1.0 / math.sqrt(HEAD)
    reach = W + blk
    used = [0]
    pending = []

    def load(src, dst):
        copy = pltpu.make_async_copy(src, dst, local_sem.at[used[0]])
        used[0] += 1
        copy.start()
        return copy

    def push(src, dst, index, to):
        copy = remote(src, dst, sems, index, to)
        copy.start()
        pending.append(copy)
        return copy

    l_dattn, l_wout = load(dattn_hbm, dattn), load(wout_hbm, wout)
    l_attn = [load(q_hbm, q_all), load(kv_hbm, kv)]
    low, high = slice(0, 32), slice(32, 64)
    l_ff = [load(s, fo.at[i]) for i, s in enumerate((ffo0, ffo1, ffo2, ffo3))]
    l_ff += [load(s, fg.at[i]) for i, s in enumerate((ffg0, ffg1, ffg2, ffg3))]
    l_wqkv, l_a1, l_mixed = load(wqkv_hbm, wqkv), load(a1_hbm, a1), load(mixed_hbm, mixed)
    l_end = [load(outp_hbm.at[0], outown), load(res_hbm, res)]
    l_end += [load(tok_hbm, tok), load(dhid_hbm, dhid)]

    greet(ring("x") + plane() + near() + [scattered(), collected()])

    p_out = [
        push(outp_hbm.at[p], outgot.at[p - 1], p, peer(x=-ORDER[p])) for p in (1, 2, 3)
    ]

    def ff_sum(i):
        for c in range(4):
            total = fo[i, c].astype(F32) + fg[i, 0, c].astype(F32) + fg[i, 1, c].astype(F32)
            fs[i, c] = total.astype(BF)

    p_ff = []

    def ff_second(i):
        axis, here = ("y", y) if i % 2 == 0 else ("z", z)
        for k in (1, 3, 2):
            src = fs.at[i, lax.rem(here + k, 4)]
            p_ff.append(push(src, fg2.at[i, k - 1], 4 + 3 * i + k, peer(**{axis: k})))

    for copy in l_ff:
        copy.wait()
    for i in range(4):
        ff_sum(i)
    ff_second(0)
    ff_second(2)
    dkv[...] = jnp.zeros(dkv.shape, F32)
    l_dattn.wait()
    l_wout.wait()
    dmix[...] = dot(
        dattn[...].reshape(span, width), wout[...].reshape(partw, width), NT
    ).astype(BF)
    for copy in l_attn:
        copy.wait()

    def block(b):
        rows = pl.ds(pl.multiple_of(b * blk, blk), blk)
        window = pl.ds(pl.multiple_of(b * blk, blk), reach)
        mask = mask_of(lengths, z * span + b * blk, blk, reach)
        for h in range(heads):
            cols = pl.ds(h * HEAD, HEAD)
            vcols = pl.ds(partw + h * HEAD, HEAD)
            q, k, v = q_all[rows, cols], kv[window, cols], kv[window, vcols]
            s = dot(q, k, NT) * scale + mask
            e = jnp.exp(s - jnp.max(s, axis=-1, keepdims=True))
            p = e * (1.0 / jnp.sum(e, axis=-1, keepdims=True))
            do = dmix[rows, cols]
            dp = dot(do, v, NT)
            ds = (p * (dp - jnp.sum(dp * p, axis=-1, keepdims=True))).astype(BF)
            dqkv[rows, cols] = (dot(ds, k, NN) * scale).astype(BF)
            dkv[window, cols] += dot(ds, q, TN) * scale
            dkv[window, vcols] += dot(p.astype(BF), do, TN)

    pl.loop(0, 2)(block)
    dedge[...] = dkv[0:W, :].astype(BF)
    p_edge = push(dedge, dedge_got, 4, peer(z=3))

    pl.loop(2, 4)(block)

    p_edge.wait_recv()
    ff_second(1)
    ff_second(3)
    dqkv[0 : span - W, partw:] = dkv[W:span, :].astype(BF)
    dqkv[span - W :, partw:] = (dkv[span:, :] + dedge_got[...].astype(F32)).astype(BF)
    sm[0, 0:5, :] = ffsmall_in[0:5, :]
    sm[0, 5:8, :] = jnp.zeros((3, width), F32)
    sm[0, 7:8, 0 : 3 * partw] = jnp.sum(dqkv[...].astype(F32), axis=0, keepdims=True)
    p_sc = push(sm.at[0], smc, 53, peer(core=1))

    ring_d = RingSum(comm, "x", lambda o, h: part.at[o, pl.ds(2 * h, 2)], part_tmp, got)
    qkv_sums = (
        RingSum(comm, "z", lambda o, h: gq.at[pl.ds(2 * h, 2), 0, o, low], q_tmp.at[0], qa),
        RingSum(comm, "y", lambda o, h: gq.at[o, 0, pl.ds(2 * h, 2), high], q_tmp.at[1], qb),
    )
    left, right = slice(0, width // 2), slice(width // 2, width)
    out_sums = (
        RingSum(
            comm, "z", lambda o, h: wout.at[core, pl.ds(2 * h, 2), o, :, left], o_tmp.at[0], oa
        ),
        RingSum(
            comm,
            "y",
            lambda o, h: wout.at[core, lax.rem(o + 3, 4), pl.ds(2 * h, 2), :, right],
            o_tmp.at[1],
            ob,
        ),
    )

    def grad_qkv(t, c):
        cols = pl.ds(pl.multiple_of(t * 512 + c * 256, 256), 256)
        return dot(a1[:, cols], dqkv[...], TN)

    def grad_out(c):
        cols = pl.ds(pl.multiple_of(c * 256, 256), 256)
        return dot(mixed[:, cols], dattn[...].reshape(span, width), TN)

    def swap(t):
        return remote(gq.at[t, 1], qkv_c.at[t], sems, 32 + t, peer(core=1))

    l_a1.wait()

    @pl.loop(0, 4)
    def _(t):
        gq[t, 1] = grad_qkv(t, other).astype(BF).reshape(4, 64, 3 * partw)
        swap(t).start()

    l_mixed.wait()
    wout[other] = grad_out(other).astype(BF).reshape(4, 4, 16, width)
    p_oc = push(wout.at[other], out_c, 36, peer(core=1))

    @pl.loop(0, 4)
    def _(t):
        swap(t).wait_recv()
        total = grad_qkv(t, core) + qkv_c[t].reshape(256, 3 * partw).astype(F32)
        gq[t, 0] = total.astype(BF).reshape(4, 64, 3 * partw)

    for total in qkv_sums:
        total.start()

    l_wqkv.wait()

    @pl.loop(0, 4)
    def _(j):
        cols = pl.ds(pl.multiple_of(j * 512, 512), 512)
        d = dot(dqkv[...], wqkv[:, j].reshape(512, 3 * partw), NT)
        part[:, :, :, cols] = d.astype(BF).reshape(4, 4, blk // 4, 512)

    ring_d.start()
    p_sc.wait_recv()
    sm[1] = sm[0] + smc[...]
    p_sz = [push(sm.at[1], smz.at[k - 1], 59 + k, peer(z=k)) for k in (1, 3, 2)]
    p_oc.wait_recv()
    wout[core] = (
        grad_out(core) + out_c[...].reshape(256, width).astype(F32)
    ).astype(BF).reshape(4, 4, 16, width)
    for total in out_sums:
        total.start()
    for total in qkv_sums:
        total.middle()
    ring_d.middle()

    for copy in l_end:
        copy.wait()
    for copy in p_out:
        copy.wait_recv()

    @pl.loop(0, blk // 16)
    def _(i):
        rows = pl.ds(pl.multiple_of(i * 16, 16), 16)
        total = res[rows, :] + vec_in[7:8, :] + outown[rows, :].astype(F32)
        for g in range(3):
            total = total + outgot[g, rows, :].astype(F32)
        out_o[rows, :] = total.astype(BF)

    for total in out_sums:
        total.middle()
    for total in qkv_sums:
        total.finish()
    for c in range(4):
        ta, tb = gq[c, 0, z, low].astype(F32), gq[y, 0, c, high].astype(F32)
        for g in range(2):
            ta, tb = ta + qa[g, c].astype(F32), tb + qb[g, c].astype(F32)
        qs[0, c], qs[1, c] = ta.astype(BF), tb.astype(BF)
    p_q2 = []
    for k in (1, 3, 2):
        tz, ty = lax.rem(z + k, 4), lax.rem(y + k, 4)
        p_q2.append(push(qs.at[0, ty], qa2.at[k - 1], 53 + k, peer(y=k)))
        p_q2.append(push(qs.at[1, tz], qb2.at[k - 1], 56 + k, peer(z=k)))

    late_sum[...] = jnp.zeros(late_sum.shape, F32)

    for copy in p_ff:
        copy.wait_recv()
    at = (y, z, y, z)
    for i in range(4):
        total = fs[i, at[i]].astype(F32)
        for g in range(3):
            total = total + fg2[i, g].astype(F32)
        into, half = (fup, fdn)[i // 2], i % 2
        into[2 * half : 2 * half + 2] = total.astype(BF).reshape(2, 16, width)
    ring_d.finish()
    p_u, p_x, kept = [], [], []
    for k in (1, 3, 2):
        p_u.append(push(fup.at[lax.rem(x + k, 4)], gux.at[x], 48 + k, peer(x=k)))
        p_x.append(push(fdn.at[lax.rem(x + k, 4)], gdn_o.at[x], 76 + k, peer(x=k)))
    gux[x] = fup[x]
    kept.append(load(fdn.at[x], gdn_o.at[x]))
    gain = vec_in[0:1, :]

    @pl.loop(0, blk // 16)
    def _(i):
        rows = pl.ds(pl.multiple_of(i * 16, 16), 16)
        c, r = i // 2, pl.ds(pl.multiple_of(lax.rem(i, 2) * 16, 16), 16)
        d = part[x, c, r, :].astype(F32)
        for g in range(2):
            d = d + got[g, c, r, :].astype(F32)
        d_in, n = norm_backward(d, tok[rows, :].astype(F32), gain)
        gtok_o[rows, :] = dhid[rows, :] + d_in
        late_sum[0:1, :] += jnp.sum(d * n, axis=0, keepdims=True)
        late_sum[1:2, :] += jnp.sum(d, axis=0, keepdims=True)

    for i in range(8):
        at = (i % 4) * (width // 4)
        late[0, i : i + 1, :] = late_sum[i // 4 : i // 4 + 1, at : at + width // 4]
    p_lc = push(late.at[0], late_c, 52, peer(core=1))
    p_lc.wait_recv()
    late[1] = late[0] + late_c[...]
    p_lz = [push(late.at[1], late_p.at[i], 98 + i, to) for i, to in enumerate(plane())]

    for copy in p_sz:
        copy.wait_recv()
    sm[2] = sm[1] + smz[0] + smz[1] + smz[2]
    p_sy = [push(sm.at[2], smy.at[k - 1], 68 + k, peer(y=k)) for k in (1, 3, 2)]
    for total in out_sums:
        total.finish()
    for c in range(4):
        ta, tb = wout[core, c, z, :, left].astype(F32), wout[core, zy, c, :, right].astype(F32)
        for g in range(2):
            ta, tb = ta + oa[g, c].astype(F32), tb + ob[g, c].astype(F32)
        os_[0, c], os_[1, c] = ta.astype(BF), tb.astype(BF)
    p_o2 = []
    for k in (1, 3, 2):
        tz, tyc = lax.rem(z + k, 4), lax.rem(y + k + 3, 4)
        p_o2.append(push(os_.at[0, tyc], oa2.at[k - 1], 62 + k, peer(y=k)))
        p_o2.append(push(os_.at[1, tz], ob2.at[k - 1], 65 + k, peer(z=k)))

    for copy in p_q2:
        copy.wait_recv()
    ta, tb = qs[0, y].astype(F32), qs[1, z].astype(F32)
    for g in range(3):
        ta, tb = ta + qa2[g].astype(F32), tb + qb2[g].astype(F32)
    fq[0:2] = ta.astype(BF).reshape(2, 16, 3 * partw)
    fq[2:4] = tb.astype(BF).reshape(2, 16, 3 * partw)
    for g in range(3):
        block_cols, own_cols = pl.ds(g * partw, partw), pl.ds(g * width + x * partw, partw)
        for k in (1, 3, 2):
            src = fq.at[lax.rem(x + k, 4), :, block_cols]
            p_x.append(push(src, gqkv_o.at[:, own_cols], 83 + 3 * g + k - 1, peer(x=k)))
        kept.append(load(fq.at[x, :, block_cols], gqkv_o.at[:, own_cols]))

    for copy in p_sy:
        copy.wait_recv()
    sm[3] = sm[2] + smy[0] + smy[1] + smy[2]
    p_x += [push(sm.at[3], small_o.at[x], 71 + k, peer(x=k)) for k in (1, 3, 2)]
    kept.append(load(sm.at[3], small_o.at[x]))


    for copy in p_o2:
        copy.wait_recv()
    ta, tb = os_[0, zy].astype(F32), os_[1, z].astype(F32)
    for g in range(3):
        ta, tb = ta + oa2[g].astype(F32), tb + ob2[g].astype(F32)
    fout[:, left], fout[:, right] = ta.astype(BF), tb.astype(BF)
    p_x.append(push(fout, gout_o, 75, collected()))

    for copy in p_lz:
        copy.wait_recv()
    total = late[1]
    for i in range(15):
        total = total + late_p[i]
    late[2] = total
    p_x += [push(late.at[2], late_o.at[x], 79 + k, peer(x=k)) for k in (1, 3, 2)]
    kept.append(load(late.at[2], late_o.at[x]))

    for copy in p_u:
        copy.wait_recv()
    slabs = width // 128
    for i in range(slabs):
        for c in range(4):
            stack[16 * i : 16 * i + 16, 128 * c : 128 * c + 128] = gux[
                c, :, 128 * i : 128 * i + 128
            ]
    spread_up = dot(stack[...], shuffle(), NT)
    for i in range(slabs):
        gup_o[:, 512 * i : 512 * i + 512] = spread_up[16 * i : 16 * i + 16, :]

    for copy in p_x:
        copy.wait_recv()
    for copy in pending:
        copy.wait_send()

    @pl.loop(0, 4)
    def _(j):
        swap(j).wait_send()

    comm.drain()

    for copy in kept:
        copy.wait()


def attention_backward(
    collective_id,
    lengths,
    vectors,
    ff_small,
    d_attn,
    wout,
    q,
    kv,
    a1,
    mixed,
    wqkv,
    tok,
    d_hidden,
    residual,
    out_part,
    ff_own,
    ff_got,
):
    blk, width = tok.shape
    span, partw = mixed.shape
    hidden = ff_own[0].shape[-1]
    vmem = pl.BlockSpec(memory_space=pltpu.VMEM)
    hbm = pl.BlockSpec(memory_space=pl.ANY)
    outs = [
        ((blk, width), BF, vmem),
        ((blk, width), F32, vmem),
        ((16, 3 * width), BF, hbm),
        ((16, width), BF, hbm),
        ((16, 4 * hidden), F32, vmem),
        ((4, 16, width), BF, hbm),
        ((4, 8, width), F32, hbm),
        ((4, 8, width // 4), F32, hbm),
    ]
    half = width // 2
    scratch = [
        ((4, blk, width), BF),
        ((2, 4, 4, 16, width), BF),
        ((span, partw), BF),
        ((span + W, 2 * partw), BF),
        ((span, width), BF),
        ((span, partw), BF),
        ((2, 4, 4, 64, 3 * partw), BF),
        ((blk, width), BF),
        ((blk, width), F32),
        ((blk, width), F32),
        ((blk, width), BF),
        ((3, blk, width), BF),
        ((4, 4, 32, width), BF),
        ((4, 2, 4, 32, width), BF),
        ((4, 4, 32, width), BF),
        ((4, 3, 32, width), BF),
        ((4, 16, hidden), BF),
        ((4, 16, width), BF),
        ((span, partw), BF),
        ((span + W, 2 * partw), F32),
        ((span, 3 * partw), BF),
        ((W, 2 * partw), BF),
        ((W, 2 * partw), BF),
        ((4, 4, blk // 4, width), BF),
        ((2, 4, blk // 4, width), BF),
        ((4, 4, 64, 3 * partw), BF),
        ((4, 4, 16, width), BF),
        ((2, 4, 32, 3 * partw), BF),
        ((2, 4, 32, 3 * partw), BF),
        ((2, 4, 16, half), BF),
        ((2, 4, 16, half), BF),
        ((2, 4, 32, 3 * partw), BF),
        ((2, 4, 16, half), BF),
        ((3, 32, 3 * partw), BF),
        ((3, 32, 3 * partw), BF),
        ((3, 16, half), BF),
        ((3, 16, half), BF),
        ((4, 16, 3 * partw), BF),
        ((16, width), BF),
        ((4, 8, width), F32),
        ((8, width), F32),
        ((3, 8, width), F32),
        ((3, 8, width), F32),
        ((3, 8, width // 4), F32),
        ((8, width // 4), F32),
        ((15, 8, width // 4), F32),
        ((2, width), F32),
        ((4, 16, hidden), BF),
        ((hidden // 8, 512), BF),
        ((4, 2, 4, 64, 3 * partw), BF),
        ((2, 2, blk // 4, width), BF),
        ((2, 2, 2, 32, 3 * partw), BF),
        ((2, 2, 2, 16, half), BF),
    ]
    return pl.pallas_call(
        attention_backward_body,
        out_shape=tuple(jax.ShapeDtypeStruct(s, d) for s, d, _ in outs),
        in_specs=[pl.BlockSpec(memory_space=pltpu.SMEM)] + [vmem] * 2 + [hbm] * 19,
        out_specs=tuple(o[2] for o in outs),
        scratch_shapes=[pltpu.VMEM(s, d) for s, d in scratch]
        + [
            pltpu.SemaphoreType.DMA((32,)),
            pltpu.SemaphoreType.DMA((114,)),
            pltpu.SemaphoreType.DMA((114,)),
            pltpu.SemaphoreType.DMA((32,)),
            pltpu.SemaphoreType.DMA((32,)),
        ],
        compiler_params=pltpu.CompilerParams(
            collective_id=collective_id, has_side_effects=True, vmem_limit_bytes=62 << 20
        ),
        name="attention_backward",
    )(
        lengths,
        vectors,
        ff_small,
        d_attn,
        wout,
        q,
        kv,
        a1,
        mixed,
        wqkv,
        tok,
        d_hidden,
        residual,
        out_part,
        *ff_own,
        *ff_got,
    )


def results_body(
    out,
    gtok,
    gqkv,
    gout,
    gup,
    gdn,
    small,
    late,
    out_o,
    gtok_o,
    gain1_o,
    shift1_o,
    gqkv_o,
    bqv_o,
    gout_o,
    bout_o,
    gain2_o,
    shift2_o,
    gup_o,
    bup_o,
    gdn_o,
    bdown_o,
    sums,
):
    me = coords()
    device = ((me["y"] * 2 + me["core"]) * 4 + me["z"]) * 4 + me["x"]
    out_o[...] = out[...]
    gtok_o[...] = gtok[...]
    gqkv_o[...] = gqkv[...].astype(F32)
    gout_o[...] = gout[...].astype(F32)
    gup_o[...] = gup[...]
    gdn_o[...] = gdn[...].reshape(gdn_o.shape).astype(F32)

    tile = pl.ds(pl.multiple_of(device // 8 * 128, 128), 128)
    turn = lax.rem(128 - 16 * lax.rem(device, 8), 128)
    shares = [pltpu.roll(small[i, :, tile], turn, 1) for i in range(4)]
    total = shares[0] + shares[1] + shares[2] + shares[3]
    gain2_o[...] = total[0:1, 0:16]
    shift2_o[...] = total[1:2, 0:16]
    bout_o[...] = total[2:3, 0:16]
    bdown_o[...] = total[4:5, 0:16]
    for i in range(4):
        bup_o[:, 16 * i : 16 * i + 16] = shares[i][3:4, 0:16]

    sums[...] = late[0] + late[1] + late[2] + late[3]
    place = lax.rem(device, 32)
    tile = pl.ds(pl.multiple_of(place // 8 * 128, 128), 128)
    turned = pltpu.roll(sums[:, tile], turn, 1)
    row = lax.broadcasted_iota(jnp.int32, turned.shape, 0)

    def only(i):
        return jnp.sum(jnp.where(row == i, turned, 0.0), axis=0, keepdims=True)[:, 0:16]

    gain1_o[...] = only(device // 32)
    shift1_o[...] = only(4 + device // 32)

    half, place = device // 64, lax.rem(device, 16)
    tile = pl.ds(pl.multiple_of(half * 1024 + place // 4 * 128, 128), 128)
    turn = lax.rem(128 - 32 * lax.rem(device, 4), 128)
    bqv_o[...] = pltpu.roll(small[lax.rem(device, 64) // 16, :, tile], turn, 1)[7:8, 0:32]


def results(*arrays):
    out, gtok, gqkv, gout, gup, gdn = arrays[:6]
    vmem = pl.BlockSpec(memory_space=pltpu.VMEM)
    rows, vector = gdn.shape[0] * gdn.shape[1], lambda n: ((1, n), F32)
    outs = [
        (out.shape, BF),
        (gtok.shape, F32),
        vector(16),
        vector(16),
        (gqkv.shape, F32),
        vector(32),
        (gout.shape, F32),
        vector(16),
        vector(16),
        vector(16),
        (gup.shape, F32),
        vector(64),
        ((rows, gdn.shape[2]), F32),
        vector(16),
    ]
    return pl.pallas_call(
        results_body,
        out_shape=tuple(jax.ShapeDtypeStruct(s, d) for s, d in outs),
        in_specs=[vmem] * 8,
        out_specs=(vmem,) * 14,
        scratch_shapes=[pltpu.VMEM(arrays[7].shape[1:], F32)],
        compiler_params=pltpu.CompilerParams(vmem_limit_bytes=40 << 20),
        name="results",
    )(*arrays)


def local(
    tokens,
    grad_out,
    lengths,
    ln1_gain,
    ln1_bias,
    w_qkv,
    b_qv,
    w_out,
    b_out,
    ln2_gain,
    ln2_bias,
    w_up,
    b_up,
    w_down,
    b_down,
):
    blk, width = tokens.shape[1:]
    part = width // 4
    hidden = w_up.shape[1] // 4
    tok = tokens.reshape(blk, width)
    dy = grad_out.reshape(blk, width)
    small = jnp.zeros((1024,), F32)
    vectors = (ln1_gain, ln1_bias, b_qv, b_out, ln2_gain, ln2_bias, b_up, b_down)
    for i, vector in enumerate(vectors):
        size = vector.shape[0]
        small = small + jnp.pad(vector.astype(F32), (i * 128, 1024 - i * 128 - size))
    (
        vectors,
        residual,
        d_hidden,
        ff_small,
        wqkv_g,
        wout_g,
        a1,
        query,
        kv,
        mixed,
        d_attn_g,
        out_part,
        up_a_own,
        up_b_own,
        down_a_own,
        down_b_own,
        up_a_got,
        up_b_got,
        down_a_got,
        down_b_got,
    ) = forward(0, lengths, tok, small.reshape(8, 128), w_up, dy, w_down, w_qkv, w_out)
    last = attention_backward(
        1,
        lengths,
        vectors,
        ff_small,
        d_attn_g,
        wout_g,
        query,
        kv,
        a1,
        mixed,
        wqkv_g,
        tok,
        d_hidden,
        residual,
        out_part,
        (up_a_own, up_b_own, down_a_own, down_b_own),
        (up_a_got, up_b_got, down_a_got, down_b_got),
    )

    final = list(results(*last))
    final[0] = final[0].reshape(1, blk, width)
    final[1] = final[1].reshape(1, blk, width)
    for i in (2, 3, 5, 7, 8, 9, 11, 13):
        final[i] = final[i].reshape(-1)
    return tuple(final)


def solution(mesh):
    fine = Mesh(mesh.devices.reshape(4, 2, 4, 4), AXES)
    rows, seq = ("y", "core"), ("z", "x")
    every = rows + seq
    token = P(rows, seq, None)
    vec, mat = P(every), P(every, None)
    in_specs = (token, token, P(rows, None), vec, vec, mat, vec, mat, vec, vec, vec, mat, vec, mat, vec)
    out_specs = (token, token, vec, vec, mat, vec, mat, vec, vec, vec, mat, vec, mat, vec)
    return jax.shard_map(local, mesh=fine, in_specs=in_specs, out_specs=out_specs, check_vma=False)
```

```python
import functools
import math

import jax
import jax.numpy as jnp
from jax import lax
from jax.experimental import pallas as pl
from jax.experimental.pallas import tpu as pltpu
from jax.sharding import Mesh, PartitionSpec as P

HEADS = 16
HEAD = 128
W = 256
EPSILON = 1e-05
NEG_FILL = -1e30

AXES = ("y", "core", "z", "x")
SIZE = {"y": 4, "core": 2, "z": 4, "x": 4}
BF = jnp.bfloat16
F32 = jnp.float32
SEMS = 264


def coords():
    return {a: lax.axis_index(a) for a in AXES}


def peer(**delta):
    me = coords()
    return tuple(lax.rem(me[a] + delta.get(a, 0) % SIZE[a], SIZE[a]) for a in AXES)


class Comm:
    def __init__(self, send_sem, recv_sem, base=0, room=SEMS):
        self.send_sem, self.recv_sem = send_sem, recv_sem
        self.count, self.last, self.open = base, base + room, []

    def push(self, src, dst, to):
        entry = self.plan(src, dst, to)
        entry[0].start()
        return entry

    def plan(self, src, dst, to):
        copy = pltpu.make_async_remote_copy(
            src_ref=src,
            dst_ref=dst,
            send_sem=self.send_sem.at[self.count],
            recv_sem=self.recv_sem.at[self.count],
            device_id=to,
            device_id_type=pl.DeviceIdType.MESH,
        )
        assert self.count < self.last
        self.count += 1
        self.open.append([copy, True, True])
        return self.open[-1]

    def local(self, src, dst):
        copy = pltpu.make_async_copy(src, dst, self.send_sem.at[self.count])
        self.count += 1
        copy.start()
        self.open.append([copy, False, True])
        return self.open[-1]

    def arrived(self, entries):
        for entry in entries:
            if entry[2]:
                if entry[1]:
                    entry[0].wait_recv()
                else:
                    entry[0].wait()
                entry[2] = False

    def drain(self):
        self.arrived(self.open)
        for copy, remote_copy, _ in self.open:
            if remote_copy:
                copy.wait_send()
        self.open = []


def greet(devices):
    barrier = pltpu.get_barrier_semaphore()
    for device in devices:
        pl.semaphore_signal(barrier, inc=1, device_id=device, device_id_type=pl.DeviceIdType.MESH)
    pl.semaphore_wait(barrier, len(devices))


def ring(axis):
    return [peer(**{axis: k}) for k in (1, 3, 2)]


def near():
    return [peer(core=1)]


def plane():
    return [peer(y=i // 4, z=i % 4) for i in range(1, 16)]


def everyone():
    return ring("x") + ring("y") + ring("z") + near()


def scattered():
    me = coords()
    return (lax.rem(me["z"] + 1, 4), me["core"], me["x"], me["y"])


def collected():
    me = coords()
    return (me["x"], me["core"], lax.rem(me["y"] + 3, 4), me["z"])


class Relay:
    def __init__(self, comm, axis, full, half):
        self.comm, self.axis, self.full, self.half = comm, axis, full, half
        self.me = lax.axis_index(axis)

    def to(self, k):
        return peer(**{self.axis: k})

    def start(self):
        a, b = self.half(self.me, 0), self.half(self.me, 1)
        self.sent = [self.comm.push(a, a, self.to(1)), self.comm.push(b, b, self.to(3))]
        self.rest = [self.comm.push(b, b, self.to(1)), self.comm.push(a, a, self.to(3))]

    def near(self):
        self.comm.arrived(self.sent)
        before, after = lax.rem(self.me + 3, 4), lax.rem(self.me + 1, 4)
        up, down = self.half(before, 0), self.half(after, 1)
        self.passed = [self.comm.push(up, up, self.to(1)), self.comm.push(down, down, self.to(3))]
        self.comm.arrived(self.rest)

    def far(self):
        self.comm.arrived(self.passed)


class RingSum:
    def __init__(self, comm, axis, ref, tmp, got):
        self.comm, self.axis, self.ref, self.tmp, self.got = comm, axis, ref, tmp, got
        self.me = lax.axis_index(axis)

    def at(self, k):
        return lax.rem(self.me + k, 4)

    def push(self, src, dst, k):
        return self.comm.push(src, dst, peer(**{self.axis: k}))

    def plan(self, src, dst, k):
        return self.comm.plan(src, dst, peer(**{self.axis: k}))

    def prepare(self):
        self.up = self.plan(self.ref(self.at(2), 0), self.tmp.at[0], 1)
        self.down = self.plan(self.ref(self.at(2), 1), self.tmp.at[1], 3)
        self.end = [
            self.plan(self.ref(self.at(1), 1), self.got.at[0, pl.ds(2, 2)], 1),
            self.plan(self.ref(self.at(3), 0), self.got.at[1, pl.ds(0, 2)], 3),
        ]
        self.first = {1: [self.end[0]], 2: [self.up, self.down], 3: [self.end[1]]}

    def start(self):
        self.prepare()
        for k in (2, 1, 3):
            for entry in self.first[k]:
                entry[0].start()

    def start_block(self, to):
        for k in (2, 1, 3):

            @pl.when(self.at(k) == to)
            def _():
                for entry in self.first[k]:
                    entry[0].start()

    def middle(self):
        for arrived, k, h, back in ((self.up, 1, 0, 0), (self.down, 3, 1, 2)):
            self.comm.arrived([arrived])
            block = self.ref(self.at(k), h)
            for c in range(2):
                total = block[c].astype(F32) + self.tmp[h, c].astype(F32)
                block[c] = total.astype(BF)
            self.end.append(self.push(block, self.got.at[h, pl.ds(back, 2)], k))

    def finish(self):
        self.comm.arrived(self.end)


class Gather:
    def __init__(self, comm, w, by_core, cut, shift=0):
        self.comm, self.w, self.by_core, self.cut = comm, w, by_core, cut
        self.shift = shift
        me = coords()
        self.y, self.core, self.z = me["y"], me["core"], me["z"]

    def slot(self, y, z, cut):
        place = (self.core, y, z) if self.by_core else (y, self.core, z)
        return self.w.at[place + self.cut[cut]]

    def row(self, y):
        return lax.rem(y + self.shift, 4)

    def first(self):
        self.first_a()
        self.first_b()
        self.one = self.one_a + self.one_b

    def first_a(self):
        a = self.slot(self.row(self.y), self.z, 0)
        self.one_a = [self.comm.push(a, a, to) for to in ring("z")]

    def first_b(self):
        b = self.slot(self.row(self.y), self.z, 1)
        self.one_b = [self.comm.push(b, b, to) for to in ring("y")]

    def second(self):
        self.second_a()
        self.second_b()

    def second_a(self):
        every = slice(None)
        self.a = Relay(
            self.comm,
            "y",
            lambda o: self.slot(self.row(o), every, 0),
            lambda o, h: self.slot(self.row(o), pl.ds(2 * h, 2), 0),
        )
        self.a.start()

    def second_b(self):
        every = slice(None)
        self.b = Relay(
            self.comm,
            "z",
            lambda o: self.slot(every, o, 1),
            lambda o, h: self.slot(pl.ds(2 * h, 2), o, 1),
        )
        self.b.start()

    def across(self, relay, k):
        block = relay.full(lax.rem(relay.me + k, 4))
        self.two.append(self.comm.push(block, block, peer(core=1)))

    def near_a(self):
        self.two = []
        self.a.near()
        for k in (0, 1, 3):
            self.across(self.a, k)

    def near_b(self):
        self.b.near()
        for k in (0, 1, 3):
            self.across(self.b, k)

    def near(self):
        self.near_a()
        self.near_b()

    def far_a(self):
        self.a.far()
        self.across(self.a, 2)

    def far_b(self):
        self.b.far()
        self.across(self.b, 2)

    def far(self):
        self.far_a()
        self.far_b()

    def done(self):
        self.comm.arrived(self.two)


def by_rows(rows):
    return [(slice(0, rows // 2),), (slice(rows // 2, rows),)]


def by_columns(columns):
    every = slice(None)
    return [(every, slice(0, columns // 2)), (every, slice(columns // 2, columns))]


def dot(a, b, dims):
    return lax.dot_general(a, b, (dims, ((), ())), preferred_element_type=F32)


NN = ((1,), (0,))
NT = ((1,), (1,))
TN = ((0,), (0,))


def mask_of(lengths, first, blk, reach):
    q = first + lax.broadcasted_iota(jnp.int32, (blk, reach), 0)
    k = first - W + lax.broadcasted_iota(jnp.int32, (blk, reach), 1)
    q_doc, k_doc = jnp.zeros((blk, reach), jnp.int32), jnp.zeros((blk, reach), jnp.int32)
    end = 0
    for i in range(lengths.shape[1]):
        end = end + lengths[0, i]
        q_doc = q_doc + jnp.where(q >= end, 1, 0)
        k_doc = k_doc + jnp.where(k >= end, 1, 0)
    seen = (q_doc == k_doc) & (k <= q) & (q - k < W) & (k >= 0)
    return jnp.where(seen, 0.0, NEG_FILL).astype(F32)


def shuffle():
    row = lax.broadcasted_iota(jnp.int32, (512, 512), 0)
    column = lax.broadcasted_iota(jnp.int32, (512, 512), 1)
    source = 64 * ((column >> 4) & 7) + 16 * (column >> 7) + (column & 15)
    return jnp.where(source == row, 1.0, 0.0).astype(BF)


def whole_vector(table, index, offset, count, size, lane):
    shift = size.bit_length() - 1
    row = lax.broadcasted_iota(jnp.int32, (128, 1024), 0)
    tile = lax.broadcasted_iota(jnp.int32, (128, 1024), 1)
    chosen = jnp.where(tile == row * 8 + index, 1.0, 0.0).astype(BF)
    share = dot(chosen, table, NN).astype(BF)
    row = lax.broadcasted_iota(jnp.int32, (128, count), 0)
    column = lax.broadcasted_iota(jnp.int32, (128, count), 1) + offset
    spread = jnp.where((column & (size - 1)) + lane == row, 1.0, 0.0).astype(BF)
    values = jnp.where((column >> shift) == row, dot(share, spread, NN), 0.0)
    return jnp.sum(values, axis=0, keepdims=True)


ORDER = (0, 1, 3, 2)


def remote(src, dst, sems, index, to):
    send, recv = sems
    return pltpu.make_async_remote_copy(
        src_ref=src,
        dst_ref=dst,
        send_sem=send.at[index],
        recv_sem=recv.at[index],
        device_id=to,
        device_id_type=pl.DeviceIdType.MESH,
    )


def forward_body(
    lengths,
    tok_in,
    small_in,
    wup_in,
    dy_in,
    wdn_in,
    wqkv_in,
    wout_in,
    vec_o,
    res_h,
    dhid_h,
    small_out,
    wq_h,
    wo_h,
    a1_h,
    q_h,
    kv_h,
    mixed_h,
    dattn_hbm,
    outp_hbm,
    up_mine,
    up_two,
    dn_a_own,
    dn_b_own,
    dn_a_got,
    dn_b_got,
    wup,
    wdn,
    cc,
    wo,
    tokg,
    act,
    dup,
    dact,
    q,
    kv,
    mixed,
    dyg,
    part,
    got,
    dattn,
    smalls,
    stack,
    uparts,
    ring_tmp,
    up_got,
    res_o,
    dhid_out,
    local_sem,
    free_sem,
    ff_send,
    ff_recv,
    send_sem,
    recv_sem,
):
    groups, taken = [], [0]

    def group(room):
        comm = Comm(send_sem, recv_sem, taken[0], room)
        taken[0] += room
        groups.append(comm)
        return comm

    c_q, c_o, c_u, c_d = group(40), group(30), group(30), group(30)
    c_small, c_tok, comm = group(28), group(6), group(40)
    sems = (ff_send, ff_recv)
    me = coords()
    x, y, z, core = me["x"], me["y"], me["z"], me["core"]
    other = 1 - core
    blk, width = tok_in.shape
    span = 4 * blk
    partw = q.shape[1]
    hidden = act.shape[1]
    heads = partw // HEAD
    reach = W + blk
    scale = 1.0 / math.sqrt(HEAD)
    mine16 = pl.ds(x * 16, 16)
    low, high = slice(0, 32), slice(32, 64)
    a1, up_c, dn_c, a2g = act, cc.at[0], cc.at[1], tokg
    wide = slice(0, 3 * partw)

    greet(ring("x") + plane() + near() + [scattered(), collected()])

    s_q = []
    for k in (1, 3, 2):
        for g in range(3):
            src = wqkv_in.at[:, pl.ds(g * width + lax.rem(x + k, 4) * partw, partw)]
            dst = cc.at[core, y, z, mine16, pl.ds(g * partw, partw)]
            s_q.append(c_q.push(src, dst, peer(x=k)))
    for g in range(3):
        src = wqkv_in.at[:, pl.ds(g * width + x * partw, partw)]
        s_q.append(c_q.local(src, cc.at[core, y, z, mine16, pl.ds(g * partw, partw)]))
    spot = smalls.at[y, core, pl.ds((z * 4 + x) * 8, 8)]
    s_small = [c_small.push(small_in, spot, to) for to in ring("x")]
    s_small.append(c_small.local(small_in, spot))
    s_o = [c_o.push(wout_in, wo.at[core, z, x], scattered())]
    tokens = Relay(
        c_tok, "x", lambda o: tokg.at[o], lambda o, h: tokg.at[o, pl.ds(h * blk // 2, blk // 2)]
    )
    tokg[x] = tok_in[...]
    tokens.start()

    qkv_g = Gather(c_q, cc, True, [cut + (wide,) for cut in by_rows(64)])
    out_g = Gather(c_o, wo, True, by_columns(width), 3)
    down_g = Gather(c_d, wdn, False, by_rows(64))
    up_g = Gather(c_u, wup, False, by_rows(64))

    c_q.arrived(s_q)
    qkv_g.first()
    c_small.arrived(s_small)
    block = smalls.at[y, core, pl.ds(z * 32, 32)]
    s_small = [c_small.push(block, block, to) for to in plane()]

    slabs = 4 * hidden // 512
    for i in range(slabs):
        stack[16 * i : 16 * i + 16, :] = wup_in[:, 512 * i : 512 * i + 512]
    mixed_up = dot(stack[...], shuffle(), NN).astype(BF)
    for i in range(slabs):
        for to in range(4):
            uparts[to, :, 128 * i : 128 * i + 128] = mixed_up[
                16 * i : 16 * i + 16, 128 * to : 128 * to + 128
            ]

    c_q.arrived(qkv_g.one)
    qkv_g.second()
    c_o.arrived(s_o)
    out_g.first()
    c_small.arrived(s_small)
    s_small = []
    for other_y in range(4):
        block = smalls.at[other_y, core]
        s_small.append(c_small.push(block, block, peer(core=1)))
    tokens.near()
    s_u, s_d = [], []
    for k in (1, 3, 2):
        to = lax.rem(x + k, 4)
        s_d.append(
            c_d.push(wdn_in.at[pl.ds(to * 16, 16)], wdn.at[y, core, z, mine16], peer(x=k))
        )
        s_u.append(c_u.push(uparts.at[to], wup.at[y, core, z, mine16], peer(x=k)))
    s_d.append(c_d.local(wdn_in.at[mine16], wdn.at[y, core, z, mine16]))
    s_u.append(c_u.local(uparts.at[x], wup.at[y, core, z, mine16]))
    s_dy = [comm.push(dy_in, dyg.at[p], peer(x=ORDER[p])) for p in (1, 2, 3)]
    dyg[0] = dy_in[...]

    c_small.arrived(s_small)
    table = smalls[...].reshape(1024, 128).astype(BF)
    vec_o[0:1, :] = whole_vector(table, 0, 0, width, 16, 0)
    vec_o[1:2, :] = whole_vector(table, 1, 0, width, 16, 0)
    gain, shift = vec_o[0:1, :], vec_o[1:2, :]

    def norm_block(o):
        @pl.loop(0, blk // 16)
        def _(i):
            rows = pl.ds(pl.multiple_of(i * 16, 16), 16)
            v = tokg[o, rows, :].astype(F32)
            centred = v - jnp.mean(v, axis=-1, keepdims=True)
            s = lax.rsqrt(jnp.mean(centred * centred, axis=-1, keepdims=True) + EPSILON)
            at = pl.ds(pl.multiple_of(o * blk + i * 16, 16), 16)
            a1[at, :] = (centred * s * gain + shift).astype(BF)

    norm_block(x)
    qkv_g.near()
    c_o.arrived(out_g.one)
    out_g.second()
    norm_block(lax.rem(x + 1, 4))
    norm_block(lax.rem(x + 3, 4))
    qkv_g.far()
    tokens.far()
    norm_block(lax.rem(x + 2, 4))
    out_g.near()
    c_d.arrived(s_d)
    down_g.first()
    c_u.arrived(s_u)
    up_g.first_b()
    keep_a1 = [comm.local(a1, a1_h)]
    vec_o[2:3, :] = jnp.zeros((1, width), F32)
    vec_o[2:3, 0:partw] = whole_vector(table, 2, x * partw, partw, 32, 0)
    vec_o[2:3, 2 * partw : 3 * partw] = whole_vector(table, 2, width + x * partw, partw, 32, 0)
    qkv_g.done()

    def project(first):
        cols = slice(first, first + partw)
        total = vec_o[2:3, cols]
        rows = [
            jnp.concatenate([cc[0, j, :, :, cols], cc[1, j, :, :, cols]]).reshape(512, partw)
            for j in range(4)
        ]
        w = jnp.concatenate(rows)
        return (dot(a1[...], w, NN) + total).astype(BF)

    kv[W:, 0:partw] = project(partw)
    kv[W:, partw:] = project(2 * partw)
    s_edge = [comm.push(kv.at[pl.ds(span, W)], kv.at[pl.ds(0, W)], peer(z=1))]
    q[...] = project(0)
    keep_q = [c_q.local(cc.at[:, :, :, :, wide], wq_h)]
    comm.local(q, q_h)

    def attend(b):
        rows = pl.ds(pl.multiple_of(b * blk, blk), blk)
        window = pl.ds(pl.multiple_of(b * blk, blk), reach)
        mask = mask_of(lengths, z * span + b * blk, blk, reach)
        for h in range(heads):
            cols, vcols = pl.ds(h * HEAD, HEAD), pl.ds(partw + h * HEAD, HEAD)
            s = dot(q[rows, cols], kv[window, cols], NT) * scale + mask
            e = jnp.exp(s - jnp.max(s, axis=-1, keepdims=True))
            p = (e * (1.0 / jnp.sum(e, axis=-1, keepdims=True))).astype(BF)
            mixed[rows, cols] = dot(p, kv[window, vcols], NN).astype(BF)

    c_sum = group(8)
    ring_a = RingSum(c_sum, "x", lambda o, h: part.at[o, pl.ds(2 * h, 2)], ring_tmp.at[0], got)
    ring_a.prepare()

    def project_out(o):
        rows = slice(o * blk, (o + 2) * blk)

        @pl.loop(0, 4)
        def _(j):
            cols = pl.ds(pl.multiple_of(j * 512, 512), 512)
            d = dot(mixed[rows, :], wo[:, :, :, :, cols].reshape(partw, 512), NN)
            part[o : o + 2, :, :, cols] = d.astype(BF).reshape(2, 4, blk // 4, 512)
            dact[rows, cols] = d

        for to in (o, o + 1):
            ring_a.start_block(to)

    pl.loop(2, 4)(attend)
    out_g.far()
    out_g.done()
    c_tok.drain()
    project_out(2)
    c_d.arrived(down_g.one)
    down_g.second_a()
    for i in (3, 4, 5, 7):
        vec_o[i : i + 1, :] = whole_vector(table, i, 0, width, 16, 0)
    vec_o[6:7, :] = whole_vector(table, 6, 0, hidden, 16, x * 16)
    comm.arrived(s_edge)
    up_g.first_a()
    down_g.second_b()
    pl.loop(0, 2)(attend)
    project_out(0)
    down_g.near_a()
    c_u.arrived(up_g.one_a + up_g.one_b)
    up_g.second_a()
    comm.local(kv, kv_h)
    comm.local(mixed, mixed_h)
    c_o.local(wo, wo_h)
    c_q.drain()
    pl.semaphore_signal(
        free_sem, inc=1, device_id=peer(core=1), device_id_type=pl.DeviceIdType.MESH
    )
    down_g.near_b()
    up_g.second_b()
    ring_a.middle()
    down_g.far_a()

    ring_a.finish()
    b_out, gain2, shift2 = vec_o[3:4, :], vec_o[4:5, :], vec_o[5:6, :]

    @pl.loop(0, blk // 16)
    def _(i):
        rows = pl.ds(pl.multiple_of(i * 16, 16), 16)
        own_rows = pl.ds(pl.multiple_of(x * blk + i * 16, 16), 16)
        v = tok_in[rows, :].astype(F32) + dact[own_rows, :] + b_out
        c, r = i // 2, pl.ds(pl.multiple_of(lax.rem(i, 2) * 16, 16), 16)
        for g in range(2):
            v = v + got[g, c, r, :].astype(F32)
        res_o[rows, :] = v
        centred = v - jnp.mean(v, axis=-1, keepdims=True)
        s = lax.rsqrt(jnp.mean(centred * centred, axis=-1, keepdims=True) + EPSILON)
        a2g[0, rows, :] = (centred * s * gain2 + shift2).astype(BF)

    top, bottom = pl.ds(0, blk // 2), pl.ds(blk // 2, blk // 2)
    spread = []
    for p, rows in ((1, top), (2, bottom), (1, bottom), (2, top)):
        spread.append(comm.push(a2g.at[0, rows], a2g.at[p, rows], peer(x=ORDER[p])))
    comm.local(res_o, res_h)
    down_g.far_b()
    up_g.near_a()
    c_sum.drain()
    comm.arrived(keep_a1 + s_dy)
    down_g.done()

    @pl.loop(0, 4)
    def _(j):
        tile = wdn[j].reshape(512, width)
        cols = pl.ds(pl.multiple_of(j * 512, 512), 512)
        dact[:, cols] = dot(dyg[...].reshape(span, width), tile, NT)

    comm.arrived(spread[:2])
    passed = [
        comm.push(a2g.at[1, top], a2g.at[3, top], peer(x=1)),
        comm.push(a2g.at[2, bottom], a2g.at[3, bottom], peer(x=3)),
    ]
    up_g.near_b()
    up_g.far_a()
    up_g.far_b()
    up_g.done()
    comm.arrived(passed + spread)

    @pl.loop(0, hidden // 256)
    def _(j):
        cols = pl.ds(pl.multiple_of(j * 256, 256), 256)
        u = dot(a2g[...].reshape(span, width), wup[:, :, :, :, cols].reshape(width, 256), NN)
        u = u + vec_o[6:7, cols]
        phi = 0.5 + 0.5 * lax.erf(u * math.sqrt(0.5))
        act[:, cols] = (u * phi).astype(BF)
        slope = phi + u * (jnp.exp(-0.5 * u * u) * (1.0 / math.sqrt(2.0 * math.pi)))
        d_up = (dact[:, cols] * slope).astype(BF)
        dup[:, cols] = d_up
        small_out[3:4, cols] = jnp.sum(d_up.astype(F32), axis=0, keepdims=True)

    c_ff = group(12)
    places = [lax.rem(x + 4 - k, 4) for k in ORDER]
    ring_f = RingSum(c_ff, "x", lambda o, h: part.at[o, pl.ds(2 * h, 2)], ring_tmp.at[1], got)

    @pl.loop(0, 4)
    def _(j):
        cols = pl.ds(pl.multiple_of(j * 512, 512), 512)
        d = dot(dup[...], wup[j].reshape(512, hidden), NT)
        dact[0:blk, cols] = d[:blk]
        for p in (1, 2, 3):
            block = d[p * blk : (p + 1) * blk].astype(BF)
            part[places[p], :, :, cols] = block.reshape(4, blk // 4, 512)

    ring_f.start()

    def grad_down(t, c):
        cols = pl.ds(pl.multiple_of(t * 512 + c * 256, 256), 256)
        return dot(act[:, cols], dyg[...].reshape(span, width), TN)

    def grad_up(t, c):
        cols = pl.ds(pl.multiple_of(t * 512 + c * 256, 256), 256)
        return dot(a2g[:, :, cols].reshape(span, 256), dup[...], TN)

    def swap_down(t):
        return remote(wdn.at[t, other], dn_c.at[t], sems, 16 + t, peer(core=1))

    def swap_up(t):
        return remote(wup.at[t, other], up_c.at[t], sems, 20 + t, peer(core=1))

    c_u.drain()
    pl.semaphore_wait(free_sem, 1)

    @pl.loop(0, 4)
    def _(t):
        wup[t, other] = grad_up(t, other).astype(BF).reshape(4, 64, hidden)
        swap_up(t).start()

    c_ring = group(34)

    def ring_sums(w, tmp_a, tmp_b, got_a, got_b):
        return (
            RingSum(c_ring, "z", lambda o, h: w.at[pl.ds(2 * h, 2), core, o, low], tmp_a, got_a),
            RingSum(c_ring, "y", lambda o, h: w.at[o, core, pl.ds(2 * h, 2), high], tmp_b, got_b),
        )

    up_sums = ring_sums(wup, ring_tmp.at[2], ring_tmp.at[3], up_got.at[0], up_got.at[1])
    down_sums = ring_sums(wdn, ring_tmp.at[4], ring_tmp.at[5], dn_a_got, dn_b_got)

    @pl.loop(0, 4)
    def _(t):
        swap_up(t).wait_recv()
        total = grad_up(t, core) + up_c[t].reshape(256, hidden).astype(F32)
        wup[t, core] = total.astype(BF).reshape(4, 64, hidden)

    for total in up_sums:
        total.start()

    @pl.loop(0, 4)
    def _(j):
        cols = pl.ds(pl.multiple_of(j * 512, 512), 512)
        o = dot(act[...], wdn[:, :, :, :, cols].reshape(hidden, 512), NN)
        dup[:, cols] = o.astype(BF)

    keep_out = pltpu.make_async_copy(dup, outp_hbm, local_sem.at[0])
    keep_out.start()
    ring_f.middle()

    c_d.drain()

    @pl.loop(0, 4)
    def _(t):
        wdn[t, other] = grad_down(t, other).astype(BF).reshape(4, 64, width)
        swap_down(t).start()

    for total in up_sums:
        total.middle()

    @pl.loop(0, 4)
    def _(t):
        swap_down(t).wait_recv()
        total = grad_down(t, core) + dn_c[t].reshape(256, width).astype(F32)
        wdn[t, core] = total.astype(BF).reshape(4, 64, width)

    for total in down_sums:
        total.start()

    ring_f.finish()
    small_out[0:3, :] = jnp.zeros((3, width), F32)
    small_out[4:8, :] = jnp.zeros((4, width), F32)
    gain = vec_o[4:5, :]

    @pl.loop(0, blk // 16)
    def _(i):
        rows = pl.ds(pl.multiple_of(i * 16, 16), 16)
        d = dact[rows, :]
        c, r = i // 2, pl.ds(pl.multiple_of(lax.rem(i, 2) * 16, 16), 16)
        for g in range(2):
            d = d + got[g, c, r, :].astype(F32)
        v = res_o[rows, :]
        centred = v - jnp.mean(v, axis=-1, keepdims=True)
        s = lax.rsqrt(jnp.mean(centred * centred, axis=-1, keepdims=True) + EPSILON)
        n = centred * s
        dn = d * gain
        d_res = s * (
            dn
            - jnp.mean(dn, axis=-1, keepdims=True)
            - n * jnp.mean(dn * n, axis=-1, keepdims=True)
        )
        dy_own = dy_in[rows, :].astype(F32)
        hid = dy_own + d_res
        low_hid = hid.astype(BF)
        dhid_out[rows, :] = hid
        dattn[x, rows, :] = low_hid
        small_out[0:1, :] += jnp.sum(d * n, axis=0, keepdims=True)
        small_out[1:2, :] += jnp.sum(d, axis=0, keepdims=True)
        small_out[2:3, :] += jnp.sum(low_hid.astype(F32), axis=0, keepdims=True)
        small_out[4:5, :] += jnp.sum(dy_own, axis=0, keepdims=True)

    attn = Relay(
        comm, "x", lambda o: dattn.at[o], lambda o, h: dattn.at[o, pl.ds(h * blk // 2, blk // 2)]
    )
    attn.start()
    comm.local(dattn.at[x], dattn_hbm.at[x])
    for total in up_sums:
        total.finish()
    for c in range(4):
        a, b = wup[c, core, z, low].astype(F32), wup[y, core, c, high].astype(F32)
        for g in range(2):
            a, b = a + up_got[0, g, c].astype(F32), b + up_got[1, g, c].astype(F32)
        wup[c, core, z, low], wup[y, core, c, high] = a.astype(BF), b.astype(BF)
    for k in (1, 3, 2):
        ty, tz = lax.rem(y + k, 4), lax.rem(z + k, 4)
        c_ring.push(wup.at[ty, core, z, low], up_two.at[0, k - 1], peer(y=k))
        c_ring.push(wup.at[y, core, tz, high], up_two.at[1, k - 1], peer(z=k))
    c_ring.local(wup.at[y, core, z, low], up_mine.at[0])
    c_ring.local(wup.at[y, core, z, high], up_mine.at[1])
    comm.local(dhid_out, dhid_h)
    kept = [keep_out]
    kept.append(pltpu.make_async_copy(wdn.at[:, core, z, low], dn_a_own, local_sem.at[2]))
    kept.append(pltpu.make_async_copy(wdn.at[y, core, :, high], dn_b_own, local_sem.at[3]))
    for copy in kept[1:]:
        copy.start()
    for total in down_sums:
        total.middle()
    attn.near()
    for k in (1, 3):
        o = lax.rem(x + k, 4)
        comm.local(dattn.at[o], dattn_hbm.at[o])
    attn.far()
    o = lax.rem(x + 2, 4)
    comm.local(dattn.at[o], dattn_hbm.at[o])

    for total in up_sums + down_sums:
        total.finish()

    @pl.loop(0, 4)
    def _(j):
        swap_down(j).wait_send()
        swap_up(j).wait_send()

    for copy in kept:
        copy.wait()
    for done in groups:
        done.drain()


def forward(collective_id, lengths, tok, small, w_up, dy, w_down, w_qkv, w_out):
    blk, width = tok.shape
    span, partw, hidden = 4 * blk, width // 4, w_up.shape[1] // 4
    vmem = pl.BlockSpec(memory_space=pltpu.VMEM)
    hbm = pl.BlockSpec(memory_space=pl.ANY)
    quarter = (4, 32, width)
    outs = [
        ((8, width), F32, vmem),
        ((blk, width), F32, hbm),
        ((blk, width), F32, hbm),
        ((8, width), F32, vmem),
        ((2, 4, 4, 64, 3 * partw), BF, hbm),
        ((2, 4, 4, 16, width), BF, hbm),
        ((span, width), BF, hbm),
        ((span, partw), BF, hbm),
        ((span + W, 2 * partw), BF, hbm),
        ((span, partw), BF, hbm),
        ((4, blk, width), BF, hbm),
        ((span, width), BF, hbm),
    ]
    outs += [((2, 32, width), BF, hbm), ((2, 3, 32, width), BF, hbm)]
    outs += [(quarter, BF, hbm)] * 2 + [((2,) + quarter, BF, hbm)] * 2
    scratch = [
        ((4, 2, 4, 64, hidden), BF),
        ((4, 2, 4, 64, width), BF),
        ((2, 4, 4, 64, width), BF),
        ((2, 4, 4, 16, width), BF),
        ((4, blk, width), BF),
        ((span, hidden), BF),
        ((span, hidden), BF),
        ((span, hidden), F32),
        ((span, partw), BF),
        ((span + W, 2 * partw), BF),
        ((span, partw), BF),
        ((4, blk, width), BF),
        ((4, 4, blk // 4, width), BF),
        ((2, 4, blk // 4, width), BF),
        ((4, blk, width), BF),
        ((4, 2, 128, 128), F32),
        ((hidden // 8, 512), BF),
        ((4, 16, hidden), BF),
        ((6, 2, 2, 32, width), BF),
        ((2, 2) + quarter, BF),
        ((blk, width), F32),
        ((blk, width), F32),
    ]
    return pl.pallas_call(
        forward_body,
        out_shape=tuple(jax.ShapeDtypeStruct(s, d) for s, d, _ in outs),
        in_specs=[pl.BlockSpec(memory_space=pltpu.SMEM)] + [vmem] * 7,
        out_specs=tuple(o[2] for o in outs),
        scratch_shapes=[pltpu.VMEM(s, d) for s, d in scratch]
        + [pltpu.SemaphoreType.DMA((8,)), pltpu.SemaphoreType.REGULAR]
        + [pltpu.SemaphoreType.DMA((n,)) for n in (40, 40, SEMS, SEMS)],
        compiler_params=pltpu.CompilerParams(
            collective_id=collective_id, has_side_effects=True, vmem_limit_bytes=63 << 20
        ),
        name="forward",
    )(lengths, tok, small, w_up, dy, w_down, w_qkv, w_out)


def norm_backward(d, v, gain):
    centred = v - jnp.mean(v, axis=-1, keepdims=True)
    s = lax.rsqrt(jnp.mean(centred * centred, axis=-1, keepdims=True) + EPSILON)
    n = centred * s
    dn = d * gain
    d_v = s * (
        dn - jnp.mean(dn, axis=-1, keepdims=True) - n * jnp.mean(dn * n, axis=-1, keepdims=True)
    )
    return d_v, n


def attention_backward_body(
    lengths,
    vec_in,
    ffsmall_in,
    dattn_hbm,
    wout_hbm,
    q_hbm,
    kv_hbm,
    a1_hbm,
    mixed_hbm,
    wqkv_hbm,
    tok_hbm,
    dhid_hbm,
    res_hbm,
    outp_hbm,
    up_mine,
    up_two,
    ffo2,
    ffo3,
    ffg2,
    ffg3,
    out_h,
    gtok_h,
    gqkv_o,
    gout_o,
    gup_o,
    gdn_o,
    small_o,
    late_o,
    dattn,
    wout,
    q_all,
    kv,
    a1,
    mixed,
    wqkv,
    tok,
    dhid,
    res,
    outown,
    outgot,
    fo,
    fg,
    fs,
    fg2,
    fmine,
    fup,
    fdn,
    dmix,
    dkv,
    dqkv,
    dedge,
    dedge_got,
    part,
    got,
    qkv_c,
    out_c,
    qa,
    qb,
    oa,
    ob,
    qs,
    os_,
    qa2,
    qb2,
    oa2,
    ob2,
    fq,
    fout,
    sm,
    smc,
    smz,
    smy,
    late,
    late_c,
    late_p,
    late_sum,
    gux,
    stack,
    gq,
    part_tmp,
    q_tmp,
    o_tmp,
    out_o,
    gtok_o,
    local_sem,
    send_sem,
    recv_sem,
    comm_send,
    comm_recv,
):
    sems = (send_sem, recv_sem)
    comm = Comm(comm_send, comm_recv, 0, 32)
    me = coords()
    x, y, z, core = me["x"], me["y"], me["z"], me["core"]
    other = 1 - core
    zy = lax.rem(y + 3, 4)
    blk, width = tok.shape
    span = 4 * blk
    partw = mixed.shape[1]
    heads = partw // HEAD
    scale = 1.0 / math.sqrt(HEAD)
    reach = W + blk
    used = [0]
    pending = []

    def load(src, dst):
        copy = pltpu.make_async_copy(src, dst, local_sem.at[used[0]])
        used[0] += 1
        copy.start()
        return copy

    def push(src, dst, index, to):
        copy = remote(src, dst, sems, index, to)
        copy.start()
        pending.append(copy)
        return copy

    l_dattn, l_wout = load(dattn_hbm, dattn), load(wout_hbm, wout)
    l_attn = [load(q_hbm, q_all), load(kv_hbm, kv)]
    low, high = slice(0, 32), slice(32, 64)
    l_ff = [load(s, fo.at[i]) for i, s in enumerate((ffo2, ffo3))]
    l_ff += [load(s, fg.at[i]) for i, s in enumerate((ffg2, ffg3))]
    l_up = [load(up_two, fg2.at[pl.ds(0, 2)]), load(up_mine, fmine)]
    l_wqkv, l_a1, l_mixed = load(wqkv_hbm, wqkv), load(a1_hbm, a1), load(mixed_hbm, mixed)
    l_end = [load(outp_hbm.at[pl.ds(0, blk)], outown), load(res_hbm, res)]
    l_end += [load(tok_hbm, tok), load(dhid_hbm, dhid)]

    greet(ring("x") + plane() + near() + [scattered(), collected()])

    p_out = [
        push(outp_hbm.at[pl.ds(p * blk, blk)], outgot.at[p - 1], p, peer(x=-ORDER[p])) for p in (1, 2, 3)
    ]

    def ff_sum(i):
        for c in range(4):
            total = fo[i, c].astype(F32) + fg[i, 0, c].astype(F32) + fg[i, 1, c].astype(F32)
            fs[i, c] = total.astype(BF)

    p_ff = []

    def ff_second(i):
        axis, here = ("y", y) if i == 0 else ("z", z)
        for k in (1, 3, 2):
            src = fs.at[i, lax.rem(here + k, 4)]
            p_ff.append(push(src, fg2.at[2 + i, k - 1], 4 + 3 * i + k, peer(**{axis: k})))

    for copy in l_ff:
        copy.wait()
    ff_sum(0)
    ff_sum(1)
    ff_second(0)

    dkv[...] = jnp.zeros(dkv.shape, F32)
    l_dattn.wait()
    l_wout.wait()
    dmix[...] = dot(
        dattn[...].reshape(span, width), wout[...].reshape(partw, width), NT
    ).astype(BF)
    for copy in l_attn:
        copy.wait()

    def block(b):
        rows = pl.ds(pl.multiple_of(b * blk, blk), blk)
        window = pl.ds(pl.multiple_of(b * blk, blk), reach)
        mask = mask_of(lengths, z * span + b * blk, blk, reach)
        for h in range(heads):
            cols = pl.ds(h * HEAD, HEAD)
            vcols = pl.ds(partw + h * HEAD, HEAD)
            q, k, v = q_all[rows, cols], kv[window, cols], kv[window, vcols]
            s = dot(q, k, NT) * scale + mask
            e = jnp.exp(s - jnp.max(s, axis=-1, keepdims=True))
            p = e * (1.0 / jnp.sum(e, axis=-1, keepdims=True))
            do = dmix[rows, cols]
            dp = dot(do, v, NT)
            ds = (p * (dp - jnp.sum(dp * p, axis=-1, keepdims=True))).astype(BF)
            dqkv[rows, cols] = (dot(ds, k, NN) * scale).astype(BF)
            dkv[window, cols] += dot(ds, q, TN) * scale
            dkv[window, vcols] += dot(p.astype(BF), do, TN)

    pl.loop(0, 2)(block)
    dedge[...] = dkv[0:W, :].astype(BF)
    p_edge = push(dedge, dedge_got, 4, peer(z=3))

    ring_d = RingSum(comm, "x", lambda o, h: part.at[o, pl.ds(2 * h, 2)], part_tmp, got)
    qkv_sums = (
        RingSum(comm, "z", lambda o, h: gq.at[pl.ds(2 * h, 2), 0, o, low], q_tmp.at[0], qa),
        RingSum(comm, "y", lambda o, h: gq.at[o, 0, pl.ds(2 * h, 2), high], q_tmp.at[1], qb),
    )
    left, right = slice(0, width // 2), slice(width // 2, width)
    out_sums = (
        RingSum(
            comm, "z", lambda o, h: wout.at[core, pl.ds(2 * h, 2), o, :, left], o_tmp.at[0], oa
        ),
        RingSum(
            comm,
            "y",
            lambda o, h: wout.at[core, lax.rem(o + 3, 4), pl.ds(2 * h, 2), :, right],
            o_tmp.at[1],
            ob,
        ),
    )

    def grad_out(c):
        cols = pl.ds(pl.multiple_of(c * 256, 256), 256)
        return dot(mixed[:, cols], dattn[...].reshape(span, width), TN)

    l_mixed.wait()
    wout[other] = grad_out(other).astype(BF).reshape(4, 4, 16, width)
    p_oc = push(wout.at[other], out_c, 36, peer(core=1))

    pl.loop(2, 4)(block)
    p_oc.wait_recv()

    wout[core] = (
        grad_out(core) + out_c[...].reshape(256, width).astype(F32)
    ).astype(BF).reshape(4, 4, 16, width)
    for total in out_sums:
        total.start()
    p_edge.wait_recv()
    dqkv[0 : span - W, partw:] = dkv[W:span, :].astype(BF)
    dqkv[span - W :, partw:] = (dkv[span:, :] + dedge_got[...].astype(F32)).astype(BF)
    sm[0, 0:5, :] = ffsmall_in[0:5, :]
    sm[0, 5:8, :] = jnp.zeros((3, width), F32)
    sm[0, 7:8, 0 : 3 * partw] = jnp.sum(dqkv[...].astype(F32), axis=0, keepdims=True)
    p_sc = push(sm.at[0], smc, 53, peer(core=1))

    def grad_qkv(t, c):
        cols = pl.ds(pl.multiple_of(t * 512 + c * 256, 256), 256)
        return dot(a1[:, cols], dqkv[...], TN)

    def swap(t):
        return remote(gq.at[t, 1], qkv_c.at[t], sems, 32 + t, peer(core=1))

    l_a1.wait()

    @pl.loop(0, 4)
    def _(t):
        gq[t, 1] = grad_qkv(t, other).astype(BF).reshape(4, 64, 3 * partw)
        swap(t).start()

    @pl.loop(0, 4)
    def _(t):
        swap(t).wait_recv()
        total = grad_qkv(t, core) + qkv_c[t].reshape(256, 3 * partw).astype(F32)
        gq[t, 0] = total.astype(BF).reshape(4, 64, 3 * partw)

    for total in qkv_sums:
        total.start()
    for total in out_sums:
        total.middle()

    l_wqkv.wait()

    @pl.loop(0, 4)
    def _(j):
        cols = pl.ds(pl.multiple_of(j * 512, 512), 512)
        d = dot(dqkv[...], wqkv[:, j].reshape(512, 3 * partw), NT)
        part[:, :, :, cols] = d.astype(BF).reshape(4, 4, blk // 4, 512)

    ring_d.start()
    p_sc.wait_recv()
    sm[1] = sm[0] + smc[...]
    p_sz = [push(sm.at[1], smz.at[k - 1], 59 + k, peer(z=k)) for k in (1, 3, 2)]
    for total in qkv_sums:
        total.middle()
    ff_second(1)
    ring_d.middle()
    for copy in p_sz:
        copy.wait_recv()
    sm[2] = sm[1] + smz[0] + smz[1] + smz[2]
    p_sy = [push(sm.at[2], smy.at[k - 1], 68 + k, peer(y=k)) for k in (1, 3, 2)]

    for copy in l_end:
        copy.wait()
    for copy in p_out:
        copy.wait_recv()

    @pl.loop(0, blk // 16)
    def _(i):
        rows = pl.ds(pl.multiple_of(i * 16, 16), 16)
        total = res[rows, :] + vec_in[7:8, :] + outown[rows, :].astype(F32)
        for g in range(3):
            total = total + outgot[g, rows, :].astype(F32)
        out_o[rows, :] = total.astype(BF)

    kept = [load(out_o, out_h)]

    for total in out_sums:
        total.finish()
    for c in range(4):
        ta, tb = wout[core, c, z, :, left].astype(F32), wout[core, zy, c, :, right].astype(F32)
        for g in range(2):
            ta, tb = ta + oa[g, c].astype(F32), tb + ob[g, c].astype(F32)
        os_[0, c], os_[1, c] = ta.astype(BF), tb.astype(BF)
    p_o2 = []
    for k in (1, 3, 2):
        tz, tyc = lax.rem(z + k, 4), lax.rem(y + k + 3, 4)
        p_o2.append(push(os_.at[0, tyc], oa2.at[k - 1], 62 + k, peer(y=k)))
        p_o2.append(push(os_.at[1, tz], ob2.at[k - 1], 65 + k, peer(z=k)))

    for total in qkv_sums:
        total.finish()
    for c in range(4):
        ta, tb = gq[c, 0, z, low].astype(F32), gq[y, 0, c, high].astype(F32)
        for g in range(2):
            ta, tb = ta + qa[g, c].astype(F32), tb + qb[g, c].astype(F32)
        qs[0, c], qs[1, c] = ta.astype(BF), tb.astype(BF)
    p_q2 = []
    for k in (1, 3, 2):
        tz, ty = lax.rem(z + k, 4), lax.rem(y + k, 4)
        p_q2.append(push(qs.at[0, ty], qa2.at[k - 1], 53 + k, peer(y=k)))
        p_q2.append(push(qs.at[1, tz], qb2.at[k - 1], 56 + k, peer(z=k)))

    late_sum[...] = jnp.zeros(late_sum.shape, F32)

    p_u, p_x = [], []
    for copy in p_sy:
        copy.wait_recv()
    sm[3] = sm[2] + smy[0] + smy[1] + smy[2]
    p_x += [push(sm.at[3], small_o.at[x], 71 + k, peer(x=k)) for k in (1, 3, 2)]
    kept.append(load(sm.at[3], small_o.at[x]))
    ring_d.finish()
    gain = vec_in[0:1, :]

    @pl.loop(0, blk // 16)
    def _(i):
        rows = pl.ds(pl.multiple_of(i * 16, 16), 16)
        c, r = i // 2, pl.ds(pl.multiple_of(lax.rem(i, 2) * 16, 16), 16)
        d = part[x, c, r, :].astype(F32)
        for g in range(2):
            d = d + got[g, c, r, :].astype(F32)
        d_in, n = norm_backward(d, tok[rows, :].astype(F32), gain)
        gtok_o[rows, :] = dhid[rows, :] + d_in
        late_sum[0:1, :] += jnp.sum(d * n, axis=0, keepdims=True)
        late_sum[1:2, :] += jnp.sum(d, axis=0, keepdims=True)

    kept.append(load(gtok_o, gtok_h))
    for i in range(8):
        at = (i % 4) * (width // 4)
        late[0, i : i + 1, :] = late_sum[i // 4 : i // 4 + 1, at : at + width // 4]
    p_lc = push(late.at[0], late_c, 52, peer(core=1))
    p_lc.wait_recv()
    late[1] = late[0] + late_c[...]
    p_lz = [push(late.at[1], late_p.at[i], 98 + i, to) for i, to in enumerate(plane())]

    for copy in p_ff:
        copy.wait_recv()
    for copy in l_up:
        copy.wait()
    for i in range(4):
        total = (fmine[i] if i < 2 else fs[i - 2, (y, z)[i - 2]]).astype(F32)
        for g in range(3):
            total = total + fg2[i, g].astype(F32)
        into, half = (fup, fdn)[i // 2], i % 2
        into[2 * half : 2 * half + 2] = total.astype(BF).reshape(2, 16, width)
    for k in (1, 3, 2):
        p_u.append(push(fup.at[lax.rem(x + k, 4)], gux.at[x], 48 + k, peer(x=k)))
        p_x.append(push(fdn.at[lax.rem(x + k, 4)], gdn_o.at[x], 76 + k, peer(x=k)))
    gux[x] = fup[x]
    kept.append(load(fdn.at[x], gdn_o.at[x]))
    for copy in p_o2:
        copy.wait_recv()
    ta, tb = os_[0, zy].astype(F32), os_[1, z].astype(F32)
    for g in range(3):
        ta, tb = ta + oa2[g].astype(F32), tb + ob2[g].astype(F32)
    fout[:, left], fout[:, right] = ta.astype(BF), tb.astype(BF)
    p_x.append(push(fout, gout_o, 75, collected()))

    for copy in p_q2:
        copy.wait_recv()
    ta, tb = qs[0, y].astype(F32), qs[1, z].astype(F32)
    for g in range(3):
        ta, tb = ta + qa2[g].astype(F32), tb + qb2[g].astype(F32)
    fq[0:2] = ta.astype(BF).reshape(2, 16, 3 * partw)
    fq[2:4] = tb.astype(BF).reshape(2, 16, 3 * partw)
    for g in range(3):
        block_cols, own_cols = pl.ds(g * partw, partw), pl.ds(g * width + x * partw, partw)
        for k in (1, 3, 2):
            src = fq.at[lax.rem(x + k, 4), :, block_cols]
            p_x.append(push(src, gqkv_o.at[:, own_cols], 83 + 3 * g + k - 1, peer(x=k)))
        kept.append(load(fq.at[x, :, block_cols], gqkv_o.at[:, own_cols]))

    for copy in p_lz:
        copy.wait_recv()
    total = late[1]
    for i in range(15):
        total = total + late_p[i]
    late[2] = total
    p_x += [push(late.at[2], late_o.at[x], 79 + k, peer(x=k)) for k in (1, 3, 2)]
    kept.append(load(late.at[2], late_o.at[x]))

    for copy in p_u:
        copy.wait_recv()
    slabs = width // 128
    for i in range(slabs):
        for c in range(4):
            stack[16 * i : 16 * i + 16, 128 * c : 128 * c + 128] = gux[
                c, :, 128 * i : 128 * i + 128
            ]
    spread_up = dot(stack[...], shuffle(), NT)
    for i in range(slabs):
        gup_o[:, 512 * i : 512 * i + 512] = spread_up[16 * i : 16 * i + 16, :]

    for copy in p_x:
        copy.wait_recv()
    for copy in pending:
        copy.wait_send()

    @pl.loop(0, 4)
    def _(j):
        swap(j).wait_send()

    comm.drain()

    for copy in kept:
        copy.wait()


def attention_backward(
    collective_id,
    lengths,
    vectors,
    ff_small,
    d_attn,
    wout,
    q,
    kv,
    a1,
    mixed,
    wqkv,
    tok,
    d_hidden,
    residual,
    out_part,
    up_mine,
    up_two,
    ff_own,
    ff_got,
):
    blk, width = tok.shape
    span, partw = mixed.shape
    hidden = ff_own[0].shape[-1]
    vmem = pl.BlockSpec(memory_space=pltpu.VMEM)
    hbm = pl.BlockSpec(memory_space=pl.ANY)
    outs = [
        ((blk, width), BF, hbm),
        ((blk, width), F32, hbm),
        ((16, 3 * width), BF, hbm),
        ((16, width), BF, hbm),
        ((16, 4 * hidden), F32, vmem),
        ((4, 16, width), BF, hbm),
        ((4, 8, width), F32, hbm),
        ((4, 8, width // 4), F32, hbm),
    ]
    half = width // 2
    scratch = [
        ((4, blk, width), BF),
        ((2, 4, 4, 16, width), BF),
        ((span, partw), BF),
        ((span + W, 2 * partw), BF),
        ((span, width), BF),
        ((span, partw), BF),
        ((2, 4, 4, 64, 3 * partw), BF),
        ((blk, width), BF),
        ((blk, width), F32),
        ((blk, width), F32),
        ((blk, width), BF),
        ((3, blk, width), BF),
        ((2, 4, 32, width), BF),
        ((2, 2, 4, 32, width), BF),
        ((2, 4, 32, width), BF),
        ((4, 3, 32, width), BF),
        ((2, 32, width), BF),
        ((4, 16, hidden), BF),
        ((4, 16, width), BF),
        ((span, partw), BF),
        ((span + W, 2 * partw), F32),
        ((span, 3 * partw), BF),
        ((W, 2 * partw), BF),
        ((W, 2 * partw), BF),
        ((4, 4, blk // 4, width), BF),
        ((2, 4, blk // 4, width), BF),
        ((4, 4, 64, 3 * partw), BF),
        ((4, 4, 16, width), BF),
        ((2, 4, 32, 3 * partw), BF),
        ((2, 4, 32, 3 * partw), BF),
        ((2, 4, 16, half), BF),
        ((2, 4, 16, half), BF),
        ((2, 4, 32, 3 * partw), BF),
        ((2, 4, 16, half), BF),
        ((3, 32, 3 * partw), BF),
        ((3, 32, 3 * partw), BF),
        ((3, 16, half), BF),
        ((3, 16, half), BF),
        ((4, 16, 3 * partw), BF),
        ((16, width), BF),
        ((4, 8, width), F32),
        ((8, width), F32),
        ((3, 8, width), F32),
        ((3, 8, width), F32),
        ((3, 8, width // 4), F32),
        ((8, width // 4), F32),
        ((15, 8, width // 4), F32),
        ((2, width), F32),
        ((4, 16, hidden), BF),
        ((hidden // 8, 512), BF),
        ((4, 2, 4, 64, 3 * partw), BF),
        ((2, 2, blk // 4, width), BF),
        ((2, 2, 2, 32, 3 * partw), BF),
        ((2, 2, 2, 16, half), BF),
        ((blk, width), BF),
        ((blk, width), F32),
    ]
    return pl.pallas_call(
        attention_backward_body,
        out_shape=tuple(jax.ShapeDtypeStruct(s, d) for s, d, _ in outs),
        in_specs=[pl.BlockSpec(memory_space=pltpu.SMEM)] + [vmem] * 2 + [hbm] * 17,
        out_specs=tuple(o[2] for o in outs),
        scratch_shapes=[pltpu.VMEM(s, d) for s, d in scratch]
        + [
            pltpu.SemaphoreType.DMA((32,)),
            pltpu.SemaphoreType.DMA((114,)),
            pltpu.SemaphoreType.DMA((114,)),
            pltpu.SemaphoreType.DMA((32,)),
            pltpu.SemaphoreType.DMA((32,)),
        ],
        compiler_params=pltpu.CompilerParams(
            collective_id=collective_id, has_side_effects=True, vmem_limit_bytes=62 << 20
        ),
        name="attention_backward",
    )(
        lengths,
        vectors,
        ff_small,
        d_attn,
        wout,
        q,
        kv,
        a1,
        mixed,
        wqkv,
        tok,
        d_hidden,
        residual,
        out_part,
        up_mine,
        up_two,
        *ff_own,
        *ff_got,
    )


def results_body(
    out,
    gtok,
    gqkv,
    gout,
    gup,
    gdn,
    small,
    late,
    out_o,
    gtok_o,
    gain1_o,
    shift1_o,
    gqkv_o,
    bqv_o,
    gout_o,
    bout_o,
    gain2_o,
    shift2_o,
    gup_o,
    bup_o,
    gdn_o,
    bdown_o,
    sums,
):
    me = coords()
    device = ((me["y"] * 2 + me["core"]) * 4 + me["z"]) * 4 + me["x"]
    out_o[...] = out[...]
    gtok_o[...] = gtok[...]
    gqkv_o[...] = gqkv[...].astype(F32)
    gout_o[...] = gout[...].astype(F32)
    gup_o[...] = gup[...]
    gdn_o[...] = gdn[...].reshape(gdn_o.shape).astype(F32)

    tile = pl.ds(pl.multiple_of(device // 8 * 128, 128), 128)
    turn = lax.rem(128 - 16 * lax.rem(device, 8), 128)
    shares = [pltpu.roll(small[i, :, tile], turn, 1) for i in range(4)]
    total = shares[0] + shares[1] + shares[2] + shares[3]
    gain2_o[...] = total[0:1, 0:16]
    shift2_o[...] = total[1:2, 0:16]
    bout_o[...] = total[2:3, 0:16]
    bdown_o[...] = total[4:5, 0:16]
    for i in range(4):
        bup_o[:, 16 * i : 16 * i + 16] = shares[i][3:4, 0:16]

    sums[...] = late[0] + late[1] + late[2] + late[3]
    place = lax.rem(device, 32)
    tile = pl.ds(pl.multiple_of(place // 8 * 128, 128), 128)
    turned = pltpu.roll(sums[:, tile], turn, 1)
    row = lax.broadcasted_iota(jnp.int32, turned.shape, 0)

    def only(i):
        return jnp.sum(jnp.where(row == i, turned, 0.0), axis=0, keepdims=True)[:, 0:16]

    gain1_o[...] = only(device // 32)
    shift1_o[...] = only(4 + device // 32)

    half, place = device // 64, lax.rem(device, 16)
    tile = pl.ds(pl.multiple_of(half * 1024 + place // 4 * 128, 128), 128)
    turn = lax.rem(128 - 32 * lax.rem(device, 4), 128)
    bqv_o[...] = pltpu.roll(small[lax.rem(device, 64) // 16, :, tile], turn, 1)[7:8, 0:32]


def results(*arrays):
    out, gtok, gqkv, gout, gup, gdn = arrays[:6]
    vmem = pl.BlockSpec(memory_space=pltpu.VMEM)
    rows, vector = gdn.shape[0] * gdn.shape[1], lambda n: ((1, n), F32)
    outs = [
        (out.shape, BF),
        (gtok.shape, F32),
        vector(16),
        vector(16),
        (gqkv.shape, F32),
        vector(32),
        (gout.shape, F32),
        vector(16),
        vector(16),
        vector(16),
        (gup.shape, F32),
        vector(64),
        ((rows, gdn.shape[2]), F32),
        vector(16),
    ]
    return pl.pallas_call(
        results_body,
        out_shape=tuple(jax.ShapeDtypeStruct(s, d) for s, d in outs),
        in_specs=[vmem] * 8,
        out_specs=(vmem,) * 14,
        scratch_shapes=[pltpu.VMEM(arrays[7].shape[1:], F32)],
        compiler_params=pltpu.CompilerParams(vmem_limit_bytes=40 << 20),
        name="results",
    )(*arrays)


def local(
    tokens,
    grad_out,
    lengths,
    ln1_gain,
    ln1_bias,
    w_qkv,
    b_qv,
    w_out,
    b_out,
    ln2_gain,
    ln2_bias,
    w_up,
    b_up,
    w_down,
    b_down,
):
    blk, width = tokens.shape[1:]
    part = width // 4
    hidden = w_up.shape[1] // 4
    tok = tokens.reshape(blk, width)
    dy = grad_out.reshape(blk, width)
    small = jnp.zeros((1024,), F32)
    vectors = (ln1_gain, ln1_bias, b_qv, b_out, ln2_gain, ln2_bias, b_up, b_down)
    for i, vector in enumerate(vectors):
        size = vector.shape[0]
        small = small + jnp.pad(vector.astype(F32), (i * 128, 1024 - i * 128 - size))
    (
        vectors,
        residual,
        d_hidden,
        ff_small,
        wqkv_g,
        wout_g,
        a1,
        query,
        kv,
        mixed,
        d_attn_g,
        out_part,
        up_mine,
        up_two,
        down_a_own,
        down_b_own,
        down_a_got,
        down_b_got,
    ) = forward(0, lengths, tok, small.reshape(8, 128), w_up, dy, w_down, w_qkv, w_out)
    last = attention_backward(
        1,
        lengths,
        vectors,
        ff_small,
        d_attn_g,
        wout_g,
        query,
        kv,
        a1,
        mixed,
        wqkv_g,
        tok,
        d_hidden,
        residual,
        out_part,
        up_mine,
        up_two,
        (down_a_own, down_b_own),
        (down_a_got, down_b_got),
    )

    final = list(results(*last))
    final[0] = final[0].reshape(1, blk, width)
    final[1] = final[1].reshape(1, blk, width)
    for i in (2, 3, 5, 7, 8, 9, 11, 13):
        final[i] = final[i].reshape(-1)
    return tuple(final)


def solution(mesh):
    fine = Mesh(mesh.devices.reshape(4, 2, 4, 4), AXES)
    rows, seq = ("y", "core"), ("z", "x")
    every = rows + seq
    token = P(rows, seq, None)
    vec, mat = P(every), P(every, None)
    in_specs = (token, token, P(rows, None), vec, vec, mat, vec, mat, vec, vec, vec, mat, vec, mat, vec)
    out_specs = (token, token, vec, vec, mat, vec, mat, vec, vec, vec, mat, vec, mat, vec)
    return jax.shard_map(local, mesh=fine, in_specs=in_specs, out_specs=out_specs, check_vma=False)
```

```python
import functools
import math

import jax
import jax.numpy as jnp
from jax import lax
from jax.experimental import pallas as pl
from jax.experimental.pallas import tpu as pltpu
from jax.sharding import Mesh, PartitionSpec as P

HEADS = 16
HEAD = 128
W = 256
EPSILON = 1e-05
NEG_FILL = -1e30

AXES = ("y", "core", "z", "x")
SIZE = {"y": 4, "core": 2, "z": 4, "x": 4}
BF = jnp.bfloat16
F32 = jnp.float32
SEMS = 264


def coords():
    return {a: lax.axis_index(a) for a in AXES}


def peer(**delta):
    me = coords()
    return tuple(lax.rem(me[a] + delta.get(a, 0) % SIZE[a], SIZE[a]) for a in AXES)


class Comm:
    def __init__(self, send_sem, recv_sem, base=0, room=SEMS):
        self.send_sem, self.recv_sem = send_sem, recv_sem
        self.count, self.last, self.open = base, base + room, []

    def push(self, src, dst, to):
        entry = self.plan(src, dst, to)
        entry[0].start()
        return entry

    def plan(self, src, dst, to):
        copy = pltpu.make_async_remote_copy(
            src_ref=src,
            dst_ref=dst,
            send_sem=self.send_sem.at[self.count],
            recv_sem=self.recv_sem.at[self.count],
            device_id=to,
            device_id_type=pl.DeviceIdType.MESH,
        )
        assert self.count < self.last
        self.count += 1
        self.open.append([copy, True, True])
        return self.open[-1]

    def local(self, src, dst):
        copy = pltpu.make_async_copy(src, dst, self.send_sem.at[self.count])
        self.count += 1
        copy.start()
        self.open.append([copy, False, True])
        return self.open[-1]

    def arrived(self, entries):
        for entry in entries:
            if entry[2]:
                if entry[1]:
                    entry[0].wait_recv()
                else:
                    entry[0].wait()
                entry[2] = False

    def drain(self):
        self.arrived(self.open)
        for copy, remote_copy, _ in self.open:
            if remote_copy:
                copy.wait_send()
        self.open = []


def greet(devices):
    barrier = pltpu.get_barrier_semaphore()
    for device in devices:
        pl.semaphore_signal(barrier, inc=1, device_id=device, device_id_type=pl.DeviceIdType.MESH)
    pl.semaphore_wait(barrier, len(devices))


def ring(axis):
    return [peer(**{axis: k}) for k in (1, 3, 2)]


def near():
    return [peer(core=1)]


def plane():
    return [peer(y=i // 4, z=i % 4) for i in range(1, 16)]


def everyone():
    return ring("x") + ring("y") + ring("z") + near()


def scattered():
    me = coords()
    return (lax.rem(me["z"] + 1, 4), me["core"], me["x"], me["y"])


def collected():
    me = coords()
    return (me["x"], me["core"], lax.rem(me["y"] + 3, 4), me["z"])


class Relay:
    def __init__(self, comm, axis, full, half):
        self.comm, self.axis, self.full, self.half = comm, axis, full, half
        self.me = lax.axis_index(axis)

    def to(self, k):
        return peer(**{self.axis: k})

    def start(self):
        a, b = self.half(self.me, 0), self.half(self.me, 1)
        self.sent = [self.comm.push(a, a, self.to(1)), self.comm.push(b, b, self.to(3))]
        self.rest = [self.comm.push(b, b, self.to(1)), self.comm.push(a, a, self.to(3))]

    def near(self):
        self.comm.arrived(self.sent)
        before, after = lax.rem(self.me + 3, 4), lax.rem(self.me + 1, 4)
        up, down = self.half(before, 0), self.half(after, 1)
        self.passed = [self.comm.push(up, up, self.to(1)), self.comm.push(down, down, self.to(3))]
        self.comm.arrived(self.rest)

    def far(self):
        self.comm.arrived(self.passed)


class RingSum:
    def __init__(self, comm, axis, ref, tmp, got):
        self.comm, self.axis, self.ref, self.tmp, self.got = comm, axis, ref, tmp, got
        self.me = lax.axis_index(axis)

    def at(self, k):
        return lax.rem(self.me + k, 4)

    def push(self, src, dst, k):
        return self.comm.push(src, dst, peer(**{self.axis: k}))

    def plan(self, src, dst, k):
        return self.comm.plan(src, dst, peer(**{self.axis: k}))

    def prepare(self):
        self.up = self.plan(self.ref(self.at(2), 0), self.tmp.at[0], 1)
        self.down = self.plan(self.ref(self.at(2), 1), self.tmp.at[1], 3)
        self.end = [
            self.plan(self.ref(self.at(1), 1), self.got.at[0, pl.ds(2, 2)], 1),
            self.plan(self.ref(self.at(3), 0), self.got.at[1, pl.ds(0, 2)], 3),
        ]
        self.first = {1: [self.end[0]], 2: [self.up, self.down], 3: [self.end[1]]}

    def start(self):
        self.prepare()
        for k in (2, 1, 3):
            for entry in self.first[k]:
                entry[0].start()

    def start_block(self, to):
        for k in (2, 1, 3):

            @pl.when(self.at(k) == to)
            def _():
                for entry in self.first[k]:
                    entry[0].start()

    def middle(self):
        for arrived, k, h, back in ((self.up, 1, 0, 0), (self.down, 3, 1, 2)):
            self.comm.arrived([arrived])
            block = self.ref(self.at(k), h)
            for c in range(2):
                total = block[c].astype(F32) + self.tmp[h, c].astype(F32)
                block[c] = total.astype(BF)
            self.end.append(self.push(block, self.got.at[h, pl.ds(back, 2)], k))

    def finish(self):
        self.comm.arrived(self.end)


class Gather:
    def __init__(self, comm, w, by_core, cut, shift=0):
        self.comm, self.w, self.by_core, self.cut = comm, w, by_core, cut
        self.shift = shift
        me = coords()
        self.y, self.core, self.z = me["y"], me["core"], me["z"]

    def slot(self, y, z, cut):
        place = (self.core, y, z) if self.by_core else (y, self.core, z)
        return self.w.at[place + self.cut[cut]]

    def row(self, y):
        return lax.rem(y + self.shift, 4)

    def first(self):
        self.first_a()
        self.first_b()
        self.one = self.one_a + self.one_b

    def first_a(self):
        a = self.slot(self.row(self.y), self.z, 0)
        self.one_a = [self.comm.push(a, a, to) for to in ring("z")]

    def first_b(self):
        b = self.slot(self.row(self.y), self.z, 1)
        self.one_b = [self.comm.push(b, b, to) for to in ring("y")]

    def second(self):
        self.second_a()
        self.second_b()

    def second_a(self):
        every = slice(None)
        self.a = Relay(
            self.comm,
            "y",
            lambda o: self.slot(self.row(o), every, 0),
            lambda o, h: self.slot(self.row(o), pl.ds(2 * h, 2), 0),
        )
        self.a.start()

    def second_b(self):
        every = slice(None)
        self.b = Relay(
            self.comm,
            "z",
            lambda o: self.slot(every, o, 1),
            lambda o, h: self.slot(pl.ds(2 * h, 2), o, 1),
        )
        self.b.start()

    def across(self, relay, k):
        block = relay.full(lax.rem(relay.me + k, 4))
        self.two.append(self.comm.push(block, block, peer(core=1)))

    def near_a(self):
        self.two = []
        self.a.near()
        for k in (0, 1, 3):
            self.across(self.a, k)

    def near_b(self):
        self.b.near()
        for k in (0, 1, 3):
            self.across(self.b, k)

    def near(self):
        self.near_a()
        self.near_b()

    def far_a(self):
        self.a.far()
        self.across(self.a, 2)

    def far_b(self):
        self.b.far()
        self.across(self.b, 2)

    def far(self):
        self.far_a()
        self.far_b()

    def done(self):
        self.comm.arrived(self.two)


def by_rows(rows):
    return [(slice(0, rows // 2),), (slice(rows // 2, rows),)]


def by_columns(columns):
    every = slice(None)
    return [(every, slice(0, columns // 2)), (every, slice(columns // 2, columns))]


def dot(a, b, dims):
    return lax.dot_general(a, b, (dims, ((), ())), preferred_element_type=F32)


NN = ((1,), (0,))
NT = ((1,), (1,))
TN = ((0,), (0,))


def mask_of(lengths, first, blk, reach):
    q = first + lax.broadcasted_iota(jnp.int32, (blk, reach), 0)
    k = first - W + lax.broadcasted_iota(jnp.int32, (blk, reach), 1)
    q_doc, k_doc = jnp.zeros((blk, reach), jnp.int32), jnp.zeros((blk, reach), jnp.int32)
    end = 0
    for i in range(lengths.shape[1]):
        end = end + lengths[0, i]
        q_doc = q_doc + jnp.where(q >= end, 1, 0)
        k_doc = k_doc + jnp.where(k >= end, 1, 0)
    seen = (q_doc == k_doc) & (k <= q) & (q - k < W) & (k >= 0)
    return jnp.where(seen, 0.0, NEG_FILL).astype(F32)


def shuffle():
    row = lax.broadcasted_iota(jnp.int32, (512, 512), 0)
    column = lax.broadcasted_iota(jnp.int32, (512, 512), 1)
    source = 64 * ((column >> 4) & 7) + 16 * (column >> 7) + (column & 15)
    return jnp.where(source == row, 1.0, 0.0).astype(BF)


def whole_vector(table, index, offset, count, size, lane):
    shift = size.bit_length() - 1
    row = lax.broadcasted_iota(jnp.int32, (128, 1024), 0)
    tile = lax.broadcasted_iota(jnp.int32, (128, 1024), 1)
    chosen = jnp.where(tile == row * 8 + index, 1.0, 0.0).astype(BF)
    share = dot(chosen, table, NN).astype(BF)
    row = lax.broadcasted_iota(jnp.int32, (128, count), 0)
    column = lax.broadcasted_iota(jnp.int32, (128, count), 1) + offset
    spread = jnp.where((column & (size - 1)) + lane == row, 1.0, 0.0).astype(BF)
    values = jnp.where((column >> shift) == row, dot(share, spread, NN), 0.0)
    return jnp.sum(values, axis=0, keepdims=True)


ORDER = (0, 1, 3, 2)


def remote(src, dst, sems, index, to):
    send, recv = sems
    return pltpu.make_async_remote_copy(
        src_ref=src,
        dst_ref=dst,
        send_sem=send.at[index],
        recv_sem=recv.at[index],
        device_id=to,
        device_id_type=pl.DeviceIdType.MESH,
    )


def forward_body(
    lengths,
    tok_in,
    small_in,
    wup_in,
    dy_in,
    wdn_in,
    wqkv_in,
    wout_in,
    vec_o,
    res_h,
    dhid_h,
    small_out,
    wq_h,
    wo_h,
    a1_h,
    q_h,
    kv_h,
    mixed_h,
    dattn_hbm,
    outp_hbm,
    up_mine,
    up_two,
    dn_a_own,
    dn_b_own,
    dn_a_got,
    dn_b_got,
    wup,
    wdn,
    cc,
    wo,
    tokg,
    act,
    dup,
    dact,
    q,
    kv,
    mixed,
    dyg,
    part,
    got,
    dattn,
    smalls,
    stack,
    uparts,
    ring_tmp,
    up_got,
    res_o,
    dhid_out,
    local_sem,
    free_sem,
    ff_send,
    ff_recv,
    send_sem,
    recv_sem,
):
    groups, taken = [], [0]

    def group(room):
        comm = Comm(send_sem, recv_sem, taken[0], room)
        taken[0] += room
        groups.append(comm)
        return comm

    c_q, c_o, c_u, c_d = group(40), group(30), group(30), group(30)
    c_small, c_tok, comm = group(28), group(6), group(40)
    sems = (ff_send, ff_recv)
    me = coords()
    x, y, z, core = me["x"], me["y"], me["z"], me["core"]
    other = 1 - core
    blk, width = tok_in.shape
    span = 4 * blk
    partw = q.shape[1]
    hidden = act.shape[1]
    heads = partw // HEAD
    reach = W + blk
    scale = 1.0 / math.sqrt(HEAD)
    mine16 = pl.ds(x * 16, 16)
    low, high = slice(0, 32), slice(32, 64)
    a1, up_c, dn_c, a2g = act, cc.at[0], cc.at[1], tokg
    wide = slice(0, 3 * partw)

    greet(ring("x") + plane() + near() + [scattered(), collected()])

    s_q = []
    for k in (1, 3, 2):
        for g in range(3):
            src = wqkv_in.at[:, pl.ds(g * width + lax.rem(x + k, 4) * partw, partw)]
            dst = cc.at[core, y, z, mine16, pl.ds(g * partw, partw)]
            s_q.append(c_q.push(src, dst, peer(x=k)))
    for g in range(3):
        src = wqkv_in.at[:, pl.ds(g * width + x * partw, partw)]
        s_q.append(c_q.local(src, cc.at[core, y, z, mine16, pl.ds(g * partw, partw)]))
    spot = smalls.at[y, core, pl.ds((z * 4 + x) * 8, 8)]
    s_small = [c_small.push(small_in, spot, to) for to in ring("x")]
    s_small.append(c_small.local(small_in, spot))
    s_o = [c_o.push(wout_in, wo.at[core, z, x], scattered())]
    tokens = Relay(
        c_tok, "x", lambda o: tokg.at[o], lambda o, h: tokg.at[o, pl.ds(h * blk // 2, blk // 2)]
    )
    tokg[x] = tok_in[...]
    tokens.start()

    qkv_g = Gather(c_q, cc, True, [cut + (wide,) for cut in by_rows(64)])
    out_g = Gather(c_o, wo, True, by_columns(width), 3)
    down_g = Gather(c_d, wdn, False, by_rows(64))
    up_g = Gather(c_u, wup, False, by_rows(64))

    c_q.arrived(s_q)
    qkv_g.first()
    c_small.arrived(s_small)
    block = smalls.at[y, core, pl.ds(z * 32, 32)]
    s_small = [c_small.push(block, block, to) for to in plane()]

    slabs = 4 * hidden // 512
    for i in range(slabs):
        stack[16 * i : 16 * i + 16, :] = wup_in[:, 512 * i : 512 * i + 512]
    mixed_up = dot(stack[...], shuffle(), NN).astype(BF)
    for i in range(slabs):
        for to in range(4):
            uparts[to, :, 128 * i : 128 * i + 128] = mixed_up[
                16 * i : 16 * i + 16, 128 * to : 128 * to + 128
            ]

    c_q.arrived(qkv_g.one)
    qkv_g.second()
    c_o.arrived(s_o)
    out_g.first()
    c_small.arrived(s_small)
    s_small = []
    for other_y in range(4):
        block = smalls.at[other_y, core]
        s_small.append(c_small.push(block, block, peer(core=1)))
    tokens.near()
    s_u, s_d = [], []
    for k in (1, 3, 2):
        to = lax.rem(x + k, 4)
        s_d.append(
            c_d.push(wdn_in.at[pl.ds(to * 16, 16)], wdn.at[y, core, z, mine16], peer(x=k))
        )
        s_u.append(c_u.push(uparts.at[to], wup.at[y, core, z, mine16], peer(x=k)))
    s_d.append(c_d.local(wdn_in.at[mine16], wdn.at[y, core, z, mine16]))
    s_u.append(c_u.local(uparts.at[x], wup.at[y, core, z, mine16]))
    s_dy = [comm.push(dy_in, dyg.at[p], peer(x=ORDER[p])) for p in (1, 2, 3)]
    dyg[0] = dy_in[...]

    c_small.arrived(s_small)
    table = smalls[...].reshape(1024, 128).astype(BF)
    vec_o[0:1, :] = whole_vector(table, 0, 0, width, 16, 0)
    vec_o[1:2, :] = whole_vector(table, 1, 0, width, 16, 0)
    gain, shift = vec_o[0:1, :], vec_o[1:2, :]

    def norm_block(o):
        @pl.loop(0, blk // 16)
        def _(i):
            rows = pl.ds(pl.multiple_of(i * 16, 16), 16)
            v = tokg[o, rows, :].astype(F32)
            centred = v - jnp.mean(v, axis=-1, keepdims=True)
            s = lax.rsqrt(jnp.mean(centred * centred, axis=-1, keepdims=True) + EPSILON)
            at = pl.ds(pl.multiple_of(o * blk + i * 16, 16), 16)
            a1[at, :] = (centred * s * gain + shift).astype(BF)

    norm_block(x)
    qkv_g.near()
    c_o.arrived(out_g.one)
    out_g.second()
    norm_block(lax.rem(x + 1, 4))
    c_d.arrived(s_d)
    down_g.first()
    norm_block(lax.rem(x + 3, 4))
    qkv_g.far()
    tokens.far()
    norm_block(lax.rem(x + 2, 4))
    out_g.near()
    c_u.arrived(s_u)
    up_g.first_b()
    keep_a1 = [comm.local(a1, a1_h)]
    vec_o[2:3, :] = jnp.zeros((1, width), F32)
    vec_o[2:3, 0:partw] = whole_vector(table, 2, x * partw, partw, 32, 0)
    vec_o[2:3, 2 * partw : 3 * partw] = whole_vector(table, 2, width + x * partw, partw, 32, 0)
    qkv_g.done()

    def project(first):
        cols = slice(first, first + partw)
        total = vec_o[2:3, cols]
        rows = [
            jnp.concatenate([cc[0, j, :, :, cols], cc[1, j, :, :, cols]]).reshape(512, partw)
            for j in range(4)
        ]
        w = jnp.concatenate(rows)
        return (dot(a1[...], w, NN) + total).astype(BF)

    kv[W:, 0:partw] = project(partw)
    kv[W:, partw:] = project(2 * partw)
    s_edge = [comm.push(kv.at[pl.ds(span, W)], kv.at[pl.ds(0, W)], peer(z=1))]
    q[...] = project(0)
    keep_q = [c_q.local(cc.at[:, :, :, :, wide], wq_h)]
    comm.local(q, q_h)

    def attend(b):
        rows = pl.ds(pl.multiple_of(b * blk, blk), blk)
        window = pl.ds(pl.multiple_of(b * blk, blk), reach)
        mask = mask_of(lengths, z * span + b * blk, blk, reach)
        for h in range(heads):
            cols, vcols = pl.ds(h * HEAD, HEAD), pl.ds(partw + h * HEAD, HEAD)
            s = dot(q[rows, cols], kv[window, cols], NT) * scale + mask
            e = jnp.exp(s - jnp.max(s, axis=-1, keepdims=True))
            p = (e * (1.0 / jnp.sum(e, axis=-1, keepdims=True))).astype(BF)
            mixed[rows, cols] = dot(p, kv[window, vcols], NN).astype(BF)

    c_sum = group(8)
    ring_a = RingSum(c_sum, "x", lambda o, h: part.at[o, pl.ds(2 * h, 2)], ring_tmp.at[0], got)
    ring_a.prepare()

    def project_out(o):
        rows = slice(o * blk, (o + 2) * blk)

        @pl.loop(0, 4)
        def _(j):
            cols = pl.ds(pl.multiple_of(j * 512, 512), 512)
            d = dot(mixed[rows, :], wo[:, :, :, :, cols].reshape(partw, 512), NN)
            part[o : o + 2, :, :, cols] = d.astype(BF).reshape(2, 4, blk // 4, 512)
            dact[rows, cols] = d

        for to in (o, o + 1):
            ring_a.start_block(to)

    pl.loop(2, 4)(attend)
    out_g.far()
    out_g.done()
    c_tok.drain()
    project_out(2)
    c_d.arrived(down_g.one)
    down_g.second_a()
    for i in (3, 4, 5, 7):
        vec_o[i : i + 1, :] = whole_vector(table, i, 0, width, 16, 0)
    vec_o[6:7, :] = whole_vector(table, 6, 0, hidden, 16, x * 16)
    comm.arrived(s_edge)
    up_g.first_a()
    down_g.second_b()
    pl.loop(0, 2)(attend)
    project_out(0)
    down_g.near_a()
    c_u.arrived(up_g.one_a + up_g.one_b)
    up_g.second_a()
    comm.local(kv, kv_h)
    comm.local(mixed, mixed_h)
    c_o.local(wo, wo_h)
    c_q.drain()
    pl.semaphore_signal(
        free_sem, inc=1, device_id=peer(core=1), device_id_type=pl.DeviceIdType.MESH
    )
    down_g.near_b()
    up_g.second_b()
    ring_a.middle()
    down_g.far_a()

    ring_a.finish()
    b_out, gain2, shift2 = vec_o[3:4, :], vec_o[4:5, :], vec_o[5:6, :]

    @pl.loop(0, blk // 16)
    def _(i):
        rows = pl.ds(pl.multiple_of(i * 16, 16), 16)
        own_rows = pl.ds(pl.multiple_of(x * blk + i * 16, 16), 16)
        v = tok_in[rows, :].astype(F32) + dact[own_rows, :] + b_out
        c, r = i // 2, pl.ds(pl.multiple_of(lax.rem(i, 2) * 16, 16), 16)
        for g in range(2):
            v = v + got[g, c, r, :].astype(F32)
        res_o[rows, :] = v
        centred = v - jnp.mean(v, axis=-1, keepdims=True)
        s = lax.rsqrt(jnp.mean(centred * centred, axis=-1, keepdims=True) + EPSILON)
        a2g[0, rows, :] = (centred * s * gain2 + shift2).astype(BF)

    top, bottom = pl.ds(0, blk // 2), pl.ds(blk // 2, blk // 2)
    spread = []
    for p, rows in ((1, top), (2, bottom), (1, bottom), (2, top)):
        spread.append(comm.push(a2g.at[0, rows], a2g.at[p, rows], peer(x=ORDER[p])))
    comm.local(res_o, res_h)
    down_g.far_b()
    up_g.near_a()
    c_sum.drain()
    comm.arrived(keep_a1 + s_dy)
    down_g.done()

    @pl.loop(0, 4)
    def _(j):
        tile = wdn[j].reshape(512, width)
        cols = pl.ds(pl.multiple_of(j * 512, 512), 512)
        dact[:, cols] = dot(dyg[...].reshape(span, width), tile, NT)

    comm.arrived(spread[:2])
    passed = [
        comm.push(a2g.at[1, top], a2g.at[3, top], peer(x=1)),
        comm.push(a2g.at[2, bottom], a2g.at[3, bottom], peer(x=3)),
    ]
    up_g.near_b()
    up_g.far_a()
    up_g.far_b()
    up_g.done()
    comm.arrived(passed + spread)

    @pl.loop(0, hidden // 256)
    def _(j):
        cols = pl.ds(pl.multiple_of(j * 256, 256), 256)
        u = dot(a2g[...].reshape(span, width), wup[:, :, :, :, cols].reshape(width, 256), NN)
        u = u + vec_o[6:7, cols]
        phi = 0.5 + 0.5 * lax.erf(u * math.sqrt(0.5))
        act[:, cols] = (u * phi).astype(BF)
        slope = phi + u * (jnp.exp(-0.5 * u * u) * (1.0 / math.sqrt(2.0 * math.pi)))
        d_up = (dact[:, cols] * slope).astype(BF)
        dup[:, cols] = d_up
        small_out[3:4, cols] = jnp.sum(d_up.astype(F32), axis=0, keepdims=True)

    c_ff = group(12)
    places = [lax.rem(x + 4 - k, 4) for k in ORDER]
    ring_f = RingSum(c_ff, "x", lambda o, h: part.at[o, pl.ds(2 * h, 2)], ring_tmp.at[1], got)

    @pl.loop(0, 4)
    def _(j):
        cols = pl.ds(pl.multiple_of(j * 512, 512), 512)
        d = dot(dup[...], wup[j].reshape(512, hidden), NT)
        dact[0:blk, cols] = d[:blk]
        for p in (1, 2, 3):
            block = d[p * blk : (p + 1) * blk].astype(BF)
            part[places[p], :, :, cols] = block.reshape(4, blk // 4, 512)

    ring_f.start()

    def grad_down(t, c):
        cols = pl.ds(pl.multiple_of(t * 512 + c * 256, 256), 256)
        return dot(act[:, cols], dyg[...].reshape(span, width), TN)

    def grad_up(t, c):
        cols = pl.ds(pl.multiple_of(t * 512 + c * 256, 256), 256)
        return dot(a2g[:, :, cols].reshape(span, 256), dup[...], TN)

    def swap_down(t):
        return remote(wdn.at[t, other], dn_c.at[t], sems, 16 + t, peer(core=1))

    def swap_up(t):
        return remote(wup.at[t, other], up_c.at[t], sems, 20 + t, peer(core=1))

    c_u.drain()
    pl.semaphore_wait(free_sem, 1)

    @pl.loop(0, 4)
    def _(t):
        wup[t, other] = grad_up(t, other).astype(BF).reshape(4, 64, hidden)
        swap_up(t).start()

    c_ring = group(34)

    def ring_sums(w, tmp_a, tmp_b, got_a, got_b):
        return (
            RingSum(c_ring, "z", lambda o, h: w.at[pl.ds(2 * h, 2), core, o, low], tmp_a, got_a),
            RingSum(c_ring, "y", lambda o, h: w.at[o, core, pl.ds(2 * h, 2), high], tmp_b, got_b),
        )

    up_sums = ring_sums(wup, ring_tmp.at[2], ring_tmp.at[3], up_got.at[0], up_got.at[1])
    down_sums = ring_sums(wdn, ring_tmp.at[4], ring_tmp.at[5], dn_a_got, dn_b_got)

    @pl.loop(0, 4)
    def _(t):
        swap_up(t).wait_recv()
        total = grad_up(t, core) + up_c[t].reshape(256, hidden).astype(F32)
        wup[t, core] = total.astype(BF).reshape(4, 64, hidden)

    for total in up_sums:
        total.start()

    @pl.loop(0, 4)
    def _(j):
        cols = pl.ds(pl.multiple_of(j * 512, 512), 512)
        o = dot(act[...], wdn[:, :, :, :, cols].reshape(hidden, 512), NN)
        dup[:, cols] = o.astype(BF)

    keep_out = pltpu.make_async_copy(dup, outp_hbm, local_sem.at[0])
    keep_out.start()
    ring_f.middle()

    c_d.drain()

    @pl.loop(0, 4)
    def _(t):
        wdn[t, other] = grad_down(t, other).astype(BF).reshape(4, 64, width)
        swap_down(t).start()

    for total in up_sums:
        total.middle()

    @pl.loop(0, 4)
    def _(t):
        swap_down(t).wait_recv()
        total = grad_down(t, core) + dn_c[t].reshape(256, width).astype(F32)
        wdn[t, core] = total.astype(BF).reshape(4, 64, width)

    for total in down_sums:
        total.start()

    ring_f.finish()
    small_out[0:3, :] = jnp.zeros((3, width), F32)
    small_out[4:8, :] = jnp.zeros((4, width), F32)
    gain = vec_o[4:5, :]

    @pl.loop(0, blk // 16)
    def _(i):
        rows = pl.ds(pl.multiple_of(i * 16, 16), 16)
        d = dact[rows, :]
        c, r = i // 2, pl.ds(pl.multiple_of(lax.rem(i, 2) * 16, 16), 16)
        for g in range(2):
            d = d + got[g, c, r, :].astype(F32)
        v = res_o[rows, :]
        centred = v - jnp.mean(v, axis=-1, keepdims=True)
        s = lax.rsqrt(jnp.mean(centred * centred, axis=-1, keepdims=True) + EPSILON)
        n = centred * s
        dn = d * gain
        d_res = s * (
            dn
            - jnp.mean(dn, axis=-1, keepdims=True)
            - n * jnp.mean(dn * n, axis=-1, keepdims=True)
        )
        dy_own = dy_in[rows, :].astype(F32)
        hid = dy_own + d_res
        low_hid = hid.astype(BF)
        dhid_out[rows, :] = hid
        dattn[x, rows, :] = low_hid
        small_out[0:1, :] += jnp.sum(d * n, axis=0, keepdims=True)
        small_out[1:2, :] += jnp.sum(d, axis=0, keepdims=True)
        small_out[2:3, :] += jnp.sum(low_hid.astype(F32), axis=0, keepdims=True)
        small_out[4:5, :] += jnp.sum(dy_own, axis=0, keepdims=True)

    attn = Relay(
        comm, "x", lambda o: dattn.at[o], lambda o, h: dattn.at[o, pl.ds(h * blk // 2, blk // 2)]
    )
    attn.start()
    comm.local(dattn.at[x], dattn_hbm.at[x])
    for total in up_sums:
        total.finish()
    for c in range(4):
        a, b = wup[c, core, z, low].astype(F32), wup[y, core, c, high].astype(F32)
        for g in range(2):
            a, b = a + up_got[0, g, c].astype(F32), b + up_got[1, g, c].astype(F32)
        wup[c, core, z, low], wup[y, core, c, high] = a.astype(BF), b.astype(BF)
    for k in (1, 3, 2):
        ty, tz = lax.rem(y + k, 4), lax.rem(z + k, 4)
        c_ring.push(wup.at[ty, core, z, low], up_two.at[0, k - 1], peer(y=k))
        c_ring.push(wup.at[y, core, tz, high], up_two.at[1, k - 1], peer(z=k))
    c_ring.local(wup.at[y, core, z, low], up_mine.at[0])
    c_ring.local(wup.at[y, core, z, high], up_mine.at[1])
    comm.local(dhid_out, dhid_h)
    kept = [keep_out]
    kept.append(pltpu.make_async_copy(wdn.at[:, core, z, low], dn_a_own, local_sem.at[2]))
    kept.append(pltpu.make_async_copy(wdn.at[y, core, :, high], dn_b_own, local_sem.at[3]))
    for copy in kept[1:]:
        copy.start()
    for total in down_sums:
        total.middle()
    attn.near()
    for k in (1, 3):
        o = lax.rem(x + k, 4)
        comm.local(dattn.at[o], dattn_hbm.at[o])
    attn.far()
    o = lax.rem(x + 2, 4)
    comm.local(dattn.at[o], dattn_hbm.at[o])

    for total in up_sums + down_sums:
        total.finish()

    @pl.loop(0, 4)
    def _(j):
        swap_down(j).wait_send()
        swap_up(j).wait_send()

    for copy in kept:
        copy.wait()
    for done in groups:
        done.drain()


def forward(collective_id, lengths, tok, small, w_up, dy, w_down, w_qkv, w_out):
    blk, width = tok.shape
    span, partw, hidden = 4 * blk, width // 4, w_up.shape[1] // 4
    vmem = pl.BlockSpec(memory_space=pltpu.VMEM)
    hbm = pl.BlockSpec(memory_space=pl.ANY)
    quarter = (4, 32, width)
    outs = [
        ((8, width), F32, vmem),
        ((blk, width), F32, hbm),
        ((blk, width), F32, hbm),
        ((8, width), F32, vmem),
        ((2, 4, 4, 64, 3 * partw), BF, hbm),
        ((2, 4, 4, 16, width), BF, hbm),
        ((span, width), BF, hbm),
        ((span, partw), BF, hbm),
        ((span + W, 2 * partw), BF, hbm),
        ((span, partw), BF, hbm),
        ((4, blk, width), BF, hbm),
        ((span, width), BF, hbm),
    ]
    outs += [((2, 32, width), BF, hbm), ((2, 3, 32, width), BF, hbm)]
    outs += [(quarter, BF, hbm)] * 2 + [((2,) + quarter, BF, hbm)] * 2
    scratch = [
        ((4, 2, 4, 64, hidden), BF),
        ((4, 2, 4, 64, width), BF),
        ((2, 4, 4, 64, width), BF),
        ((2, 4, 4, 16, width), BF),
        ((4, blk, width), BF),
        ((span, hidden), BF),
        ((span, hidden), BF),
        ((span, hidden), F32),
        ((span, partw), BF),
        ((span + W, 2 * partw), BF),
        ((span, partw), BF),
        ((4, blk, width), BF),
        ((4, 4, blk // 4, width), BF),
        ((2, 4, blk // 4, width), BF),
        ((4, blk, width), BF),
        ((4, 2, 128, 128), F32),
        ((hidden // 8, 512), BF),
        ((4, 16, hidden), BF),
        ((6, 2, 2, 32, width), BF),
        ((2, 2) + quarter, BF),
        ((blk, width), F32),
        ((blk, width), F32),
    ]
    return pl.pallas_call(
        forward_body,
        out_shape=tuple(jax.ShapeDtypeStruct(s, d) for s, d, _ in outs),
        in_specs=[pl.BlockSpec(memory_space=pltpu.SMEM)] + [vmem] * 7,
        out_specs=tuple(o[2] for o in outs),
        scratch_shapes=[pltpu.VMEM(s, d) for s, d in scratch]
        + [pltpu.SemaphoreType.DMA((8,)), pltpu.SemaphoreType.REGULAR]
        + [pltpu.SemaphoreType.DMA((n,)) for n in (40, 40, SEMS, SEMS)],
        compiler_params=pltpu.CompilerParams(
            collective_id=collective_id, has_side_effects=True, vmem_limit_bytes=63 << 20
        ),
        name="forward",
    )(lengths, tok, small, w_up, dy, w_down, w_qkv, w_out)


def norm_backward(d, v, gain):
    centred = v - jnp.mean(v, axis=-1, keepdims=True)
    s = lax.rsqrt(jnp.mean(centred * centred, axis=-1, keepdims=True) + EPSILON)
    n = centred * s
    dn = d * gain
    d_v = s * (
        dn - jnp.mean(dn, axis=-1, keepdims=True) - n * jnp.mean(dn * n, axis=-1, keepdims=True)
    )
    return d_v, n


def attention_backward_body(
    lengths,
    vec_in,
    ffsmall_in,
    dattn_hbm,
    wout_hbm,
    q_hbm,
    kv_hbm,
    a1_hbm,
    mixed_hbm,
    wqkv_hbm,
    tok_hbm,
    dhid_hbm,
    res_hbm,
    outp_hbm,
    up_mine,
    up_two,
    ffo2,
    ffo3,
    ffg2,
    ffg3,
    out_h,
    gtok_h,
    gqkv_o,
    gout_o,
    gup_o,
    gdn_o,
    small_o,
    late_o,
    dattn,
    wout,
    q_all,
    kv,
    a1,
    mixed,
    wqkv,
    tok,
    dhid,
    res,
    outown,
    outgot,
    fo,
    fg,
    fs,
    fg2,
    fmine,
    fup,
    fdn,
    dmix,
    dkv,
    dqkv,
    dedge,
    dedge_got,
    part,
    got,
    qkv_c,
    out_c,
    qa,
    qb,
    oa,
    ob,
    qs,
    os_,
    qa2,
    qb2,
    oa2,
    ob2,
    fq,
    fout,
    sm,
    smc,
    smz,
    smy,
    late,
    late_c,
    late_p,
    late_sum,
    gux,
    stack,
    gq,
    part_tmp,
    q_tmp,
    o_tmp,
    out_o,
    gtok_o,
    local_sem,
    send_sem,
    recv_sem,
    comm_send,
    comm_recv,
):
    sems = (send_sem, recv_sem)
    comm = Comm(comm_send, comm_recv, 0, 32)
    me = coords()
    x, y, z, core = me["x"], me["y"], me["z"], me["core"]
    other = 1 - core
    zy = lax.rem(y + 3, 4)
    blk, width = tok.shape
    span = 4 * blk
    partw = mixed.shape[1]
    heads = partw // HEAD
    scale = 1.0 / math.sqrt(HEAD)
    reach = W + blk
    used = [0]
    pending = []

    def load(src, dst):
        copy = pltpu.make_async_copy(src, dst, local_sem.at[used[0]])
        used[0] += 1
        copy.start()
        return copy

    def push(src, dst, index, to):
        copy = remote(src, dst, sems, index, to)
        copy.start()
        pending.append(copy)
        return copy

    l_dattn, l_wout = load(dattn_hbm, dattn), load(wout_hbm, wout)
    l_attn = [load(q_hbm, q_all), load(kv_hbm, kv)]
    low, high = slice(0, 32), slice(32, 64)
    l_ff = [load(s, fo.at[i]) for i, s in enumerate((ffo2, ffo3))]
    l_ff += [load(s, fg.at[i]) for i, s in enumerate((ffg2, ffg3))]
    l_up = [load(up_two, fg2.at[pl.ds(0, 2)]), load(up_mine, fmine)]
    l_wqkv, l_a1, l_mixed = load(wqkv_hbm, wqkv), load(a1_hbm, a1), load(mixed_hbm, mixed)
    l_end = [load(outp_hbm.at[pl.ds(0, blk)], outown), load(res_hbm, res)]
    l_end += [load(tok_hbm, tok), load(dhid_hbm, dhid)]

    greet(ring("x") + plane() + near() + [scattered(), collected()])

    p_out = [
        push(outp_hbm.at[pl.ds(p * blk, blk)], outgot.at[p - 1], p, peer(x=-ORDER[p])) for p in (1, 2, 3)
    ]

    def ff_sum(i):
        for c in range(4):
            total = fo[i, c].astype(F32) + fg[i, 0, c].astype(F32) + fg[i, 1, c].astype(F32)
            fs[i, c] = total.astype(BF)

    p_ff = []

    def ff_second(i):
        axis, here = ("y", y) if i == 0 else ("z", z)
        for k in (1, 3, 2):
            src = fs.at[i, lax.rem(here + k, 4)]
            p_ff.append(push(src, fg2.at[2 + i, k - 1], 4 + 3 * i + k, peer(**{axis: k})))

    for copy in l_ff:
        copy.wait()
    ff_sum(0)
    ff_sum(1)
    ff_second(0)

    dkv[...] = jnp.zeros(dkv.shape, F32)
    l_dattn.wait()
    l_wout.wait()
    dmix[...] = dot(
        dattn[...].reshape(span, width), wout[...].reshape(partw, width), NT
    ).astype(BF)
    for copy in l_attn:
        copy.wait()

    def block(b):
        rows = pl.ds(pl.multiple_of(b * blk, blk), blk)
        window = pl.ds(pl.multiple_of(b * blk, blk), reach)
        mask = mask_of(lengths, z * span + b * blk, blk, reach)
        for h in range(heads):
            cols = pl.ds(h * HEAD, HEAD)
            vcols = pl.ds(partw + h * HEAD, HEAD)
            q, k, v = q_all[rows, cols], kv[window, cols], kv[window, vcols]
            s = dot(q, k, NT) * scale + mask
            e = jnp.exp(s - jnp.max(s, axis=-1, keepdims=True))
            p = e * (1.0 / jnp.sum(e, axis=-1, keepdims=True))
            do = dmix[rows, cols]
            dp = dot(do, v, NT)
            ds = (p * (dp - jnp.sum(dp * p, axis=-1, keepdims=True))).astype(BF)
            dqkv[rows, cols] = (dot(ds, k, NN) * scale).astype(BF)
            dkv[window, cols] += dot(ds, q, TN) * scale
            dkv[window, vcols] += dot(p.astype(BF), do, TN)

    pl.loop(0, 2)(block)
    dedge[...] = dkv[0:W, :].astype(BF)
    p_edge = push(dedge, dedge_got, 4, peer(z=3))

    ring_d = RingSum(comm, "x", lambda o, h: part.at[o, pl.ds(2 * h, 2)], part_tmp, got)
    qkv_sums = (
        RingSum(comm, "z", lambda o, h: gq.at[pl.ds(2 * h, 2), 0, o, low], q_tmp.at[0], qa),
        RingSum(comm, "y", lambda o, h: gq.at[o, 0, pl.ds(2 * h, 2), high], q_tmp.at[1], qb),
    )
    left, right = slice(0, width // 2), slice(width // 2, width)
    out_sums = (
        RingSum(
            comm, "z", lambda o, h: wout.at[core, pl.ds(2 * h, 2), o, :, left], o_tmp.at[0], oa
        ),
        RingSum(
            comm,
            "y",
            lambda o, h: wout.at[core, lax.rem(o + 3, 4), pl.ds(2 * h, 2), :, right],
            o_tmp.at[1],
            ob,
        ),
    )

    def grad_out(c):
        cols = pl.ds(pl.multiple_of(c * 256, 256), 256)
        return dot(mixed[:, cols], dattn[...].reshape(span, width), TN)

    l_mixed.wait()
    wout[other] = grad_out(other).astype(BF).reshape(4, 4, 16, width)
    p_oc = push(wout.at[other], out_c, 36, peer(core=1))

    pl.loop(2, 4)(block)
    p_oc.wait_recv()

    wout[core] = (
        grad_out(core) + out_c[...].reshape(256, width).astype(F32)
    ).astype(BF).reshape(4, 4, 16, width)
    for total in out_sums:
        total.start()
    p_edge.wait_recv()
    dqkv[0 : span - W, partw:] = dkv[W:span, :].astype(BF)
    dqkv[span - W :, partw:] = (dkv[span:, :] + dedge_got[...].astype(F32)).astype(BF)
    sm[0, 0:5, :] = ffsmall_in[0:5, :]
    sm[0, 5:8, :] = jnp.zeros((3, width), F32)
    sm[0, 7:8, 0 : 3 * partw] = jnp.sum(dqkv[...].astype(F32), axis=0, keepdims=True)
    p_sc = push(sm.at[0], smc, 53, peer(core=1))

    def grad_qkv(t, c):
        cols = pl.ds(pl.multiple_of(t * 512 + c * 256, 256), 256)
        return dot(a1[:, cols], dqkv[...], TN)

    def swap(t):
        return remote(gq.at[t, 1], qkv_c.at[t], sems, 32 + t, peer(core=1))

    l_a1.wait()

    @pl.loop(0, 4)
    def _(t):
        gq[t, 1] = grad_qkv(t, other).astype(BF).reshape(4, 64, 3 * partw)
        swap(t).start()

    @pl.loop(0, 4)
    def _(t):
        swap(t).wait_recv()
        total = grad_qkv(t, core) + qkv_c[t].reshape(256, 3 * partw).astype(F32)
        gq[t, 0] = total.astype(BF).reshape(4, 64, 3 * partw)

    for total in qkv_sums:
        total.start()
    for total in out_sums:
        total.middle()

    l_wqkv.wait()

    @pl.loop(0, 4)
    def _(j):
        cols = pl.ds(pl.multiple_of(j * 512, 512), 512)
        d = dot(dqkv[...], wqkv[:, j].reshape(512, 3 * partw), NT)
        part[:, :, :, cols] = d.astype(BF).reshape(4, 4, blk // 4, 512)

    ring_d.start()
    p_sc.wait_recv()
    sm[1] = sm[0] + smc[...]
    p_sz = [push(sm.at[1], smz.at[k - 1], 59 + k, peer(z=k)) for k in (1, 3, 2)]
    for total in qkv_sums:
        total.middle()
    ff_second(1)
    ring_d.middle()
    for copy in p_sz:
        copy.wait_recv()
    sm[2] = sm[1] + smz[0] + smz[1] + smz[2]
    p_sy = [push(sm.at[2], smy.at[k - 1], 68 + k, peer(y=k)) for k in (1, 3, 2)]

    for copy in l_end:
        copy.wait()
    for copy in p_out:
        copy.wait_recv()

    @pl.loop(0, blk // 16)
    def _(i):
        rows = pl.ds(pl.multiple_of(i * 16, 16), 16)
        total = res[rows, :] + vec_in[7:8, :] + outown[rows, :].astype(F32)
        for g in range(3):
            total = total + outgot[g, rows, :].astype(F32)
        out_o[rows, :] = total.astype(BF)

    kept = [load(out_o, out_h)]

    for total in out_sums:
        total.finish()
    for c in range(4):
        ta, tb = wout[core, c, z, :, left].astype(F32), wout[core, zy, c, :, right].astype(F32)
        for g in range(2):
            ta, tb = ta + oa[g, c].astype(F32), tb + ob[g, c].astype(F32)
        os_[0, c], os_[1, c] = ta.astype(BF), tb.astype(BF)
    p_o2 = []
    for k in (1, 3, 2):
        tz, tyc = lax.rem(z + k, 4), lax.rem(y + k + 3, 4)
        p_o2.append(push(os_.at[0, tyc], oa2.at[k - 1], 62 + k, peer(y=k)))
        p_o2.append(push(os_.at[1, tz], ob2.at[k - 1], 65 + k, peer(z=k)))

    for total in qkv_sums:
        total.finish()
    for c in range(4):
        ta, tb = gq[c, 0, z, low].astype(F32), gq[y, 0, c, high].astype(F32)
        for g in range(2):
            ta, tb = ta + qa[g, c].astype(F32), tb + qb[g, c].astype(F32)
        qs[0, c], qs[1, c] = ta.astype(BF), tb.astype(BF)
    p_q2 = []
    for k in (1, 3, 2):
        tz, ty = lax.rem(z + k, 4), lax.rem(y + k, 4)
        p_q2.append(push(qs.at[0, ty], qa2.at[k - 1], 53 + k, peer(y=k)))
        p_q2.append(push(qs.at[1, tz], qb2.at[k - 1], 56 + k, peer(z=k)))

    late_sum[...] = jnp.zeros(late_sum.shape, F32)

    p_u, p_x = [], []
    for copy in p_sy:
        copy.wait_recv()
    sm[3] = sm[2] + smy[0] + smy[1] + smy[2]
    p_x += [push(sm.at[3], small_o.at[x], 71 + k, peer(x=k)) for k in (1, 3, 2)]
    kept.append(load(sm.at[3], small_o.at[x]))
    ring_d.finish()
    gain = vec_in[0:1, :]

    @pl.loop(0, blk // 16)
    def _(i):
        rows = pl.ds(pl.multiple_of(i * 16, 16), 16)
        c, r = i // 2, pl.ds(pl.multiple_of(lax.rem(i, 2) * 16, 16), 16)
        d = part[x, c, r, :].astype(F32)
        for g in range(2):
            d = d + got[g, c, r, :].astype(F32)
        d_in, n = norm_backward(d, tok[rows, :].astype(F32), gain)
        gtok_o[rows, :] = dhid[rows, :] + d_in
        late_sum[0:1, :] += jnp.sum(d * n, axis=0, keepdims=True)
        late_sum[1:2, :] += jnp.sum(d, axis=0, keepdims=True)

    kept.append(load(gtok_o, gtok_h))
    for i in range(8):
        at = (i % 4) * (width // 4)
        late[0, i : i + 1, :] = late_sum[i // 4 : i // 4 + 1, at : at + width // 4]
    p_lc = push(late.at[0], late_c, 52, peer(core=1))
    p_lc.wait_recv()
    late[1] = late[0] + late_c[...]
    p_lz = [push(late.at[1], late_p.at[i], 98 + i, to) for i, to in enumerate(plane())]

    for copy in p_ff:
        copy.wait_recv()
    for copy in l_up:
        copy.wait()
    for i in range(4):
        total = (fmine[i] if i < 2 else fs[i - 2, (y, z)[i - 2]]).astype(F32)
        for g in range(3):
            total = total + fg2[i, g].astype(F32)
        into, half = (fup, fdn)[i // 2], i % 2
        into[2 * half : 2 * half + 2] = total.astype(BF).reshape(2, 16, width)
    for k in (1, 3, 2):
        p_u.append(push(fup.at[lax.rem(x + k, 4)], gux.at[x], 48 + k, peer(x=k)))
        p_x.append(push(fdn.at[lax.rem(x + k, 4)], gdn_o.at[x], 76 + k, peer(x=k)))
    gux[x] = fup[x]
    kept.append(load(fdn.at[x], gdn_o.at[x]))
    for copy in p_o2:
        copy.wait_recv()
    ta, tb = os_[0, zy].astype(F32), os_[1, z].astype(F32)
    for g in range(3):
        ta, tb = ta + oa2[g].astype(F32), tb + ob2[g].astype(F32)
    fout[:, left], fout[:, right] = ta.astype(BF), tb.astype(BF)
    p_x.append(push(fout, gout_o, 75, collected()))

    for copy in p_q2:
        copy.wait_recv()
    ta, tb = qs[0, y].astype(F32), qs[1, z].astype(F32)
    for g in range(3):
        ta, tb = ta + qa2[g].astype(F32), tb + qb2[g].astype(F32)
    fq[0:2] = ta.astype(BF).reshape(2, 16, 3 * partw)
    fq[2:4] = tb.astype(BF).reshape(2, 16, 3 * partw)
    for g in range(3):
        block_cols, own_cols = pl.ds(g * partw, partw), pl.ds(g * width + x * partw, partw)
        for k in (1, 3, 2):
            src = fq.at[lax.rem(x + k, 4), :, block_cols]
            p_x.append(push(src, gqkv_o.at[:, own_cols], 83 + 3 * g + k - 1, peer(x=k)))
        kept.append(load(fq.at[x, :, block_cols], gqkv_o.at[:, own_cols]))

    for copy in p_lz:
        copy.wait_recv()
    total = late[1]
    for i in range(15):
        total = total + late_p[i]
    late[2] = total
    p_x += [push(late.at[2], late_o.at[x], 79 + k, peer(x=k)) for k in (1, 3, 2)]
    kept.append(load(late.at[2], late_o.at[x]))

    for copy in p_u:
        copy.wait_recv()
    slabs = width // 128
    for i in range(slabs):
        for c in range(4):
            stack[16 * i : 16 * i + 16, 128 * c : 128 * c + 128] = gux[
                c, :, 128 * i : 128 * i + 128
            ]
    spread_up = dot(stack[...], shuffle(), NT)
    for i in range(slabs):
        gup_o[:, 512 * i : 512 * i + 512] = spread_up[16 * i : 16 * i + 16, :]

    for copy in p_x:
        copy.wait_recv()
    for copy in pending:
        copy.wait_send()

    @pl.loop(0, 4)
    def _(j):
        swap(j).wait_send()

    comm.drain()

    for copy in kept:
        copy.wait()


def attention_backward(
    collective_id,
    lengths,
    vectors,
    ff_small,
    d_attn,
    wout,
    q,
    kv,
    a1,
    mixed,
    wqkv,
    tok,
    d_hidden,
    residual,
    out_part,
    up_mine,
    up_two,
    ff_own,
    ff_got,
):
    blk, width = tok.shape
    span, partw = mixed.shape
    hidden = ff_own[0].shape[-1]
    vmem = pl.BlockSpec(memory_space=pltpu.VMEM)
    hbm = pl.BlockSpec(memory_space=pl.ANY)
    outs = [
        ((blk, width), BF, hbm),
        ((blk, width), F32, hbm),
        ((16, 3 * width), BF, hbm),
        ((16, width), BF, hbm),
        ((16, 4 * hidden), F32, vmem),
        ((4, 16, width), BF, hbm),
        ((4, 8, width), F32, hbm),
        ((4, 8, width // 4), F32, hbm),
    ]
    half = width // 2
    scratch = [
        ((4, blk, width), BF),
        ((2, 4, 4, 16, width), BF),
        ((span, partw), BF),
        ((span + W, 2 * partw), BF),
        ((span, width), BF),
        ((span, partw), BF),
        ((2, 4, 4, 64, 3 * partw), BF),
        ((blk, width), BF),
        ((blk, width), F32),
        ((blk, width), F32),
        ((blk, width), BF),
        ((3, blk, width), BF),
        ((2, 4, 32, width), BF),
        ((2, 2, 4, 32, width), BF),
        ((2, 4, 32, width), BF),
        ((4, 3, 32, width), BF),
        ((2, 32, width), BF),
        ((4, 16, hidden), BF),
        ((4, 16, width), BF),
        ((span, partw), BF),
        ((span + W, 2 * partw), F32),
        ((span, 3 * partw), BF),
        ((W, 2 * partw), BF),
        ((W, 2 * partw), BF),
        ((4, 4, blk // 4, width), BF),
        ((2, 4, blk // 4, width), BF),
        ((4, 4, 64, 3 * partw), BF),
        ((4, 4, 16, width), BF),
        ((2, 4, 32, 3 * partw), BF),
        ((2, 4, 32, 3 * partw), BF),
        ((2, 4, 16, half), BF),
        ((2, 4, 16, half), BF),
        ((2, 4, 32, 3 * partw), BF),
        ((2, 4, 16, half), BF),
        ((3, 32, 3 * partw), BF),
        ((3, 32, 3 * partw), BF),
        ((3, 16, half), BF),
        ((3, 16, half), BF),
        ((4, 16, 3 * partw), BF),
        ((16, width), BF),
        ((4, 8, width), F32),
        ((8, width), F32),
        ((3, 8, width), F32),
        ((3, 8, width), F32),
        ((3, 8, width // 4), F32),
        ((8, width // 4), F32),
        ((15, 8, width // 4), F32),
        ((2, width), F32),
        ((4, 16, hidden), BF),
        ((hidden // 8, 512), BF),
        ((4, 2, 4, 64, 3 * partw), BF),
        ((2, 2, blk // 4, width), BF),
        ((2, 2, 2, 32, 3 * partw), BF),
        ((2, 2, 2, 16, half), BF),
        ((blk, width), BF),
        ((blk, width), F32),
    ]
    return pl.pallas_call(
        attention_backward_body,
        out_shape=tuple(jax.ShapeDtypeStruct(s, d) for s, d, _ in outs),
        in_specs=[pl.BlockSpec(memory_space=pltpu.SMEM)] + [vmem] * 2 + [hbm] * 17,
        out_specs=tuple(o[2] for o in outs),
        scratch_shapes=[pltpu.VMEM(s, d) for s, d in scratch]
        + [
            pltpu.SemaphoreType.DMA((32,)),
            pltpu.SemaphoreType.DMA((114,)),
            pltpu.SemaphoreType.DMA((114,)),
            pltpu.SemaphoreType.DMA((32,)),
            pltpu.SemaphoreType.DMA((32,)),
        ],
        compiler_params=pltpu.CompilerParams(
            collective_id=collective_id, has_side_effects=True, vmem_limit_bytes=62 << 20
        ),
        name="attention_backward",
    )(
        lengths,
        vectors,
        ff_small,
        d_attn,
        wout,
        q,
        kv,
        a1,
        mixed,
        wqkv,
        tok,
        d_hidden,
        residual,
        out_part,
        up_mine,
        up_two,
        *ff_own,
        *ff_got,
    )


def results_body(
    out,
    gtok,
    gqkv,
    gout,
    gup,
    gdn,
    small,
    late,
    out_o,
    gtok_o,
    gain1_o,
    shift1_o,
    gqkv_o,
    bqv_o,
    gout_o,
    bout_o,
    gain2_o,
    shift2_o,
    gup_o,
    bup_o,
    gdn_o,
    bdown_o,
    sums,
):
    me = coords()
    device = ((me["y"] * 2 + me["core"]) * 4 + me["z"]) * 4 + me["x"]
    out_o[...] = out[...]
    gtok_o[...] = gtok[...]
    gqkv_o[...] = gqkv[...].astype(F32)
    gout_o[...] = gout[...].astype(F32)
    gup_o[...] = gup[...]
    gdn_o[...] = gdn[...].reshape(gdn_o.shape).astype(F32)

    tile = pl.ds(pl.multiple_of(device // 8 * 128, 128), 128)
    turn = lax.rem(128 - 16 * lax.rem(device, 8), 128)
    shares = [pltpu.roll(small[i, :, tile], turn, 1) for i in range(4)]
    total = shares[0] + shares[1] + shares[2] + shares[3]
    gain2_o[...] = total[0:1, 0:16]
    shift2_o[...] = total[1:2, 0:16]
    bout_o[...] = total[2:3, 0:16]
    bdown_o[...] = total[4:5, 0:16]
    for i in range(4):
        bup_o[:, 16 * i : 16 * i + 16] = shares[i][3:4, 0:16]

    sums[...] = late[0] + late[1] + late[2] + late[3]
    place = lax.rem(device, 32)
    tile = pl.ds(pl.multiple_of(place // 8 * 128, 128), 128)
    turned = pltpu.roll(sums[:, tile], turn, 1)
    row = lax.broadcasted_iota(jnp.int32, turned.shape, 0)

    def only(i):
        return jnp.sum(jnp.where(row == i, turned, 0.0), axis=0, keepdims=True)[:, 0:16]

    gain1_o[...] = only(device // 32)
    shift1_o[...] = only(4 + device // 32)

    half, place = device // 64, lax.rem(device, 16)
    tile = pl.ds(pl.multiple_of(half * 1024 + place // 4 * 128, 128), 128)
    turn = lax.rem(128 - 32 * lax.rem(device, 4), 128)
    bqv_o[...] = pltpu.roll(small[lax.rem(device, 64) // 16, :, tile], turn, 1)[7:8, 0:32]


def results(*arrays):
    out, gtok, gqkv, gout, gup, gdn = arrays[:6]
    vmem = pl.BlockSpec(memory_space=pltpu.VMEM)
    rows, vector = gdn.shape[0] * gdn.shape[1], lambda n: ((1, n), F32)
    outs = [
        (out.shape, BF),
        (gtok.shape, F32),
        vector(16),
        vector(16),
        (gqkv.shape, F32),
        vector(32),
        (gout.shape, F32),
        vector(16),
        vector(16),
        vector(16),
        (gup.shape, F32),
        vector(64),
        ((rows, gdn.shape[2]), F32),
        vector(16),
    ]
    return pl.pallas_call(
        results_body,
        out_shape=tuple(jax.ShapeDtypeStruct(s, d) for s, d in outs),
        in_specs=[vmem] * 8,
        out_specs=(vmem,) * 14,
        scratch_shapes=[pltpu.VMEM(arrays[7].shape[1:], F32)],
        compiler_params=pltpu.CompilerParams(vmem_limit_bytes=40 << 20),
        name="results",
    )(*arrays)


def local(
    tokens,
    grad_out,
    lengths,
    ln1_gain,
    ln1_bias,
    w_qkv,
    b_qv,
    w_out,
    b_out,
    ln2_gain,
    ln2_bias,
    w_up,
    b_up,
    w_down,
    b_down,
):
    blk, width = tokens.shape[1:]
    part = width // 4
    hidden = w_up.shape[1] // 4
    tok = tokens.reshape(blk, width)
    dy = grad_out.reshape(blk, width)
    small = jnp.zeros((1024,), F32)
    vectors = (ln1_gain, ln1_bias, b_qv, b_out, ln2_gain, ln2_bias, b_up, b_down)
    for i, vector in enumerate(vectors):
        size = vector.shape[0]
        small = small + jnp.pad(vector.astype(F32), (i * 128, 1024 - i * 128 - size))
    (
        vectors,
        residual,
        d_hidden,
        ff_small,
        wqkv_g,
        wout_g,
        a1,
        query,
        kv,
        mixed,
        d_attn_g,
        out_part,
        up_mine,
        up_two,
        down_a_own,
        down_b_own,
        down_a_got,
        down_b_got,
    ) = forward(0, lengths, tok, small.reshape(8, 128), w_up, dy, w_down, w_qkv, w_out)
    last = attention_backward(
        1,
        lengths,
        vectors,
        ff_small,
        d_attn_g,
        wout_g,
        query,
        kv,
        a1,
        mixed,
        wqkv_g,
        tok,
        d_hidden,
        residual,
        out_part,
        up_mine,
        up_two,
        (down_a_own, down_b_own),
        (down_a_got, down_b_got),
    )

    final = list(results(*last))
    final[0] = final[0].reshape(1, blk, width)
    final[1] = final[1].reshape(1, blk, width)
    for i in (2, 3, 5, 7, 8, 9, 11, 13):
        final[i] = final[i].reshape(-1)
    return tuple(final)


def solution(mesh):
    fine = Mesh(mesh.devices.reshape(4, 2, 4, 4), AXES)
    rows, seq = ("y", "core"), ("z", "x")
    every = rows + seq
    token = P(rows, seq, None)
    vec, mat = P(every), P(every, None)
    in_specs = (token, token, P(rows, None), vec, vec, mat, vec, mat, vec, vec, vec, mat, vec, mat, vec)
    out_specs = (token, token, vec, vec, mat, vec, mat, vec, vec, vec, mat, vec, mat, vec)
    return jax.shard_map(local, mesh=fine, in_specs=in_specs, out_specs=out_specs, check_vma=False)
```

```python
import functools
import math

import jax
import jax.numpy as jnp
from jax import lax
from jax.experimental import pallas as pl
from jax.experimental.pallas import tpu as pltpu
from jax.sharding import Mesh, PartitionSpec as P

HEADS = 16
HEAD = 128
W = 256
EPSILON = 1e-05
NEG_FILL = -1e30

AXES = ("y", "core", "z", "x")
SIZE = {"y": 4, "core": 2, "z": 4, "x": 4}
BF = jnp.bfloat16
F32 = jnp.float32
SEMS = 264


def coords():
    return {a: lax.axis_index(a) for a in AXES}


def peer(**delta):
    me = coords()
    return tuple(lax.rem(me[a] + delta.get(a, 0) % SIZE[a], SIZE[a]) for a in AXES)


class Comm:
    def __init__(self, send_sem, recv_sem, base=0, room=SEMS):
        self.send_sem, self.recv_sem = send_sem, recv_sem
        self.count, self.last, self.open = base, base + room, []

    def push(self, src, dst, to):
        entry = self.plan(src, dst, to)
        entry[0].start()
        return entry

    def plan(self, src, dst, to):
        copy = pltpu.make_async_remote_copy(
            src_ref=src,
            dst_ref=dst,
            send_sem=self.send_sem.at[self.count],
            recv_sem=self.recv_sem.at[self.count],
            device_id=to,
            device_id_type=pl.DeviceIdType.MESH,
        )
        assert self.count < self.last
        self.count += 1
        self.open.append([copy, True, True])
        return self.open[-1]

    def local(self, src, dst):
        copy = pltpu.make_async_copy(src, dst, self.send_sem.at[self.count])
        self.count += 1
        copy.start()
        self.open.append([copy, False, True])
        return self.open[-1]

    def arrived(self, entries):
        for entry in entries:
            if entry[2]:
                if entry[1]:
                    entry[0].wait_recv()
                else:
                    entry[0].wait()
                entry[2] = False

    def drain(self):
        self.arrived(self.open)
        for copy, remote_copy, _ in self.open:
            if remote_copy:
                copy.wait_send()
        self.open = []


def greet(devices):
    barrier = pltpu.get_barrier_semaphore()
    for device in devices:
        pl.semaphore_signal(barrier, inc=1, device_id=device, device_id_type=pl.DeviceIdType.MESH)
    pl.semaphore_wait(barrier, len(devices))


def ring(axis):
    return [peer(**{axis: k}) for k in (1, 3, 2)]


def near():
    return [peer(core=1)]


def plane():
    return [peer(y=i // 4, z=i % 4) for i in range(1, 16)]


def everyone():
    return ring("x") + ring("y") + ring("z") + near()


def scattered():
    me = coords()
    return (lax.rem(me["z"] + 1, 4), me["core"], me["x"], me["y"])


def collected():
    me = coords()
    return (me["x"], me["core"], lax.rem(me["y"] + 3, 4), me["z"])


class Relay:
    def __init__(self, comm, axis, full, half):
        self.comm, self.axis, self.full, self.half = comm, axis, full, half
        self.me = lax.axis_index(axis)

    def to(self, k):
        return peer(**{self.axis: k})

    def start(self):
        a, b = self.half(self.me, 0), self.half(self.me, 1)
        self.sent = [self.comm.push(a, a, self.to(1)), self.comm.push(b, b, self.to(3))]
        self.rest = [self.comm.push(b, b, self.to(1)), self.comm.push(a, a, self.to(3))]

    def near(self):
        self.comm.arrived(self.sent)
        before, after = lax.rem(self.me + 3, 4), lax.rem(self.me + 1, 4)
        up, down = self.half(before, 0), self.half(after, 1)
        self.passed = [self.comm.push(up, up, self.to(1)), self.comm.push(down, down, self.to(3))]
        self.comm.arrived(self.rest)

    def far(self):
        self.comm.arrived(self.passed)


class RingSum:
    def __init__(self, comm, axis, ref, tmp, got):
        self.comm, self.axis, self.ref, self.tmp, self.got = comm, axis, ref, tmp, got
        self.me = lax.axis_index(axis)

    def at(self, k):
        return lax.rem(self.me + k, 4)

    def push(self, src, dst, k):
        return self.comm.push(src, dst, peer(**{self.axis: k}))

    def plan(self, src, dst, k):
        return self.comm.plan(src, dst, peer(**{self.axis: k}))

    def prepare(self):
        self.up = self.plan(self.ref(self.at(2), 0), self.tmp.at[0], 1)
        self.down = self.plan(self.ref(self.at(2), 1), self.tmp.at[1], 3)
        self.end = [
            self.plan(self.ref(self.at(1), 1), self.got.at[0, pl.ds(2, 2)], 1),
            self.plan(self.ref(self.at(3), 0), self.got.at[1, pl.ds(0, 2)], 3),
        ]
        self.first = {1: [self.end[0]], 2: [self.up, self.down], 3: [self.end[1]]}

    def start(self):
        self.prepare()
        for k in (2, 1, 3):
            for entry in self.first[k]:
                entry[0].start()

    def start_block(self, to):
        for k in (2, 1, 3):

            @pl.when(self.at(k) == to)
            def _():
                for entry in self.first[k]:
                    entry[0].start()

    def middle(self):
        for arrived, k, h, back in ((self.up, 1, 0, 0), (self.down, 3, 1, 2)):
            self.comm.arrived([arrived])
            block = self.ref(self.at(k), h)
            for c in range(2):
                total = block[c].astype(F32) + self.tmp[h, c].astype(F32)
                block[c] = total.astype(BF)
            self.end.append(self.push(block, self.got.at[h, pl.ds(back, 2)], k))

    def finish(self):
        self.comm.arrived(self.end)


class Gather:
    def __init__(self, comm, w, by_core, cut, shift=0):
        self.comm, self.w, self.by_core, self.cut = comm, w, by_core, cut
        self.shift = shift
        me = coords()
        self.y, self.core, self.z = me["y"], me["core"], me["z"]

    def slot(self, y, z, cut):
        place = (self.core, y, z) if self.by_core else (y, self.core, z)
        return self.w.at[place + self.cut[cut]]

    def row(self, y):
        return lax.rem(y + self.shift, 4)

    def first(self):
        self.first_a()
        self.first_b()
        self.one = self.one_a + self.one_b

    def first_a(self):
        a = self.slot(self.row(self.y), self.z, 0)
        self.one_a = [self.comm.push(a, a, to) for to in ring("z")]

    def first_b(self):
        b = self.slot(self.row(self.y), self.z, 1)
        self.one_b = [self.comm.push(b, b, to) for to in ring("y")]

    def second(self):
        self.second_a()
        self.second_b()

    def second_a(self):
        every = slice(None)
        self.a = Relay(
            self.comm,
            "y",
            lambda o: self.slot(self.row(o), every, 0),
            lambda o, h: self.slot(self.row(o), pl.ds(2 * h, 2), 0),
        )
        self.a.start()

    def second_b(self):
        every = slice(None)
        self.b = Relay(
            self.comm,
            "z",
            lambda o: self.slot(every, o, 1),
            lambda o, h: self.slot(pl.ds(2 * h, 2), o, 1),
        )
        self.b.start()

    def across(self, relay, k):
        block = relay.full(lax.rem(relay.me + k, 4))
        self.two.append(self.comm.push(block, block, peer(core=1)))

    def near_a(self):
        self.two = []
        self.a.near()
        for k in (0, 1, 3):
            self.across(self.a, k)

    def near_b(self):
        self.b.near()
        for k in (0, 1, 3):
            self.across(self.b, k)

    def near(self):
        self.near_a()
        self.near_b()

    def far_a(self):
        self.a.far()
        self.across(self.a, 2)

    def far_b(self):
        self.b.far()
        self.across(self.b, 2)

    def far(self):
        self.far_a()
        self.far_b()

    def done(self):
        self.comm.arrived(self.two)


def by_rows(rows):
    return [(slice(0, rows // 2),), (slice(rows // 2, rows),)]


def by_columns(columns):
    every = slice(None)
    return [(every, slice(0, columns // 2)), (every, slice(columns // 2, columns))]


def dot(a, b, dims):
    return lax.dot_general(a, b, (dims, ((), ())), preferred_element_type=F32)


NN = ((1,), (0,))
NT = ((1,), (1,))
TN = ((0,), (0,))


def mask_of(lengths, first, blk, reach):
    q = first + lax.broadcasted_iota(jnp.int32, (blk, reach), 0)
    k = first - W + lax.broadcasted_iota(jnp.int32, (blk, reach), 1)
    q_doc, k_doc = jnp.zeros((blk, reach), jnp.int32), jnp.zeros((blk, reach), jnp.int32)
    end = 0
    for i in range(lengths.shape[1]):
        end = end + lengths[0, i]
        q_doc = q_doc + jnp.where(q >= end, 1, 0)
        k_doc = k_doc + jnp.where(k >= end, 1, 0)
    seen = (q_doc == k_doc) & (k <= q) & (q - k < W) & (k >= 0)
    return jnp.where(seen, 0.0, NEG_FILL).astype(F32)


def shuffle():
    row = lax.broadcasted_iota(jnp.int32, (512, 512), 0)
    column = lax.broadcasted_iota(jnp.int32, (512, 512), 1)
    source = 64 * ((column >> 4) & 7) + 16 * (column >> 7) + (column & 15)
    return jnp.where(source == row, 1.0, 0.0).astype(BF)


def whole_vector(table, index, offset, count, size, lane):
    shift = size.bit_length() - 1
    row = lax.broadcasted_iota(jnp.int32, (128, 1024), 0)
    tile = lax.broadcasted_iota(jnp.int32, (128, 1024), 1)
    chosen = jnp.where(tile == row * 8 + index, 1.0, 0.0).astype(BF)
    share = dot(chosen, table, NN).astype(BF)
    row = lax.broadcasted_iota(jnp.int32, (128, count), 0)
    column = lax.broadcasted_iota(jnp.int32, (128, count), 1) + offset
    spread = jnp.where((column & (size - 1)) + lane == row, 1.0, 0.0).astype(BF)
    values = jnp.where((column >> shift) == row, dot(share, spread, NN), 0.0)
    return jnp.sum(values, axis=0, keepdims=True)


ORDER = (0, 1, 3, 2)


def remote(src, dst, sems, index, to):
    send, recv = sems
    return pltpu.make_async_remote_copy(
        src_ref=src,
        dst_ref=dst,
        send_sem=send.at[index],
        recv_sem=recv.at[index],
        device_id=to,
        device_id_type=pl.DeviceIdType.MESH,
    )


def forward_body(
    lengths,
    tok_in,
    small_in,
    wup_in,
    dy_in,
    wdn_in,
    wqkv_in,
    wout_in,
    vec_o,
    res_h,
    dhid_h,
    small_out,
    wq_h,
    wo_h,
    a1_h,
    q_h,
    kv_h,
    mixed_h,
    dattn_hbm,
    outp_hbm,
    up_mine,
    up_two,
    dn_a_own,
    dn_b_own,
    dn_a_got,
    dn_b_got,
    wup,
    wdn,
    cc,
    wo,
    tokg,
    act,
    dup,
    dact,
    q,
    kv,
    mixed,
    dyg,
    part,
    got,
    dattn,
    smalls,
    stack,
    uparts,
    ring_tmp,
    up_got,
    res_o,
    dhid_out,
    local_sem,
    free_sem,
    ff_send,
    ff_recv,
    send_sem,
    recv_sem,
):
    groups, taken = [], [0]

    def group(room):
        comm = Comm(send_sem, recv_sem, taken[0], room)
        taken[0] += room
        groups.append(comm)
        return comm

    c_q, c_o, c_u, c_d = group(40), group(30), group(30), group(30)
    c_small, c_tok, comm = group(28), group(6), group(40)
    sems = (ff_send, ff_recv)
    me = coords()
    x, y, z, core = me["x"], me["y"], me["z"], me["core"]
    other = 1 - core
    blk, width = tok_in.shape
    span = 4 * blk
    partw = q.shape[1]
    hidden = act.shape[1]
    heads = partw // HEAD
    reach = W + blk
    scale = 1.0 / math.sqrt(HEAD)
    mine16 = pl.ds(x * 16, 16)
    low, high = slice(0, 32), slice(32, 64)
    a1, up_c, dn_c, a2g = act, cc.at[0], cc.at[1], tokg
    wide = slice(0, 3 * partw)

    greet(ring("x") + plane() + near() + [scattered(), collected()])

    s_q = []
    for k in (1, 3, 2):
        for g in range(3):
            src = wqkv_in.at[:, pl.ds(g * width + lax.rem(x + k, 4) * partw, partw)]
            dst = cc.at[core, y, z, mine16, pl.ds(g * partw, partw)]
            s_q.append(c_q.push(src, dst, peer(x=k)))
    for g in range(3):
        src = wqkv_in.at[:, pl.ds(g * width + x * partw, partw)]
        s_q.append(c_q.local(src, cc.at[core, y, z, mine16, pl.ds(g * partw, partw)]))
    spot = smalls.at[y, core, pl.ds((z * 4 + x) * 8, 8)]
    s_small = [c_small.push(small_in, spot, to) for to in ring("x")]
    s_small.append(c_small.local(small_in, spot))
    s_o = [c_o.push(wout_in, wo.at[core, z, x], scattered())]
    tokens = Relay(
        c_tok, "x", lambda o: tokg.at[o], lambda o, h: tokg.at[o, pl.ds(h * blk // 2, blk // 2)]
    )
    tokg[x] = tok_in[...]
    tokens.start()

    qkv_g = Gather(c_q, cc, True, [cut + (wide,) for cut in by_rows(64)])
    out_g = Gather(c_o, wo, True, by_columns(width), 3)
    down_g = Gather(c_d, wdn, False, by_rows(64))
    up_g = Gather(c_u, wup, False, by_rows(64))

    c_q.arrived(s_q)
    qkv_g.first()
    c_small.arrived(s_small)
    block = smalls.at[y, core, pl.ds(z * 32, 32)]
    s_small = [c_small.push(block, block, to) for to in plane()]

    slabs = 4 * hidden // 512
    for i in range(slabs):
        stack[16 * i : 16 * i + 16, :] = wup_in[:, 512 * i : 512 * i + 512]
    mixed_up = dot(stack[...], shuffle(), NN).astype(BF)
    for i in range(slabs):
        for to in range(4):
            uparts[to, :, 128 * i : 128 * i + 128] = mixed_up[
                16 * i : 16 * i + 16, 128 * to : 128 * to + 128
            ]

    c_q.arrived(qkv_g.one)
    qkv_g.second()
    c_o.arrived(s_o)
    out_g.first()
    c_small.arrived(s_small)
    s_small = []
    for other_y in range(4):
        block = smalls.at[other_y, core]
        s_small.append(c_small.push(block, block, peer(core=1)))
    tokens.near()
    s_u, s_d = [], []
    for k in (1, 3, 2):
        to = lax.rem(x + k, 4)
        s_d.append(
            c_d.push(wdn_in.at[pl.ds(to * 16, 16)], wdn.at[y, core, z, mine16], peer(x=k))
        )
        s_u.append(c_u.push(uparts.at[to], wup.at[y, core, z, mine16], peer(x=k)))
    s_d.append(c_d.local(wdn_in.at[mine16], wdn.at[y, core, z, mine16]))
    s_u.append(c_u.local(uparts.at[x], wup.at[y, core, z, mine16]))
    s_dy = [comm.push(dy_in, dyg.at[p], peer(x=ORDER[p])) for p in (1, 2, 3)]
    dyg[0] = dy_in[...]

    c_small.arrived(s_small)
    table = smalls[...].reshape(1024, 128).astype(BF)
    vec_o[0:1, :] = whole_vector(table, 0, 0, width, 16, 0)
    vec_o[1:2, :] = whole_vector(table, 1, 0, width, 16, 0)
    gain, shift = vec_o[0:1, :], vec_o[1:2, :]

    def norm_block(o):
        @pl.loop(0, blk // 16)
        def _(i):
            rows = pl.ds(pl.multiple_of(i * 16, 16), 16)
            v = tokg[o, rows, :].astype(F32)
            centred = v - jnp.mean(v, axis=-1, keepdims=True)
            s = lax.rsqrt(jnp.mean(centred * centred, axis=-1, keepdims=True) + EPSILON)
            at = pl.ds(pl.multiple_of(o * blk + i * 16, 16), 16)
            a1[at, :] = (centred * s * gain + shift).astype(BF)

    norm_block(x)
    qkv_g.near()
    c_o.arrived(out_g.one)
    out_g.second()
    norm_block(lax.rem(x + 1, 4))
    c_d.arrived(s_d)
    down_g.first()
    norm_block(lax.rem(x + 3, 4))
    qkv_g.far()
    tokens.far()
    norm_block(lax.rem(x + 2, 4))
    out_g.near()
    c_u.arrived(s_u)
    up_g.first_b()
    keep_a1 = [comm.local(a1, a1_h)]
    vec_o[2:3, :] = jnp.zeros((1, width), F32)
    vec_o[2:3, 0:partw] = whole_vector(table, 2, x * partw, partw, 32, 0)
    vec_o[2:3, 2 * partw : 3 * partw] = whole_vector(table, 2, width + x * partw, partw, 32, 0)
    qkv_g.done()

    def project(first):
        cols = slice(first, first + partw)
        total = vec_o[2:3, cols]
        rows = [
            jnp.concatenate([cc[0, j, :, :, cols], cc[1, j, :, :, cols]]).reshape(512, partw)
            for j in range(4)
        ]
        w = jnp.concatenate(rows)
        return (dot(a1[...], w, NN) + total).astype(BF)

    kv[W:, 0:partw] = project(partw)
    kv[W:, partw:] = project(2 * partw)
    s_edge = [comm.push(kv.at[pl.ds(span, W)], kv.at[pl.ds(0, W)], peer(z=1))]
    q[...] = project(0)
    keep_q = [c_q.local(cc.at[:, :, :, :, wide], wq_h)]
    comm.local(q, q_h)

    def attend(b):
        rows = pl.ds(pl.multiple_of(b * blk, blk), blk)
        window = pl.ds(pl.multiple_of(b * blk, blk), reach)
        mask = mask_of(lengths, z * span + b * blk, blk, reach)
        for h in range(heads):
            cols, vcols = pl.ds(h * HEAD, HEAD), pl.ds(partw + h * HEAD, HEAD)
            s = dot(q[rows, cols], kv[window, cols], NT) * scale + mask
            e = jnp.exp(s - jnp.max(s, axis=-1, keepdims=True))
            p = (e * (1.0 / jnp.sum(e, axis=-1, keepdims=True))).astype(BF)
            mixed[rows, cols] = dot(p, kv[window, vcols], NN).astype(BF)

    c_sum = group(8)
    ring_a = RingSum(c_sum, "x", lambda o, h: part.at[o, pl.ds(2 * h, 2)], ring_tmp.at[0], got)
    ring_a.prepare()

    def project_out(o):
        rows = slice(o * blk, (o + 2) * blk)

        @pl.loop(0, 4)
        def _(j):
            cols = pl.ds(pl.multiple_of(j * 512, 512), 512)
            d = dot(mixed[rows, :], wo[:, :, :, :, cols].reshape(partw, 512), NN)
            part[o : o + 2, :, :, cols] = d.astype(BF).reshape(2, 4, blk // 4, 512)
            dact[rows, cols] = d

        for to in (o, o + 1):
            ring_a.start_block(to)

    pl.loop(2, 4)(attend)
    out_g.far()
    out_g.done()
    c_tok.drain()
    project_out(2)
    c_d.arrived(down_g.one)
    down_g.second_a()
    for i in (3, 4, 5, 7):
        vec_o[i : i + 1, :] = whole_vector(table, i, 0, width, 16, 0)
    vec_o[6:7, :] = whole_vector(table, 6, 0, hidden, 16, x * 16)
    comm.arrived(s_edge)
    up_g.first_a()
    down_g.second_b()
    pl.loop(0, 2)(attend)
    project_out(0)
    down_g.near_a()
    c_u.arrived(up_g.one_a + up_g.one_b)
    up_g.second_a()
    comm.local(kv, kv_h)
    comm.local(mixed, mixed_h)
    c_o.local(wo, wo_h)
    c_q.drain()
    pl.semaphore_signal(
        free_sem, inc=1, device_id=peer(core=1), device_id_type=pl.DeviceIdType.MESH
    )
    down_g.near_b()
    up_g.second_b()
    ring_a.middle()
    down_g.far_a()

    ring_a.finish()
    b_out, gain2, shift2 = vec_o[3:4, :], vec_o[4:5, :], vec_o[5:6, :]

    @pl.loop(0, blk // 16)
    def _(i):
        rows = pl.ds(pl.multiple_of(i * 16, 16), 16)
        own_rows = pl.ds(pl.multiple_of(x * blk + i * 16, 16), 16)
        v = tok_in[rows, :].astype(F32) + dact[own_rows, :] + b_out
        c, r = i // 2, pl.ds(pl.multiple_of(lax.rem(i, 2) * 16, 16), 16)
        for g in range(2):
            v = v + got[g, c, r, :].astype(F32)
        res_o[rows, :] = v
        centred = v - jnp.mean(v, axis=-1, keepdims=True)
        s = lax.rsqrt(jnp.mean(centred * centred, axis=-1, keepdims=True) + EPSILON)
        a2g[0, rows, :] = (centred * s * gain2 + shift2).astype(BF)

    top, bottom = pl.ds(0, blk // 2), pl.ds(blk // 2, blk // 2)
    spread = []
    for p, rows in ((1, top), (2, bottom), (1, bottom), (2, top)):
        spread.append(comm.push(a2g.at[0, rows], a2g.at[p, rows], peer(x=ORDER[p])))
    comm.local(res_o, res_h)
    down_g.far_b()
    up_g.near_a()
    c_sum.drain()
    comm.arrived(keep_a1 + s_dy)
    down_g.done()

    @pl.loop(0, 4)
    def _(j):
        tile = wdn[j].reshape(512, width)
        cols = pl.ds(pl.multiple_of(j * 512, 512), 512)
        dact[:, cols] = dot(dyg[...].reshape(span, width), tile, NT)

    comm.arrived(spread[:2])
    passed = [
        comm.push(a2g.at[1, top], a2g.at[3, top], peer(x=1)),
        comm.push(a2g.at[2, bottom], a2g.at[3, bottom], peer(x=3)),
    ]
    up_g.near_b()
    up_g.far_a()
    up_g.far_b()
    up_g.done()
    comm.arrived(passed + spread)

    @pl.loop(0, hidden // 256)
    def _(j):
        cols = pl.ds(pl.multiple_of(j * 256, 256), 256)
        u = dot(a2g[...].reshape(span, width), wup[:, :, :, :, cols].reshape(width, 256), NN)
        u = u + vec_o[6:7, cols]
        phi = 0.5 + 0.5 * lax.erf(u * math.sqrt(0.5))
        act[:, cols] = (u * phi).astype(BF)
        slope = phi + u * (jnp.exp(-0.5 * u * u) * (1.0 / math.sqrt(2.0 * math.pi)))
        d_up = (dact[:, cols] * slope).astype(BF)
        dup[:, cols] = d_up
        small_out[3:4, cols] = jnp.sum(d_up.astype(F32), axis=0, keepdims=True)

    c_ff = group(12)
    places = [lax.rem(x + 4 - k, 4) for k in ORDER]
    ring_f = RingSum(c_ff, "x", lambda o, h: part.at[o, pl.ds(2 * h, 2)], ring_tmp.at[1], got)

    @pl.loop(0, 4)
    def _(j):
        cols = pl.ds(pl.multiple_of(j * 512, 512), 512)
        d = dot(dup[...], wup[j].reshape(512, hidden), NT)
        dact[0:blk, cols] = d[:blk]
        for p in (1, 2, 3):
            block = d[p * blk : (p + 1) * blk].astype(BF)
            part[places[p], :, :, cols] = block.reshape(4, blk // 4, 512)

    ring_f.start()

    def grad_down(t, c):
        cols = pl.ds(pl.multiple_of(t * 512 + c * 256, 256), 256)
        return dot(act[:, cols], dyg[...].reshape(span, width), TN)

    def grad_up(t, c):
        cols = pl.ds(pl.multiple_of(t * 512 + c * 256, 256), 256)
        return dot(a2g[:, :, cols].reshape(span, 256), dup[...], TN)

    def swap_down(t):
        return remote(wdn.at[t, other], dn_c.at[t], sems, 16 + t, peer(core=1))

    def swap_up(t):
        return remote(wup.at[t, other], up_c.at[t], sems, 20 + t, peer(core=1))

    c_u.drain()
    pl.semaphore_wait(free_sem, 1)

    @pl.loop(0, 4)
    def _(t):
        wup[t, other] = grad_up(t, other).astype(BF).reshape(4, 64, hidden)
        swap_up(t).start()

    c_ring = group(34)

    def ring_sums(w, tmp_a, tmp_b, got_a, got_b):
        return (
            RingSum(c_ring, "z", lambda o, h: w.at[pl.ds(2 * h, 2), core, o, low], tmp_a, got_a),
            RingSum(c_ring, "y", lambda o, h: w.at[o, core, pl.ds(2 * h, 2), high], tmp_b, got_b),
        )

    up_sums = ring_sums(wup, ring_tmp.at[2], ring_tmp.at[3], up_got.at[0], up_got.at[1])
    down_sums = ring_sums(wdn, ring_tmp.at[4], ring_tmp.at[5], dn_a_got, dn_b_got)

    @pl.loop(0, 4)
    def _(t):
        swap_up(t).wait_recv()
        total = grad_up(t, core) + up_c[t].reshape(256, hidden).astype(F32)
        wup[t, core] = total.astype(BF).reshape(4, 64, hidden)

    for total in up_sums:
        total.start()

    @pl.loop(0, 4)
    def _(j):
        cols = pl.ds(pl.multiple_of(j * 512, 512), 512)
        o = dot(act[...], wdn[:, :, :, :, cols].reshape(hidden, 512), NN)
        dup[:, cols] = o.astype(BF)

    keep_out = pltpu.make_async_copy(dup, outp_hbm, local_sem.at[0])
    keep_out.start()
    ring_f.middle()

    c_d.drain()

    @pl.loop(0, 4)
    def _(t):
        wdn[t, other] = grad_down(t, other).astype(BF).reshape(4, 64, width)
        swap_down(t).start()

    for total in up_sums:
        total.middle()

    @pl.loop(0, 4)
    def _(t):
        swap_down(t).wait_recv()
        total = grad_down(t, core) + dn_c[t].reshape(256, width).astype(F32)
        wdn[t, core] = total.astype(BF).reshape(4, 64, width)

    for total in down_sums:
        total.start()

    ring_f.finish()
    small_out[0:3, :] = jnp.zeros((3, width), F32)
    small_out[4:8, :] = jnp.zeros((4, width), F32)
    gain = vec_o[4:5, :]

    @pl.loop(0, blk // 16)
    def _(i):
        rows = pl.ds(pl.multiple_of(i * 16, 16), 16)
        d = dact[rows, :]
        c, r = i // 2, pl.ds(pl.multiple_of(lax.rem(i, 2) * 16, 16), 16)
        for g in range(2):
            d = d + got[g, c, r, :].astype(F32)
        v = res_o[rows, :]
        centred = v - jnp.mean(v, axis=-1, keepdims=True)
        s = lax.rsqrt(jnp.mean(centred * centred, axis=-1, keepdims=True) + EPSILON)
        n = centred * s
        dn = d * gain
        d_res = s * (
            dn
            - jnp.mean(dn, axis=-1, keepdims=True)
            - n * jnp.mean(dn * n, axis=-1, keepdims=True)
        )
        dy_own = dy_in[rows, :].astype(F32)
        hid = dy_own + d_res
        low_hid = hid.astype(BF)
        dhid_out[rows, :] = hid
        dattn[x, rows, :] = low_hid
        small_out[0:1, :] += jnp.sum(d * n, axis=0, keepdims=True)
        small_out[1:2, :] += jnp.sum(d, axis=0, keepdims=True)
        small_out[2:3, :] += jnp.sum(low_hid.astype(F32), axis=0, keepdims=True)
        small_out[4:5, :] += jnp.sum(dy_own, axis=0, keepdims=True)

    attn = Relay(
        comm, "x", lambda o: dattn.at[o], lambda o, h: dattn.at[o, pl.ds(h * blk // 2, blk // 2)]
    )
    attn.start()
    comm.local(dattn.at[x], dattn_hbm.at[x])
    for total in up_sums:
        total.finish()
    for c in range(4):
        a, b = wup[c, core, z, low].astype(F32), wup[y, core, c, high].astype(F32)
        for g in range(2):
            a, b = a + up_got[0, g, c].astype(F32), b + up_got[1, g, c].astype(F32)
        wup[c, core, z, low], wup[y, core, c, high] = a.astype(BF), b.astype(BF)
    for k in (1, 3, 2):
        ty, tz = lax.rem(y + k, 4), lax.rem(z + k, 4)
        c_ring.push(wup.at[ty, core, z, low], up_two.at[0, k - 1], peer(y=k))
        c_ring.push(wup.at[y, core, tz, high], up_two.at[1, k - 1], peer(z=k))
    c_ring.local(wup.at[y, core, z, low], up_mine.at[0])
    c_ring.local(wup.at[y, core, z, high], up_mine.at[1])
    comm.local(dhid_out, dhid_h)
    kept = [keep_out]
    kept.append(pltpu.make_async_copy(wdn.at[:, core, z, low], dn_a_own, local_sem.at[2]))
    kept.append(pltpu.make_async_copy(wdn.at[y, core, :, high], dn_b_own, local_sem.at[3]))
    for copy in kept[1:]:
        copy.start()
    for total in down_sums:
        total.middle()
    attn.near()
    for k in (1, 3):
        o = lax.rem(x + k, 4)
        comm.local(dattn.at[o], dattn_hbm.at[o])
    attn.far()
    o = lax.rem(x + 2, 4)
    comm.local(dattn.at[o], dattn_hbm.at[o])

    for total in up_sums + down_sums:
        total.finish()

    @pl.loop(0, 4)
    def _(j):
        swap_down(j).wait_send()
        swap_up(j).wait_send()

    for copy in kept:
        copy.wait()
    for done in groups:
        done.drain()


def forward(collective_id, lengths, tok, small, w_up, dy, w_down, w_qkv, w_out):
    blk, width = tok.shape
    span, partw, hidden = 4 * blk, width // 4, w_up.shape[1] // 4
    vmem = pl.BlockSpec(memory_space=pltpu.VMEM)
    hbm = pl.BlockSpec(memory_space=pl.ANY)
    quarter = (4, 32, width)
    outs = [
        ((8, width), F32, vmem),
        ((blk, width), F32, hbm),
        ((blk, width), F32, hbm),
        ((8, width), F32, vmem),
        ((2, 4, 4, 64, 3 * partw), BF, hbm),
        ((2, 4, 4, 16, width), BF, hbm),
        ((span, width), BF, hbm),
        ((span, partw), BF, hbm),
        ((span + W, 2 * partw), BF, hbm),
        ((span, partw), BF, hbm),
        ((4, blk, width), BF, hbm),
        ((span, width), BF, hbm),
    ]
    outs += [((2, 32, width), BF, hbm), ((2, 3, 32, width), BF, hbm)]
    outs += [(quarter, BF, hbm)] * 2 + [((2,) + quarter, BF, hbm)] * 2
    scratch = [
        ((4, 2, 4, 64, hidden), BF),
        ((4, 2, 4, 64, width), BF),
        ((2, 4, 4, 64, width), BF),
        ((2, 4, 4, 16, width), BF),
        ((4, blk, width), BF),
        ((span, hidden), BF),
        ((span, hidden), BF),
        ((span, hidden), F32),
        ((span, partw), BF),
        ((span + W, 2 * partw), BF),
        ((span, partw), BF),
        ((4, blk, width), BF),
        ((4, 4, blk // 4, width), BF),
        ((2, 4, blk // 4, width), BF),
        ((4, blk, width), BF),
        ((4, 2, 128, 128), F32),
        ((hidden // 8, 512), BF),
        ((4, 16, hidden), BF),
        ((6, 2, 2, 32, width), BF),
        ((2, 2) + quarter, BF),
        ((blk, width), F32),
        ((blk, width), F32),
    ]
    return pl.pallas_call(
        forward_body,
        out_shape=tuple(jax.ShapeDtypeStruct(s, d) for s, d, _ in outs),
        in_specs=[pl.BlockSpec(memory_space=pltpu.SMEM)] + [vmem] * 7,
        out_specs=tuple(o[2] for o in outs),
        scratch_shapes=[pltpu.VMEM(s, d) for s, d in scratch]
        + [pltpu.SemaphoreType.DMA((8,)), pltpu.SemaphoreType.REGULAR]
        + [pltpu.SemaphoreType.DMA((n,)) for n in (40, 40, SEMS, SEMS)],
        compiler_params=pltpu.CompilerParams(
            collective_id=collective_id, has_side_effects=True, vmem_limit_bytes=63 << 20
        ),
        name="forward",
    )(lengths, tok, small, w_up, dy, w_down, w_qkv, w_out)


def norm_backward(d, v, gain):
    centred = v - jnp.mean(v, axis=-1, keepdims=True)
    s = lax.rsqrt(jnp.mean(centred * centred, axis=-1, keepdims=True) + EPSILON)
    n = centred * s
    dn = d * gain
    d_v = s * (
        dn - jnp.mean(dn, axis=-1, keepdims=True) - n * jnp.mean(dn * n, axis=-1, keepdims=True)
    )
    return d_v, n


def attention_backward_body(
    lengths,
    vec_in,
    ffsmall_in,
    dattn_hbm,
    wout_hbm,
    q_hbm,
    kv_hbm,
    a1_hbm,
    mixed_hbm,
    wqkv_hbm,
    tok_hbm,
    dhid_hbm,
    res_hbm,
    outp_hbm,
    up_mine,
    up_two,
    ffo2,
    ffo3,
    ffg2,
    ffg3,
    out_h,
    gtok_h,
    gqkv_o,
    gout_o,
    gup_o,
    gdn_o,
    small_o,
    late_o,
    dattn,
    wout,
    q_all,
    kv,
    a1,
    mixed,
    wqkv,
    tok,
    dhid,
    res,
    outown,
    outgot,
    fo,
    fg,
    fs,
    fg2,
    fmine,
    fup,
    fdn,
    dmix,
    dkv,
    dqkv,
    dedge,
    dedge_got,
    part,
    got,
    qkv_c,
    out_c,
    qa,
    qb,
    oa,
    ob,
    qs,
    os_,
    qa2,
    qb2,
    oa2,
    ob2,
    fq,
    fout,
    sm,
    smc,
    smz,
    smy,
    late,
    late_c,
    late_p,
    late_sum,
    gux,
    stack,
    gq,
    part_tmp,
    q_tmp,
    o_tmp,
    out_o,
    gtok_o,
    local_sem,
    send_sem,
    recv_sem,
    comm_send,
    comm_recv,
):
    sems = (send_sem, recv_sem)
    comm = Comm(comm_send, comm_recv, 0, 32)
    me = coords()
    x, y, z, core = me["x"], me["y"], me["z"], me["core"]
    other = 1 - core
    zy = lax.rem(y + 3, 4)
    blk, width = tok.shape
    span = 4 * blk
    partw = mixed.shape[1]
    heads = partw // HEAD
    scale = 1.0 / math.sqrt(HEAD)
    reach = W + blk
    used = [0]
    pending = []

    def load(src, dst):
        copy = pltpu.make_async_copy(src, dst, local_sem.at[used[0]])
        used[0] += 1
        copy.start()
        return copy

    def push(src, dst, index, to):
        copy = remote(src, dst, sems, index, to)
        copy.start()
        pending.append(copy)
        return copy

    l_dattn, l_wout = load(dattn_hbm, dattn), load(wout_hbm, wout)
    l_attn = [load(q_hbm, q_all), load(kv_hbm, kv)]
    low, high = slice(0, 32), slice(32, 64)
    l_ff = [load(s, fo.at[i]) for i, s in enumerate((ffo2, ffo3))]
    l_ff += [load(s, fg.at[i]) for i, s in enumerate((ffg2, ffg3))]
    l_up = [load(up_two, fg2.at[pl.ds(0, 2)]), load(up_mine, fmine)]
    l_wqkv, l_a1, l_mixed = load(wqkv_hbm, wqkv), load(a1_hbm, a1), load(mixed_hbm, mixed)
    l_end = [load(outp_hbm.at[pl.ds(0, blk)], outown), load(res_hbm, res)]
    l_end += [load(tok_hbm, tok), load(dhid_hbm, dhid)]

    greet(ring("x") + plane() + near() + [scattered(), collected()])

    p_out = [
        push(outp_hbm.at[pl.ds(p * blk, blk)], outgot.at[p - 1], p, peer(x=-ORDER[p])) for p in (1, 2, 3)
    ]

    def ff_sum(i):
        for c in range(4):
            total = fo[i, c].astype(F32) + fg[i, 0, c].astype(F32) + fg[i, 1, c].astype(F32)
            fs[i, c] = total.astype(BF)

    p_ff = []

    def ff_second(i):
        axis, here = ("y", y) if i == 0 else ("z", z)
        for k in (1, 3, 2):
            src = fs.at[i, lax.rem(here + k, 4)]
            p_ff.append(push(src, fg2.at[2 + i, k - 1], 4 + 3 * i + k, peer(**{axis: k})))

    for copy in l_ff:
        copy.wait()
    ff_sum(0)
    ff_sum(1)
    ff_second(0)

    dkv[...] = jnp.zeros(dkv.shape, F32)
    l_dattn.wait()
    l_wout.wait()
    dmix[...] = dot(
        dattn[...].reshape(span, width), wout[...].reshape(partw, width), NT
    ).astype(BF)
    for copy in l_attn:
        copy.wait()

    def block(b):
        rows = pl.ds(pl.multiple_of(b * blk, blk), blk)
        window = pl.ds(pl.multiple_of(b * blk, blk), reach)
        mask = mask_of(lengths, z * span + b * blk, blk, reach)
        for h in range(heads):
            cols = pl.ds(h * HEAD, HEAD)
            vcols = pl.ds(partw + h * HEAD, HEAD)
            q, k, v = q_all[rows, cols], kv[window, cols], kv[window, vcols]
            s = dot(q, k, NT) * scale + mask
            e = jnp.exp(s - jnp.max(s, axis=-1, keepdims=True))
            p = e * (1.0 / jnp.sum(e, axis=-1, keepdims=True))
            do = dmix[rows, cols]
            dp = dot(do, v, NT)
            ds = (p * (dp - jnp.sum(dp * p, axis=-1, keepdims=True))).astype(BF)
            dqkv[rows, cols] = (dot(ds, k, NN) * scale).astype(BF)
            dkv[window, cols] += dot(ds, q, TN) * scale
            dkv[window, vcols] += dot(p.astype(BF), do, TN)

    pl.loop(0, 2)(block)
    dedge[...] = dkv[0:W, :].astype(BF)
    p_edge = push(dedge, dedge_got, 4, peer(z=3))

    ring_d = RingSum(comm, "x", lambda o, h: part.at[o, pl.ds(2 * h, 2)], part_tmp, got)
    qkv_sums = (
        RingSum(comm, "z", lambda o, h: gq.at[pl.ds(2 * h, 2), 0, o, low], q_tmp.at[0], qa),
        RingSum(comm, "y", lambda o, h: gq.at[o, 0, pl.ds(2 * h, 2), high], q_tmp.at[1], qb),
    )
    left, right = slice(0, width // 2), slice(width // 2, width)
    out_sums = (
        RingSum(
            comm, "z", lambda o, h: wout.at[core, pl.ds(2 * h, 2), o, :, left], o_tmp.at[0], oa
        ),
        RingSum(
            comm,
            "y",
            lambda o, h: wout.at[core, lax.rem(o + 3, 4), pl.ds(2 * h, 2), :, right],
            o_tmp.at[1],
            ob,
        ),
    )

    def grad_out(c):
        cols = pl.ds(pl.multiple_of(c * 256, 256), 256)
        return dot(mixed[:, cols], dattn[...].reshape(span, width), TN)

    l_mixed.wait()
    wout[other] = grad_out(other).astype(BF).reshape(4, 4, 16, width)
    p_oc = push(wout.at[other], out_c, 36, peer(core=1))

    pl.loop(2, 4)(block)
    p_oc.wait_recv()

    wout[core] = (
        grad_out(core) + out_c[...].reshape(256, width).astype(F32)
    ).astype(BF).reshape(4, 4, 16, width)
    for total in out_sums:
        total.start()
    p_edge.wait_recv()
    dqkv[0 : span - W, partw:] = dkv[W:span, :].astype(BF)
    dqkv[span - W :, partw:] = (dkv[span:, :] + dedge_got[...].astype(F32)).astype(BF)
    sm[0, 0:5, :] = ffsmall_in[0:5, :]
    sm[0, 5:8, :] = jnp.zeros((3, width), F32)
    sm[0, 7:8, 0 : 3 * partw] = jnp.sum(dqkv[...].astype(F32), axis=0, keepdims=True)
    p_sc = push(sm.at[0], smc, 53, peer(core=1))

    def grad_qkv(t, c):
        cols = pl.ds(pl.multiple_of(t * 512 + c * 256, 256), 256)
        return dot(a1[:, cols], dqkv[...], TN)

    def swap(t):
        return remote(gq.at[t, 1], qkv_c.at[t], sems, 32 + t, peer(core=1))

    l_a1.wait()

    @pl.loop(0, 4)
    def _(t):
        gq[t, 1] = grad_qkv(t, other).astype(BF).reshape(4, 64, 3 * partw)
        swap(t).start()

    @pl.loop(0, 4)
    def _(t):
        swap(t).wait_recv()
        total = grad_qkv(t, core) + qkv_c[t].reshape(256, 3 * partw).astype(F32)
        gq[t, 0] = total.astype(BF).reshape(4, 64, 3 * partw)

    for total in qkv_sums:
        total.start()
    for total in out_sums:
        total.middle()

    l_wqkv.wait()

    @pl.loop(0, 4)
    def _(j):
        cols = pl.ds(pl.multiple_of(j * 512, 512), 512)
        d = dot(dqkv[...], wqkv[:, j].reshape(512, 3 * partw), NT)
        part[:, :, :, cols] = d.astype(BF).reshape(4, 4, blk // 4, 512)

    ring_d.start()
    p_sc.wait_recv()
    sm[1] = sm[0] + smc[...]
    p_sz = [push(sm.at[1], smz.at[k - 1], 59 + k, peer(z=k)) for k in (1, 3, 2)]
    for total in qkv_sums:
        total.middle()
    ff_second(1)
    ring_d.middle()
    for copy in p_sz:
        copy.wait_recv()
    sm[2] = sm[1] + smz[0] + smz[1] + smz[2]
    p_sy = [push(sm.at[2], smy.at[k - 1], 68 + k, peer(y=k)) for k in (1, 3, 2)]

    for copy in l_end:
        copy.wait()
    for copy in p_out:
        copy.wait_recv()

    @pl.loop(0, blk // 16)
    def _(i):
        rows = pl.ds(pl.multiple_of(i * 16, 16), 16)
        total = res[rows, :] + vec_in[7:8, :] + outown[rows, :].astype(F32)
        for g in range(3):
            total = total + outgot[g, rows, :].astype(F32)
        out_o[rows, :] = total.astype(BF)

    kept = [load(out_o, out_h)]

    for total in out_sums:
        total.finish()
    for c in range(4):
        ta, tb = wout[core, c, z, :, left].astype(F32), wout[core, zy, c, :, right].astype(F32)
        for g in range(2):
            ta, tb = ta + oa[g, c].astype(F32), tb + ob[g, c].astype(F32)
        os_[0, c], os_[1, c] = ta.astype(BF), tb.astype(BF)
    p_o2 = []
    for k in (1, 3, 2):
        tz, tyc = lax.rem(z + k, 4), lax.rem(y + k + 3, 4)
        p_o2.append(push(os_.at[0, tyc], oa2.at[k - 1], 62 + k, peer(y=k)))
        p_o2.append(push(os_.at[1, tz], ob2.at[k - 1], 65 + k, peer(z=k)))

    for total in qkv_sums:
        total.finish()
    for c in range(4):
        ta, tb = gq[c, 0, z, low].astype(F32), gq[y, 0, c, high].astype(F32)
        for g in range(2):
            ta, tb = ta + qa[g, c].astype(F32), tb + qb[g, c].astype(F32)
        qs[0, c], qs[1, c] = ta.astype(BF), tb.astype(BF)
    p_q2 = []
    for k in (1, 3, 2):
        tz, ty = lax.rem(z + k, 4), lax.rem(y + k, 4)
        p_q2.append(push(qs.at[0, ty], qa2.at[k - 1], 53 + k, peer(y=k)))
        p_q2.append(push(qs.at[1, tz], qb2.at[k - 1], 56 + k, peer(z=k)))

    late_sum[...] = jnp.zeros(late_sum.shape, F32)

    p_u, p_x = [], []
    for copy in p_sy:
        copy.wait_recv()
    sm[3] = sm[2] + smy[0] + smy[1] + smy[2]
    p_x += [push(sm.at[3], small_o.at[x], 71 + k, peer(x=k)) for k in (1, 3, 2)]
    kept.append(load(sm.at[3], small_o.at[x]))
    ring_d.finish()
    gain = vec_in[0:1, :]

    @pl.loop(0, blk // 16)
    def _(i):
        rows = pl.ds(pl.multiple_of(i * 16, 16), 16)
        c, r = i // 2, pl.ds(pl.multiple_of(lax.rem(i, 2) * 16, 16), 16)
        d = part[x, c, r, :].astype(F32)
        for g in range(2):
            d = d + got[g, c, r, :].astype(F32)
        d_in, n = norm_backward(d, tok[rows, :].astype(F32), gain)
        gtok_o[rows, :] = dhid[rows, :] + d_in
        late_sum[0:1, :] += jnp.sum(d * n, axis=0, keepdims=True)
        late_sum[1:2, :] += jnp.sum(d, axis=0, keepdims=True)

    kept.append(load(gtok_o, gtok_h))
    for i in range(8):
        at = (i % 4) * (width // 4)
        late[0, i : i + 1, :] = late_sum[i // 4 : i // 4 + 1, at : at + width // 4]
    p_lc = push(late.at[0], late_c, 52, peer(core=1))
    p_lc.wait_recv()
    late[1] = late[0] + late_c[...]
    p_lz = [push(late.at[1], late_p.at[i], 98 + i, to) for i, to in enumerate(plane())]

    for copy in p_ff:
        copy.wait_recv()
    for copy in l_up:
        copy.wait()
    for i in range(4):
        total = (fmine[i] if i < 2 else fs[i - 2, (y, z)[i - 2]]).astype(F32)
        for g in range(3):
            total = total + fg2[i, g].astype(F32)
        into, half = (fup, fdn)[i // 2], i % 2
        into[2 * half : 2 * half + 2] = total.astype(BF).reshape(2, 16, width)
    for k in (1, 3, 2):
        p_u.append(push(fup.at[lax.rem(x + k, 4)], gux.at[x], 48 + k, peer(x=k)))
        p_x.append(push(fdn.at[lax.rem(x + k, 4)], gdn_o.at[x], 76 + k, peer(x=k)))
    gux[x] = fup[x]
    kept.append(load(fdn.at[x], gdn_o.at[x]))
    for copy in p_o2:
        copy.wait_recv()
    ta, tb = os_[0, zy].astype(F32), os_[1, z].astype(F32)
    for g in range(3):
        ta, tb = ta + oa2[g].astype(F32), tb + ob2[g].astype(F32)
    fout[:, left], fout[:, right] = ta.astype(BF), tb.astype(BF)
    p_x.append(push(fout, gout_o, 75, collected()))

    for copy in p_q2:
        copy.wait_recv()
    ta, tb = qs[0, y].astype(F32), qs[1, z].astype(F32)
    for g in range(3):
        ta, tb = ta + qa2[g].astype(F32), tb + qb2[g].astype(F32)
    fq[0:2] = ta.astype(BF).reshape(2, 16, 3 * partw)
    fq[2:4] = tb.astype(BF).reshape(2, 16, 3 * partw)
    for k in (1, 3, 2):
        p_x.append(push(fq.at[lax.rem(x + k, 4)], gqkv_o.at[x], 82 + k, peer(x=k)))
    kept.append(load(fq.at[x], gqkv_o.at[x]))

    for copy in p_lz:
        copy.wait_recv()
    total = late[1]
    for i in range(15):
        total = total + late_p[i]
    late[2] = total
    p_x += [push(late.at[2], late_o.at[x], 79 + k, peer(x=k)) for k in (1, 3, 2)]
    kept.append(load(late.at[2], late_o.at[x]))

    for copy in p_u:
        copy.wait_recv()
    slabs = width // 128
    for i in range(slabs):
        for c in range(4):
            stack[16 * i : 16 * i + 16, 128 * c : 128 * c + 128] = gux[
                c, :, 128 * i : 128 * i + 128
            ]
    spread_up = dot(stack[...], shuffle(), NT)
    for i in range(slabs):
        gup_o[:, 512 * i : 512 * i + 512] = spread_up[16 * i : 16 * i + 16, :]

    for copy in p_x:
        copy.wait_recv()
    for copy in pending:
        copy.wait_send()

    @pl.loop(0, 4)
    def _(j):
        swap(j).wait_send()

    comm.drain()

    for copy in kept:
        copy.wait()


def attention_backward(
    collective_id,
    lengths,
    vectors,
    ff_small,
    d_attn,
    wout,
    q,
    kv,
    a1,
    mixed,
    wqkv,
    tok,
    d_hidden,
    residual,
    out_part,
    up_mine,
    up_two,
    ff_own,
    ff_got,
):
    blk, width = tok.shape
    span, partw = mixed.shape
    hidden = ff_own[0].shape[-1]
    vmem = pl.BlockSpec(memory_space=pltpu.VMEM)
    hbm = pl.BlockSpec(memory_space=pl.ANY)
    outs = [
        ((blk, width), BF, hbm),
        ((blk, width), F32, hbm),
        ((4, 16, 3 * partw), BF, hbm),
        ((16, width), BF, hbm),
        ((16, 4 * hidden), F32, vmem),
        ((4, 16, width), BF, hbm),
        ((4, 8, width), F32, hbm),
        ((4, 8, width // 4), F32, hbm),
    ]
    half = width // 2
    scratch = [
        ((4, blk, width), BF),
        ((2, 4, 4, 16, width), BF),
        ((span, partw), BF),
        ((span + W, 2 * partw), BF),
        ((span, width), BF),
        ((span, partw), BF),
        ((2, 4, 4, 64, 3 * partw), BF),
        ((blk, width), BF),
        ((blk, width), F32),
        ((blk, width), F32),
        ((blk, width), BF),
        ((3, blk, width), BF),
        ((2, 4, 32, width), BF),
        ((2, 2, 4, 32, width), BF),
        ((2, 4, 32, width), BF),
        ((4, 3, 32, width), BF),
        ((2, 32, width), BF),
        ((4, 16, hidden), BF),
        ((4, 16, width), BF),
        ((span, partw), BF),
        ((span + W, 2 * partw), F32),
        ((span, 3 * partw), BF),
        ((W, 2 * partw), BF),
        ((W, 2 * partw), BF),
        ((4, 4, blk // 4, width), BF),
        ((2, 4, blk // 4, width), BF),
        ((4, 4, 64, 3 * partw), BF),
        ((4, 4, 16, width), BF),
        ((2, 4, 32, 3 * partw), BF),
        ((2, 4, 32, 3 * partw), BF),
        ((2, 4, 16, half), BF),
        ((2, 4, 16, half), BF),
        ((2, 4, 32, 3 * partw), BF),
        ((2, 4, 16, half), BF),
        ((3, 32, 3 * partw), BF),
        ((3, 32, 3 * partw), BF),
        ((3, 16, half), BF),
        ((3, 16, half), BF),
        ((4, 16, 3 * partw), BF),
        ((16, width), BF),
        ((4, 8, width), F32),
        ((8, width), F32),
        ((3, 8, width), F32),
        ((3, 8, width), F32),
        ((3, 8, width // 4), F32),
        ((8, width // 4), F32),
        ((15, 8, width // 4), F32),
        ((2, width), F32),
        ((4, 16, hidden), BF),
        ((hidden // 8, 512), BF),
        ((4, 2, 4, 64, 3 * partw), BF),
        ((2, 2, blk // 4, width), BF),
        ((2, 2, 2, 32, 3 * partw), BF),
        ((2, 2, 2, 16, half), BF),
        ((blk, width), BF),
        ((blk, width), F32),
    ]
    return pl.pallas_call(
        attention_backward_body,
        out_shape=tuple(jax.ShapeDtypeStruct(s, d) for s, d, _ in outs),
        in_specs=[pl.BlockSpec(memory_space=pltpu.SMEM)] + [vmem] * 2 + [hbm] * 17,
        out_specs=tuple(o[2] for o in outs),
        scratch_shapes=[pltpu.VMEM(s, d) for s, d in scratch]
        + [
            pltpu.SemaphoreType.DMA((32,)),
            pltpu.SemaphoreType.DMA((114,)),
            pltpu.SemaphoreType.DMA((114,)),
            pltpu.SemaphoreType.DMA((32,)),
            pltpu.SemaphoreType.DMA((32,)),
        ],
        compiler_params=pltpu.CompilerParams(
            collective_id=collective_id, has_side_effects=True, vmem_limit_bytes=62 << 20
        ),
        name="attention_backward",
    )(
        lengths,
        vectors,
        ff_small,
        d_attn,
        wout,
        q,
        kv,
        a1,
        mixed,
        wqkv,
        tok,
        d_hidden,
        residual,
        out_part,
        up_mine,
        up_two,
        *ff_own,
        *ff_got,
    )


def results_body(
    out,
    gtok,
    gqkv,
    gout,
    gup,
    gdn,
    small,
    late,
    out_o,
    gtok_o,
    gain1_o,
    shift1_o,
    gqkv_o,
    bqv_o,
    gout_o,
    bout_o,
    gain2_o,
    shift2_o,
    gup_o,
    bup_o,
    gdn_o,
    bdown_o,
    sums,
):
    me = coords()
    device = ((me["y"] * 2 + me["core"]) * 4 + me["z"]) * 4 + me["x"]
    out_o[...] = out[...]
    gtok_o[...] = gtok[...]
    cut = gqkv.shape[2] // 3
    for g in range(3):
        for c in range(4):
            at = (4 * g + c) * cut
            gqkv_o[:, at : at + cut] = gqkv[c, :, g * cut : (g + 1) * cut].astype(F32)
    gout_o[...] = gout[...].astype(F32)
    gup_o[...] = gup[...]
    gdn_o[...] = gdn[...].reshape(gdn_o.shape).astype(F32)

    tile = pl.ds(pl.multiple_of(device // 8 * 128, 128), 128)
    turn = lax.rem(128 - 16 * lax.rem(device, 8), 128)
    shares = [pltpu.roll(small[i, :, tile], turn, 1) for i in range(4)]
    total = shares[0] + shares[1] + shares[2] + shares[3]
    gain2_o[...] = total[0:1, 0:16]
    shift2_o[...] = total[1:2, 0:16]
    bout_o[...] = total[2:3, 0:16]
    bdown_o[...] = total[4:5, 0:16]
    for i in range(4):
        bup_o[:, 16 * i : 16 * i + 16] = shares[i][3:4, 0:16]

    sums[...] = late[0] + late[1] + late[2] + late[3]
    place = lax.rem(device, 32)
    tile = pl.ds(pl.multiple_of(place // 8 * 128, 128), 128)
    turned = pltpu.roll(sums[:, tile], turn, 1)
    row = lax.broadcasted_iota(jnp.int32, turned.shape, 0)

    def only(i):
        return jnp.sum(jnp.where(row == i, turned, 0.0), axis=0, keepdims=True)[:, 0:16]

    gain1_o[...] = only(device // 32)
    shift1_o[...] = only(4 + device // 32)

    half, place = device // 64, lax.rem(device, 16)
    tile = pl.ds(pl.multiple_of(half * 1024 + place // 4 * 128, 128), 128)
    turn = lax.rem(128 - 32 * lax.rem(device, 4), 128)
    bqv_o[...] = pltpu.roll(small[lax.rem(device, 64) // 16, :, tile], turn, 1)[7:8, 0:32]


def results(*arrays):
    out, gtok, gqkv, gout, gup, gdn = arrays[:6]
    vmem = pl.BlockSpec(memory_space=pltpu.VMEM)
    rows, vector = gdn.shape[0] * gdn.shape[1], lambda n: ((1, n), F32)
    outs = [
        (out.shape, BF),
        (gtok.shape, F32),
        vector(16),
        vector(16),
        ((16, 4 * gqkv.shape[2]), F32),
        vector(32),
        (gout.shape, F32),
        vector(16),
        vector(16),
        vector(16),
        (gup.shape, F32),
        vector(64),
        ((rows, gdn.shape[2]), F32),
        vector(16),
    ]
    return pl.pallas_call(
        results_body,
        out_shape=tuple(jax.ShapeDtypeStruct(s, d) for s, d in outs),
        in_specs=[vmem] * 8,
        out_specs=(vmem,) * 14,
        scratch_shapes=[pltpu.VMEM(arrays[7].shape[1:], F32)],
        compiler_params=pltpu.CompilerParams(vmem_limit_bytes=40 << 20),
        name="results",
    )(*arrays)


def local(
    tokens,
    grad_out,
    lengths,
    ln1_gain,
    ln1_bias,
    w_qkv,
    b_qv,
    w_out,
    b_out,
    ln2_gain,
    ln2_bias,
    w_up,
    b_up,
    w_down,
    b_down,
):
    blk, width = tokens.shape[1:]
    part = width // 4
    hidden = w_up.shape[1] // 4
    tok = tokens.reshape(blk, width)
    dy = grad_out.reshape(blk, width)
    small = jnp.zeros((1024,), F32)
    vectors = (ln1_gain, ln1_bias, b_qv, b_out, ln2_gain, ln2_bias, b_up, b_down)
    for i, vector in enumerate(vectors):
        size = vector.shape[0]
        small = small + jnp.pad(vector.astype(F32), (i * 128, 1024 - i * 128 - size))
    (
        vectors,
        residual,
        d_hidden,
        ff_small,
        wqkv_g,
        wout_g,
        a1,
        query,
        kv,
        mixed,
        d_attn_g,
        out_part,
        up_mine,
        up_two,
        down_a_own,
        down_b_own,
        down_a_got,
        down_b_got,
    ) = forward(0, lengths, tok, small.reshape(8, 128), w_up, dy, w_down, w_qkv, w_out)
    last = attention_backward(
        1,
        lengths,
        vectors,
        ff_small,
        d_attn_g,
        wout_g,
        query,
        kv,
        a1,
        mixed,
        wqkv_g,
        tok,
        d_hidden,
        residual,
        out_part,
        up_mine,
        up_two,
        (down_a_own, down_b_own),
        (down_a_got, down_b_got),
    )

    final = list(results(*last))
    final[0] = final[0].reshape(1, blk, width)
    final[1] = final[1].reshape(1, blk, width)
    for i in (2, 3, 5, 7, 8, 9, 11, 13):
        final[i] = final[i].reshape(-1)
    return tuple(final)


def solution(mesh):
    fine = Mesh(mesh.devices.reshape(4, 2, 4, 4), AXES)
    rows, seq = ("y", "core"), ("z", "x")
    every = rows + seq
    token = P(rows, seq, None)
    vec, mat = P(every), P(every, None)
    in_specs = (token, token, P(rows, None), vec, vec, mat, vec, mat, vec, vec, vec, mat, vec, mat, vec)
    out_specs = (token, token, vec, vec, mat, vec, mat, vec, vec, vec, mat, vec, mat, vec)
    return jax.shard_map(local, mesh=fine, in_specs=in_specs, out_specs=out_specs, check_vma=False)
```
